32 devices in a mesh: section: 2 (over core), tensor: 2 (over x), dp: 8 (over z, y).
Axes of the slice: x: 2, y: 2, z: 4, core: 2. Of those that a mesh axis runs over, the one named last changes fastest.
Arguments:
- byte_states: bfloat16 [32, 1024, 1024], P('dp'), may hold values from -6 to 6
- patch_ids: int32 [32, 1024], P('dp'), may hold values from 0 to 255, as said below
- attn_in: bfloat16 [2, 3, 1024, 1024], P('section', None, None, 'tensor'), may hold values from -0.1875 to 0.1875
- attn_out: bfloat16 [2, 1024, 1024], P('section', 'tensor'), may hold values from -0.5 to 0.5
- gains: float32 [2, 2, 1024], P('section'), may hold values from 0.1 to 1.9
- ffn_in: bfloat16 [1024, 2, 2816], P(None, None, 'tensor'), may hold values from -0.1875 to 0.1875
- ffn_out: bfloat16 [2816, 1024], P('tensor'), may hold values from -0.109375 to 0.109375
- latent_grad: bfloat16 [32, 256, 1024], P('dp'), may hold values from -6 to 6
Outputs:
- latents: bfloat16 [32, 256, 1024], P('dp', 'section', 'tensor')
- byte_grad: bfloat16 [32, 1024, 1024], P('dp', 'tensor', 'section')
- grad_attn_in: float32 [2, 3, 1024, 1024], P('section', None, None, 'tensor')
- grad_attn_out: float32 [2, 1024, 1024], P('section', 'tensor')
- grad_gains: float32 [2, 2, 1024], P('section')
- grad_ffn_in: float32 [1024, 2, 2816], P('section', None, 'tensor')
- grad_ffn_out: float32 [2816, 1024], P('tensor', 'section')
The draws below stay inside these ranges and needn't reach their ends.
Inputs may be any that keep to these rules, and one draw needn't show every extreme that they name: `patch_ids`: in each sequence the ids start at 0 and rise by 0 or 1 from one byte to the next; a sequence has from 64 to 256 patches, and some sequence has exactly 256.
All inputs are finite; a program needn't handle non-finite values.
Results may differ from the reference program's by a relative error of at most 0.023.
Values may be sent and summed in bfloat16 or wider, within the bound.
A program may use at most 512 MiB of HBM per device.

```python
import jax
import jax.numpy as jnp
from jax import lax

D = 1024
H = 16
HD = 64
FF = 2816
LEN = 1024
PCAP = 256
SEQS = 32


def draw_patch_ids(key, part):
    key = jax.random.fold_in(key, 7)
    count_key, pick_key, shuffle_key = jax.random.split(key, 3)
    patch_totals = jax.random.randint(count_key, (SEQS,), LEN // 16, PCAP + 1)
    widest = jax.random.randint(pick_key, (), 0, SEQS)
    patch_totals = jnp.where(jnp.arange(SEQS) == widest, PCAP, patch_totals)

    def one_sequence(shuffle_seed, total_count):
        shuffled = jax.random.permutation(shuffle_seed, LEN - 1)
        rank_of = jnp.zeros((LEN - 1,), jnp.int32).at[shuffled].set(jnp.arange(LEN - 1, dtype=jnp.int32))
        boundary = (rank_of < total_count - 1).astype(jnp.int32)
        return jnp.concatenate([jnp.zeros((1,), jnp.int32), jnp.cumsum(boundary).astype(jnp.int32)])
    return jax.vmap(one_sequence)(jax.random.split(shuffle_key, SEQS), patch_totals)


def levels(rng, extent, cuts, smallest, top_value):
    def one(dim, blocks):
        heights = jax.random.uniform(jax.random.fold_in(jax.random.fold_in(rng, 6), dim), (blocks,), jnp.float32, smallest / len(cuts), top_value / len(cuts))
        return jnp.repeat(jnp.exp(heights), extent[dim] // blocks).reshape((-1,) + (1,) * (len(extent) - dim - 1))

    gain = one(*cuts[0])
    for cut in cuts[1:]:
        gain = gain * one(*cut)
    return gain


def scatter_about(own_key, shape, scale, reach, pieces=(), held_as=jnp.bfloat16):
    entries = scale * jax.random.normal(own_key, shape, jnp.float32)
    if pieces:
        entries = entries * levels(own_key, shape, pieces, -0.22, 0.18)
    return jnp.clip(entries, -reach, reach).astype(held_as)


def setup_inputs(seed: int = 0) -> dict:
    arg_keys = jax.random.split(jax.random.key(seed), 9)
    return {
        "byte_states": scatter_about(arg_keys[0], (SEQS, LEN, D), 1.0, 6.0, ((0, 8),)),
        "patch_ids": draw_patch_ids(jax.random.fold_in(arg_keys[8], 71), 0),
        "attn_in": scatter_about(arg_keys[2], (2, 3, D, D), D ** -0.5, 0.1875, ((0, 2), (3, 2))),
        "attn_out": scatter_about(arg_keys[3], (2, D, D), (D // 8) ** -0.5, 0.5, ((0, 2), (1, 2))),
        "gains": jnp.clip(1.0 + 0.18 * jax.random.normal(arg_keys[4], (2, 2, D), jnp.float32), 0.1, 1.9),
        "ffn_in": scatter_about(arg_keys[5], (D, 2, FF), D ** -0.5, 0.1875, ((2, 2),)),
        "ffn_out": scatter_about(arg_keys[6], (FF, D), FF ** -0.5, 0.109375, ((0, 2),)),
        "latent_grad": scatter_about(arg_keys[7], (SEQS, PCAP, D), 1.0, 6.0, ((0, 8),)),
    }


EPSILON = 1e-05
NEGATIVE = -1000000000.0
HIGHEST_PRECISION = lax.Precision.HIGHEST

@jax.custom_vjp
def low(v):
    return lax.optimization_barrier(v.astype(jnp.bfloat16)).astype(jnp.float32)

@jax.custom_vjp
def low_back(v):
    return v

def low_keep(v):
    return (low(v), None)

def low_pass(kept, grad):
    return (grad,)

def back_keep(v):
    return (v, None)

def back_low(kept, grad):
    return (low(grad),)
low.defvjp(low_keep, low_pass)
low_back.defvjp(back_keep, back_low)

def rms_norm(values, gain_row):
    return values * lax.rsqrt(lax.optimization_barrier(jnp.mean(values * values, axis=-1, keepdims=True)) + EPSILON) * gain_row

def split_heads(values):
    return values.reshape(values.shape[0], H, HD).transpose(1, 0, 2)

def join_heads(values):
    return values.transpose(1, 0, 2).reshape(values.shape[1], H * HD)

def project(inputs, weight):
    return low(low_back(jnp.dot(inputs, weight, precision=HIGHEST_PRECISION)))

def attend(query_heads, key_heads, value_heads, allowed):
    scores = jnp.einsum('hqd,hkd->hqk', query_heads, key_heads, precision=HIGHEST_PRECISION) * HD ** (-0.5)
    scores = jnp.where(allowed[None], low_back(scores), NEGATIVE)
    highest = lax.optimization_barrier(jnp.max(scores, axis=-1, keepdims=True))
    raised = jnp.exp(scores - highest)
    weights = low(raised / lax.optimization_barrier(jnp.sum(raised, axis=-1, keepdims=True)))
    return join_heads(jnp.einsum('hqk,hkd->hqd', weights, value_heads, precision=HIGHEST_PRECISION))

def layers(states, ids_row, attn_in, attn_out, gains, ffn_in, ffn_out):
    slot_ids = jnp.arange(PCAP, dtype=jnp.int32)
    counts = jax.ops.segment_sum(jnp.ones((LEN,), states.dtype), ids_row, num_segments=PCAP)
    row_valid = (slot_ids <= ids_row[LEN - 1]).astype(states.dtype)[:, None]
    pooled = jax.ops.segment_sum(states, ids_row, num_segments=PCAP) / jnp.maximum(counts, 1.0)[:, None]
    query_in = low(rms_norm(pooled, gains[0, 0]))
    source_in = low(rms_norm(states, gains[0, 1]))
    member = ids_row[None, :] == slot_ids[:, None]
    cross = attend(split_heads(project(query_in, attn_in[0, 0])), split_heads(project(source_in, attn_in[0, 1])), split_heads(project(source_in, attn_in[0, 2])), member)
    cross = low(low_back(cross * row_valid))
    latent = low(low_back(pooled + low_back(jnp.dot(cross, attn_out[0], precision=HIGHEST_PRECISION))))
    normed = low(rms_norm(latent, gains[1, 0]))
    causal = slot_ids[None, :] <= slot_ids[:, None]
    mixed = attend(split_heads(project(normed, attn_in[1, 0])), split_heads(project(normed, attn_in[1, 1])), split_heads(project(normed, attn_in[1, 2])), causal)
    mixed = low(low_back(mixed))
    middle = latent + low_back(jnp.dot(mixed, attn_out[1], precision=HIGHEST_PRECISION))
    inner = low(rms_norm(middle, gains[1, 1]))
    gate_value = low_back(jnp.dot(inner, ffn_in[:, 0, :], precision=HIGHEST_PRECISION))
    up_value = low_back(jnp.dot(inner, ffn_in[:, 1, :], precision=HIGHEST_PRECISION))
    hidden = low(jax.nn.silu(gate_value) * up_value)
    return (middle + low_back(jnp.dot(hidden, ffn_out, precision=HIGHEST_PRECISION))) * row_valid

def reference(byte_states, patch_ids, attn_in, attn_out, gains, ffn_in, ffn_out, latent_grad):
    weights = (attn_in.astype(jnp.float32), attn_out.astype(jnp.float32), gains.astype(jnp.float32), ffn_in.astype(jnp.float32), ffn_out.astype(jnp.float32))

    def one_sequence(running, inputs):
        states16, ids_row, upstream16 = inputs

        def forward(states, *params):
            return layers(states, ids_row, *params)
        outputs, pull_back = jax.vjp(forward, states16.astype(jnp.float32), *weights)
        gradients = pull_back(upstream16.astype(jnp.float32))
        running = tuple((earlier + gradient for earlier, gradient in zip(running, gradients[1:])))
        return (running, (outputs.astype(jnp.bfloat16), gradients[0].astype(jnp.bfloat16)))
    start_totals = tuple((jnp.zeros(weight.shape, jnp.float32) for weight in weights))
    totals, (latents, byte_grad) = lax.scan(one_sequence, start_totals, (byte_states, patch_ids, latent_grad))
    return (latents, byte_grad, totals[0], totals[1], totals[2], totals[3], totals[4])
```

```python
import functools

import jax
import jax.numpy as jnp
from jax import lax
from jax.experimental import pallas as pl
from jax.experimental.pallas import tpu as pltpu
from jax.sharding import PartitionSpec as P

HD = 64
LANES = 128
BLOCK = 256
EPSILON = 1e-05
NEGATIVE = -1000000000.0
SCALE = HD ** (-0.5)
VMEM_BYTES = 56 * 1024 * 1024

f32 = jnp.float32
b16 = jnp.bfloat16


def dot(a, b):
    return jnp.dot(a, b, preferred_element_type=f32)


def dot_rt(a, b):
    return lax.dot_general(a, b, (((1,), (1,)), ((), ())), preferred_element_type=f32)


def dot_lt(a, b):
    return lax.dot_general(a, b, (((0,), (0,)), ((), ())), preferred_element_type=f32)


def inverse_rms(values):
    return lax.rsqrt(jnp.mean(values * values, axis=-1, keepdims=True) + EPSILON)


def norm_back(values, gain_row, upstream):
    inverse = inverse_rms(values)
    unit = values * inverse
    scaled = upstream * gain_row
    return (scaled - unit * jnp.mean(unit * scaled, axis=-1, keepdims=True)) * inverse, unit


def iota(shape, dim):
    return lax.broadcasted_iota(jnp.int32, shape, dim)


def one_hot(condition):
    return jnp.where(condition, 1.0, 0.0).astype(b16)


def head_sum(products, heads_in):
    high = products.astype(b16)
    low = (products - high.astype(f32)).astype(b16)
    return dot(high, heads_in) + dot(low, heads_in)


def spread_heads(small, heads_out):
    count, width = small.shape
    filled = jnp.concatenate([small, jnp.zeros((LANES - count, width), f32)], axis=0)
    return dot(filled.T.astype(b16), heads_out)


def scan_segments(values, ids, forward, combine, neutral):
    width = values.shape[1]
    lane = iota(ids.shape, 1)
    step = 1
    while step < width:
        shift = step if forward else width - step
        there = pltpu.roll(ids, shift, axis=1)
        inside = (lane >= step) if forward else (lane < width - step)
        same = jnp.logical_and(there == ids, inside)
        moved = pltpu.roll(values, shift, axis=1)
        values = combine(values, jnp.where(same, moved, neutral))
        step *= 2
    return values


def segment_max(values, ids):
    lowest = -3.0e38
    ahead = scan_segments(values, ids, True, jnp.maximum, lowest)
    return scan_segments(ahead, ids, False, jnp.maximum, lowest)


def segment_sum(values, ids):
    ahead = scan_segments(values, ids, True, jnp.add, 0.0)
    behind = scan_segments(values, ids, False, jnp.add, 0.0)
    return ahead + behind - values


def head_masks(width):
    heads_in = one_hot(iota((width, LANES), 0) // HD == iota((width, LANES), 1))
    heads_out = one_hot(iota((LANES, width), 1) // HD == iota((LANES, width), 0))
    return heads_in, heads_out


def each_block(count, body):
    @pl.loop(0, count // BLOCK)
    def _(index):
        body(pl.ds(pl.multiple_of(index * BLOCK, BLOCK), BLOCK))


def first_forward_kernel(
    states, id_row, id_col, wq, wk, wv, wo, gain,
    part, pooled, query_in, source_in, q, k, v, probs, mixed,
    pooled_sum, scores, mixed_sum,
):
    patches, width = pooled.shape
    byte_count = states.shape[0]
    columns = q.shape[1]
    heads = columns // HD
    heads_in, heads_out = head_masks(columns)
    pooled_sum[...] = jnp.zeros_like(pooled_sum)
    mixed_sum[...] = jnp.zeros_like(mixed_sum)

    def members(rows):
        return one_hot(iota((patches, BLOCK), 0) == id_row[:, rows])

    def project(rows):
        block = states[rows, :]
        pooled_sum[...] += dot(members(rows), block)
        values = block.astype(f32)
        normed = (values * inverse_rms(values) * gain[1:2, :]).astype(b16)
        source_in[rows, :] = normed
        k[rows, :] = dot(normed, wk[...]).astype(b16)
        v[rows, :] = dot(normed, wv[...]).astype(b16)

    each_block(byte_count, project)
    counts = jnp.sum(
        jnp.where(iota((patches, byte_count), 0) == id_row[...], 1.0, 0.0), axis=1, keepdims=True
    )
    pool = pooled_sum[...] / jnp.maximum(counts, 1.0)
    pooled[...] = pool
    normed_pool = (pool * inverse_rms(pool) * gain[0:1, :]).astype(b16)
    query_in[...] = normed_pool
    q[...] = dot(normed_pool, wq[...]).astype(b16)

    def score(rows):
        place = one_hot(id_col[rows, :] == iota((BLOCK, patches), 1))
        products = dot(place, q[...]) * k[rows, :].astype(f32)
        block_scores = head_sum(products, heads_in) * SCALE
        scores[:, rows] = block_scores.T[:heads, :]

    each_block(byte_count, score)
    ids = id_row[...]
    raised = jnp.exp(scores[...] - segment_max(scores[...], ids))
    probs[...] = raised / segment_sum(raised, ids)

    def mix(rows):
        weighted = spread_heads(probs[:, rows], heads_out) * v[rows, :].astype(f32)
        mixed_sum[...] += dot(members(rows), weighted.astype(b16))

    each_block(byte_count, mix)
    mixed16 = mixed_sum[...].astype(b16)
    mixed[...] = mixed16
    part[...] = dot(mixed16, wo[...]).astype(b16)


def second_attention_kernel(
    pooled, part_in, part_got, wq, wk, wv, wo, gain,
    latent, normed, q, k, v, totals, mixed, part,
):
    rows = pooled.shape[0]
    heads = q.shape[1] // HD
    latent16 = (pooled[...] + part_in[...].astype(f32) + part_got[...].astype(f32)).astype(b16)
    latent[...] = latent16
    values = latent16.astype(f32)
    normed16 = (values * inverse_rms(values) * gain[0:1, :]).astype(b16)
    normed[...] = normed16
    q[...] = dot(normed16, wq[...]).astype(b16)
    k[...] = dot(normed16, wk[...]).astype(b16)
    v[...] = dot(normed16, wv[...]).astype(b16)
    allowed = iota((rows, rows), 1) <= iota((rows, rows), 0)
    lane = iota((rows, LANES), 1)
    kept = jnp.zeros((rows, LANES), f32)
    outs = []
    for head in range(heads):
        own = slice(head * HD, (head + 1) * HD)
        scores = jnp.where(allowed, dot_rt(q[:, own], k[:, own]) * SCALE, NEGATIVE)
        highest = jnp.max(scores, axis=-1, keepdims=True)
        raised = jnp.exp(scores - highest)
        total = jnp.sum(raised, axis=-1, keepdims=True)
        outs.append(dot((raised / total).astype(b16), v[:, own]))
        kept = jnp.where(lane == head, highest + jnp.log(total), kept)
    totals[...] = kept
    mixed16 = jnp.concatenate(outs, axis=1).astype(b16)
    mixed[...] = mixed16
    part[...] = dot(mixed16, wo[...]).astype(b16)


def feed_forward_kernel(
    latent, part_in, part_got, upstream, gain, w_in, w_out,
    middle, inner, hidden, both_grad, out_part, inner_part,
    out_sum, inner_sum,
):
    step = pl.program_id(0)

    @pl.when(step == 0)
    def _():
        values = (
            latent[...].astype(f32) + part_in[...].astype(f32) + part_got[...].astype(f32)
        )
        middle[...] = values
        inner[...] = (values * inverse_rms(values) * gain[1:2, :]).astype(b16)
        out_sum[...] = jnp.zeros_like(out_sum)
        inner_sum[...] = jnp.zeros_like(inner_sum)

    both = dot(inner[...], w_in[...])
    gate = both[:, :LANES]
    up = both[:, LANES:]
    gated = 1.0 / (1.0 + jnp.exp(-gate))
    act = gate * gated
    hidden16 = (act * up).astype(b16)
    hidden[...] = hidden16
    out_sum[...] += dot(hidden16, w_out[...])
    hidden_grad = dot_rt(upstream[...], w_out[...])
    gate_grad = hidden_grad * up * (gated * (1.0 + gate * (1.0 - gated)))
    up_grad = hidden_grad * act
    grads = jnp.concatenate([gate_grad, up_grad], axis=1).astype(b16)
    both_grad[...] = grads
    inner_sum[...] += dot_rt(grads, w_in[...])

    @pl.when(step == pl.num_programs(0) - 1)
    def _():
        out_part[...] = out_sum[...]
        inner_part[...] = inner_sum[...].astype(b16)


def second_backward_kernel(
    middle, inner_part, inner_got, upstream, gain, q, k, v, totals, wq, wk, wv, wo,
    middle_grad, branch, dq, dk, dv, normed_part, gain_part,
):
    rows = middle.shape[0]
    heads = q.shape[1] // HD
    own_part = inner_part[...].astype(f32)
    back, unit = norm_back(middle[...], gain[1:2, :], own_part + inner_got[...].astype(f32))
    gain_part[...] = jnp.sum(unit * own_part, axis=0, keepdims=True)
    grad = upstream[...].astype(f32) + back
    middle_grad[...] = grad
    branch16 = grad.astype(b16)
    branch[...] = branch16
    mixed_grad = dot_rt(branch16, wo[...]).astype(b16)
    allowed = iota((rows, rows), 1) <= iota((rows, rows), 0)
    kept = totals[...]
    q_outs, k_outs, v_outs = [], [], []
    for head in range(heads):
        own = slice(head * HD, (head + 1) * HD)
        query, key, value, upper = q[:, own], k[:, own], v[:, own], mixed_grad[:, own]
        scores = jnp.where(allowed, dot_rt(query, key) * SCALE, NEGATIVE)
        probs = jnp.exp(scores - kept[:, head : head + 1])
        prob_grad = dot_rt(upper, value)
        delta = jnp.sum(probs * prob_grad, axis=-1, keepdims=True)
        score_grad = (probs * (prob_grad - delta)).astype(b16)
        q_outs.append(dot(score_grad, key) * SCALE)
        k_outs.append(dot_lt(score_grad, query) * SCALE)
        v_outs.append(dot_lt(probs.astype(b16), upper))
    q_grad = jnp.concatenate(q_outs, axis=1).astype(b16)
    k_grad = jnp.concatenate(k_outs, axis=1).astype(b16)
    v_grad = jnp.concatenate(v_outs, axis=1).astype(b16)
    dq[...] = q_grad
    dk[...] = k_grad
    dv[...] = v_grad
    normed_part[...] = (
        dot_rt(q_grad, wq[...]) + dot_rt(k_grad, wk[...]) + dot_rt(v_grad, wv[...])
    ).astype(b16)


def first_backward_kernel(
    latent, middle_grad, normed_part, normed_got, gain_up, gain, states, id_row, id_col, pooled,
    q, k, v, probs, wq, wk, wv, wo,
    branch, dq, dk, dv, query_part, source_part, gain_part,
    mixed_grad, scores, q_sum,
):
    patches, width = latent.shape
    byte_count = states.shape[0]
    columns = q.shape[1]
    heads = columns // HD
    heads_in, heads_out = head_masks(columns)
    own_part = normed_part[...].astype(f32)
    back, unit = norm_back(
        latent[...].astype(f32), gain_up[0:1, :], own_part + normed_got[...].astype(f32)
    )
    gain_part[0:1, :] = jnp.sum(unit * own_part, axis=0, keepdims=True)
    branch16 = (middle_grad[...] + back).astype(b16)
    branch[...] = branch16
    mixed_grad[...] = dot_rt(branch16, wo[...]).astype(b16)
    q_sum[...] = jnp.zeros_like(q_sum)

    def place(rows):
        return one_hot(id_col[rows, :] == iota((BLOCK, patches), 1))

    def value_side(rows):
        spread = dot(place(rows), mixed_grad[...])
        dv[rows, :] = (spread_heads(probs[:, rows], heads_out) * spread).astype(b16)
        sums = head_sum(spread * v[rows, :].astype(f32), heads_in)
        scores[:, rows] = sums.T[:heads, :]

    each_block(byte_count, value_side)
    ids = id_row[...]
    weights = probs[...]
    prob_grad = scores[...]
    scores[...] = weights * (prob_grad - segment_sum(weights * prob_grad, ids))
    gain_part[2:3, :] = jnp.zeros((1, width), f32)

    def key_side(rows):
        spread = spread_heads(scores[:, rows], heads_out)
        k_grad = (spread * dot(place(rows), q[...]) * SCALE).astype(b16)
        dk[rows, :] = k_grad
        members = one_hot(iota((patches, BLOCK), 0) == id_row[:, rows])
        q_sum[...] += dot(members, (spread * k[rows, :].astype(f32)).astype(b16))
        source = dot_rt(k_grad, wk[...]) + dot_rt(dv[rows, :], wv[...])
        source_part[rows, :] = source.astype(b16)
        values = states[rows, :].astype(f32)
        unit_block = values * inverse_rms(values)
        gain_part[2:3, :] += jnp.sum(unit_block * source, axis=0, keepdims=True)

    each_block(byte_count, key_side)
    q_grad = (q_sum[...] * SCALE).astype(b16)
    dq[...] = q_grad
    query = dot_rt(q_grad, wq[...])
    query_part[...] = query.astype(b16)
    pool = pooled[...]
    gain_part[1:2, :] = jnp.sum(pool * inverse_rms(pool) * query, axis=0, keepdims=True)


def byte_grad_kernel(
    branch, pooled, query_part, query_got, id_row, id_col, gain, states, source_part, source_got,
    out,
):
    patches, width = pooled.shape
    own_bytes = states.shape[0]
    byte_count = id_row.shape[1]
    query = query_part[...].astype(f32) + query_got[...].astype(f32)
    back, _ = norm_back(pooled[...], gain[0:1, :], query)
    counts = jnp.sum(
        jnp.where(iota((patches, byte_count), 0) == id_row[...], 1.0, 0.0), axis=1, keepdims=True
    )
    pool_grad = (branch[...].astype(f32) + back) / jnp.maximum(counts, 1.0)
    high = pool_grad.astype(b16)
    low = (pool_grad - high.astype(f32)).astype(b16)

    def finish(rows):
        place = one_hot(id_col[rows, :] == iota((BLOCK, patches), 1))
        spread = dot(place, high) + dot(place, low)
        source = source_part[rows, :].astype(f32) + source_got[rows, :].astype(f32)
        own, _ = norm_back(states[rows, :].astype(f32), gain[1:2, :], source)
        out[rows, :] = (own + spread).astype(b16)

    each_block(own_bytes, finish)


def shape(dims, dtype):
    return jax.ShapeDtypeStruct(dims, dtype)


def run(kernel, outs, args, scratch=(), flops=0):
    moved = sum(a.size * a.dtype.itemsize for a in args)
    moved += sum(o.size * o.dtype.itemsize for o in outs)
    whole = pl.BlockSpec(memory_space=pltpu.VMEM)
    return pl.pallas_call(
        kernel,
        out_shape=tuple(outs),
        in_specs=[whole] * len(args),
        out_specs=tuple([whole] * len(outs)),
        scratch_shapes=list(scratch),
        compiler_params=pltpu.CompilerParams(vmem_limit_bytes=VMEM_BYTES),
        cost_estimate=pl.CostEstimate(flops=flops, bytes_accessed=moved, transcendentals=0),
    )(*args)


def first_forward(states, ids, weights, w_out, gain):
    byte_count, width = states.shape
    patches = byte_count // 4
    columns = weights.shape[-1]
    heads = columns // HD
    outs = [
        shape((patches, width), b16),
        shape((patches, width), f32),
        shape((patches, width), b16),
        shape((byte_count, width), b16),
        shape((patches, columns), b16),
        shape((byte_count, columns), b16),
        shape((byte_count, columns), b16),
        shape((heads, byte_count), f32),
        shape((patches, columns), b16),
    ]
    scratch = [
        pltpu.VMEM((patches, width), f32),
        pltpu.VMEM((heads, byte_count), f32),
        pltpu.VMEM((patches, columns), f32),
    ]
    args = (states, ids[None, :], ids[:, None], weights[0], weights[1], weights[2], w_out, gain)
    flops = 2 * byte_count * width * columns * 3
    return run(first_forward_kernel, outs, args, scratch, flops)


def second_attention(pooled, part, got, weights, w_out, gain):
    patches, width = pooled.shape
    columns = weights.shape[-1]
    outs = [
        shape((patches, width), b16),
        shape((patches, width), b16),
        shape((patches, columns), b16),
        shape((patches, columns), b16),
        shape((patches, columns), b16),
        shape((patches, LANES), f32),
        shape((patches, columns), b16),
        shape((patches, width), b16),
    ]
    args = (pooled, part, got, weights[0], weights[1], weights[2], w_out, gain)
    return run(second_attention_kernel, outs, args, (), 2 * patches * width * columns * 6)


def feed_forward(latent, part, got, upstream, gain, w_in, w_out):
    patches, width = latent.shape
    hidden = w_out.shape[0]
    steps = hidden // LANES

    def fixed(dims):
        return pl.BlockSpec(dims, lambda i: (0, 0))

    rows = fixed((patches, width))
    outs = (
        shape((patches, width), f32),
        shape((patches, width), b16),
        shape((patches, hidden), b16),
        shape((patches, 2 * hidden), b16),
        shape((patches, width), f32),
        shape((patches, width), b16),
    )
    return pl.pallas_call(
        feed_forward_kernel,
        grid=(steps,),
        out_shape=outs,
        in_specs=[
            rows, rows, rows, rows, fixed(gain.shape),
            pl.BlockSpec((width, 2 * LANES), lambda i: (0, i)),
            pl.BlockSpec((LANES, width), lambda i: (i, 0)),
        ],
        out_specs=(
            rows, rows,
            pl.BlockSpec((patches, LANES), lambda i: (0, i)),
            pl.BlockSpec((patches, 2 * LANES), lambda i: (0, i)),
            rows, rows,
        ),
        scratch_shapes=[pltpu.VMEM((patches, width), f32), pltpu.VMEM((patches, width), f32)],
        compiler_params=pltpu.CompilerParams(
            vmem_limit_bytes=VMEM_BYTES, dimension_semantics=("arbitrary",)
        ),
        cost_estimate=pl.CostEstimate(
            flops=2 * patches * width * hidden * 6,
            bytes_accessed=hidden * width * 6 + patches * width * 40,
            transcendentals=0,
        ),
    )(latent, part, got, upstream, gain, w_in, w_out)


def second_backward(middle, part, got, upstream, gain, kept, weights, w_out):
    patches, width = middle.shape
    columns = weights.shape[-1]
    outs = [
        shape((patches, width), f32),
        shape((patches, width), b16),
        shape((patches, columns), b16),
        shape((patches, columns), b16),
        shape((patches, columns), b16),
        shape((patches, width), b16),
        shape((1, width), f32),
    ]
    args = (middle, part, got, upstream, gain, *kept, weights[0], weights[1], weights[2], w_out)
    return run(second_backward_kernel, outs, args, (), 2 * patches * width * columns * 6)


def first_backward(latent, middle_grad, part, got, gain_up, gain, states, ids, kept, weights, w_out):
    patches, width = latent.shape
    byte_count = states.shape[0]
    columns = weights.shape[-1]
    heads = columns // HD
    outs = [
        shape((patches, width), b16),
        shape((patches, columns), b16),
        shape((byte_count, columns), b16),
        shape((byte_count, columns), b16),
        shape((patches, width), b16),
        shape((byte_count, width), b16),
        shape((3, width), f32),
    ]
    scratch = [
        pltpu.VMEM((patches, columns), b16),
        pltpu.VMEM((heads, byte_count), f32),
        pltpu.VMEM((patches, columns), f32),
    ]
    pooled, q, k, v, probs = kept
    args = (
        latent, middle_grad, part, got, gain_up, gain, states, ids[None, :], ids[:, None], pooled,
        q, k, v, probs, weights[0], weights[1], weights[2], w_out,
    )
    flops = 2 * byte_count * width * columns * 3
    return run(first_backward_kernel, outs, args, scratch, flops)


def byte_gradient(branch, pooled, part, got, ids, own_ids, gain, states, source, source_got):
    args = (
        branch, pooled, part, got, ids[None, :], own_ids[:, None], gain, states, source, source_got,
    )
    (out,) = run(byte_grad_kernel, [shape(states.shape, b16)], args, (), 10**9)
    return out


def rows_at(values, start, count, axis=0):
    return lax.dynamic_slice_in_dim(values, start, count, axis)


def swap(values, axis):
    return lax.ppermute(values, axis, [(0, 1), (1, 0)])


def add(a, b):
    return (a.astype(f32) + b.astype(f32)).astype(b16)


def pick(values, index):
    return lax.dynamic_index_in_dim(values, index, 0, keepdims=False)


LONG, SHORT = 4, 2


class Grid:
    def __init__(self, sections):
        self.sections = sections
        place = lax.axis_index("dp")
        self.z = place // SHORT
        self.y = place % SHORT

    def send(self, values, moves):
        count = LONG * SHORT
        pairs = [(s * count + a, s * count + b) for s in self.sections for a, b in moves]
        return lax.ppermute(values, ("section", "dp"), pairs)

    def along(self, values, by, senders):
        moves = [
            (z * SHORT + y, (z + by) * SHORT + y) for z in senders for y in range(SHORT)
        ]
        return self.send(values, moves)

    def across(self, values):
        return self.send(values, [(i, i ^ 1) for i in range(LONG * SHORT)])

    def scatter_long(self, values):
        parts = values.reshape(LONG, -1, values.shape[-1])
        total = pick(parts, self.z)
        for by in (1, -1):
            running = pick(parts, (self.z - by) % LONG)
            for step in range(1, LONG):
                senders = range(0, step) if by > 0 else range(LONG - step, LONG)
                got = self.along(running, by, senders)
                if step < LONG - 1:
                    running = add(got, pick(parts, (self.z - by * (step + 1)) % LONG))
            total = add(total, got)
        return total

    def gather_long(self, value):
        full = jnp.zeros((LONG, *value.shape), value.dtype)
        full = lax.dynamic_update_index_in_dim(full, value, self.z, 0)
        for by in (1, -1):
            running = value
            for step in range(1, LONG):
                senders = range(step - 1, LONG - 1) if by > 0 else range(1, LONG - step + 1)
                running = self.along(running, by, senders)
                place = self.z - by * step
                inside = jnp.logical_and(place >= 0, place < LONG)
                spot = place % LONG
                current = pick(full, spot)
                full = lax.dynamic_update_index_in_dim(
                    full, jnp.where(inside, running, current), spot, 0
                )
        return full.reshape(-1, value.shape[-1])

    def scatter_short(self, values):
        parts = values.reshape(SHORT, -1, values.shape[-1])
        got = self.across(pick(parts, 1 - self.y))
        return add(got, pick(parts, self.y))

    def gather_short(self, value):
        got = self.across(value)
        low = jnp.where(self.y == 0, value, got)
        high = jnp.where(self.y == 0, got, value)
        return jnp.concatenate([low, high], axis=0)

    def long_first(self, values):
        mine = self.scatter_long(values)
        return self.gather_long(add(mine, self.across(mine)))

    def short_first(self, values):
        return self.gather_short(self.gather_long(self.scatter_long(self.scatter_short(values))))


def sum_over_groups(values, sections):
    if lax.axis_size("dp") == 1:
        return values
    if lax.axis_size("dp") != LONG * SHORT:
        return lax.psum(values, "dp")
    grid = Grid(sections)
    cut = values.shape[0] // 2
    return jnp.concatenate([grid.long_first(values[:cut]), grid.short_first(values[cut:])], axis=0)


def sum_small(values):
    values = values + swap(values, "tensor")
    values = values + swap(values, "section")
    if lax.axis_size("dp") != LONG * SHORT:
        return lax.psum(values, "dp")
    for apart in (1, 2, 4):
        values = values + lax.ppermute(
            values, "dp", [(i, i ^ apart) for i in range(LONG * SHORT)]
        )
    return values


def weight_grad(inputs, upstream):
    return jnp.einsum("rd,rc->dc", inputs, upstream, preferred_element_type=f32).astype(b16)


def per_device(byte_states, patch_ids, attn_in, attn_out, gains, ffn_in, ffn_out, latent_grad):
    sequences, byte_count, width = byte_states.shape
    patches = byte_count // 4
    columns = attn_in.shape[-1]
    hidden = ffn_out.shape[0]
    chunks = hidden // LANES
    own_count = sequences // 2
    own_bytes = byte_count // 2
    half_rows = patches // 2
    half_width = width // 2
    section = lax.axis_index("section")
    tensor = lax.axis_index("tensor")
    is_first = section == 0

    def both_layers(mine):
        other = swap(mine, "section")
        return jnp.where(is_first, mine, other), jnp.where(is_first, other, mine)

    first_in, second_in = both_layers(attn_in[0])
    first_out, second_out = both_layers(attn_out[0])
    first_gain, second_gain = both_layers(gains[0])
    w_in = ffn_in.reshape(width, 2, chunks, LANES).transpose(0, 2, 1, 3).reshape(width, 2 * hidden)
    w_out = ffn_out

    start = section * own_count
    states = [pick(byte_states, start + i) for i in range(own_count)]
    ids = [pick(patch_ids, start + i) for i in range(own_count)]
    valid = [
        (jnp.arange(patches, dtype=jnp.int32) <= row[byte_count - 1])[:, None] for row in ids
    ]
    upstream = [
        jnp.where(valid[i], pick(latent_grad, start + i), 0).astype(b16) for i in range(own_count)
    ]
    each = range(own_count)

    one = [first_forward(states[i], ids[i], first_in, first_out, first_gain) for i in each]
    got_one = [swap(one[i][0], "tensor") for i in each]
    two = [
        second_attention(one[i][1], one[i][0], got_one[i], second_in, second_out, second_gain)
        for i in each
    ]
    got_two = [swap(two[i][7], "tensor") for i in each]
    three = [
        feed_forward(two[i][0], two[i][7], got_two[i], upstream[i], second_gain, w_in, w_out)
        for i in each
    ]
    got_three = [swap(three[i][5], "tensor") for i in each]

    rows = lambda pieces: jnp.concatenate(pieces, axis=0)
    upstream_all = rows(upstream)
    hidden_all = rows([three[i][2] for i in each])
    inner_all = rows([three[i][1] for i in each])
    both_all = rows([three[i][3] for i in each])
    keep, give = section * half_width, (1 - section) * half_width
    down = add(
        weight_grad(hidden_all, rows_at(upstream_all, keep, half_width, 1)),
        swap(weight_grad(hidden_all, rows_at(upstream_all, give, half_width, 1)), "section"),
    )
    up = add(
        weight_grad(rows_at(inner_all, keep, half_width, 1), both_all),
        swap(weight_grad(rows_at(inner_all, give, half_width, 1), both_all), "section"),
    )
    down_sum = sum_over_groups(down, (0, 1))
    up_sum = sum_over_groups(up, (0, 1))

    four = [
        second_backward(
            three[i][0], three[i][5], got_three[i], upstream[i], second_gain,
            (two[i][2], two[i][3], two[i][4], two[i][5]), second_in, second_out,
        )
        for i in each
    ]
    got_four = [swap(four[i][5], "tensor") for i in each]

    def to_core(mine, source):
        return add(mine, lax.ppermute(mine, "section", [(source, 1 - source)]))

    second_grad_in = weight_grad(
        rows([two[i][1] for i in each]),
        rows([jnp.concatenate([four[i][2], four[i][3], four[i][4]], axis=1) for i in each]),
    )
    second_grad_out = weight_grad(rows([two[i][6] for i in each]), rows([four[i][1] for i in each]))
    second_in_sum = sum_over_groups(to_core(second_grad_in, 0), (1,))
    second_out_sum = sum_over_groups(to_core(second_grad_out, 0), (1,))

    five = [
        first_backward(
            two[i][0], four[i][0], four[i][5], got_four[i], second_gain, first_gain, states[i],
            ids[i], (one[i][1], one[i][4], one[i][5], one[i][6], one[i][7]), first_in, first_out,
        )
        for i in each
    ]
    source_all = rows([one[i][3] for i in each])
    first_grad_in = jnp.concatenate(
        [
            weight_grad(rows([one[i][2] for i in each]), rows([five[i][1] for i in each])),
            weight_grad(source_all, rows([five[i][2] for i in each])),
            weight_grad(source_all, rows([five[i][3] for i in each])),
        ],
        axis=1,
    )
    first_grad_out = weight_grad(rows([one[i][8] for i in each]), rows([five[i][0] for i in each]))
    first_in_sum = sum_over_groups(to_core(first_grad_in, 1), (0,))
    first_out_sum = sum_over_groups(to_core(first_grad_out, 1), (0,))

    byte_start, byte_other = tensor * own_bytes, (1 - tensor) * own_bytes
    finished = []
    for i in each:
        query_got = swap(five[i][4], "tensor")
        source_got = swap(rows_at(five[i][5], byte_other, own_bytes), "tensor")
        finished.append(
            byte_gradient(
                five[i][0], one[i][1], five[i][4], query_got, ids[i],
                rows_at(ids[i], byte_start, own_bytes), first_gain,
                rows_at(states[i], byte_start, own_bytes),
                rows_at(five[i][5], byte_start, own_bytes), source_got,
            )
        )
    byte_own = jnp.stack(finished)
    byte_keep = rows_at(byte_own, keep, half_width, 2)
    byte_got = swap(rows_at(byte_own, give, half_width, 2), "section")
    byte_grad = jnp.where(
        is_first,
        jnp.concatenate([byte_keep, byte_got]),
        jnp.concatenate([byte_got, byte_keep]),
    )

    latent_parts = []
    mine, theirs = tensor * columns, (1 - tensor) * columns
    for i in each:
        total = three[i][4]
        got = swap(rows_at(total, theirs, columns, 1).astype(b16), "tensor")
        value = rows_at(three[i][0] + total, mine, columns, 1) + got.astype(f32)
        latent_parts.append(jnp.where(valid[i], value, 0.0).astype(b16))
    latent_own = jnp.stack(latent_parts)
    latent_keep = rows_at(latent_own, section * half_rows, half_rows, 1)
    latent_got = swap(rows_at(latent_own, (1 - section) * half_rows, half_rows, 1), "section")
    latents = jnp.where(
        is_first,
        jnp.concatenate([latent_keep, latent_got]),
        jnp.concatenate([latent_got, latent_keep]),
    )

    gain_rows = sum(
        jnp.concatenate([five[i][6][1:3], five[i][6][0:1], four[i][6]], axis=0) for i in each
    )
    gain_sum = sum_small(gain_rows)
    gain_out = jnp.where(is_first, gain_sum[0:2], gain_sum[2:4])
    in_sum = jnp.where(is_first, first_in_sum, second_in_sum).astype(f32)
    in_out = in_sum.reshape(width, 3, columns).transpose(1, 0, 2)
    out_out = jnp.where(is_first, first_out_sum, second_out_sum).astype(f32)
    up_out = (
        up_sum.astype(f32).reshape(half_width, chunks, 2, LANES).transpose(0, 2, 1, 3)
    ).reshape(half_width, 2, hidden)
    down_out = down_sum.astype(f32)
    return (latents, byte_grad, in_out[None], out_out[None], gain_out[None], up_out, down_out)


def solution(mesh):
    return jax.shard_map(
        per_device,
        mesh=mesh,
        in_specs=(
            P("dp", None, None),
            P("dp", None),
            P("section", None, None, "tensor"),
            P("section", "tensor", None),
            P("section", None, None),
            P(None, None, "tensor"),
            P("tensor", None),
            P("dp", None, None),
        ),
        out_specs=(
            P("dp", "section", "tensor"),
            P("dp", "tensor", "section"),
            P("section", None, None, "tensor"),
            P("section", "tensor", None),
            P("section", None, None),
            P("section", None, "tensor"),
            P("tensor", "section"),
        ),
        check_vma=False,
    )
```

```python
import functools
import types

import jax
import jax.numpy as jnp
from jax import lax
from jax.experimental import pallas as pl
from jax.experimental.pallas import tpu as pltpu
from jax.sharding import PartitionSpec as P

HD = 64
LANES = 128
BLOCK = 256
EPSILON = 1e-05
NEGATIVE = -1000000000.0
SCALE = HD ** (-0.5)
VMEM_BYTES = 62 * 1024 * 1024

f32 = jnp.float32
b16 = jnp.bfloat16


def dot(a, b):
    return jnp.dot(a, b, preferred_element_type=f32)


def dot_rt(a, b):
    return lax.dot_general(a, b, (((1,), (1,)), ((), ())), preferred_element_type=f32)


def dot_lt(a, b):
    return lax.dot_general(a, b, (((0,), (0,)), ((), ())), preferred_element_type=f32)


def inverse_rms(values):
    return lax.rsqrt(jnp.mean(values * values, axis=-1, keepdims=True) + EPSILON)


def iota(shape, dim):
    return lax.broadcasted_iota(jnp.int32, shape, dim)


def one_hot(condition):
    return jnp.where(condition, 1.0, 0.0).astype(b16)


def segment_max(values, ids):
    width = values.shape[1]
    lane = iota(ids.shape, 1)
    lowest = -3.0e38
    ahead, behind = values, values
    step = 1
    while step < width:
        left, right = step, width - step
        same_left = jnp.logical_and(pltpu.roll(ids, left, axis=1) == ids, lane >= step)
        same_right = jnp.logical_and(pltpu.roll(ids, right, axis=1) == ids, lane < right)
        ahead = jnp.maximum(ahead, jnp.where(same_left, pltpu.roll(ahead, left, axis=1), lowest))
        behind = jnp.maximum(
            behind, jnp.where(same_right, pltpu.roll(behind, right, axis=1), lowest)
        )
        step *= 2
    return jnp.maximum(ahead, behind)


def head_masks(width):
    heads_in = one_hot(iota((width, LANES), 0) // HD == iota((width, LANES), 1))
    heads_out = one_hot(iota((LANES, width), 1) // HD == iota((LANES, width), 0))
    return heads_in, heads_out


def split_dot(values, matrix):
    high = values.astype(b16)
    low = (values - high.astype(f32)).astype(b16)
    return dot(high, matrix) + dot(low, matrix)


def block_at(index, size=BLOCK):
    return pl.ds(pl.multiple_of(index * size, size), size)


def each_block(count, body, size=BLOCK):
    @pl.loop(0, count // size)
    def _(index):
        body(block_at(index, size))


MESH = pl.DeviceIdType.MESH


def remote(src, dst, send, recv, axis, index):
    return pltpu.make_async_remote_copy(
        src_ref=src, dst_ref=dst, send_sem=send, recv_sem=recv,
        device_id={axis: index}, device_id_type=MESH,
    )


def greet(places):
    barrier = pltpu.get_barrier_semaphore()
    for axis, index in places:
        pl.semaphore_signal(barrier, inc=1, device_id={axis: index}, device_id_type=MESH)
    pl.semaphore_wait(barrier, len(places))


def exchange_layer(r, section):
    copies = []
    for n, (src, dst) in enumerate(
        [(r.attn_in.at[0, j], r.w_in.at[section, j]) for j in (1, 2, 0)]
        + [(r.attn_out.at[0], r.w_out.at[section]), (r.gains.at[0], r.gain.at[section])]
    ):
        near = pltpu.make_async_copy(src, dst, r.near_sem.at[n])
        far = remote(src, dst, r.far_send.at[n], r.far_recv.at[n], "section", 1 - section)
        near.start()
        far.start()
        copies.append((near, far))
    return copies


def arrived(copies):
    for near, far in copies:
        near.wait()
        far.wait()


def members_of(r, seq, rows, patches):
    return one_hot(iota((patches, BLOCK), 0) == r.ids[pl.ds(seq, 1), rows])


FIRST_KEPT = ("query_in", "source_in", "byte_norms")
CROSS_KEPT = ("q1", "k1", "v1", "raised", "inverse", "mixed1")
SECOND_KEPT = ("normed", "q2", "k2", "v2", "totals", "mixed2")
FEED_KEPT = (
    "inner", "hidden", "gate_grad", "up_grad", "grad_in", "inner_part", "patch_norms",
    "latent_own", "latent_send",
)
KEPT = FIRST_KEPT + CROSS_KEPT + SECOND_KEPT + FEED_KEPT
LAYERS = ("w_in", "w_out", "gain")


def forward_kernel(r):
    section, tensor = lax.axis_index("section"), lax.axis_index("tensor")
    own_count, patches, width = r.normed.shape
    byte_count = r.states.shape[1]
    columns = r.q1.shape[2]
    hidden = r.hidden.shape[2]
    heads = columns // HD
    greet([("section", 1 - section), ("tensor", 1 - tensor)])
    state_copies = [
        pltpu.make_async_copy(
            r.states.at[section * own_count + i], r.state_in.at[i], r.state_sem.at[i]
        )
        for i in range(own_count)
    ]
    for copy in state_copies:
        copy.start()
    layer = exchange_layer(r, section)
    grad_copies = [
        pltpu.make_async_copy(
            r.upstream.at[section * own_count + i], r.grad_in.at[i], r.grad_sem.at[i]
        )
        for i in range(own_count)
    ]
    feed_copies = [
        pltpu.make_async_copy(r.ffn_in, r.feed_in, r.feed_sem.at[0]),
        pltpu.make_async_copy(r.ffn_out, r.feed_out, r.feed_sem.at[1]),
    ]
    for copy in grad_copies + feed_copies:
        copy.start()
    heads_in, heads_out = head_masks(columns)

    def keep(name, i):
        n = KEPT.index(name)
        return pltpu.make_async_copy(
            getattr(r, name).at[i], getattr(r, "out_" + name).at[i], r.keep_sem.at[n, i]
        )

    def save(names, i):
        for name in names:
            keep(name, i).start()

    def exchange(step, i):
        return remote(
            r.part.at[step, i], r.got.at[step, i], r.part_send.at[step, i], r.part_recv.at[step, i],
            "tensor", 1 - tensor,
        )

    for copy in state_copies:
        copy.wait()
    layer[-1][0].wait()
    layer[-1][1].wait()
    first_gain = r.gain.at[0]

    @pl.loop(0, own_count)
    def _(i):
        seq = section * own_count + i
        r.pool_sum[...] = jnp.zeros_like(r.pool_sum)

        def pool(rows):
            block = r.state_in[i, rows, :]
            r.pool_sum[...] += dot(members_of(r, seq, rows, patches), block)
            values = block.astype(f32)
            scale = inverse_rms(values)
            r.byte_norms[i, rows, :] = jnp.broadcast_to(scale, (BLOCK, LANES))
            r.source_in[i, rows, :] = (values * scale * first_gain[1:2, :]).astype(b16)

        each_block(byte_count, pool)
        row_ids = r.ids[pl.ds(seq, 1), :]
        counts = jnp.sum(
            jnp.where(iota((patches, byte_count), 0) == row_ids, 1.0, 0.0), axis=1, keepdims=True
        )
        values = r.pool_sum[...] / jnp.maximum(counts, 1.0)
        r.pooled[i] = values
        scale = inverse_rms(values)
        r.patch_norms[i] = jnp.broadcast_to(scale, (patches, LANES))
        r.query_in[i] = (values * scale * first_gain[0:1, :]).astype(b16)
        save(FIRST_KEPT, i)

    arrived(layer[:4])
    layer_saves = [
        pltpu.make_async_copy(getattr(r, name), getattr(r, "out_" + name), r.layer_sem.at[n])
        for n, name in enumerate(LAYERS)
    ]
    for copy in layer_saves:
        copy.start()

    @pl.loop(0, own_count)
    def _(i):
        seq = section * own_count + i
        r.q1[i] = dot(r.query_in[i], r.w_in[0, 0]).astype(b16)

        def project(rows):
            normed = r.source_in[i, rows, :]
            keys = dot(normed, r.w_in[0, 1]).astype(b16)
            r.k1[i, rows, :] = keys
            r.v1[i, rows, :] = dot(normed, r.w_in[0, 2]).astype(b16)
            spread = dot_lt(members_of(r, seq, rows, patches), r.q1[i])
            block_scores = split_dot(spread * keys.astype(f32), heads_in) * SCALE
            r.scores[:, rows] = block_scores.T[:heads, :]

        each_block(byte_count, project)
        scores = r.scores[...]
        r.scores[...] = jnp.exp(scores - segment_max(scores, r.ids[pl.ds(seq, 1), :]))
        r.mix_sum[...] = jnp.zeros_like(r.mix_sum)
        r.total_sum[...] = jnp.zeros_like(r.total_sum)

        def mix(rows):
            short = r.scores[:, rows]
            filled = jnp.concatenate([short, jnp.zeros((LANES - heads, BLOCK), f32)], axis=0)
            raised = filled.T.astype(b16)
            r.raised[i, rows, :] = raised
            members = members_of(r, seq, rows, patches)
            weighted = (dot(raised, heads_out) * r.v1[i, rows, :].astype(f32)).astype(b16)
            r.mix_sum[...] += dot(members, weighted)
            r.total_sum[...] += dot(members, raised)

        each_block(byte_count, mix)
        totals = r.total_sum[...]
        inverse = jnp.where(totals > 0.0, 1.0 / totals, 0.0)
        r.inverse[i] = inverse
        mixed = (r.mix_sum[...] * split_dot(inverse, heads_out)).astype(b16)
        r.mixed1[i] = mixed
        r.part[0, i] = dot(mixed, r.w_out[0]).astype(b16)
        exchange(0, i).start()
        save(CROSS_KEPT, i)

    second_gain = r.gain.at[1]
    allowed = iota((patches, patches), 1) <= iota((patches, patches), 0)
    lane = iota((patches, LANES), 1)

    @pl.loop(0, own_count)
    def _(i):
        exchange(0, i).wait()
        latent = (
            r.pooled[i] + r.part[0, i].astype(f32) + r.got[0, i].astype(f32)
        ).astype(b16)
        r.latent[i] = latent
        values = latent.astype(f32)
        scale = inverse_rms(values)
        r.patch_norms[i] = jnp.where(lane == 1, scale, r.patch_norms[i])
        normed = (values * scale * second_gain[0:1, :]).astype(b16)
        r.normed[i] = normed
        query = dot(normed, r.w_in[1, 0]).astype(b16)
        key = dot(normed, r.w_in[1, 1]).astype(b16)
        value = dot(normed, r.w_in[1, 2]).astype(b16)
        r.q2[i] = query
        r.k2[i] = key
        r.v2[i] = value
        kept = jnp.zeros((patches, LANES), f32)
        outs = []
        for head in range(heads):
            own = slice(head * HD, (head + 1) * HD)
            scores = jnp.where(allowed, dot_rt(query[:, own], key[:, own]) * SCALE, NEGATIVE)
            highest = jnp.max(scores, axis=-1, keepdims=True)
            raised = jnp.exp(scores - highest)
            total = jnp.sum(raised, axis=-1, keepdims=True)
            outs.append(dot((raised / total).astype(b16), value[:, own]))
            kept = jnp.where(lane == head, highest + jnp.log(total), kept)
        r.totals[i] = kept
        mixed = jnp.concatenate(outs, axis=1).astype(b16)
        r.mixed2[i] = mixed
        r.part[1, i] = dot(mixed, r.w_out[1]).astype(b16)
        exchange(1, i).start()
        save(SECOND_KEPT, i)

    for copy in grad_copies + feed_copies:
        copy.wait()

    @pl.loop(0, own_count)
    def _(i):
        seq = section * own_count + i
        exchange(1, i).wait()
        values = (
            r.latent[i].astype(f32) + r.part[1, i].astype(f32) + r.got[1, i].astype(f32)
        )
        r.middle[...] = values
        scale = inverse_rms(values)
        r.patch_norms[i] = jnp.where(lane == 2, scale, r.patch_norms[i])
        r.inner[i] = (values * scale * second_gain[1:2, :]).astype(b16)
        valid = iota((patches, 1), 0) <= jnp.max(r.ids[pl.ds(seq, 1), :], axis=1, keepdims=True)
        r.grad_in[i] = jnp.where(valid, r.grad_in[i].astype(f32), 0.0).astype(b16)

        def part(cols):
            gate = dot(r.inner[i], r.feed_in[0, :, cols])
            up = dot(r.inner[i], r.feed_in[1, :, cols])
            hidden_grad = dot_rt(r.grad_in[i], r.feed_out[cols, :])
            gated = 1.0 / (1.0 + jnp.exp(-gate))
            act = gate * gated
            r.hidden[i, :, cols] = (act * up).astype(b16)
            r.gate_grad[i, :, cols] = (
                hidden_grad * up * (gated * (1.0 + gate * (1.0 - gated)))
            ).astype(b16)
            r.up_grad[i, :, cols] = (hidden_grad * act).astype(b16)

        each_block(hidden, part)
        rest = hidden % BLOCK
        if rest:
            part(pl.ds(hidden - rest, rest))

        def sums(cols):
            r.out_sum[:, cols] = dot(r.hidden[i], r.feed_out[:, cols])
            r.inner_part[i, :, cols] = (
                dot_rt(r.gate_grad[i], r.feed_in[0, cols, :])
                + dot_rt(r.up_grad[i], r.feed_in[1, cols, :])
            ).astype(b16)

        each_block(width, sums)
        mine, theirs = block_at(tensor, columns), block_at(1 - tensor, columns)
        r.latent_own[i] = (r.middle[:, mine] + r.out_sum[:, mine]).astype(b16)
        r.latent_send[i] = r.out_sum[:, theirs].astype(b16)
        save(FEED_KEPT, i)

    @pl.loop(0, own_count)
    def _(i):
        for name in KEPT:
            keep(name, i).wait()

    for copy in layer_saves:
        copy.wait()


def shape(dims, dtype):
    return jax.ShapeDtypeStruct(dims, dtype)


def named_call(kernel, ins, outs, scratch, **params):
    any_space = pl.BlockSpec(memory_space=pl.ANY)
    whole = pl.BlockSpec(memory_space=pltpu.VMEM)
    names = [name for name, _, _ in ins] + [name for name, _ in outs] + list(scratch)

    def body(*refs):
        kernel(types.SimpleNamespace(**dict(zip(names, refs, strict=True))))

    got = pl.pallas_call(
        body,
        out_shape=tuple(s for _, s in outs),
        in_specs=[whole if inside else any_space for _, _, inside in ins],
        out_specs=tuple(any_space for _ in outs),
        scratch_shapes=list(scratch.values()),
        compiler_params=pltpu.CompilerParams(
            vmem_limit_bytes=VMEM_BYTES, has_side_effects=True, **params
        ),
    )(*(array for _, array, _ in ins))
    return {name: value for (name, _), value in zip(outs, got, strict=True)}


def forward(byte_states, patch_ids, attn_in, attn_out, gains, feed_in, feed_out, latent_grad):
    sequences, byte_count, width = byte_states.shape
    patches = byte_count // 4
    columns = attn_in.shape[-1]
    hidden = feed_out.shape[0]
    own = sequences // 2
    heads = columns // HD
    dims = dict(
        query_in=(own, patches, width, b16),
        source_in=(own, byte_count, width, b16),
        q1=(own, patches, columns, b16),
        k1=(own, byte_count, columns, b16),
        v1=(own, byte_count, columns, b16),
        raised=(own, byte_count, LANES, b16),
        inverse=(own, patches, LANES, f32),
        mixed1=(own, patches, columns, b16),
        byte_norms=(own, byte_count, LANES, f32),
        normed=(own, patches, width, b16),
        q2=(own, patches, columns, b16),
        k2=(own, patches, columns, b16),
        v2=(own, patches, columns, b16),
        totals=(own, patches, LANES, f32),
        mixed2=(own, patches, columns, b16),
        inner=(own, patches, width, b16),
        hidden=(own, patches, hidden, b16),
        gate_grad=(own, patches, hidden, b16),
        up_grad=(own, patches, hidden, b16),
        grad_in=(own, patches, width, b16),
        inner_part=(own, patches, width, b16),
        patch_norms=(own, patches, LANES, f32),
        latent_own=(own, patches, columns, b16),
        latent_send=(own, patches, columns, b16),
    )
    sems = pltpu.SemaphoreType.DMA
    scratch = {name: pltpu.VMEM(dims[name][:-1], dims[name][-1]) for name in KEPT}
    scratch |= dict(
        state_in=pltpu.VMEM((own, byte_count, width), b16),
        pooled=pltpu.VMEM((own, patches, width), f32),
        latent=pltpu.VMEM((own, patches, width), b16),
        middle=pltpu.VMEM((patches, width), f32),
        out_sum=pltpu.VMEM((patches, width), f32),
        w_in=pltpu.VMEM((2, 3, width, columns), b16),
        w_out=pltpu.VMEM((2, columns, width), b16),
        gain=pltpu.VMEM((2, 2, width), f32),
        feed_in=pltpu.VMEM((2, width, hidden), b16),
        feed_out=pltpu.VMEM((hidden, width), b16),
        pool_sum=pltpu.VMEM((patches, width), f32),
        scores=pltpu.VMEM((heads, byte_count), f32),
        mix_sum=pltpu.VMEM((patches, columns), f32),
        total_sum=pltpu.VMEM((patches, LANES), f32),
        part=pltpu.VMEM((2, own, patches, width), b16),
        got=pltpu.VMEM((2, own, patches, width), b16),
        state_sem=sems((own,)),
        grad_sem=sems((own,)),
        feed_sem=sems((2,)),
        near_sem=sems((5,)),
        far_send=sems((5,)),
        far_recv=sems((5,)),
        part_send=sems((2, own)),
        part_recv=sems((2, own)),
        keep_sem=sems((len(KEPT), own)),
        layer_sem=sems((len(LAYERS),)),
    )
    ins = [
        ("states", byte_states, False), ("ids", patch_ids, True), ("attn_in", attn_in, False),
        ("attn_out", attn_out, False), ("gains", gains, False), ("ffn_in", feed_in, False),
        ("ffn_out", feed_out, False), ("upstream", latent_grad, False),
    ]
    dims |= dict(
        w_in=(2, 3, width, columns, b16),
        w_out=(2, columns, width, b16),
        gain=(2, 2, width, f32),
    )
    names = (*KEPT, *LAYERS)
    outs = [("out_" + name, shape(dims[name][:-1], dims[name][-1])) for name in names]
    got = named_call(forward_kernel, ins, outs, scratch, collective_id=0)
    return {name: got["out_" + name] for name in names}


def flat(ref, cols):
    block = ref[:, :, cols]
    return block.reshape(block.shape[0] * block.shape[1], block.shape[2])


def total(target, got):
    def tile(rows):
        target[rows, :] = (target[rows, :].astype(f32) + got[rows, :].astype(f32)).astype(b16)

    each_block(target.shape[0], tile, LANES)


LONG, SHORT = 4, 2


class Flows:
    def __init__(self, r):
        self.r = r
        place = lax.axis_index("dp")
        self.z, self.y = place // SHORT, lax.rem(place, SHORT)
        self.right, self.left = place + SHORT, place - SHORT
        self.beside = place + 1 - 2 * self.y
        self.active = []

    def hop(self, src, dst, n, j, target):
        r = self.r
        return pltpu.make_async_remote_copy(
            src_ref=src, dst_ref=dst, send_sem=r.flow_send.at[n, j], recv_sem=r.flow_recv.at[n, j],
            device_id={"dp": target}, device_id_type=MESH,
        )

    def at(self, places, body):
        condition = self.z == places[0]
        for z in places[1:]:
            condition = jnp.logical_or(condition, self.z == z)
        pl.when(condition)(body)

    @staticmethod
    def add(target, got):
        rows, width = target.shape

        @pl.loop(0, rows // 16)
        def _(t):
            at = block_at(t, 16)
            target[at, :] = (target[at, :].astype(f32) + got[at, :].astype(f32)).astype(b16)

    def reduce_steps(self, n, part, slot):
        def up(k):
            src = slot(k - 1)
            return self.hop(src, src, n, k - 1, self.right)

        def down(k):
            src = slot(3 + k)
            return self.hop(src, src, n, 3 + k, self.left)

        def pass_on(copy, place, k):
            copy.wait_recv()
            self.add(place, part(k))
            copy.start()

        def begin():
            def first():
                for k in (3, 2, 1):
                    self.hop(part(k), slot(k - 1), n, k - 1, self.right).start()

            def last():
                for k in (0, 1, 2):
                    self.hop(part(k), slot(3 + k), n, 3 + k, self.left).start()

            self.at([0], first)
            self.at([3], last)

        def second():
            self.at([1], lambda: pass_on(up(3), slot(2), 3))
            self.at([2], lambda: pass_on(down(0), slot(3), 0))

        def third():
            def at_one():
                pass_on(up(2), slot(1), 2)
                pass_on(down(0), slot(3), 0)

            def at_two():
                pass_on(down(1), slot(4), 1)
                pass_on(up(3), slot(2), 3)

            self.at([1], at_one)
            self.at([2], at_two)

        def close():
            def finish(k):
                def body():
                    if k >= 1:
                        up(k).wait_recv()
                        self.add(part(k), slot(k - 1))
                    if k <= 2:
                        down(k).wait_recv()
                        self.add(part(k), slot(3 + k))

                return body

            for k in range(LONG):
                self.at([k], finish(k))

        def sent():
            ups = {0: (1, 2, 3), 1: (2, 3), 2: (3,), 3: ()}
            downs = {0: (), 1: (0,), 2: (0, 1), 3: (0, 1, 2)}
            for z in range(LONG):

                def body(z=z):
                    for k in ups[z]:
                        up(k).wait_send()
                    for k in downs[z]:
                        down(k).wait_send()

                self.at([z], body)

        return [begin, second, third, close], sent

    def gather_steps(self, n, own, out, extra=None):
        def up(src, k, d):
            return self.hop(src, out(k), n, 7 + d, self.right)

        def down(src, k, d):
            return self.hop(src, out(k), n, 10 + d, self.left)

        def near():
            return pltpu.make_async_copy(own(), out(self.z), self.r.flow_near.at[n])

        def begin():
            near().start()
            self.at([0, 1, 2], lambda: up(own(), self.z, 0).start())
            self.at([1, 2, 3], lambda: down(own(), self.z, 0).start())
            if extra:
                extra(own(), self.z).start()

        def step(d):
            def from_left():
                k = self.z - d
                up(out(k), k, d - 1).wait_recv()
                if d < LONG - 1:
                    pl.when(self.z < LONG - 1)(lambda: up(out(k), k, d).start())
                if extra:
                    extra(out(k), k).start()

            def from_right():
                k = self.z + d
                down(out(k), k, d - 1).wait_recv()
                if d < LONG - 1:
                    pl.when(self.z > 0)(lambda: down(out(k), k, d).start())
                if extra:
                    extra(out(k), k).start()

            def body():
                self.at(list(range(d, LONG)), from_left)
                self.at(list(range(0, LONG - d)), from_right)

            return body

        def sent():
            near().wait()
            self.at([0, 1, 2], lambda: up(own(), self.z, 0).wait_send())
            self.at([1, 2, 3], lambda: down(own(), self.z, 0).wait_send())
            if extra:
                extra(own(), self.z).wait_send()
            for d in (1, 2, 3):

                def left_sent(d=d):
                    k = self.z - d
                    if d < LONG - 1:
                        pl.when(self.z < LONG - 1)(lambda: up(out(k), k, d).wait_send())
                    if extra:
                        extra(out(k), k).wait_send()

                def right_sent(d=d):
                    k = self.z + d
                    if d < LONG - 1:
                        pl.when(self.z > 0)(lambda: down(out(k), k, d).wait_send())
                    if extra:
                        extra(out(k), k).wait_send()

                self.at(list(range(d, LONG)), left_sent)
                self.at(list(range(0, LONG - d)), right_sent)

        return [begin, step(1), step(2), step(3)], sent

    def long_first(self, n, data, out, slots, start, rows):
        c = rows // LONG

        def part(k):
            return data(pl.multiple_of(start + k * c, 16), c)

        def place(k):
            return out.at[pl.ds(pl.multiple_of(start + k * c, 16), c), :]

        def slot(j):
            return slots.at[pl.ds(j * c, c), :]

        def beside():
            return self.hop(part(self.z), slot(6), n, 6, self.beside)

        reduce, reduce_sent = self.reduce_steps(n, part, slot)
        gather, gather_sent = self.gather_steps(n, lambda: slot(6), place)

        def middle():
            reduce[3]()
            beside().start()

        def turn():
            beside().wait_recv()
            self.add(slot(6), part(self.z))
            gather[0]()

        def end():
            gather[3]()
            reduce_sent()
            beside().wait_send()
            gather_sent()

        return [*reduce[:3], middle, turn, gather[1], gather[2], end]

    def short_first(self, n, data, out, slots, start, rows):
        half = rows // SHORT
        c = half // LONG

        def part(k):
            return data(pl.multiple_of(start + self.y * half + k * c, 16), c)

        def place(k, y=None):
            y = self.y if y is None else y
            return out.at[pl.ds(pl.multiple_of(start + y * half + k * c, 16), c), :]

        def slot(j):
            return slots.at[pl.ds(j * c, c), :]

        landing = slots.at[pl.ds(6 * c, half), :]

        def mine(y):
            return data(pl.multiple_of(start + y * half, 16), half)

        def beside():
            return self.hop(mine(1 - self.y), landing, n, 6, self.beside)

        def spread(src, k):
            return self.hop(src, place(k), n, 13 + k, self.beside)

        reduce, reduce_sent = self.reduce_steps(n, part, slot)
        gather, gather_sent = self.gather_steps(n, lambda: part(self.z), place, spread)

        def begin():
            beside().start()

        def turn():
            beside().wait_recv()
            self.add(mine(self.y), landing)
            reduce[0]()

        def middle():
            reduce[3]()
            gather[0]()

        def end():
            reduce_sent()
            beside().wait_send()
            gather_sent()
            for k in range(LONG):
                there = place(k, 1 - self.y)
                self.hop(there, there, n, 13 + k, self.beside).wait_recv()

        return [begin, turn, reduce[1], reduce[2], middle, *gather[1:], end]

    def open(self, *flows):
        self.active += [list(flow) for flow in flows]

    def tick(self):
        for flow in self.active:
            flow.pop(0)()
        self.active = [flow for flow in self.active if flow]

    def drain(self):
        while self.active:
            self.tick()


def on_grid():
    return lax.axis_size("dp") == LONG * SHORT


def backward_kernel(r):
    section, tensor = lax.axis_index("section"), lax.axis_index("tensor")
    own_count, patches, width = r.normed.shape
    byte_count = r.ids.shape[1]
    columns = r.w_in.shape[2]
    hidden = r.down.shape[0]
    heads = columns // HD
    half = width // 2
    half_bytes = byte_count // 2
    summing = on_grid()
    loads = {}

    def load(name, src, dst, *sem):
        copy = pltpu.make_async_copy(src, dst, r.load_sem.at[sem])
        copy.start()
        loads[name] = copy

    held_names = ("inner", "grad_in", "inner_part", "normed", "patch_norms", "gain")
    for n, name in enumerate(held_names):
        load(name, getattr(r, "in_" + name), getattr(r, name), n)
    load("w_in", r.in_w_in.at[1], r.w_in, 6)
    load("w_out", r.in_w_out.at[1], r.w_out, 7)
    others = [("section", 1 - section), ("tensor", 1 - tensor)]
    flows = Flows(r) if summing else None
    if summing:
        greet_grid(flows, others)
    else:
        greet(others)

    def cross(src, dst, i, sem):
        return remote(
            src, dst, r.cross_send.at[sem, i], r.cross_recv.at[sem, i], "tensor", 1 - tensor
        )

    def inner_exchange(i):
        return cross(r.in_inner_part.at[i], r.inner_got.at[i], i, 0)

    def normed_exchange(i):
        return cross(r.normed_part.at[i], r.normed_got.at[i], i, 1)

    def query_exchange(i):
        return cross(r.inner_part.at[i], r.inner_got.at[i], i, 2)

    def source_exchange(i):
        theirs = block_at(1 - tensor, half_bytes)
        return cross(r.source_part.at[i, theirs, :], r.source_got.at[i], i, 3)

    def latent_exchange(i):
        return cross(r.in_latent_send.at[i], r.latent_got.at[i], i, 4)

    for i in range(own_count):
        inner_exchange(i).start()
    for i in range(own_count):
        latent_exchange(i).start()

    def give(n, src, dst):
        return remote(src, dst, r.give_send.at[n], r.give_recv.at[n], "section", 1 - section)

    def tick():
        if summing:
            flows.tick()

    def summed(n, data, out, slots, long_rows, base=0):
        rows = slots[1]
        if summing:
            flows.open(
                flows.long_first(n, data, out, slots[0], base, long_rows),
                flows.short_first(n + 1, data, out, slots[2], base + long_rows, rows - long_rows),
            )

    def whole(ref):
        return lambda start, rows: ref.at[pl.ds(start, rows), :]

    @functools.partial(
        pl.run_scoped,
        hidden_all=pltpu.VMEM((own_count, patches, hidden), b16),
        gate_all=pltpu.VMEM((own_count, patches, hidden), b16),
        up_all=pltpu.VMEM((own_count, patches, hidden), b16),
        down_give=pltpu.VMEM((hidden, half), b16),
    )
    def _(hidden_all, gate_all, up_all, down_give):
        parts = {"hidden": hidden_all, "gate_grad": gate_all, "up_grad": up_all}
        for n, (name, ref) in enumerate(parts.items()):
            load(name, getattr(r, "in_" + name), ref, n + 8)
        for name in (*parts, "inner", "grad_in"):
            loads[name].wait()

        def down_grad(target, side):
            upstream = flat(r.grad_in, block_at(side, half))

            def tile(cols):
                target[cols, :] = dot_lt(flat(hidden_all, cols), upstream).astype(b16)

            each_block(hidden, tile)
            if hidden % BLOCK:
                tile(pl.ds(hidden - hidden % BLOCK, hidden % BLOCK))

        def up_grad(target, ref, side):
            upstream = flat(ref, slice(None))

            def tile(rows):
                cols = pl.ds(pl.multiple_of(side * half + rows.start, BLOCK), BLOCK)
                target[rows, :] = dot_lt(flat(r.inner, cols), upstream).astype(b16)

            each_block(half, tile)

        used = pl.ds(0, hidden)
        give_rows = [pl.ds(0, half), pl.ds(half, half)]
        gate_give, up_give = [r.attn_in_part.at[1, rows, used] for rows in give_rows]
        gate_got, up_got = [r.big_got.at[rows, used] for rows in give_rows]
        gate_own, up_own = [r.up.at[rows, :] for rows in give_rows]
        gifts = [
            give(0, down_give, r.down_got), give(1, gate_give, gate_got), give(2, up_give, up_got)
        ]
        other = 1 - section
        down_grad(down_give, other)
        gifts[0].start()
        down_grad(r.down, section)
        up_grad(gate_give, gate_all, other)
        gifts[1].start()
        gifts[0].wait()
        total(r.down, r.down_got)
        summed(0, whole(r.down), r.down_sum, r.slots_down, r.cuts["down"])
        tick()
        up_grad(gate_own, gate_all, section)
        up_grad(up_give, up_all, other)
        gifts[2].start()
        gifts[1].wait()
        total(gate_own, gate_got)
        summed(2, whole(gate_own), r.up_sum.at[give_rows[0], :], r.slots_gate, r.cuts["up"])
        tick()
        up_grad(up_own, up_all, section)
        gifts[2].wait()
        total(up_own, up_got)
        summed(4, whole(up_own), r.up_sum.at[give_rows[1], :], r.slots_up, r.cuts["up"])
        tick()
        pl.semaphore_signal(
            r.free_sem, inc=1, device_id={"section": other}, device_id_type=MESH
        )

    first_gain, second_gain = r.gain.at[0], r.gain.at[1]

    def back_through(normed, gain_row, scale, upstream):
        unit = normed.astype(f32) / gain_row
        scaled = upstream * gain_row
        mean = jnp.mean(unit * scaled, axis=-1, keepdims=True)
        return (scaled - unit * mean) * scale, unit

    @functools.partial(
        pl.run_scoped,
        q2=pltpu.VMEM((own_count, patches, columns), b16),
        k2=pltpu.VMEM((own_count, patches, columns), b16),
        v2=pltpu.VMEM((own_count, patches, columns), b16),
        totals=pltpu.VMEM((own_count, patches, LANES), f32),
        mixed2=pltpu.VMEM((own_count, patches, columns), b16),
        second_grads=pltpu.VMEM((own_count, patches, 3 * columns), b16),
    )
    def _(q2, k2, v2, totals, mixed2, second_grads):
        parts = {"q2": q2, "k2": k2, "v2": v2, "totals": totals, "mixed2": mixed2}
        for n, (name, ref) in enumerate(parts.items()):
            load(name, getattr(r, "in_" + name), ref, n + 11)
        for name in (*held_names[2:], "w_in", "w_out", *parts):
            loads[name].wait()
        r.gain_sum[...] = jnp.zeros_like(r.gain_sum)
        allowed = iota((patches, patches), 1) <= iota((patches, patches), 0)
        for i in range(own_count):
            inner_exchange(i).wait()
            own_part = r.inner_part[i].astype(f32)
            back, unit = back_through(
                r.inner[i], second_gain[1:2, :], r.patch_norms[i, :, 2:3],
                own_part + r.inner_got[i].astype(f32),
            )
            r.gain_sum[3:4, :] += jnp.sum(unit * own_part, axis=0, keepdims=True)
            branch = (r.grad_in[i].astype(f32) + back).astype(b16)
            r.branch[i] = branch
            mixed_grad = dot_rt(branch, r.w_out[...]).astype(b16)
            q_outs, k_outs, v_outs = [], [], []
            for head in range(heads):
                own = slice(head * HD, (head + 1) * HD)
                query, key, value = q2[i, :, own], k2[i, :, own], v2[i, :, own]
                upper = mixed_grad[:, own]
                scores = jnp.where(allowed, dot_rt(query, key) * SCALE, NEGATIVE)
                probs = jnp.exp(scores - totals[i, :, head : head + 1])
                prob_grad = dot_rt(upper, value)
                delta = jnp.sum(probs * prob_grad, axis=-1, keepdims=True)
                score_grad = (probs * (prob_grad - delta)).astype(b16)
                q_outs.append(dot(score_grad, key) * SCALE)
                k_outs.append(dot_lt(score_grad, query) * SCALE)
                v_outs.append(dot_lt(probs.astype(b16), upper))
            normed_grad = jnp.zeros((patches, width), f32)
            for j, outs in enumerate((q_outs, k_outs, v_outs)):
                grads = jnp.concatenate(outs, axis=1).astype(b16)
                second_grads[i, :, j * columns : (j + 1) * columns] = grads
                normed_grad += dot_rt(grads, r.w_in[j])
            r.normed_part[i] = normed_grad.astype(b16)
            normed_exchange(i).start()
            tick()

        def outer(target, rows_ref, upstream, tiles):
            @pl.loop(0, tiles)
            def _(t):
                cols = block_at(t)
                target[cols, :] = dot_lt(flat(rows_ref, cols), upstream).astype(b16)

        outer(r.attn_in_part.at[1], r.normed, flat(second_grads, slice(None)), width // BLOCK)
        outer(r.attn_out_part.at[1], mixed2, flat(r.branch, slice(None)), columns // BLOCK)
        tick()

    heads_in, heads_out = head_masks(columns)

    def first_layer(i, scoped):
        seq = section * own_count + i
        s = types.SimpleNamespace(**scoped)
        copies = {}
        names = (*CROSS_KEPT, "source_in", "query_in")
        for n, name in enumerate(names):
            copy = pltpu.make_async_copy(
                getattr(r, "in_" + name).at[i], getattr(s, name), r.first_sem.at[n]
            )
            copy.start()
            copies[name] = copy
        normed_exchange(i).wait()
        own_part = r.normed_part[i].astype(f32)
        back, unit = back_through(
            r.normed[i], second_gain[0:1, :], r.patch_norms[i, :, 1:2],
            own_part + r.normed_got[i].astype(f32),
        )
        r.gain_sum[2:3, :] += jnp.sum(unit * own_part, axis=0, keepdims=True)
        branch = (r.branch[i].astype(f32) + back).astype(b16)
        r.branch[i] = branch
        s.mixed_grad[...] = dot_rt(branch, r.w_out[...]).astype(b16)
        s.q_sum[...] = jnp.zeros_like(s.q_sum)
        s.delta_sum[...] = jnp.zeros_like(s.delta_sum)
        for copy in copies.values():
            copy.wait()
        inverse = s.inverse[...]
        inverse_high = inverse.astype(b16)
        inverse_low = (inverse - inverse_high.astype(f32)).astype(b16)

        def value_side(rows):
            members = members_of(r, seq, rows, patches)
            spread = dot_lt(members, s.mixed_grad[...])
            scale = dot_lt(members, inverse_high) + dot_lt(members, inverse_low)
            probs = s.raised[rows, :].astype(f32) * scale
            s.probs[rows, :] = probs
            s.dv[rows, :] = (dot(probs.astype(b16), heads_out) * spread).astype(b16)
            prob_grad = split_dot(spread * s.v1[rows, :].astype(f32), heads_in)
            s.prob_grad[rows, :] = prob_grad
            product = probs * prob_grad
            high = product.astype(b16)
            low = (product - high.astype(f32)).astype(b16)
            s.delta_sum[...] += dot(members, high) + dot(members, low)

        each_block(byte_count, value_side)
        tick()
        delta = s.delta_sum[...]
        delta_high = delta.astype(b16)
        delta_low = (delta - delta_high.astype(f32)).astype(b16)

        def key_side(rows):
            members = members_of(r, seq, rows, patches)
            shift = dot_lt(members, delta_high) + dot_lt(members, delta_low)
            score_grad = (s.probs[rows, :] * (s.prob_grad[rows, :] - shift)).astype(b16)
            spread = dot(score_grad, heads_out)
            k_grad = (spread * dot_lt(members, s.q1[...]) * SCALE).astype(b16)
            s.dk[rows, :] = k_grad
            s.q_sum[...] += dot(members, (spread * s.k1[rows, :].astype(f32)).astype(b16))
            source = dot_rt(k_grad, r.w_in[1]) + dot_rt(s.dv[rows, :], r.w_in[2])
            r.source_part[i, rows, :] = source.astype(b16)
            unit_block = s.source_in[rows, :].astype(f32)
            r.gain_sum[1:2, :] += (
                jnp.sum(unit_block * source, axis=0, keepdims=True) / first_gain[1:2, :]
            )

        each_block(byte_count, key_side)
        source_exchange(i).start()
        q_grad = (s.q_sum[...] * SCALE).astype(b16)
        query = dot_rt(q_grad, r.w_in[0])
        r.inner_part[i] = query.astype(b16)
        query_exchange(i).start()
        unit_pool = s.query_in[...].astype(f32)
        r.gain_sum[0:1, :] += (
            jnp.sum(unit_pool * query, axis=0, keepdims=True) / first_gain[0:1, :]
        )
        tick()

        def add_to(target, rows, cols, value):
            if i:
                value = target[rows, cols].astype(f32) + value
            target[rows, cols] = value.astype(b16)

        @pl.loop(0, width // BLOCK)
        def _(t):
            cols = block_at(t)
            source = s.source_in[:, cols]
            target = r.attn_in_part.at[0]
            add_to(target, cols, slice(0, columns), dot_lt(s.query_in[:, cols], q_grad))
            add_to(target, cols, slice(columns, 2 * columns), dot_lt(source, s.dk[...]))
            add_to(target, cols, slice(2 * columns, 3 * columns), dot_lt(source, s.dv[...]))

        @pl.loop(0, columns // BLOCK)
        def _(t):
            cols = block_at(t)
            add_to(
                r.attn_out_part.at[0], cols, slice(None), dot_lt(s.mixed1[:, cols], branch)
            )

        tick()

    def last_parts(s):
        half_rows = patches // 2
        rows_keep, rows_give = block_at(section, half_rows), block_at(1 - section, half_rows)
        outs = []
        for i in range(own_count):
            seq = section * own_count + i
            s_load = pltpu.make_async_copy(r.in_latent_own.at[i], s.latent.at[i], r.first_sem.at[i])
            s_load.start()
            s_load.wait()
            latent_exchange(i).wait()
            last = jnp.max(r.ids[pl.ds(seq, 1), :], axis=1, keepdims=True)
            valid = iota((patches, 1), 0) <= last
            values = s.latent[i].astype(f32) + r.latent_got[i].astype(f32)
            s.latent[i] = jnp.where(valid, values, 0.0).astype(b16)
            near = pltpu.make_async_copy(
                s.latent.at[i, rows_keep, :], r.latents.at[seq], r.out_sem.at[0, i]
            )
            far = remote(
                s.latent.at[i, rows_give, :], r.latents.at[seq],
                r.out_send.at[0, i], r.out_recv.at[0, i], "section", 1 - section,
            )
            near.start()
            far.start()
            outs += [near, far]

        own_rows = block_at(tensor, half_bytes)
        cols_keep, cols_give = block_at(section, half), block_at(1 - section, half)
        for i in range(own_count):
            seq = section * own_count + i
            finals = [
                pltpu.make_async_copy(
                    r.in_source_in.at[i, own_rows, :], s.source_in, r.first_sem.at[0]
                ),
                pltpu.make_async_copy(
                    r.in_byte_norms.at[i, own_rows, :], s.byte_norms, r.first_sem.at[1]
                ),
                pltpu.make_async_copy(r.in_query_in.at[i], s.query_in, r.first_sem.at[2]),
            ]
            for copy in finals:
                copy.start()
            query_exchange(i).wait()
            source_exchange(i).wait()
            for copy in finals:
                copy.wait()
            back, _ = back_through(
                s.query_in[...], first_gain[0:1, :], r.patch_norms[i, :, 0:1],
                r.inner_part[i].astype(f32) + r.inner_got[i].astype(f32),
            )
            counts = jnp.sum(
                jnp.where(iota((patches, byte_count), 0) == r.ids[pl.ds(seq, 1), :], 1.0, 0.0),
                axis=1, keepdims=True,
            )
            pool_grad = (r.branch[i].astype(f32) + back) / jnp.maximum(counts, 1.0)
            high = pool_grad.astype(b16)
            s.pool_high[...] = high
            s.pool_low[...] = (pool_grad - high.astype(f32)).astype(b16)

            @pl.loop(0, half_bytes // BLOCK)
            def _(t, i=i, seq=seq):
                rows = block_at(t)
                place = pl.ds(pl.multiple_of(tensor * half_bytes + t * BLOCK, BLOCK), BLOCK)
                members = members_of(r, seq, place, patches)
                spread = dot_lt(members, s.pool_high[...]) + dot_lt(members, s.pool_low[...])
                part = r.source_part[i, place, :].astype(f32)
                own, _ = back_through(
                    s.source_in[rows, :], first_gain[1:2, :], s.byte_norms[rows, 0:1],
                    part + r.source_got[i, rows, :].astype(f32),
                )
                r.source_got[i, rows, :] = (own + spread).astype(b16)

            near = pltpu.make_async_copy(
                r.source_got.at[i, :, cols_keep], r.byte_grad.at[seq], r.out_sem.at[1, i]
            )
            far = remote(
                r.source_got.at[i, :, cols_give], r.byte_grad.at[seq],
                r.out_send.at[1, i], r.out_recv.at[1, i], "section", 1 - section,
            )
            near.start()
            far.start()
            outs += [near, far]
            tick()
        for copy in outs:
            copy.wait()

    load("w_in", r.in_w_in.at[0], r.w_in, 6)
    load("w_out", r.in_w_out.at[0], r.w_out, 7)
    loads["w_in"].wait()
    loads["w_out"].wait()
    one = dict(
        source_in=pltpu.VMEM((byte_count, width), b16),
        k1=pltpu.VMEM((byte_count, columns), b16),
        v1=pltpu.VMEM((byte_count, columns), b16),
        dk=pltpu.VMEM((byte_count, columns), b16),
        dv=pltpu.VMEM((byte_count, columns), b16),
        probs=pltpu.VMEM((byte_count, LANES), f32),
        prob_grad=pltpu.VMEM((byte_count, LANES), f32),
        raised=pltpu.VMEM((byte_count, LANES), b16),
        inverse=pltpu.VMEM((patches, LANES), f32),
        q1=pltpu.VMEM((patches, columns), b16),
        mixed1=pltpu.VMEM((patches, columns), b16),
        query_in=pltpu.VMEM((patches, width), b16),
        mixed_grad=pltpu.VMEM((patches, columns), b16),
        q_sum=pltpu.VMEM((patches, columns), f32),
        delta_sum=pltpu.VMEM((patches, LANES), f32),
    )

    @functools.partial(pl.run_scoped, **one)
    def _(**scoped):
        for i in range(own_count):
            first_layer(i, scoped)

    attn_in_own, attn_out_own = r.attn_in_part.at[section], r.attn_out_part.at[section]
    gifts = [
        give(3, r.attn_in_part.at[1 - section], r.big_got),
        give(4, r.attn_out_part.at[1 - section], r.attn_out_got),
    ]
    pl.semaphore_wait(r.free_sem, 1)
    for gift in gifts:
        gift.start()

    last = dict(
        source_in=pltpu.VMEM((half_bytes, width), b16),
        byte_norms=pltpu.VMEM((half_bytes, LANES), f32),
        query_in=pltpu.VMEM((patches, width), b16),
        pool_high=pltpu.VMEM((patches, width), b16),
        pool_low=pltpu.VMEM((patches, width), b16),
        latent=pltpu.VMEM((own_count, patches, columns), b16),
    )

    @functools.partial(pl.run_scoped, **last)
    def _(**scoped):
        last_parts(types.SimpleNamespace(**scoped))

    gifts[1].wait()
    total(attn_out_own, r.attn_out_got)

    def picked(ref, base):
        return lambda start, rows: ref.at[section, pl.ds(base + start, rows), :]

    cut = r.cuts
    summed(6, picked(r.attn_out_part, 0), r.attn_out_sum, r.slots_out, cut["out"])
    tick()
    gifts[0].wait()
    total(attn_in_own, r.big_got)
    for n in range(2):
        rows = pl.ds(n * half, half)
        summed(
            8 + 2 * n, picked(r.attn_in_part, n * half), r.attn_in_sum.at[rows, :],
            (r.slots_in0, r.slots_in1)[n], cut["in"],
        )
        tick()
    if summing:
        flows.drain()
    ends = [pltpu.make_async_copy(r.gain_sum, r.gain_out, r.end_sem.at[4])]
    if not summing:
        ends += [
            pltpu.make_async_copy(r.up, r.up_sum, r.end_sem.at[0]),
            pltpu.make_async_copy(r.down, r.down_sum, r.end_sem.at[1]),
            pltpu.make_async_copy(attn_in_own, r.attn_in_sum, r.end_sem.at[2]),
            pltpu.make_async_copy(attn_out_own, r.attn_out_sum, r.end_sem.at[3]),
        ]
    for copy in ends:
        copy.start()
    for copy in ends:
        copy.wait()


def greet_grid(flows, others):
    barrier = pltpu.get_barrier_semaphore()

    def signal(place):
        pl.semaphore_signal(barrier, inc=1, device_id=place, device_id_type=MESH)

    for axis, index in others:
        signal({axis: index})
    signal({"dp": flows.beside})
    pl.when(flows.z < LONG - 1)(lambda: signal({"dp": flows.right}))
    pl.when(flows.z > 0)(lambda: signal({"dp": flows.left}))
    inner = jnp.logical_and(flows.z > 0, flows.z < LONG - 1)
    pl.semaphore_wait(barrier, jnp.where(inner, len(others) + 3, len(others) + 2))


def backward(kept, patch_ids):
    own, patches, width = kept["normed"].shape
    sequences, byte_count = patch_ids.shape
    columns = kept["q1"].shape[-1]
    hidden = kept["hidden"].shape[-1]
    half, half_bytes = width // 2, byte_count // 2
    sems = pltpu.SemaphoreType.DMA
    vmem = pltpu.VMEM
    rows16 = vmem((own, patches, width), b16)
    scratch = dict(
        inner=rows16,
        grad_in=rows16,
        inner_part=rows16,
        inner_got=rows16,
        normed=rows16,
        patch_norms=vmem((own, patches, LANES), f32),
        branch=rows16,
        normed_part=rows16,
        normed_got=rows16,
        source_part=vmem((own, byte_count, width), b16),
        source_got=vmem((own, half_bytes, width), b16),
        latent_got=vmem((own, patches, columns), b16),
        w_in=vmem((3, width, columns), b16),
        w_out=vmem((columns, width), b16),
        gain=vmem((2, 2, width), f32),
        gain_sum=vmem((4, width), f32),
        down_got=vmem((hidden, half), b16),
        down=vmem((hidden, half), b16),
        up=vmem((width, hidden), b16),
        attn_in_part=vmem((2, width, 3 * columns), b16),
        attn_out_part=vmem((2, columns, width), b16),
        big_got=vmem((width, 3 * columns), b16),
        attn_out_got=vmem((columns, width), b16),
        load_sem=sems((16,)),
        first_sem=sems((8,)),
        cross_send=sems((5, own)),
        cross_recv=sems((5, own)),
        give_send=sems((5,)),
        give_recv=sems((5,)),
        out_sem=sems((2, own)),
        out_send=sems((2, own)),
        out_recv=sems((2, own)),
        end_sem=sems((5,)),
        free_sem=pltpu.SemaphoreType.REGULAR,
    )
    cuts = {"down": hidden - hidden // 256 * 128 - 128, "up": half // 2, "in": half // 2}
    cuts["out"] = columns // 2
    slots = {}
    if on_grid():
        for name, rows, cols, cut in (
            ("down", hidden, half, cuts["down"]), ("gate", half, hidden, cuts["up"]),
            ("up", half, hidden, cuts["up"]), ("out", columns, width, cuts["out"]),
            ("in0", half, 3 * columns, cuts["in"]), ("in1", half, 3 * columns, cuts["in"]),
        ):
            scratch["long_" + name] = vmem((7 * cut // LONG, cols), b16)
            scratch["short_" + name] = vmem((10 * (rows - cut) // (SHORT * LONG), cols), b16)
            slots[name] = rows
        scratch |= dict(
            flow_send=sems((12, 17)),
            flow_recv=sems((12, 17)),
            flow_near=sems((12,)),
        )
    ins = [("ids", patch_ids, True)]
    ins += [("in_" + name, kept[name], False) for name in (*KEPT, *LAYERS)]
    outs = [
        ("latents", shape((sequences, patches // 2, columns), b16)),
        ("byte_grad", shape((sequences, half_bytes, half), b16)),
        ("attn_in_sum", shape((width, 3 * columns), b16)),
        ("attn_out_sum", shape((columns, width), b16)),
        ("gain_out", shape((4, width), f32)),
        ("up_sum", shape((width, hidden), b16)),
        ("down_sum", shape((hidden, half), b16)),
    ]

    def kernel(r):
        r.cuts = cuts
        for name in ("down", "gate", "up", "out", "in0", "in1"):
            held = (None, 0, None)
            if name in slots:
                held = (getattr(r, "long_" + name), slots[name], getattr(r, "short_" + name))
            setattr(r, "slots_" + name, held)
        backward_kernel(r)

    return named_call(kernel, ins, outs, scratch, collective_id=1)


def swap(values, axis):
    return lax.ppermute(values, axis, [(0, 1), (1, 0)])


def sum_small(values):
    values = values + swap(values, "tensor")
    values = values + swap(values, "section")
    if lax.axis_size("dp") != LONG * SHORT:
        return lax.psum(values, "dp")
    for apart in (1, 2, 4):
        values = values + lax.ppermute(
            values, "dp", [(i, i ^ apart) for i in range(LONG * SHORT)]
        )
    return values


def per_device(byte_states, patch_ids, attn_in, attn_out, gains, ffn_in, ffn_out, latent_grad):
    width = byte_states.shape[-1]
    columns = attn_in.shape[-1]
    hidden = ffn_out.shape[0]
    half = width // 2
    is_first = lax.axis_index("section") == 0
    kept = forward(
        byte_states, patch_ids, attn_in, attn_out, gains, ffn_in.transpose(1, 0, 2), ffn_out,
        latent_grad,
    )
    got = backward(kept, patch_ids)
    sums = [got[name] for name in ("down_sum", "up_sum", "attn_in_sum", "attn_out_sum")]
    if not on_grid():
        sums = [lax.psum(value, "dp") for value in sums]
    down, up, in_sum, out_sum = [value.astype(f32) for value in sums]
    gain_sum = sum_small(got["gain_out"])
    gain_out = jnp.where(is_first, gain_sum[0:2], gain_sum[2:4])
    in_out = in_sum.reshape(width, 3, columns).transpose(1, 0, 2)
    up_out = up.reshape(2, half, hidden).transpose(1, 0, 2)
    return (
        got["latents"], got["byte_grad"], in_out[None], out_sum[None], gain_out[None], up_out, down
    )


def solution(mesh):
    return jax.shard_map(
        per_device,
        mesh=mesh,
        in_specs=(
            P("dp", None, None),
            P("dp", None),
            P("section", None, None, "tensor"),
            P("section", "tensor", None),
            P("section", None, None),
            P(None, None, "tensor"),
            P("tensor", None),
            P("dp", None, None),
        ),
        out_specs=(
            P("dp", "section", "tensor"),
            P("dp", "tensor", "section"),
            P("section", None, None, "tensor"),
            P("section", "tensor", None),
            P("section", None, None),
            P("section", None, "tensor"),
            P("tensor", "section"),
        ),
        check_vma=False,
    )
```

```python
import functools
import types

import jax
import jax.numpy as jnp
from jax import lax
from jax.experimental import pallas as pl
from jax.experimental.pallas import tpu as pltpu
from jax.sharding import PartitionSpec as P

HD = 64
LANES = 128
BLOCK = 256
WIDE = 512
EPSILON = 1e-05
NEGATIVE = -1000000000.0
SCALE = HD ** (-0.5)
VMEM_BYTES = 63 * 1024 * 1024

f32 = jnp.float32
b16 = jnp.bfloat16


def dot(a, b):
    return jnp.dot(a, b, preferred_element_type=f32)


def dot_rt(a, b):
    return lax.dot_general(a, b, (((1,), (1,)), ((), ())), preferred_element_type=f32)


def dot_lt(a, b):
    return lax.dot_general(a, b, (((0,), (0,)), ((), ())), preferred_element_type=f32)


def inverse_rms(values):
    return lax.rsqrt(jnp.mean(values * values, axis=-1, keepdims=True) + EPSILON)


def iota(shape, dim):
    return lax.broadcasted_iota(jnp.int32, shape, dim)


def one_hot(condition):
    return jnp.where(condition, 1.0, 0.0).astype(b16)


def segment_max(values, ids):
    width = values.shape[1]
    lane = iota(ids.shape, 1)
    lowest = -3.0e38
    ahead, behind = values, values
    step = 1
    while step < width:
        left, right = step, width - step
        same_left = jnp.logical_and(pltpu.roll(ids, left, axis=1) == ids, lane >= step)
        same_right = jnp.logical_and(pltpu.roll(ids, right, axis=1) == ids, lane < right)
        ahead = jnp.maximum(ahead, jnp.where(same_left, pltpu.roll(ahead, left, axis=1), lowest))
        behind = jnp.maximum(
            behind, jnp.where(same_right, pltpu.roll(behind, right, axis=1), lowest)
        )
        step *= 2
    return jnp.maximum(ahead, behind)


def head_masks(width):
    heads_in = one_hot(iota((width, LANES), 0) // HD == iota((width, LANES), 1))
    heads_out = one_hot(iota((LANES, width), 1) // HD == iota((LANES, width), 0))
    return heads_in, heads_out


def split_dot(values, matrix):
    high = values.astype(b16)
    low = (values - high.astype(f32)).astype(b16)
    return dot(high, matrix) + dot(low, matrix)


def block_at(index, size=BLOCK):
    return pl.ds(pl.multiple_of(index * size, size), size)


def each_block(count, body, size=BLOCK):
    @pl.loop(0, count // size)
    def _(index):
        body(block_at(index, size))


MESH = pl.DeviceIdType.MESH


def remote(src, dst, send, recv, axis, index):
    return pltpu.make_async_remote_copy(
        src_ref=src, dst_ref=dst, send_sem=send, recv_sem=recv,
        device_id={axis: index}, device_id_type=MESH,
    )


def greet(places):
    barrier = pltpu.get_barrier_semaphore()
    for axis, index in places:
        pl.semaphore_signal(barrier, inc=1, device_id={axis: index}, device_id_type=MESH)
    pl.semaphore_wait(barrier, len(places))


def exchange_layer(r, section):
    columns = r.attn_in.shape[3]
    copies = []
    for n, (src, dst) in enumerate(
        [
            (r.attn_in.at[0, j], r.w_in.at[section, :, pl.ds(j * columns, columns)])
            for j in (1, 2, 0)
        ]
        + [(r.attn_out.at[0], r.w_out.at[section]), (r.gains.at[0], r.gain.at[section])]
    ):
        near = pltpu.make_async_copy(src, dst, r.near_sem.at[n])
        far = remote(src, dst, r.far_send.at[n], r.far_recv.at[n], "section", 1 - section)
        near.start()
        far.start()
        copies.append((near, far))
    return copies


def arrived(copies):
    for near, far in copies:
        near.wait()
        far.wait()


def members_of(r, seq, rows, patches):
    return one_hot(iota((patches, rows.size), 0) == r.ids[pl.ds(seq, 1), rows])


def names(**kinds):
    return tuple(kinds)


FIRST_KEPT = names(query_in=1, source_in=1, byte_norms=1)
CROSS_KEPT = names(q1=1, k1=1, v1=1, raised=1, inverse=1, mixed1=1)
SECOND_KEPT = names(normed=1, q2=1, k2=1, v2=1, totals=1, mixed2=1)
FEED_KEPT = names(
    inner=1, hidden=1, gate_grad=1, up_grad=1, grad_in=1, inner_part=1, patch_norms=1,
    latent_own=1, latent_send=1,
)
KEPT = FIRST_KEPT + CROSS_KEPT + SECOND_KEPT + FEED_KEPT
LAYERS = names(w_in=1, w_out=1, gain=1)


def forward_kernel(r):
    section, tensor = lax.axis_index("section"), lax.axis_index("tensor")
    own_count, patches, width = r.normed.shape
    byte_count = r.states.shape[1]
    columns = r.q1.shape[2]
    hidden = r.hidden.shape[2]
    heads = columns // HD
    greet([("section", 1 - section), ("tensor", 1 - tensor)])
    state_copies = [
        pltpu.make_async_copy(
            r.states.at[section * own_count + i], r.state_in.at[i], r.state_sem.at[i]
        )
        for i in range(own_count)
    ]
    for copy in state_copies:
        copy.start()
    layer = exchange_layer(r, section)
    grad_copies = [
        pltpu.make_async_copy(
            r.upstream.at[section * own_count + i], r.grad_in.at[i], r.grad_sem.at[i]
        )
        for i in range(own_count)
    ]
    feed_copies = [
        pltpu.make_async_copy(r.ffn_in, r.feed_in, r.feed_sem.at[0]),
        pltpu.make_async_copy(r.ffn_out, r.feed_out, r.feed_sem.at[1]),
    ]
    for copy in grad_copies + feed_copies:
        copy.start()
    heads_in, heads_out = head_masks(columns)

    def keep(name, i):
        n = KEPT.index(name)
        return pltpu.make_async_copy(
            getattr(r, name).at[i], getattr(r, "out_" + name).at[i], r.keep_sem.at[n, i]
        )

    def save(names, i):
        for name in names:
            keep(name, i).start()

    def exchange(step, i):
        return remote(
            r.part.at[step, i], r.got.at[step, i], r.part_send.at[step, i], r.part_recv.at[step, i],
            "tensor", 1 - tensor,
        )

    for copy in state_copies:
        copy.wait()
    layer[-1][0].wait()
    layer[-1][1].wait()
    first_gain = r.gain.at[0]

    @pl.loop(0, own_count)
    def _(i):
        seq = section * own_count + i
        r.pool_sum[...] = jnp.zeros_like(r.pool_sum)

        def pool(rows):
            block = r.state_in[i, rows, :]
            r.pool_sum[...] += dot(members_of(r, seq, rows, patches), block)
            values = block.astype(f32)
            scale = inverse_rms(values)
            r.byte_norms[i, rows, :] = jnp.broadcast_to(scale, (BLOCK, LANES))
            r.source_in[i, rows, :] = (values * scale * first_gain[1:2, :]).astype(b16)

        each_block(byte_count, pool)
        row_ids = r.ids[pl.ds(seq, 1), :]
        counts = jnp.sum(
            jnp.where(iota((patches, byte_count), 0) == row_ids, 1.0, 0.0), axis=1, keepdims=True
        )
        values = r.pool_sum[...] / jnp.maximum(counts, 1.0)
        r.pooled[i] = values
        scale = inverse_rms(values)
        r.patch_norms[i] = jnp.broadcast_to(scale, (patches, LANES))
        r.query_in[i] = (values * scale * first_gain[0:1, :]).astype(b16)
        save(FIRST_KEPT, i)

    arrived(layer[:4])
    layer_saves = [
        pltpu.make_async_copy(getattr(r, name), getattr(r, "out_" + name), r.layer_sem.at[n])
        for n, name in enumerate(LAYERS)
    ]
    for copy in layer_saves:
        copy.start()

    @pl.loop(0, own_count)
    def _(i):
        seq = section * own_count + i
        r.q1[i] = dot(r.query_in[i], r.w_in[0, :, :columns]).astype(b16)

        def project(rows):
            both = dot(r.source_in[i, rows, :], r.w_in[0, :, columns:])
            keys = both[:, :columns].astype(b16)
            r.k1[i, rows, :] = keys
            r.v1[i, rows, :] = both[:, columns:].astype(b16)
            spread = dot_lt(members_of(r, seq, rows, patches), r.q1[i])
            block_scores = split_dot(spread * keys.astype(f32), heads_in) * SCALE
            r.scores[:, rows] = block_scores.T[:heads, :]

        each_block(byte_count, project, WIDE)
        scores = r.scores[...]
        r.scores[...] = jnp.exp(scores - segment_max(scores, r.ids[pl.ds(seq, 1), :]))
        r.mix_sum[...] = jnp.zeros_like(r.mix_sum)
        r.total_sum[...] = jnp.zeros_like(r.total_sum)

        def mix(rows):
            short = r.scores[:, rows]
            filled = jnp.concatenate([short, jnp.zeros((LANES - heads, WIDE), f32)], axis=0)
            raised = filled.T.astype(b16)
            r.raised[i, rows, :] = raised
            members = members_of(r, seq, rows, patches)
            weighted = (dot(raised, heads_out) * r.v1[i, rows, :].astype(f32)).astype(b16)
            r.mix_sum[...] += dot(members, weighted)
            r.total_sum[...] += dot(members, raised)

        each_block(byte_count, mix, WIDE)
        totals = r.total_sum[...]
        inverse = jnp.where(totals > 0.0, 1.0 / totals, 0.0)
        r.inverse[i] = inverse
        mixed = (r.mix_sum[...] * split_dot(inverse, heads_out)).astype(b16)
        r.mixed1[i] = mixed
        r.part[0, i] = dot(mixed, r.w_out[0]).astype(b16)
        exchange(0, i).start()
        save(CROSS_KEPT, i)

    second_gain = r.gain.at[1]
    allowed = iota((patches, patches), 1) <= iota((patches, patches), 0)
    lane = iota((patches, LANES), 1)

    @pl.loop(0, own_count)
    def _(i):
        exchange(0, i).wait()
        latent = (
            r.pooled[i] + r.part[0, i].astype(f32) + r.got[0, i].astype(f32)
        ).astype(b16)
        r.latent[i] = latent
        values = latent.astype(f32)
        scale = inverse_rms(values)
        r.patch_norms[i] = jnp.where(lane == 1, scale, r.patch_norms[i])
        normed = (values * scale * second_gain[0:1, :]).astype(b16)
        r.normed[i] = normed
        projected = dot(normed, r.w_in[1]).astype(b16)
        query, key, value = [projected[:, j * columns : (j + 1) * columns] for j in range(3)]
        r.q2[i] = query
        r.k2[i] = key
        r.v2[i] = value
        kept = jnp.zeros((patches, LANES), f32)
        outs = []
        for head in range(heads):
            own = slice(head * HD, (head + 1) * HD)
            scores = jnp.where(allowed, dot_rt(query[:, own], key[:, own]) * SCALE, NEGATIVE)
            highest = jnp.max(scores, axis=-1, keepdims=True)
            raised = jnp.exp(scores - highest)
            total = jnp.sum(raised, axis=-1, keepdims=True)
            outs.append(dot((raised / total).astype(b16), value[:, own]))
            kept = jnp.where(lane == head, highest + jnp.log(total), kept)
        r.totals[i] = kept
        mixed = jnp.concatenate(outs, axis=1).astype(b16)
        r.mixed2[i] = mixed
        r.part[1, i] = dot(mixed, r.w_out[1]).astype(b16)
        exchange(1, i).start()
        save(SECOND_KEPT, i)

    for copy in grad_copies + feed_copies:
        copy.wait()

    @pl.loop(0, own_count)
    def _(i):
        seq = section * own_count + i
        exchange(1, i).wait()
        values = (
            r.latent[i].astype(f32) + r.part[1, i].astype(f32) + r.got[1, i].astype(f32)
        )
        r.middle[...] = values
        scale = inverse_rms(values)
        r.patch_norms[i] = jnp.where(lane == 2, scale, r.patch_norms[i])
        r.inner[i] = (values * scale * second_gain[1:2, :]).astype(b16)
        valid = iota((patches, 1), 0) <= jnp.max(r.ids[pl.ds(seq, 1), :], axis=1, keepdims=True)
        r.grad_in[i] = jnp.where(valid, r.grad_in[i].astype(f32), 0.0).astype(b16)

        gate = dot(r.inner[i], r.feed_in[0])
        up = dot(r.inner[i], r.feed_in[1])
        hidden_grad = dot_rt(r.grad_in[i], r.feed_out[...])
        gated = 1.0 / (1.0 + jnp.exp(-gate))
        act = gate * gated
        r.hidden[i] = (act * up).astype(b16)
        r.gate_grad[i] = (hidden_grad * up * (gated * (1.0 + gate * (1.0 - gated)))).astype(b16)
        r.up_grad[i] = (hidden_grad * act).astype(b16)
        inner_grad = dot_rt(r.gate_grad[i], r.feed_in[0]) + dot_rt(r.up_grad[i], r.feed_in[1])
        r.inner_part[i] = inner_grad.astype(b16)
        r.out_sum[...] = dot(r.hidden[i], r.feed_out[...])
        mine, theirs = block_at(tensor, columns), block_at(1 - tensor, columns)
        r.latent_own[i] = (r.middle[:, mine] + r.out_sum[:, mine]).astype(b16)
        r.latent_send[i] = r.out_sum[:, theirs].astype(b16)
        save(FEED_KEPT, i)

    @pl.loop(0, own_count)
    def _(i):
        for name in KEPT:
            keep(name, i).wait()

    for copy in layer_saves:
        copy.wait()


def shape(dims, dtype):
    return jax.ShapeDtypeStruct(dims, dtype)


def named_call(kernel, ins, outs, scratch, **params):
    any_space = pl.BlockSpec(memory_space=pl.ANY)
    whole = pl.BlockSpec(memory_space=pltpu.VMEM)
    names = [name for name, _, _ in ins] + [name for name, _ in outs] + list(scratch)

    def body(*refs):
        kernel(types.SimpleNamespace(**dict(zip(names, refs, strict=True))))

    got = pl.pallas_call(
        body,
        out_shape=tuple(s for _, s in outs),
        in_specs=[whole if inside else any_space for _, _, inside in ins],
        out_specs=tuple(any_space for _ in outs),
        scratch_shapes=list(scratch.values()),
        compiler_params=pltpu.CompilerParams(
            vmem_limit_bytes=VMEM_BYTES, has_side_effects=True, **params
        ),
    )(*(array for _, array, _ in ins))
    return {name: value for (name, _), value in zip(outs, got, strict=True)}


def forward(byte_states, patch_ids, attn_in, attn_out, gains, feed_in, feed_out, latent_grad):
    sequences, byte_count, width = byte_states.shape
    patches = byte_count // 4
    columns = attn_in.shape[-1]
    hidden = feed_out.shape[0]
    own = sequences // 2
    heads = columns // HD
    dims = dict(
        query_in=(own, patches, width, b16),
        source_in=(own, byte_count, width, b16),
        q1=(own, patches, columns, b16),
        k1=(own, byte_count, columns, b16),
        v1=(own, byte_count, columns, b16),
        raised=(own, byte_count, LANES, b16),
        inverse=(own, patches, LANES, f32),
        mixed1=(own, patches, columns, b16),
        byte_norms=(own, byte_count, LANES, f32),
        normed=(own, patches, width, b16),
        q2=(own, patches, columns, b16),
        k2=(own, patches, columns, b16),
        v2=(own, patches, columns, b16),
        totals=(own, patches, LANES, f32),
        mixed2=(own, patches, columns, b16),
        inner=(own, patches, width, b16),
        hidden=(own, patches, hidden, b16),
        gate_grad=(own, patches, hidden, b16),
        up_grad=(own, patches, hidden, b16),
        grad_in=(own, patches, width, b16),
        inner_part=(own, patches, width, b16),
        patch_norms=(own, patches, LANES, f32),
        latent_own=(own, patches, columns, b16),
        latent_send=(own, patches, columns, b16),
    )
    sems = pltpu.SemaphoreType.DMA
    scratch = {name: pltpu.VMEM(dims[name][:-1], dims[name][-1]) for name in KEPT}
    scratch |= dict(
        state_in=pltpu.VMEM((own, byte_count, width), b16),
        pooled=pltpu.VMEM((own, patches, width), f32),
        latent=pltpu.VMEM((own, patches, width), b16),
        middle=pltpu.VMEM((patches, width), f32),
        out_sum=pltpu.VMEM((patches, width), f32),
        w_in=pltpu.VMEM((2, width, 3 * columns), b16),
        w_out=pltpu.VMEM((2, columns, width), b16),
        gain=pltpu.VMEM((2, 2, width), f32),
        feed_in=pltpu.VMEM((2, width, hidden), b16),
        feed_out=pltpu.VMEM((hidden, width), b16),
        pool_sum=pltpu.VMEM((patches, width), f32),
        scores=pltpu.VMEM((heads, byte_count), f32),
        mix_sum=pltpu.VMEM((patches, columns), f32),
        total_sum=pltpu.VMEM((patches, LANES), f32),
        part=pltpu.VMEM((2, own, patches, width), b16),
        got=pltpu.VMEM((2, own, patches, width), b16),
        state_sem=sems((own,)),
        grad_sem=sems((own,)),
        feed_sem=sems((2,)),
        near_sem=sems((5,)),
        far_send=sems((5,)),
        far_recv=sems((5,)),
        part_send=sems((2, own)),
        part_recv=sems((2, own)),
        keep_sem=sems((len(KEPT), own)),
        layer_sem=sems((len(LAYERS),)),
    )
    ins = [
        ("states", byte_states, False), ("ids", patch_ids, True), ("attn_in", attn_in, False),
        ("attn_out", attn_out, False), ("gains", gains, False), ("ffn_in", feed_in, False),
        ("ffn_out", feed_out, False), ("upstream", latent_grad, False),
    ]
    dims |= dict(
        w_in=(2, width, 3 * columns, b16),
        w_out=(2, columns, width, b16),
        gain=(2, 2, width, f32),
    )
    names = (*KEPT, *LAYERS)
    outs = [("out_" + name, shape(dims[name][:-1], dims[name][-1])) for name in names]
    got = named_call(forward_kernel, ins, outs, scratch, collective_id=0)
    return {name: got["out_" + name] for name in names}


def flat(ref, cols):
    block = ref[:, :, cols]
    return block.reshape(block.shape[0] * block.shape[1], block.shape[2])


def total(target, got):
    def tile(rows):
        target[rows, :] = (target[rows, :].astype(f32) + got[rows, :].astype(f32)).astype(b16)

    each_block(target.shape[0], tile, LANES)


LONG, SHORT = 4, 2


class Flows:
    def __init__(self, r, section):
        self.r = r
        self.section = section
        place = lax.axis_index("dp")
        self.z, self.y = place // SHORT, lax.rem(place, SHORT)
        self.right, self.left = place + SHORT, place - SHORT
        self.beside = place + 1 - 2 * self.y
        self.active = []

    def hop(self, src, dst, n, j, target):
        r = self.r
        return pltpu.make_async_remote_copy(
            src_ref=src, dst_ref=dst, send_sem=r.flow_send.at[n, j], recv_sem=r.flow_recv.at[n, j],
            device_id={"dp": target}, device_id_type=MESH,
        )

    def at(self, places, body):
        condition = self.z == places[0]
        for z in places[1:]:
            condition = jnp.logical_or(condition, self.z == z)
        pl.when(condition)(body)

    @staticmethod
    def add(target, got):
        rows, width = target.shape

        @pl.loop(0, rows // 16)
        def _(t):
            at = block_at(t, 16)
            target[at, :] = (target[at, :].astype(f32) + got[at, :].astype(f32)).astype(b16)

    def reduce_steps(self, n, part, slot):
        def up(k):
            src = slot(k - 1)
            return self.hop(src, src, n, k - 1, self.right)

        def down(k):
            src = slot(3 + k)
            return self.hop(src, src, n, 3 + k, self.left)

        def pass_on(copy, place, k):
            copy.wait_recv()
            self.add(place, part(k))
            copy.start()

        def begin():
            def first():
                for k in (3, 2, 1):
                    self.hop(part(k), slot(k - 1), n, k - 1, self.right).start()

            def last():
                for k in (0, 1, 2):
                    self.hop(part(k), slot(3 + k), n, 3 + k, self.left).start()

            self.at([0], first)
            self.at([3], last)

        def second():
            self.at([1], lambda: pass_on(up(3), slot(2), 3))
            self.at([2], lambda: pass_on(down(0), slot(3), 0))

        def third():
            def at_one():
                pass_on(up(2), slot(1), 2)
                pass_on(down(0), slot(3), 0)

            def at_two():
                pass_on(down(1), slot(4), 1)
                pass_on(up(3), slot(2), 3)

            self.at([1], at_one)
            self.at([2], at_two)

        def close():
            def finish(k):
                def body():
                    if k >= 1:
                        up(k).wait_recv()
                        self.add(part(k), slot(k - 1))
                    if k <= 2:
                        down(k).wait_recv()
                        self.add(part(k), slot(3 + k))

                return body

            for k in range(LONG):
                self.at([k], finish(k))

        def sent():
            ups = {0: (1, 2, 3), 1: (2, 3), 2: (3,), 3: ()}
            downs = {0: (), 1: (0,), 2: (0, 1), 3: (0, 1, 2)}
            for z in range(LONG):

                def body(z=z):
                    for k in ups[z]:
                        up(k).wait_send()
                    for k in downs[z]:
                        down(k).wait_send()

                self.at([z], body)

        return [begin, second, third, close], sent

    def gather_steps(self, n, own, out, extra=None):
        def up(src, k, d):
            return self.hop(src, out(k), n, 7 + d, self.right)

        def down(src, k, d):
            return self.hop(src, out(k), n, 10 + d, self.left)

        def near():
            return pltpu.make_async_copy(own(), out(self.z), self.r.flow_near.at[n])

        def begin():
            near().start()
            self.at([0, 1, 2], lambda: up(own(), self.z, 0).start())
            self.at([1, 2, 3], lambda: down(own(), self.z, 0).start())
            if extra:
                extra(own(), self.z).start()

        def step(d):
            def from_left():
                k = self.z - d
                up(out(k), k, d - 1).wait_recv()
                if d < LONG - 1:
                    pl.when(self.z < LONG - 1)(lambda: up(out(k), k, d).start())
                if extra:
                    extra(out(k), k).start()

            def from_right():
                k = self.z + d
                down(out(k), k, d - 1).wait_recv()
                if d < LONG - 1:
                    pl.when(self.z > 0)(lambda: down(out(k), k, d).start())
                if extra:
                    extra(out(k), k).start()

            def body():
                self.at(list(range(d, LONG)), from_left)
                self.at(list(range(0, LONG - d)), from_right)

            return body

        def sent():
            near().wait()
            self.at([0, 1, 2], lambda: up(own(), self.z, 0).wait_send())
            self.at([1, 2, 3], lambda: down(own(), self.z, 0).wait_send())
            if extra:
                extra(own(), self.z).wait_send()
            for d in (1, 2, 3):

                def left_sent(d=d):
                    k = self.z - d
                    if d < LONG - 1:
                        pl.when(self.z < LONG - 1)(lambda: up(out(k), k, d).wait_send())
                    if extra:
                        extra(out(k), k).wait_send()

                def right_sent(d=d):
                    k = self.z + d
                    if d < LONG - 1:
                        pl.when(self.z > 0)(lambda: down(out(k), k, d).wait_send())
                    if extra:
                        extra(out(k), k).wait_send()

                self.at(list(range(d, LONG)), left_sent)
                self.at(list(range(0, LONG - d)), right_sent)

        return [begin, step(1), step(2), step(3)], sent

    def long_first(self, n, data, out, slots, start, rows):
        c = rows // LONG

        def part(k):
            return data(pl.multiple_of(start + k * c, 16), c)

        def place(k):
            return out(pl.multiple_of(start + k * c, 16), c)

        def slot(j):
            return slots.at[pl.ds(j * c, c), :]

        def beside():
            return self.hop(part(self.z), slot(6), n, 6, self.beside)

        reduce, reduce_sent = self.reduce_steps(n, part, slot)
        gather, gather_sent = self.gather_steps(n, lambda: slot(6), place)

        def middle():
            reduce[3]()
            beside().start()

        def turn():
            beside().wait_recv()
            self.add(slot(6), part(self.z))
            gather[0]()

        def end():
            gather[3]()
            reduce_sent()
            beside().wait_send()
            gather_sent()

        return [*reduce[:3], middle, turn, gather[1], gather[2], end]

    def short_first(self, n, data, out, slots, start, rows):
        half = rows // SHORT
        c = half // LONG

        def part(k):
            return data(pl.multiple_of(start + self.y * half + k * c, 16), c)

        def place(k, y=None):
            y = self.y if y is None else y
            return out(pl.multiple_of(start + y * half + k * c, 16), c)

        def slot(j):
            return slots.at[pl.ds(j * c, c), :]

        landing = slots.at[pl.ds(6 * c, half), :]

        def mine(y):
            return data(pl.multiple_of(start + y * half, 16), half)

        def beside():
            return self.hop(mine(1 - self.y), landing, n, 6, self.beside)

        def spread(src, k):
            return self.hop(src, place(k), n, 13 + k, self.beside)

        reduce, reduce_sent = self.reduce_steps(n, part, slot)
        gather, gather_sent = self.gather_steps(n, lambda: part(self.z), place, spread)

        def begin():
            beside().start()

        def turn():
            beside().wait_recv()
            self.add(mine(self.y), landing)
            reduce[0]()

        def middle():
            reduce[3]()
            gather[0]()

        def end():
            reduce_sent()
            beside().wait_send()
            gather_sent()
            for k in range(LONG):
                there = place(k, 1 - self.y)
                self.hop(there, there, n, 13 + k, self.beside).wait_recv()

        return [begin, turn, reduce[1], reduce[2], middle, *gather[1:], end]

    def open(self, only, *flows):
        for flow in flows:
            self.active.append([(only, step) for step in flow])

    def tick(self):
        for flow in self.active:
            only, step = flow.pop(0)
            if only is None:
                step()
            else:
                pl.when(self.section == only)(step)
        self.active = [flow for flow in self.active if flow]

    def drain(self):
        while self.active:
            self.tick()


def on_grid():
    return lax.axis_size("dp") == LONG * SHORT


def backward_kernel(r):
    section, tensor = lax.axis_index("section"), lax.axis_index("tensor")
    own_count, patches, width = r.normed.shape
    byte_count = r.ids.shape[1]
    columns = r.w_out.shape[0]
    hidden = r.down.shape[0]
    heads = columns // HD
    half = width // 2
    half_bytes = byte_count // 2
    summing = on_grid()
    loads = {}

    def load(name, src, dst, *sem):
        copy = pltpu.make_async_copy(src, dst, r.load_sem.at[sem])
        copy.start()
        loads[name] = copy

    held_names = ("inner", "grad_in", "inner_part", "normed", "patch_norms", "gain")
    for n, name in enumerate(held_names):
        load(name, getattr(r, "in_" + name), getattr(r, name), n)
    load("w_in", r.in_w_in.at[1], r.w_in, 6)
    load("w_out", r.in_w_out.at[1], r.w_out, 7)
    others = [("section", 1 - section), ("tensor", 1 - tensor)]
    flows = Flows(r, section) if summing else None
    if summing:
        greet_grid(flows, others)
    else:
        greet(others)

    def cross(src, dst, i, sem):
        return remote(
            src, dst, r.cross_send.at[sem, i], r.cross_recv.at[sem, i], "tensor", 1 - tensor
        )

    def inner_exchange(i):
        return cross(r.in_inner_part.at[i], r.inner_got.at[i], i, 0)

    def normed_exchange(i):
        return cross(r.normed_part.at[i], r.normed_got.at[i], i, 1)

    def query_exchange(i):
        return cross(r.inner_part.at[i], r.inner_got.at[i], i, 2)

    def source_exchange(i):
        theirs = block_at(1 - tensor, half_bytes)
        return cross(r.source_part.at[i, theirs, :], r.source_got.at[i], i, 3)

    def latent_exchange(i):
        return cross(r.in_latent_send.at[i], r.latent_got.at[i], i, 4)

    for i in range(own_count):
        inner_exchange(i).start()
    for i in range(own_count):
        latent_exchange(i).start()

    def give(n, src, dst):
        return remote(src, dst, r.give_send.at[n], r.give_recv.at[n], "section", 1 - section)

    def tick():
        if summing:
            flows.tick()

    def summed(n, data, out, only=None):
        if summing:
            long_slots, short_slots, rows, cut = r.slots[n]
            flows.open(
                only,
                flows.long_first(2 * n, data, out, long_slots, 0, cut),
                flows.short_first(2 * n + 1, data, out, short_slots, cut, rows - cut),
            )

    def whole(ref):
        return lambda start, rows: ref.at[pl.ds(start, rows), :]

    @functools.partial(
        pl.run_scoped,
        hidden_all=pltpu.VMEM((own_count, patches, hidden), b16),
        gate_all=pltpu.VMEM((own_count, patches, hidden), b16),
        up_all=pltpu.VMEM((own_count, patches, hidden), b16),
        down_give=pltpu.VMEM((hidden, half), b16),
    )
    def _(hidden_all, gate_all, up_all, down_give):
        parts = {"hidden": hidden_all, "gate_grad": gate_all, "up_grad": up_all}
        for n, (name, ref) in enumerate(parts.items()):
            load(name, getattr(r, "in_" + name), ref, n + 8)
        for name in (*parts, "inner", "grad_in"):
            loads[name].wait()

        def down_grad(target, side):
            upstream = flat(r.grad_in, block_at(side, half))

            def tile(cols):
                target[cols, :] = dot_lt(flat(hidden_all, cols), upstream).astype(b16)

            each_block(hidden, tile)
            if hidden % BLOCK:
                tile(pl.ds(hidden - hidden % BLOCK, hidden % BLOCK))

        def up_grad(target, ref, side):
            upstream = flat(ref, slice(None))

            def tile(rows):
                cols = pl.ds(pl.multiple_of(side * half + rows.start, BLOCK), BLOCK)
                target[rows, :] = dot_lt(flat(r.inner, cols), upstream).astype(b16)

            each_block(half, tile)

        used = pl.ds(0, hidden)
        give_rows = [pl.ds(0, half), pl.ds(half, half)]
        gate_give, up_give = [r.attn_in_part.at[1, rows, used] for rows in give_rows]
        gate_got, up_got = [r.big_got.at[rows, used] for rows in give_rows]
        gate_own, up_own = [r.up.at[rows, :] for rows in give_rows]
        gifts = [
            give(0, down_give, r.down_got), give(1, gate_give, gate_got), give(2, up_give, up_got)
        ]
        other = 1 - section
        down_grad(down_give, other)
        gifts[0].start()
        down_grad(r.down, section)
        up_grad(gate_give, gate_all, other)
        gifts[1].start()
        gifts[0].wait()
        total(r.down, r.down_got)
        summed(0, whole(r.down), whole(r.down_sum))
        tick()
        up_grad(gate_own, gate_all, section)
        up_grad(up_give, up_all, other)
        gifts[2].start()
        gifts[1].wait()
        total(gate_own, gate_got)
        summed(1, whole(gate_own), whole(r.up_sum.at[give_rows[0], :]))
        tick()
        up_grad(up_own, up_all, section)
        gifts[2].wait()
        total(up_own, up_got)
        summed(2, whole(up_own), whole(r.up_sum.at[give_rows[1], :]))
        tick()
        pl.semaphore_signal(
            r.free_sem, inc=1, device_id={"section": other}, device_id_type=MESH
        )

    def gifts_of(layer):
        return [
            give(3, r.attn_in_part.at[layer], r.big_got),
            give(4, r.attn_out_part.at[layer], r.attn_out_got),
        ]

    def hand_over(layer):
        @pl.when(section != layer)
        def _():
            pl.semaphore_wait(r.free_sem, 1)
            for gift in gifts_of(layer):
                gift.start()

    def take_over(layer):
        @pl.when(section != layer)
        def _():
            for gift in gifts_of(layer):
                gift.wait_send()

        @pl.when(section == layer)
        def _():
            for gift in gifts_of(layer):
                gift.wait_recv()
            total(r.attn_out_part.at[layer], r.attn_out_got)
            total(r.attn_in_part.at[layer], r.big_got)

    def sum_layer(layer, which):
        def columns_of(j):
            cols = pl.ds(j * columns, columns)
            return lambda start, rows: r.attn_in_part.at[layer, pl.ds(start, rows), cols]

        if which == 3:
            summed(3, whole(r.attn_out_part.at[layer]), whole(r.attn_out_sum), layer)
        else:
            summed(4 + which, columns_of(which), whole(r.attn_in_sum.at[which]), layer)

    first_gain, second_gain = r.gain.at[0], r.gain.at[1]

    def back_through(normed, gain_row, scale, upstream):
        unit = normed.astype(f32) / gain_row
        scaled = upstream * gain_row
        mean = jnp.mean(unit * scaled, axis=-1, keepdims=True)
        return (scaled - unit * mean) * scale, unit

    @functools.partial(
        pl.run_scoped,
        q2=pltpu.VMEM((own_count, patches, columns), b16),
        k2=pltpu.VMEM((own_count, patches, columns), b16),
        v2=pltpu.VMEM((own_count, patches, columns), b16),
        totals=pltpu.VMEM((own_count, patches, LANES), f32),
        mixed2=pltpu.VMEM((own_count, patches, columns), b16),
        second_grads=pltpu.VMEM((own_count, patches, 3 * columns), b16),
    )
    def _(q2, k2, v2, totals, mixed2, second_grads):
        parts = {"q2": q2, "k2": k2, "v2": v2, "totals": totals, "mixed2": mixed2}
        for n, (name, ref) in enumerate(parts.items()):
            load(name, getattr(r, "in_" + name), ref, n + 11)
        for name in (*held_names[2:], "w_in", "w_out", *parts):
            loads[name].wait()
        r.gain_sum[...] = jnp.zeros_like(r.gain_sum)
        allowed = iota((patches, patches), 1) <= iota((patches, patches), 0)
        for i in range(own_count):
            inner_exchange(i).wait()
            own_part = r.inner_part[i].astype(f32)
            back, unit = back_through(
                r.inner[i], second_gain[1:2, :], r.patch_norms[i, :, 2:3],
                own_part + r.inner_got[i].astype(f32),
            )
            r.gain_sum[3:4, :] += jnp.sum(unit * own_part, axis=0, keepdims=True)
            branch = (r.grad_in[i].astype(f32) + back).astype(b16)
            r.branch[i] = branch
            mixed_grad = dot_rt(branch, r.w_out[...]).astype(b16)
            q_outs, k_outs, v_outs = [], [], []
            for head in range(heads):
                own = slice(head * HD, (head + 1) * HD)
                query, key, value = q2[i, :, own], k2[i, :, own], v2[i, :, own]
                upper = mixed_grad[:, own]
                scores = jnp.where(allowed, dot_rt(query, key) * SCALE, NEGATIVE)
                probs = jnp.exp(scores - totals[i, :, head : head + 1])
                prob_grad = dot_rt(upper, value)
                delta = jnp.sum(probs * prob_grad, axis=-1, keepdims=True)
                score_grad = (probs * (prob_grad - delta)).astype(b16)
                q_outs.append(dot(score_grad, key) * SCALE)
                k_outs.append(dot_lt(score_grad, query) * SCALE)
                v_outs.append(dot_lt(probs.astype(b16), upper))
            grads = jnp.concatenate(q_outs + k_outs + v_outs, axis=1).astype(b16)
            second_grads[i] = grads
            r.normed_part[i] = dot_rt(grads, r.w_in[...]).astype(b16)
            normed_exchange(i).start()
            tick()

        def outer(target, rows_ref, upstream, tiles):
            @pl.loop(0, tiles)
            def _(t):
                cols = block_at(t)
                target[cols, :] = dot_lt(flat(rows_ref, cols), upstream).astype(b16)

        outer(r.attn_in_part.at[1], r.normed, flat(second_grads, slice(None)), width // BLOCK)
        outer(r.attn_out_part.at[1], mixed2, flat(r.branch, slice(None)), columns // BLOCK)
        hand_over(1)
        tick()

    heads_in, heads_out = head_masks(columns)

    def first_layer(i, scoped):
        seq = section * own_count + i
        s = types.SimpleNamespace(**scoped)
        copies = {}
        names = (*CROSS_KEPT, "source_in", "query_in")
        for n, name in enumerate(names):
            copy = pltpu.make_async_copy(
                getattr(r, "in_" + name).at[i], getattr(s, name), r.first_sem.at[n]
            )
            copy.start()
            copies[name] = copy
        normed_exchange(i).wait()
        own_part = r.normed_part[i].astype(f32)
        back, unit = back_through(
            r.normed[i], second_gain[0:1, :], r.patch_norms[i, :, 1:2],
            own_part + r.normed_got[i].astype(f32),
        )
        r.gain_sum[2:3, :] += jnp.sum(unit * own_part, axis=0, keepdims=True)
        branch = (r.branch[i].astype(f32) + back).astype(b16)
        r.branch[i] = branch
        s.mixed_grad[...] = dot_rt(branch, r.w_out[...]).astype(b16)
        s.q_sum[...] = jnp.zeros_like(s.q_sum)
        s.delta_sum[...] = jnp.zeros_like(s.delta_sum)
        for copy in copies.values():
            copy.wait()
        inverse = s.inverse[...]
        inverse_high = inverse.astype(b16)
        inverse_low = (inverse - inverse_high.astype(f32)).astype(b16)

        def value_side(rows):
            members = members_of(r, seq, rows, patches)
            spread = dot_lt(members, s.mixed_grad[...])
            scale = dot_lt(members, inverse_high) + dot_lt(members, inverse_low)
            probs = s.raised[rows, :].astype(f32) * scale
            s.probs[rows, :] = probs
            s.dkv[rows, columns:] = (dot(probs.astype(b16), heads_out) * spread).astype(b16)
            prob_grad = split_dot(spread * s.v1[rows, :].astype(f32), heads_in)
            s.prob_grad[rows, :] = prob_grad
            product = probs * prob_grad
            high = product.astype(b16)
            low = (product - high.astype(f32)).astype(b16)
            s.delta_sum[...] += dot(members, high) + dot(members, low)

        each_block(byte_count, value_side, WIDE)
        tick()
        delta = s.delta_sum[...]
        delta_high = delta.astype(b16)
        delta_low = (delta - delta_high.astype(f32)).astype(b16)

        def key_side(rows):
            members = members_of(r, seq, rows, patches)
            shift = dot_lt(members, delta_high) + dot_lt(members, delta_low)
            score_grad = (s.probs[rows, :] * (s.prob_grad[rows, :] - shift)).astype(b16)
            spread = dot(score_grad, heads_out)
            s.dkv[rows, :columns] = (spread * dot_lt(members, s.q1[...]) * SCALE).astype(b16)
            s.q_sum[...] += dot(members, (spread * s.k1[rows, :].astype(f32)).astype(b16))
            source = dot_rt(s.dkv[rows, :], r.w_in[:, columns:])
            r.source_part[i, rows, :] = source.astype(b16)
            unit_block = s.source_in[rows, :].astype(f32)
            r.gain_sum[1:2, :] += (
                jnp.sum(unit_block * source, axis=0, keepdims=True) / first_gain[1:2, :]
            )

        each_block(byte_count, key_side, WIDE)
        source_exchange(i).start()
        q_grad = (s.q_sum[...] * SCALE).astype(b16)
        query = dot_rt(q_grad, r.w_in[:, :columns])
        r.inner_part[i] = query.astype(b16)
        query_exchange(i).start()
        unit_pool = s.query_in[...].astype(f32)
        r.gain_sum[0:1, :] += (
            jnp.sum(unit_pool * query, axis=0, keepdims=True) / first_gain[0:1, :]
        )
        tick()

        def add_to(target, rows, cols, value):
            if i:
                value = target[rows, cols].astype(f32) + value
            target[rows, cols] = value.astype(b16)

        @pl.loop(0, width // BLOCK)
        def _(t):
            cols = block_at(t)
            source = s.source_in[:, cols]
            target = r.attn_in_part.at[0]
            add_to(target, cols, slice(0, columns), dot_lt(s.query_in[:, cols], q_grad))
            add_to(target, cols, slice(columns, 3 * columns), dot_lt(source, s.dkv[...]))

        @pl.loop(0, columns // BLOCK)
        def _(t):
            cols = block_at(t)
            add_to(
                r.attn_out_part.at[0], cols, slice(None), dot_lt(s.mixed1[:, cols], branch)
            )

        tick()

    def last_parts(s):
        half_rows = patches // 2
        rows_keep, rows_give = block_at(section, half_rows), block_at(1 - section, half_rows)
        outs = []
        for i in range(own_count):
            seq = section * own_count + i
            s_load = pltpu.make_async_copy(r.in_latent_own.at[i], s.latent.at[i], r.first_sem.at[i])
            s_load.start()
            s_load.wait()
            latent_exchange(i).wait()
            last = jnp.max(r.ids[pl.ds(seq, 1), :], axis=1, keepdims=True)
            valid = iota((patches, 1), 0) <= last
            values = s.latent[i].astype(f32) + r.latent_got[i].astype(f32)
            s.latent[i] = jnp.where(valid, values, 0.0).astype(b16)
            near = pltpu.make_async_copy(
                s.latent.at[i, rows_keep, :], r.latents.at[seq], r.out_sem.at[0, i]
            )
            far = remote(
                s.latent.at[i, rows_give, :], r.latents.at[seq],
                r.out_send.at[0, i], r.out_recv.at[0, i], "section", 1 - section,
            )
            near.start()
            far.start()
            outs += [near, far]

        own_rows = block_at(tensor, half_bytes)
        cols_keep, cols_give = block_at(section, half), block_at(1 - section, half)
        for i in range(own_count):
            seq = section * own_count + i
            finals = [
                pltpu.make_async_copy(
                    r.in_source_in.at[i, own_rows, :], s.source_in, r.first_sem.at[0]
                ),
                pltpu.make_async_copy(
                    r.in_byte_norms.at[i, own_rows, :], s.byte_norms, r.first_sem.at[1]
                ),
                pltpu.make_async_copy(r.in_query_in.at[i], s.query_in, r.first_sem.at[2]),
            ]
            for copy in finals:
                copy.start()
            query_exchange(i).wait()
            source_exchange(i).wait()
            for copy in finals:
                copy.wait()
            back, _ = back_through(
                s.query_in[...], first_gain[0:1, :], r.patch_norms[i, :, 0:1],
                r.inner_part[i].astype(f32) + r.inner_got[i].astype(f32),
            )
            counts = jnp.sum(
                jnp.where(iota((patches, byte_count), 0) == r.ids[pl.ds(seq, 1), :], 1.0, 0.0),
                axis=1, keepdims=True,
            )
            pool_grad = (r.branch[i].astype(f32) + back) / jnp.maximum(counts, 1.0)
            high = pool_grad.astype(b16)
            s.pool_high[...] = high
            s.pool_low[...] = (pool_grad - high.astype(f32)).astype(b16)

            @pl.loop(0, half_bytes // BLOCK)
            def _(t, i=i, seq=seq):
                rows = block_at(t)
                place = pl.ds(pl.multiple_of(tensor * half_bytes + t * BLOCK, BLOCK), BLOCK)
                members = members_of(r, seq, place, patches)
                spread = dot_lt(members, s.pool_high[...]) + dot_lt(members, s.pool_low[...])
                part = r.source_part[i, place, :].astype(f32)
                own, _ = back_through(
                    s.source_in[rows, :], first_gain[1:2, :], s.byte_norms[rows, 0:1],
                    part + r.source_got[i, rows, :].astype(f32),
                )
                r.source_got[i, rows, :] = (own + spread).astype(b16)

            near = pltpu.make_async_copy(
                r.source_got.at[i, :, cols_keep], r.byte_grad.at[seq], r.out_sem.at[1, i]
            )
            far = remote(
                r.source_got.at[i, :, cols_give], r.byte_grad.at[seq],
                r.out_send.at[1, i], r.out_recv.at[1, i], "section", 1 - section,
            )
            near.start()
            far.start()
            outs += [near, far]
            tick()
        for copy in outs:
            copy.wait()

    load("w_in", r.in_w_in.at[0], r.w_in, 6)
    load("w_out", r.in_w_out.at[0], r.w_out, 7)
    loads["w_in"].wait()
    loads["w_out"].wait()
    take_over(1)
    sum_layer(1, 3)
    sum_layer(1, 0)
    tick()
    sum_layer(1, 1)
    tick()
    sum_layer(1, 2)
    tick()
    one = dict(
        source_in=pltpu.VMEM((byte_count, width), b16),
        k1=pltpu.VMEM((byte_count, columns), b16),
        v1=pltpu.VMEM((byte_count, columns), b16),
        dkv=pltpu.VMEM((byte_count, 2 * columns), b16),
        probs=pltpu.VMEM((byte_count, LANES), f32),
        prob_grad=pltpu.VMEM((byte_count, LANES), f32),
        raised=pltpu.VMEM((byte_count, LANES), b16),
        inverse=pltpu.VMEM((patches, LANES), f32),
        q1=pltpu.VMEM((patches, columns), b16),
        mixed1=pltpu.VMEM((patches, columns), b16),
        query_in=pltpu.VMEM((patches, width), b16),
        mixed_grad=pltpu.VMEM((patches, columns), b16),
        q_sum=pltpu.VMEM((patches, columns), f32),
        delta_sum=pltpu.VMEM((patches, LANES), f32),
    )

    @functools.partial(pl.run_scoped, **one)
    def _(**scoped):
        for i in range(own_count):
            first_layer(i, scoped)

    hand_over(0)
    take_over(0)
    sum_layer(0, 3)
    tick()
    sum_layer(0, 0)
    tick()
    gains = Gains(r, section, tensor, flows) if summing else None
    last = dict(
        source_in=pltpu.VMEM((half_bytes, width), b16),
        byte_norms=pltpu.VMEM((half_bytes, LANES), f32),
        query_in=pltpu.VMEM((patches, width), b16),
        pool_high=pltpu.VMEM((patches, width), b16),
        pool_low=pltpu.VMEM((patches, width), b16),
        latent=pltpu.VMEM((own_count, patches, columns), b16),
    )

    @functools.partial(pl.run_scoped, **last)
    def _(**scoped):
        last_parts(types.SimpleNamespace(**scoped))

    sum_layer(0, 1)
    if summing:
        gains.tick()
    tick()
    sum_layer(0, 2)
    if summing:
        while flows.active or gains.steps:
            gains.tick()
            tick()
    ends = [pltpu.make_async_copy(r.gain_sum, r.gain_out, r.end_sem.at[4])]
    if not summing:
        ends += [
            pltpu.make_async_copy(r.up, r.up_sum, r.end_sem.at[0]),
            pltpu.make_async_copy(r.down, r.down_sum, r.end_sem.at[1]),
            pltpu.make_async_copy(r.attn_out_part.at[section], r.attn_out_sum, r.end_sem.at[3]),
        ]
        ends += [
            pltpu.make_async_copy(
                r.attn_in_part.at[section, :, pl.ds(j * columns, columns)], r.attn_in_sum.at[j],
                r.end_sem.at[5 + j],
            )
            for j in range(3)
        ]
    for copy in ends:
        copy.start()
    for copy in ends:
        copy.wait()


class Gains:
    def __init__(self, r, section, tensor, flows):
        self.r = r
        z = flows.z
        place = lax.axis_index("dp")
        near = place + SHORT * (1 - 2 * lax.rem(z, 2))
        far = place + 2 * SHORT * (1 - 2 * (z // 2))
        self.targets = [
            {"tensor": 1 - tensor}, {"section": 1 - section}, {"dp": flows.beside},
            {"dp": near}, {"dp": far},
        ]
        self.steps = list(range(len(self.targets) + 1))

    def copy(self, n):
        r = self.r
        return pltpu.make_async_remote_copy(
            src_ref=r.gain_held.at[n], dst_ref=r.gain_got.at[n], send_sem=r.gain_send.at[n],
            recv_sem=r.gain_recv.at[n], device_id=self.targets[n], device_id_type=MESH,
        )

    def tick(self):
        if not self.steps:
            return
        r, n = self.r, self.steps.pop(0)
        if n == 0:
            r.gain_held[0] = r.gain_sum[...]
        else:
            self.copy(n - 1).wait()
            value = r.gain_held[n - 1] + r.gain_got[n - 1]
            if n < len(self.targets):
                r.gain_held[n] = value
            else:
                r.gain_sum[...] = value
        if n < len(self.targets):
            self.copy(n).start()


def greet_grid(flows, others):
    barrier = pltpu.get_barrier_semaphore()

    def signal(place):
        pl.semaphore_signal(barrier, inc=1, device_id=place, device_id_type=MESH)

    for axis, index in others:
        signal({axis: index})
    signal({"dp": flows.beside})
    signal({"dp": lax.axis_index("dp") + 2 * SHORT * (1 - 2 * (flows.z // 2))})
    pl.when(flows.z < LONG - 1)(lambda: signal({"dp": flows.right}))
    pl.when(flows.z > 0)(lambda: signal({"dp": flows.left}))
    inner = jnp.logical_and(flows.z > 0, flows.z < LONG - 1)
    pl.semaphore_wait(barrier, jnp.where(inner, len(others) + 4, len(others) + 3))


def backward(kept, patch_ids):
    own, patches, width = kept["normed"].shape
    sequences, byte_count = patch_ids.shape
    columns = kept["q1"].shape[-1]
    hidden = kept["hidden"].shape[-1]
    half, half_bytes = width // 2, byte_count // 2
    sems = pltpu.SemaphoreType.DMA
    vmem = pltpu.VMEM
    rows16 = vmem((own, patches, width), b16)
    scratch = dict(
        inner=rows16,
        grad_in=rows16,
        inner_part=rows16,
        inner_got=rows16,
        normed=rows16,
        patch_norms=vmem((own, patches, LANES), f32),
        branch=rows16,
        normed_part=rows16,
        normed_got=rows16,
        source_part=vmem((own, byte_count, width), b16),
        source_got=vmem((own, half_bytes, width), b16),
        latent_got=vmem((own, patches, columns), b16),
        w_in=vmem((width, 3 * columns), b16),
        w_out=vmem((columns, width), b16),
        gain=vmem((2, 2, width), f32),
        gain_sum=vmem((4, width), f32),
        down_got=vmem((hidden, half), b16),
        down=vmem((hidden, half), b16),
        up=vmem((width, hidden), b16),
        attn_in_part=vmem((2, width, 3 * columns), b16),
        attn_out_part=vmem((2, columns, width), b16),
        big_got=vmem((width, 3 * columns), b16),
        attn_out_got=vmem((columns, width), b16),
        load_sem=sems((16,)),
        first_sem=sems((8,)),
        cross_send=sems((5, own)),
        cross_recv=sems((5, own)),
        give_send=sems((5,)),
        give_recv=sems((5,)),
        out_sem=sems((2, own)),
        out_send=sems((2, own)),
        out_recv=sems((2, own)),
        end_sem=sems((8,)),
        free_sem=pltpu.SemaphoreType.REGULAR,
    )
    slots = []
    if on_grid():
        arrays = [(hidden, half, 512), (half, hidden, 128), (half, hidden, 256)]
        arrays += [(columns, width, 128)] + [(width, columns, 384)] * 3
        for n, (rows, cols, cut) in enumerate(arrays):
            slots.append((f"l{n}", f"s{n}", rows, cut))
            scratch[f"l{n}"] = vmem((7 * cut // LONG, cols), b16)
            scratch[f"s{n}"] = vmem((10 * (rows - cut) // (SHORT * LONG), cols), b16)
        scratch |= dict(
            flow_send=sems((2 * len(arrays), 17)),
            flow_recv=sems((2 * len(arrays), 17)),
            flow_near=sems((2 * len(arrays),)),
            gain_held=vmem((5, 4, width), f32),
            gain_got=vmem((5, 4, width), f32),
            gain_send=sems((5,)),
            gain_recv=sems((5,)),
        )
    ins = [("ids", patch_ids, True)]
    ins += [("in_" + name, kept[name], False) for name in (*KEPT, *LAYERS)]
    outs = [
        ("latents", shape((sequences, patches // 2, columns), b16)),
        ("byte_grad", shape((sequences, half_bytes, half), b16)),
        ("attn_in_sum", shape((3, width, columns), b16)),
        ("attn_out_sum", shape((columns, width), b16)),
        ("gain_out", shape((4, width), f32)),
        ("up_sum", shape((width, hidden), b16)),
        ("down_sum", shape((hidden, half), b16)),
    ]

    def kernel(r):
        r.slots = [
            (getattr(r, long), getattr(r, short), rows, cut) for long, short, rows, cut in slots
        ]
        backward_kernel(r)

    return named_call(kernel, ins, outs, scratch, collective_id=1)


def swap(values, axis):
    return lax.ppermute(values, axis, [(0, 1), (1, 0)])


def sum_small(values):
    values = values + swap(values, "tensor")
    values = values + swap(values, "section")
    return lax.psum(values, "dp")


def per_device(byte_states, patch_ids, attn_in, attn_out, gains, ffn_in, ffn_out, latent_grad):
    width = byte_states.shape[-1]
    hidden = ffn_out.shape[0]
    half = width // 2
    is_first = lax.axis_index("section") == 0
    kept = forward(
        byte_states, patch_ids, attn_in, attn_out, gains, ffn_in.transpose(1, 0, 2), ffn_out,
        latent_grad,
    )
    got = backward(kept, patch_ids)
    sums = [got[name] for name in ("down_sum", "up_sum", "attn_in_sum", "attn_out_sum")]
    if not on_grid():
        sums = [lax.psum(value, "dp") for value in sums]
    down, up, in_sum, out_sum = [value.astype(f32) for value in sums]
    gain_sum = got["gain_out"] if on_grid() else sum_small(got["gain_out"])
    gain_out = jnp.where(is_first, gain_sum[0:2], gain_sum[2:4])
    up_out = up.reshape(2, half, hidden).transpose(1, 0, 2)
    return (
        got["latents"], got["byte_grad"], in_sum[None], out_sum[None], gain_out[None], up_out, down
    )


def solution(mesh):
    return jax.shard_map(
        per_device,
        mesh=mesh,
        in_specs=(
            P("dp", None, None),
            P("dp", None),
            P("section", None, None, "tensor"),
            P("section", "tensor", None),
            P("section", None, None),
            P(None, None, "tensor"),
            P("tensor", None),
            P("dp", None, None),
        ),
        out_specs=(
            P("dp", "section", "tensor"),
            P("dp", "tensor", "section"),
            P("section", None, None, "tensor"),
            P("section", "tensor", None),
            P("section", None, None),
            P("section", None, "tensor"),
            P("tensor", "section"),
        ),
        check_vma=False,
    )
```

```python
import functools
import types

import jax
import jax.numpy as jnp
from jax import lax
from jax.experimental import pallas as pl
from jax.experimental.pallas import tpu as pltpu
from jax.sharding import PartitionSpec as P

HD = 64
LANES = 128
BLOCK = 256
WIDE = 512
EPSILON = 1e-05
NEGATIVE = -1000000000.0
SCALE = HD ** (-0.5)
VMEM_BYTES = 63 * 1024 * 1024

f32 = jnp.float32
b16 = jnp.bfloat16


def dot(a, b):
    return jnp.dot(a, b, preferred_element_type=f32)


def dot_rt(a, b):
    return lax.dot_general(a, b, (((1,), (1,)), ((), ())), preferred_element_type=f32)


def dot_lt(a, b):
    return lax.dot_general(a, b, (((0,), (0,)), ((), ())), preferred_element_type=f32)


def inverse_rms(values):
    return lax.rsqrt(jnp.mean(values * values, axis=-1, keepdims=True) + EPSILON)


def iota(shape, dim):
    return lax.broadcasted_iota(jnp.int32, shape, dim)


def one_hot(condition):
    return jnp.where(condition, 1.0, 0.0).astype(b16)


def segment_max(values, ids):
    width = values.shape[1]
    lane = iota(ids.shape, 1)
    lowest = -3.0e38
    ahead, behind = values, values
    step = 1
    while step < width:
        left, right = step, width - step
        same_left = jnp.logical_and(pltpu.roll(ids, left, axis=1) == ids, lane >= step)
        same_right = jnp.logical_and(pltpu.roll(ids, right, axis=1) == ids, lane < right)
        ahead = jnp.maximum(ahead, jnp.where(same_left, pltpu.roll(ahead, left, axis=1), lowest))
        behind = jnp.maximum(
            behind, jnp.where(same_right, pltpu.roll(behind, right, axis=1), lowest)
        )
        step *= 2
    return jnp.maximum(ahead, behind)


def head_masks(width):
    heads_in = one_hot(iota((width, LANES), 0) // HD == iota((width, LANES), 1))
    heads_out = one_hot(iota((LANES, width), 1) // HD == iota((LANES, width), 0))
    return heads_in, heads_out


def split_dot(values, matrix):
    high = values.astype(b16)
    low = (values - high.astype(f32)).astype(b16)
    return dot(high, matrix) + dot(low, matrix)


def block_at(index, size=BLOCK):
    return pl.ds(pl.multiple_of(index * size, size), size)


def each_block(count, body, size=BLOCK):
    @pl.loop(0, count // size)
    def _(index):
        body(block_at(index, size))


MESH = pl.DeviceIdType.MESH


def remote(src, dst, send, recv, axis, index):
    return pltpu.make_async_remote_copy(
        src_ref=src, dst_ref=dst, send_sem=send, recv_sem=recv,
        device_id={axis: index}, device_id_type=MESH,
    )


def greet(places):
    barrier = pltpu.get_barrier_semaphore()
    for axis, index in places:
        pl.semaphore_signal(barrier, inc=1, device_id={axis: index}, device_id_type=MESH)
    pl.semaphore_wait(barrier, len(places))


def exchange_layer(r, section):
    columns = r.attn_in.shape[3]
    copies = []
    for n, (src, dst) in enumerate(
        [
            (r.attn_in.at[0, j], r.w_in.at[section, :, pl.ds(j * columns, columns)])
            for j in (1, 2, 0)
        ]
        + [(r.attn_out.at[0], r.w_out.at[section]), (r.gains.at[0], r.gain.at[section])]
    ):
        near = pltpu.make_async_copy(src, dst, r.near_sem.at[n])
        far = remote(src, dst, r.far_send.at[n], r.far_recv.at[n], "section", 1 - section)
        near.start()
        far.start()
        copies.append((near, far))
    return copies


def arrived(copies):
    for near, far in copies:
        near.wait()
        far.wait()


def members_of(r, seq, rows, patches):
    return one_hot(iota((patches, rows.size), 0) == r.ids[pl.ds(seq, 1), rows])


def names(**kinds):
    return tuple(kinds)


FIRST_KEPT = names(query_in=1, source_in=1, byte_norms=1)
CROSS_KEPT = names(q1=1, k1=1, v1=1, raised=1, inverse=1, mixed1=1)
SECOND_KEPT = names(normed=1, q2=1, k2=1, v2=1, totals=1, mixed2=1)
FEED_KEPT = names(
    inner=1, hidden=1, gate_grad=1, up_grad=1, grad_in=1, inner_part=1, patch_norms=1,
    latent_own=1, latent_send=1,
)
KEPT = FIRST_KEPT + CROSS_KEPT + SECOND_KEPT + FEED_KEPT
LAYERS = names(w_in=1, w_out=1, gain=1)


def forward_kernel(r):
    section, tensor = lax.axis_index("section"), lax.axis_index("tensor")
    own_count, patches, width = r.normed.shape
    byte_count = r.states.shape[1]
    columns = r.q1.shape[2]
    hidden = r.hidden.shape[2]
    heads = columns // HD
    greet([("section", 1 - section), ("tensor", 1 - tensor)])
    state_copies = [
        pltpu.make_async_copy(
            r.states.at[section * own_count + i], r.state_in.at[i], r.state_sem.at[i]
        )
        for i in range(own_count)
    ]
    for copy in state_copies:
        copy.start()
    layer = exchange_layer(r, section)
    grad_copies = [
        pltpu.make_async_copy(
            r.upstream.at[section * own_count + i], r.grad_in.at[i], r.grad_sem.at[i]
        )
        for i in range(own_count)
    ]
    feed_copies = [
        pltpu.make_async_copy(r.ffn_in, r.feed_in, r.feed_sem.at[0]),
        pltpu.make_async_copy(r.ffn_out, r.feed_out, r.feed_sem.at[1]),
    ]
    for copy in grad_copies + feed_copies:
        copy.start()
    heads_in, heads_out = head_masks(columns)

    def keep(name, i):
        n = KEPT.index(name)
        return pltpu.make_async_copy(
            getattr(r, name).at[i], getattr(r, "out_" + name).at[i], r.keep_sem.at[n, i]
        )

    def save(names, i):
        for name in names:
            keep(name, i).start()

    def exchange(step, i):
        return remote(
            r.part.at[step, i], r.got.at[step, i], r.part_send.at[step, i], r.part_recv.at[step, i],
            "tensor", 1 - tensor,
        )

    for copy in state_copies:
        copy.wait()
    layer[-1][0].wait()
    layer[-1][1].wait()
    first_gain = r.gain.at[0]

    @pl.loop(0, own_count)
    def _(i):
        seq = section * own_count + i
        r.pool_sum[...] = jnp.zeros_like(r.pool_sum)

        def pool(rows):
            block = r.state_in[i, rows, :]
            r.pool_sum[...] += dot(members_of(r, seq, rows, patches), block)
            values = block.astype(f32)
            scale = inverse_rms(values)
            r.byte_norms[i, rows, :] = jnp.broadcast_to(scale, (BLOCK, LANES))
            r.source_in[i, rows, :] = (values * scale * first_gain[1:2, :]).astype(b16)

        each_block(byte_count, pool)
        row_ids = r.ids[pl.ds(seq, 1), :]
        counts = jnp.sum(
            jnp.where(iota((patches, byte_count), 0) == row_ids, 1.0, 0.0), axis=1, keepdims=True
        )
        values = r.pool_sum[...] / jnp.maximum(counts, 1.0)
        r.pooled[i] = values
        scale = inverse_rms(values)
        r.patch_norms[i] = jnp.broadcast_to(scale, (patches, LANES))
        r.query_in[i] = (values * scale * first_gain[0:1, :]).astype(b16)
        save(FIRST_KEPT, i)

    arrived(layer[:4])
    layer_saves = [
        pltpu.make_async_copy(getattr(r, name), getattr(r, "out_" + name), r.layer_sem.at[n])
        for n, name in enumerate(LAYERS)
    ]
    for copy in layer_saves:
        copy.start()

    @pl.loop(0, own_count)
    def _(i):
        seq = section * own_count + i
        r.q1[i] = dot(r.query_in[i], r.w_in[0, :, :columns]).astype(b16)

        def project(rows):
            both = dot(r.source_in[i, rows, :], r.w_in[0, :, columns:])
            keys = both[:, :columns].astype(b16)
            r.k1[i, rows, :] = keys
            r.v1[i, rows, :] = both[:, columns:].astype(b16)
            spread = dot_lt(members_of(r, seq, rows, patches), r.q1[i])
            block_scores = split_dot(spread * keys.astype(f32), heads_in) * SCALE
            r.scores[:, rows] = block_scores.T[:heads, :]

        each_block(byte_count, project, WIDE)
        scores = r.scores[...]
        r.scores[...] = jnp.exp(scores - segment_max(scores, r.ids[pl.ds(seq, 1), :]))
        r.mix_sum[...] = jnp.zeros_like(r.mix_sum)
        r.total_sum[...] = jnp.zeros_like(r.total_sum)

        def mix(rows):
            short = r.scores[:, rows]
            filled = jnp.concatenate([short, jnp.zeros((LANES - heads, WIDE), f32)], axis=0)
            raised = filled.T.astype(b16)
            r.raised[i, rows, :] = raised
            members = members_of(r, seq, rows, patches)
            weighted = (dot(raised, heads_out) * r.v1[i, rows, :].astype(f32)).astype(b16)
            r.mix_sum[...] += dot(members, weighted)
            r.total_sum[...] += dot(members, raised)

        each_block(byte_count, mix, WIDE)
        totals = r.total_sum[...]
        inverse = jnp.where(totals > 0.0, 1.0 / totals, 0.0)
        r.inverse[i] = inverse
        mixed = (r.mix_sum[...] * split_dot(inverse, heads_out)).astype(b16)
        r.mixed1[i] = mixed
        r.part[0, i] = dot(mixed, r.w_out[0]).astype(b16)
        exchange(0, i).start()
        save(CROSS_KEPT, i)

    second_gain = r.gain.at[1]
    allowed = iota((patches, patches), 1) <= iota((patches, patches), 0)
    lane = iota((patches, LANES), 1)

    @pl.loop(0, own_count)
    def _(i):
        exchange(0, i).wait()
        latent = (
            r.pooled[i] + r.part[0, i].astype(f32) + r.got[0, i].astype(f32)
        ).astype(b16)
        r.latent[i] = latent
        values = latent.astype(f32)
        scale = inverse_rms(values)
        r.patch_norms[i] = jnp.where(lane == 1, scale, r.patch_norms[i])
        normed = (values * scale * second_gain[0:1, :]).astype(b16)
        r.normed[i] = normed
        projected = dot(normed, r.w_in[1]).astype(b16)
        query, key, value = [projected[:, j * columns : (j + 1) * columns] for j in range(3)]
        r.q2[i] = query
        r.k2[i] = key
        r.v2[i] = value
        kept = jnp.zeros((patches, LANES), f32)
        outs = []
        for head in range(heads):
            own = slice(head * HD, (head + 1) * HD)
            scores = jnp.where(allowed, dot_rt(query[:, own], key[:, own]) * SCALE, NEGATIVE)
            highest = jnp.max(scores, axis=-1, keepdims=True)
            raised = jnp.exp(scores - highest)
            total = jnp.sum(raised, axis=-1, keepdims=True)
            outs.append(dot((raised / total).astype(b16), value[:, own]))
            kept = jnp.where(lane == head, highest + jnp.log(total), kept)
        r.totals[i] = kept
        mixed = jnp.concatenate(outs, axis=1).astype(b16)
        r.mixed2[i] = mixed
        r.part[1, i] = dot(mixed, r.w_out[1]).astype(b16)
        exchange(1, i).start()
        save(SECOND_KEPT, i)

    for copy in grad_copies + feed_copies:
        copy.wait()

    @pl.loop(0, own_count)
    def _(i):
        seq = section * own_count + i
        exchange(1, i).wait()
        values = (
            r.latent[i].astype(f32) + r.part[1, i].astype(f32) + r.got[1, i].astype(f32)
        )
        r.middle[...] = values
        scale = inverse_rms(values)
        r.patch_norms[i] = jnp.where(lane == 2, scale, r.patch_norms[i])
        r.inner[i] = (values * scale * second_gain[1:2, :]).astype(b16)
        valid = iota((patches, 1), 0) <= jnp.max(r.ids[pl.ds(seq, 1), :], axis=1, keepdims=True)
        r.grad_in[i] = jnp.where(valid, r.grad_in[i].astype(f32), 0.0).astype(b16)

        gate = dot(r.inner[i], r.feed_in[0])
        up = dot(r.inner[i], r.feed_in[1])
        hidden_grad = dot_rt(r.grad_in[i], r.feed_out[...])
        gated = 1.0 / (1.0 + jnp.exp(-gate))
        act = gate * gated
        r.hidden[i] = (act * up).astype(b16)
        r.gate_grad[i] = (hidden_grad * up * (gated * (1.0 + gate * (1.0 - gated)))).astype(b16)
        r.up_grad[i] = (hidden_grad * act).astype(b16)
        inner_grad = dot_rt(r.gate_grad[i], r.feed_in[0]) + dot_rt(r.up_grad[i], r.feed_in[1])
        r.inner_part[i] = inner_grad.astype(b16)
        r.out_sum[...] = dot(r.hidden[i], r.feed_out[...])
        mine, theirs = block_at(tensor, columns), block_at(1 - tensor, columns)
        r.latent_own[i] = (r.middle[:, mine] + r.out_sum[:, mine]).astype(b16)
        r.latent_send[i] = r.out_sum[:, theirs].astype(b16)
        save(FEED_KEPT, i)

    @pl.loop(0, own_count)
    def _(i):
        for name in KEPT:
            keep(name, i).wait()

    for copy in layer_saves:
        copy.wait()


def shape(dims, dtype):
    return jax.ShapeDtypeStruct(dims, dtype)


def named_call(kernel, ins, outs, scratch, **params):
    any_space = pl.BlockSpec(memory_space=pl.ANY)
    whole = pl.BlockSpec(memory_space=pltpu.VMEM)
    names = [name for name, _, _ in ins] + [name for name, _ in outs] + list(scratch)

    def body(*refs):
        kernel(types.SimpleNamespace(**dict(zip(names, refs, strict=True))))

    got = pl.pallas_call(
        body,
        out_shape=tuple(s for _, s in outs),
        in_specs=[whole if inside else any_space for _, _, inside in ins],
        out_specs=tuple(any_space for _ in outs),
        scratch_shapes=list(scratch.values()),
        compiler_params=pltpu.CompilerParams(
            vmem_limit_bytes=VMEM_BYTES, has_side_effects=True, **params
        ),
    )(*(array for _, array, _ in ins))
    return {name: value for (name, _), value in zip(outs, got, strict=True)}


def forward(byte_states, patch_ids, attn_in, attn_out, gains, feed_in, feed_out, latent_grad):
    sequences, byte_count, width = byte_states.shape
    patches = byte_count // 4
    columns = attn_in.shape[-1]
    hidden = feed_out.shape[0]
    own = sequences // 2
    heads = columns // HD
    dims = dict(
        query_in=(own, patches, width, b16),
        source_in=(own, byte_count, width, b16),
        q1=(own, patches, columns, b16),
        k1=(own, byte_count, columns, b16),
        v1=(own, byte_count, columns, b16),
        raised=(own, byte_count, LANES, b16),
        inverse=(own, patches, LANES, f32),
        mixed1=(own, patches, columns, b16),
        byte_norms=(own, byte_count, LANES, f32),
        normed=(own, patches, width, b16),
        q2=(own, patches, columns, b16),
        k2=(own, patches, columns, b16),
        v2=(own, patches, columns, b16),
        totals=(own, patches, LANES, f32),
        mixed2=(own, patches, columns, b16),
        inner=(own, patches, width, b16),
        hidden=(own, patches, hidden, b16),
        gate_grad=(own, patches, hidden, b16),
        up_grad=(own, patches, hidden, b16),
        grad_in=(own, patches, width, b16),
        inner_part=(own, patches, width, b16),
        patch_norms=(own, patches, LANES, f32),
        latent_own=(own, patches, columns, b16),
        latent_send=(own, patches, columns, b16),
    )
    sems = pltpu.SemaphoreType.DMA
    scratch = {name: pltpu.VMEM(dims[name][:-1], dims[name][-1]) for name in KEPT}
    scratch |= dict(
        state_in=pltpu.VMEM((own, byte_count, width), b16),
        pooled=pltpu.VMEM((own, patches, width), f32),
        latent=pltpu.VMEM((own, patches, width), b16),
        middle=pltpu.VMEM((patches, width), f32),
        out_sum=pltpu.VMEM((patches, width), f32),
        w_in=pltpu.VMEM((2, width, 3 * columns), b16),
        w_out=pltpu.VMEM((2, columns, width), b16),
        gain=pltpu.VMEM((2, 2, width), f32),
        feed_in=pltpu.VMEM((2, width, hidden), b16),
        feed_out=pltpu.VMEM((hidden, width), b16),
        pool_sum=pltpu.VMEM((patches, width), f32),
        scores=pltpu.VMEM((heads, byte_count), f32),
        mix_sum=pltpu.VMEM((patches, columns), f32),
        total_sum=pltpu.VMEM((patches, LANES), f32),
        part=pltpu.VMEM((2, own, patches, width), b16),
        got=pltpu.VMEM((2, own, patches, width), b16),
        state_sem=sems((own,)),
        grad_sem=sems((own,)),
        feed_sem=sems((2,)),
        near_sem=sems((5,)),
        far_send=sems((5,)),
        far_recv=sems((5,)),
        part_send=sems((2, own)),
        part_recv=sems((2, own)),
        keep_sem=sems((len(KEPT), own)),
        layer_sem=sems((len(LAYERS),)),
    )
    ins = [
        ("states", byte_states, False), ("ids", patch_ids, True), ("attn_in", attn_in, False),
        ("attn_out", attn_out, False), ("gains", gains, False), ("ffn_in", feed_in, False),
        ("ffn_out", feed_out, False), ("upstream", latent_grad, False),
    ]
    dims |= dict(
        w_in=(2, width, 3 * columns, b16),
        w_out=(2, columns, width, b16),
        gain=(2, 2, width, f32),
    )
    names = (*KEPT, *LAYERS)
    outs = [("out_" + name, shape(dims[name][:-1], dims[name][-1])) for name in names]
    got = named_call(forward_kernel, ins, outs, scratch, collective_id=0)
    return {name: got["out_" + name] for name in names}


def flat(ref, cols):
    block = ref[:, :, cols]
    return block.reshape(block.shape[0] * block.shape[1], block.shape[2])


LONG, SHORT = 4, 2


def rows_of(ref, start, rows):
    if not isinstance(start, int):
        start = pl.multiple_of(start, 16)
    return ref.at[pl.ds(start, rows), :]


def add_rows(target, *others):
    rows, width = target.shape
    step = rows
    while step * width > 100 * 1408 and step % 32 == 0:
        step //= 2

    def add(at):
        value = target[at, :]
        for other in others:
            value = value + other[at, :]
        target[at, :] = value

    if step == rows:
        add(slice(None))
    else:
        each_block(rows, add, step)


PLAN = ((((), ()), ((0,), (1, 0)), ((0,), ()), ((1,), ())), (((0, 0, 0, 1, 0), (0, 1, 0, 0, 0)), ((1,), ()), ((1, 0), (2, 0, 1)), ((0, 0, 0, 0, 2, 2, 2), (0, 0))), (((2, 2, 2, 3), (5, 2, 3, 2, 2, 2)), ((2, 3), (3,)), ((), (3,)), ((2, 3), (0, 0, 2, 1, 3, 2, 2))), (((4, 2), ()), ((), ()), ((3, 2), (4,)), ((5,), ())), (((4, 4, 5, 1, 1, 1, 1), (4, 4, 1, 4, 4)), ((0, 5, 2, 2), (5,)), ((4, 5), (5,)), ((4, 4, 4, 1, 1, 4, 1, 1), (5, 4, 2, 1, 4, 4, 4))), (((), ()), ((0, 0, 4), (4, 0, 0, 0, 2)), ((2, 1, 0), (0,)), ((), ())), (((), (1, 1, 1)), ((), (1, 2)), ((2, 0), (2, 0, 1, 0, 0, 2)), ((), (1, 3, 3, 1, 1, 0))), (((0, 3, 3, 4, 3, 3), ()), ((1, 4, 0, 2, 2, 3, 4), (0, 2, 4, 2, 2)), ((0, 3, 2, 4, 4), (4, 2)), ((3,), ())), (((), (0,)), ((), ()), ((), (2,)), ((3,), ())), (((2,), (3, 3, 3, 2)), ((4, 1, 1, 5), (3, 5)), ((2, 1, 1), (4, 4)), ((3, 2), (3, 2))), (((2, 5, 5, 5), ()), ((), (4, 4)), ((4, 4, 0, 5, 1, 1), (3, 2)), ((5, 3, 5, 0), ())), (((5, 0, 0, 1, 1), (5, 5, 5, 5, 3)), ((4, 0, 1, 1, 3), ()), ((3, 2), (1, 0, 5)), ((1, 5, 4), (5, 3, 5, 0))), (((), (6, 7, 0, 0, 2, 13, 9, 8, 2, 11, 6, 4, 10, 10, 12, 12, 6, 8, 8, 8, 12, 12, 0, 6, 10, 10)), ((), (0, 1, 1, 11, 8, 4, 7, 10, 12, 9, 2, 13, 1, 3)), ((), (4, 7, 1, 12, 8, 10, 3, 5, 6, 9, 0, 4, 11, 1)), ((), (5, 2, 5, 11, 7, 9, 6, 8, 13, 10, 6, 12, 6, 4, 10, 10, 12, 12, 12, 6, 8, 8, 8, 10))), (((2, 3), (7, 7, 0, 9, 7, 1, 7)), ((2, 3), (4, 5, 6, 3, 6, 5, 0)), ((), (2, 13, 3)), ((0, 5, 0), (7, 7, 0, 7, 9, 7, 0, 9, 9, 9))), (((0, 0, 1), (9, 2, 2, 9, 11, 11, 11, 9, 1, 11, 4, 4)), ((), (1,)), ((0, 1, 3, 2), (2, 6, 0, 6)), ((2, 0), (2, 1, 2, 11, 11, 11))), (((1,), (4, 4, 13, 1, 13, 13, 13, 1)), ((), (0, 0, 7, 2, 6, 2)), ((5, 5, 4, 3, 3), (5, 7, 1, 3, 8, 8)), ((2,), (4, 13, 4, 4, 11, 0, 13, 13, 13))), (((4, 2, 2), ()), ((3, 2), (8, 2, 8, 3)), ((), (9, 3, 11, 10, 10, 12)), ((1, 1, 1, 2, 1, 0), ())), (((3,), (0, 0, 3, 2)), ((4, 5, 3, 2), (10, 11, 3, 10, 13, 5)), ((), ()), ((0,), (2, 0, 1, 2))), (((3, 3, 1), (2, 3)), ((0, 0, 0, 2, 5, 1, 1), (0, 12, 12, 2, 9)), ((1, 0, 5), (12, 1, 4)), ((2, 2, 4, 3), (3, 3))), (((4, 4, 4, 1), (3,)), ((), (7, 0)), ((4, 2), ()), ((3,), (3, 1))), (((4, 2, 0), ()), ((), ()), ((), (5, 0, 13, 5, 7, 0, 0, 0, 6)), ((4, 5, 3, 4), (4,))), (((0,), ()), ((5, 5, 1), (5, 6, 0, 2)), ((), (2, 1, 6, 2, 7, 2, 9, 2, 11, 9)), ((4,), ())), (((), (3, 5, 5)), ((1,), (6, 7, 1, 1, 1, 4, 9, 4, 2, 4, 8, 9)), ((5,), (3, 4, 8, 13)), ((5, 4, 1), (1, 1, 4))), (((2, 5, 5, 1), (5, 5)), ((3, 1, 1), ()), ((1, 1, 1, 1, 3, 3, 0, 0), (8,)), ((), (5, 2))), (((1, 5, 0), ()), ((1, 0, 0, 0, 2, 2, 2), (13, 10, 11, 8)), ((2, 0, 0, 1, 4, 2, 2, 2), (10, 10, 12)), ((), (2, 0, 5, 0))), (((5,), (4, 0)), ((3, 3), (13, 12, 10, 7)), ((), (4, 4, 11, 3, 12, 5, 13)), ((3, 1, 3, 5), (8, 3))), (((), (8, 6, 2, 1)), ((4, 4, 4), (6, 11, 3, 3, 8, 3)), ((5,), (6, 1, 4)), ((), (10,))), (((), (4, 10, 1)), ((), (10, 12, 4, 4, 4)), ((), (7, 1, 1, 4, 1, 7)), ((), (6,))), (((), ()), ((), (1, 1, 1, 5, 5, 5)), ((), (8, 10)), ((), ())), (((), (12,)), ((5, 4, 4, 5), (13, 9, 9)), ((), (9, 9)), ((), (5, 12, 3, 5))), (((), ()), ((), (7,)), ((), (5, 11)), ((), ())), (((15, 16, 17, 14, 20, 14, 4, 4, 20, 21, 19, 18, 16, 18, 14, 14, 2, 18, 3, 20, 18, 16, 16, 3, 20), (6,)), ((16, 15, 19, 20, 4, 14, 17, 18, 21), ()), ((17, 15, 16, 21, 18, 20, 19, 5, 14, 4, 4, 4, 3, 3, 3, 3), ()), ((18, 16, 14, 14, 15, 20, 20, 20, 19, 17, 14, 16, 18, 20, 21, 18, 2, 0, 16, 14, 4, 16, 2, 0, 1, 5, 4, 18), (6,))), (((5, 5, 17, 15, 15, 15, 3, 19), (6, 3, 8, 8, 3)), ((5, 3, 3), (11, 11, 12, 3, 5)), ((), (12, 13, 3, 13, 11, 3, 9, 3, 3)), ((), (1,))), (((4, 15, 17, 17, 21, 21, 19, 19, 17), (10, 10, 1, 6, 7, 6, 7, 8, 8, 12, 12, 4, 5, 5, 9, 7, 7, 9, 9, 9, 10, 11, 11, 12, 11, 11, 13, 12, 13, 13, 10, 10, 6, 3, 1, 6, 6, 8, 12, 13, 5, 9, 8, 7, 8, 11, 12, 10, 3, 5, 10, 7)), ((3, 14, 14, 16, 5, 16, 15, 5, 18, 20, 18, 5, 14, 19, 16, 20, 14, 17, 16, 21, 15, 18), (3, 3, 1, 6, 13, 5, 6, 6, 6, 5, 3, 6, 8, 12, 6, 10, 8, 5, 10, 10, 7, 12, 7, 9, 7, 12, 8, 8, 8, 11, 9, 8, 11, 9, 13, 11, 13, 10, 10, 13, 12, 12, 10, 12, 7)), ((14, 14, 4, 18, 18, 16, 16, 5, 5, 5, 5, 15, 14, 14, 20, 18, 19, 17, 16, 18, 15, 20, 20, 20, 14), (6, 7, 5, 5, 1, 10, 8, 5, 5, 6, 10, 12, 11, 6, 7, 6, 6, 13, 3, 8, 6, 9, 5, 10, 12, 11, 10, 13, 8, 10, 8, 8, 8, 10)), ((15, 15, 5, 15, 3, 17, 17, 17, 17, 19), (8, 4, 7, 4, 1, 6, 6, 8, 12, 7, 7, 5, 8, 11, 10, 9, 10, 12, 12, 9, 9, 13, 10, 11, 6, 1, 6, 3, 7, 8, 11, 8, 13, 3, 5, 10, 12, 7, 11, 12, 5, 13, 9, 9, 6, 6, 13, 10, 11, 13, 12, 8, 8))), (((21, 16, 5, 20, 3, 5, 14, 18, 21), (11,)), ((20, 18, 19, 17, 17, 15, 15, 3, 21, 19, 21, 20, 17, 14, 16, 15, 18, 5, 20, 21), (9, 7, 7, 9, 9)), ((16, 17, 18, 21, 17, 15, 15, 3, 15, 17, 17, 19, 5, 16, 21, 16, 19, 19, 21, 20, 18), (12, 12, 7, 7, 12, 12, 7, 7, 9, 13)), ((15, 21, 3, 21, 5, 19, 19, 19, 5, 5, 21, 16, 14, 16, 21, 20, 14, 14, 15, 18, 14), ())), (((15, 19, 14, 14, 14, 14, 18, 15, 15, 15, 16, 16, 16, 16, 20, 17, 17, 20, 18, 18, 20, 18, 19, 19, 17), (12,)), ((19, 17, 21, 19, 14), ()), ((15, 14, 19, 21, 15, 16, 14, 21, 20, 19, 17, 18, 17, 20), (11, 9, 9, 9)), ((16, 3, 20, 18, 15, 18, 16, 17, 15, 17, 17, 18, 20, 14, 20, 15, 19, 19, 21, 15), (3,))), (((20,), (9, 9, 7, 13, 13, 13, 11)), ((15, 15, 15, 15, 15, 15, 14, 14, 14), (11, 9, 11)), ((), (11, 13, 13, 13, 9)), ((14, 19), (11, 7, 10, 13, 9, 9, 5, 13, 12, 11, 7, 7))), (((17, 19, 19, 21, 14, 21, 21, 14, 14, 15), (9,)), ((16, 14, 14, 16, 16, 16, 17, 16, 20, 16, 20, 17, 18, 18, 17, 18, 17, 18), (11, 7, 13, 13, 13)), ((19, 21), (7, 11, 11)), ((16, 16, 21, 14, 17, 18, 17, 18, 21, 19, 19), (10,))), (((21, 16, 20, 16, 16, 18, 18, 20, 15, 15, 17, 17, 17, 19, 19, 15, 21, 18, 17, 21, 19, 21, 20, 19, 21), (11, 13, 7)), ((17, 18, 17, 19, 19, 19, 20, 20, 18, 21, 20, 20, 21, 21, 19, 19, 17, 19, 21, 21, 19, 21, 21, 15), (11, 13)), ((14, 16, 14, 14, 16, 16, 16, 15, 21, 15, 15, 18, 18, 14, 15, 18, 17, 20, 17, 20, 20, 20, 18, 17, 17, 19, 19, 19, 19, 21, 21, 19, 21, 21, 21, 17, 15), (13, 11)), ((20, 14, 21, 15, 20, 15, 16, 16, 18, 17, 20, 20, 19, 19, 18, 17, 21, 21, 19, 17, 21, 21, 15), (13, 9, 11))))


class Flows:
    def __init__(self, r, section):
        self.r = r
        self.section = section
        place = lax.axis_index("dp")
        self.z, self.y = place // SHORT, lax.rem(place, SHORT)
        self.right, self.left = place + SHORT, place - SHORT
        self.beside = place + 1 - 2 * self.y
        self.flows = []
        self.done = {(z, s): [] for z in range(LONG) for s in range(2)}
        self.points = 0

    def hop(self, src, dst, n, j, target):
        r = self.r
        return pltpu.make_async_remote_copy(
            src_ref=src, dst_ref=dst, send_sem=r.flow_send.at[n, j], recv_sem=r.flow_recv.at[n, j],
            device_id={"dp": target}, device_id_type=MESH,
        )

    def reduce_events(self, n, part, slot):
        def up(k):
            return self.hop(slot(k - 1), slot(k - 1), n, k - 1, self.right)

        def down(k):
            return self.hop(slot(3 + k), slot(3 + k), n, 3 + k, self.left)

        def pass_on(copy, held, k):
            copy(k).wait_recv()
            add_rows(held, part(k))
            copy(k).start()

        def begin(z):
            if z == 0:
                for k in (3, 2, 1):
                    self.hop(part(k), slot(k - 1), n, k - 1, self.right).start()
            if z == 3:
                for k in (0, 1, 2):
                    self.hop(part(k), slot(3 + k), n, 3 + k, self.left).start()

        def passing(at_one, at_two):
            def event(z):
                if z in (1, 2):
                    way, k = (at_one, at_two)[z - 1]
                    pass_on(*((up, slot(k - 1)) if way > 0 else (down, slot(3 + k))), k)

            return event

        def close(z):
            got = []
            if z >= 1:
                up(z).wait_recv()
                got.append(slot(z - 1))
            if z <= 2:
                down(z).wait_recv()
                got.append(slot(3 + z))
            add_rows(part(z), *got)

        def sent(z):
            for k in ((1, 2, 3), (2, 3), (3,), ())[z]:
                up(k).wait_send()
            for k in ((), (0,), (0, 1), (0, 1, 2))[z]:
                down(k).wait_send()

        passes = [
            passing((1, 3), (-1, 0)), passing((1, 2), (-1, 1)), passing((-1, 0), (1, 3)),
        ]
        return begin, passes, close, sent

    def gather_events(self, n, own, out, extra=None):
        def up(src, k, d):
            return self.hop(src, out(k), n, 7 + d, self.right)

        def down(src, k, d):
            return self.hop(src, out(k), n, 10 + d, self.left)

        def near(z):
            return pltpu.make_async_copy(own(z), out(z), self.r.flow_near.at[n])

        def starts(z, d, way):
            k = z - d * way
            src = own(z) if d == 0 else out(k)
            copies = []
            if d < LONG - 1 and 0 <= z + way < LONG:
                copies.append((up if way > 0 else down)(src, k, d))
            if extra and (d or way > 0):
                copies.append(extra(src, k))
            return copies

        def begin(z):
            near(z).start()
            for copy in starts(z, 0, 1) + starts(z, 0, -1):
                copy.start()

        def step(d, way):
            def event(z):
                k = z - d * way
                if 0 <= k < LONG:
                    (up if way > 0 else down)(out(k), k, d - 1).wait_recv()
                    for copy in starts(z, d, way):
                        copy.start()

            return event

        def sent(z):
            near(z).wait()
            for way in (1, -1):
                for d in range(LONG):
                    if 0 <= z - d * way < LONG:
                        for copy in starts(z, d, way):
                            copy.wait_send()

        return begin, [step(d, way) for d in (1, 2, 3) for way in (1, -1)], sent

    def long_first(self, n, data, out, slots, start, rows):
        c = rows // LONG

        def part(k):
            return data(start + k * c, c)

        def slot(j):
            return rows_of(slots, j * c, c)

        def beside(z):
            return self.hop(part(z), slot(6), n, 6, self.beside)

        begin, passes, close, reduce_sent = self.reduce_events(n, part, slot)
        gather, steps, gather_sent = self.gather_events(
            n, lambda z: slot(6), lambda k: out(start + k * c, c)
        )

        def middle(z):
            close(z)
            beside(z).start()

        def turn(z):
            beside(z).wait_recv()
            add_rows(slot(6), part(z))
            gather(z)

        def sent(z):
            reduce_sent(z)
            beside(z).wait_send()
            gather_sent(z)

        return [begin, *passes, middle, turn, *steps], sent

    def short_first(self, n, data, out, slots, start, rows):
        half = rows // SHORT
        c = half // LONG

        def part(k):
            return data(start + self.y * half + k * c, c)

        def place(k, y=None):
            return out(start + (self.y if y is None else y) * half + k * c, c)

        def slot(j):
            return rows_of(slots, j * c, c)

        def beside():
            landing = rows_of(slots, 6 * c, half)
            return self.hop(data(start + (1 - self.y) * half, half), landing, n, 6, self.beside)

        def spread(src, k):
            return self.hop(src, place(k), n, 13 + k, self.beside)

        begin, passes, close, reduce_sent = self.reduce_events(n, part, slot)
        gather, steps, gather_sent = self.gather_events(n, part, place, spread)

        def first(z):
            beside().start()

        def turn(z):
            beside().wait_recv()
            add_rows(data(start + self.y * half, half), rows_of(slots, 6 * c, half))
            begin(z)

        def middle(z):
            close(z)
            gather(z)

        def end(z):
            for k in range(LONG):
                there = place(k, 1 - self.y)
                self.hop(there, there, n, 13 + k, self.beside).wait_recv()

        def sent(z):
            reduce_sent(z)
            beside().wait_send()
            gather_sent(z)

        return [first, turn, *passes, middle, *steps, end], sent

    def open(self, only, *flows):
        for events, sent in flows:
            self.flows.append((only, events, sent))
            for counts in self.done.values():
                counts.append(0)

    def advance(self, z, s, todo):
        def body():
            for n in todo:
                self.flows[n][1][self.done[z, s][n]](z)
                self.done[z, s][n] += 1

        return body

    def point(self):
        plan = PLAN[self.points] if self.points < len(PLAN) else ()
        self.points += 1
        for z, lists in enumerate(plan):
            first, second = self.done[z, 0], self.done[z, 1]
            if lists[0] == lists[1] and all(first[n] == second[n] for n in lists[0]):
                if lists[0]:
                    pl.when(self.z == z)(self.advance(z, 0, lists[0]))
                    for n in lists[0]:
                        second[n] = first[n]
                continue
            for s in range(2):
                here = jnp.logical_and(self.z == z, self.section == s)
                pl.when(here)(self.advance(z, s, lists[s]))

    def drain(self):
        for (z, s), counts in self.done.items():

            def body(z=z, s=s, counts=counts):
                mine = [n for n, flow in enumerate(self.flows) if flow[0] in (None, s)]
                longest = max(len(self.flows[n][1]) for n in mine)
                for k in range(longest):
                    for n in mine:
                        if counts[n] <= k < len(self.flows[n][1]):
                            self.flows[n][1][k](z)
                for n in mine:
                    self.flows[n][2](z)

            pl.when(jnp.logical_and(self.z == z, self.section == s))(body)


def on_grid():
    return lax.axis_size("dp") == LONG * SHORT


def backward_kernel(r):
    section, tensor = lax.axis_index("section"), lax.axis_index("tensor")
    own_count, patches, width = r.normed.shape
    byte_count = r.ids.shape[1]
    columns = r.w_out.shape[0]
    hidden = r.down.shape[0]
    heads = columns // HD
    half = width // 2
    half_bytes = byte_count // 2
    summing = on_grid()
    loads = {}

    def load(name, src, dst, *sem):
        copy = pltpu.make_async_copy(src, dst, r.load_sem.at[sem])
        copy.start()
        loads[name] = copy

    held_names = ("inner", "grad_in", "inner_part", "normed", "patch_norms", "gain")
    for n, name in enumerate(held_names):
        load(name, getattr(r, "in_" + name), getattr(r, name), n)
    load("w_in", r.in_w_in.at[1], r.w_in, 6)
    load("w_out", r.in_w_out.at[1], r.w_out, 7)
    others = [("section", 1 - section), ("tensor", 1 - tensor)]
    flows = Flows(r, section) if summing else None
    if summing:
        greet_grid(flows, others)
    else:
        greet(others)

    def cross(src, dst, i, sem):
        return remote(
            src, dst, r.cross_send.at[sem, i], r.cross_recv.at[sem, i], "tensor", 1 - tensor
        )

    def inner_exchange(i):
        return cross(r.in_inner_part.at[i], r.inner_got.at[i], i, 0)

    def normed_exchange(i):
        return cross(r.normed_part.at[i], r.normed_got.at[i], i, 1)

    def query_exchange(i):
        return cross(r.inner_part.at[i], r.inner_got.at[i], i, 2)

    def source_exchange(i):
        theirs = block_at(1 - tensor, half_bytes)
        return cross(r.source_part.at[i, theirs, :], r.source_got.at[i], i, 3)

    def latent_exchange(i):
        return cross(r.in_latent_send.at[i], r.latent_got.at[i], i, 4)

    for i in range(own_count):
        inner_exchange(i).start()
    def give(n, src, dst):
        return remote(src, dst, r.give_send.at[n], r.give_recv.at[n], "section", 1 - section)

    def point():
        if summing:
            flows.point()

    def summed(n, data, out, only=None):
        if summing:
            long_slots, short_slots, rows, cut = r.slots[n]
            flows.open(
                only,
                flows.long_first(2 * n, data, out, long_slots, 0, cut),
                flows.short_first(2 * n + 1, data, out, short_slots, cut, rows - cut),
            )

    def up_half(ref, n):
        return ref.at[pl.ds(n * half, half), :]

    def whole(view):
        return lambda start, rows: rows_of(view(), start, rows)

    @functools.partial(
        pl.run_scoped,
        hidden_all=pltpu.VMEM((own_count, patches, hidden), b16),
        gate_all=pltpu.VMEM((own_count, patches, hidden), b16),
        up_all=pltpu.VMEM((own_count, patches, hidden), b16),
        down_give=pltpu.VMEM((hidden, half), b16),
    )
    def _(hidden_all, gate_all, up_all, down_give):
        parts = {"hidden": hidden_all, "gate_grad": gate_all, "up_grad": up_all}
        for n, (name, ref) in enumerate(parts.items()):
            load(name, getattr(r, "in_" + name), ref, n + 8)
        for name in (*parts, "inner", "grad_in"):
            loads[name].wait()

        def down_grad(target, side):
            upstream = flat(r.grad_in, block_at(side, half))

            def tile(cols):
                target[cols, :] = dot_lt(flat(hidden_all, cols), upstream).astype(b16)

            each_block(hidden, tile)
            if hidden % BLOCK:
                tile(pl.ds(hidden - hidden % BLOCK, hidden % BLOCK))

        def up_grad(target, ref, side):
            upstream = flat(ref, slice(None))

            def tile(rows):
                cols = pl.ds(pl.multiple_of(side * half + rows.start, BLOCK), BLOCK)
                target[rows, :] = dot_lt(flat(r.inner, cols), upstream).astype(b16)

            each_block(half, tile)

        used = pl.ds(0, hidden)
        give_rows = [pl.ds(0, half), pl.ds(half, half)]
        gate_give, up_give = [r.attn_in_part.at[1, rows, used] for rows in give_rows]
        gate_got, up_got = [r.big_got.at[rows, used] for rows in give_rows]
        gate_own, up_own = [r.up.at[rows, :] for rows in give_rows]
        gifts = [
            give(0, down_give, r.down_got), give(1, gate_give, gate_got), give(2, up_give, up_got)
        ]
        other = 1 - section
        down_grad(down_give, other)
        gifts[0].start()
        down_grad(r.down, section)
        up_grad(gate_give, gate_all, other)
        gifts[1].start()
        gifts[0].wait()
        add_rows(r.down, r.down_got)
        summed(0, whole(lambda: r.down), whole(lambda: r.down_sum))
        point()
        up_grad(gate_own, gate_all, section)
        up_grad(up_give, up_all, other)
        gifts[2].start()
        gifts[1].wait()
        add_rows(gate_own, gate_got)
        summed(1, whole(lambda: up_half(r.up, 0)), whole(lambda: up_half(r.up_sum, 0)))
        point()
        up_grad(up_own, up_all, section)
        gifts[2].wait()
        add_rows(up_own, up_got)
        summed(2, whole(lambda: up_half(r.up, 1)), whole(lambda: up_half(r.up_sum, 1)))
        point()
        pl.semaphore_signal(
            r.free_sem, inc=1, device_id={"section": other}, device_id_type=MESH
        )

    def gifts_of(layer):
        return [
            give(3, r.attn_in_part.at[layer], r.big_got),
            give(4, r.attn_out_part.at[layer], r.attn_out_got),
        ]

    def hand_over(layer):
        @pl.when(section != layer)
        def _():
            pl.semaphore_wait(r.free_sem, 1)
            for gift in gifts_of(layer):
                gift.start()

    def take_over(layer):
        @pl.when(section != layer)
        def _():
            for gift in gifts_of(layer):
                gift.wait_send()

        @pl.when(section == layer)
        def _():
            for gift in gifts_of(layer):
                gift.wait_recv()
            add_rows(r.attn_out_part.at[layer], r.attn_out_got)
            add_rows(r.attn_in_part.at[layer], r.big_got)

    def sum_layer(layer, which):
        def columns_of(j):
            return whole(lambda: r.attn_in_part.at[layer, :, pl.ds(j * columns, columns)])

        if which == 3:
            summed(
                3, whole(lambda: r.attn_out_part.at[layer]), whole(lambda: r.attn_out_sum), layer
            )
        else:
            summed(4 + which, columns_of(which), whole(lambda: r.attn_in_sum.at[which]), layer)

    first_gain, second_gain = r.gain.at[0], r.gain.at[1]

    def back_through(normed, gain_row, scale, upstream):
        unit = normed.astype(f32) / gain_row
        scaled = upstream * gain_row
        mean = jnp.mean(unit * scaled, axis=-1, keepdims=True)
        return (scaled - unit * mean) * scale, unit

    @functools.partial(
        pl.run_scoped,
        q2=pltpu.VMEM((own_count, patches, columns), b16),
        k2=pltpu.VMEM((own_count, patches, columns), b16),
        v2=pltpu.VMEM((own_count, patches, columns), b16),
        totals=pltpu.VMEM((own_count, patches, LANES), f32),
        mixed2=pltpu.VMEM((own_count, patches, columns), b16),
        second_grads=pltpu.VMEM((own_count, patches, 3 * columns), b16),
        mixed_grads=pltpu.VMEM((patches, columns), b16),
    )
    def _(q2, k2, v2, totals, mixed2, second_grads, mixed_grads):
        parts = {"q2": q2, "k2": k2, "v2": v2, "totals": totals, "mixed2": mixed2}
        for n, (name, ref) in enumerate(parts.items()):
            load(name, getattr(r, "in_" + name), ref, n + 11)
        for name in (*held_names[2:], "w_in", "w_out", *parts):
            loads[name].wait()
        r.gain_sum[...] = jnp.zeros_like(r.gain_sum)
        allowed = iota((patches, patches), 1) <= iota((patches, patches), 0)
        for i in range(own_count):
            inner_exchange(i).wait()
            own_part = r.inner_part[i].astype(f32)
            back, unit = back_through(
                r.inner[i], second_gain[1:2, :], r.patch_norms[i, :, 2:3],
                own_part + r.inner_got[i].astype(f32),
            )
            r.gain_sum[3:4, :] += jnp.sum(unit * own_part, axis=0, keepdims=True)
            branch = (r.grad_in[i].astype(f32) + back).astype(b16)
            r.branch[i] = branch
            mixed_grads[...] = dot_rt(branch, r.w_out[...]).astype(b16)
            point()

            mixed_grad = mixed_grads[...]
            outs = [[], [], []]
            for head in range(heads):
                own = slice(head * HD, (head + 1) * HD)
                query, key, value = q2[i, :, own], k2[i, :, own], v2[i, :, own]
                upper = mixed_grad[:, own]
                scores = jnp.where(allowed, dot_rt(query, key) * SCALE, NEGATIVE)
                probs = jnp.exp(scores - totals[i, :, head : head + 1])
                prob_grad = dot_rt(upper, value)
                delta = jnp.sum(probs * prob_grad, axis=-1, keepdims=True)
                score_grad = (probs * (prob_grad - delta)).astype(b16)
                outs[0].append(dot(score_grad, key) * SCALE)
                outs[1].append(dot_lt(score_grad, query) * SCALE)
                outs[2].append(dot_lt(probs.astype(b16), upper))
            grads = jnp.concatenate(outs[0] + outs[1] + outs[2], axis=1).astype(b16)
            second_grads[i] = grads
            point()
            r.normed_part[i] = dot_rt(grads, r.w_in[...]).astype(b16)
            normed_exchange(i).start()
            point()

        def outer(target, rows_ref, upstream, tiles):
            @pl.loop(0, tiles)
            def _(t):
                cols = block_at(t)
                target[cols, :] = dot_lt(flat(rows_ref, cols), upstream).astype(b16)

        outer(r.attn_in_part.at[1], r.normed, flat(second_grads, slice(None)), width // BLOCK)
        point()
        outer(r.attn_out_part.at[1], mixed2, flat(r.branch, slice(None)), columns // BLOCK)
        hand_over(1)
        point()

    heads_in, heads_out = head_masks(columns)

    def first_layer(i, scoped):
        seq = section * own_count + i
        s = types.SimpleNamespace(**scoped)
        copies = {}
        names = (*CROSS_KEPT, "source_in", "query_in")
        for n, name in enumerate(names):
            copy = pltpu.make_async_copy(
                getattr(r, "in_" + name).at[i], getattr(s, name), r.first_sem.at[n]
            )
            copy.start()
            copies[name] = copy
        normed_exchange(i).wait()
        own_part = r.normed_part[i].astype(f32)
        back, unit = back_through(
            r.normed[i], second_gain[0:1, :], r.patch_norms[i, :, 1:2],
            own_part + r.normed_got[i].astype(f32),
        )
        r.gain_sum[2:3, :] += jnp.sum(unit * own_part, axis=0, keepdims=True)
        branch = (r.branch[i].astype(f32) + back).astype(b16)
        r.branch[i] = branch
        s.mixed_grad[...] = dot_rt(branch, r.w_out[...]).astype(b16)
        s.q_sum[...] = jnp.zeros_like(s.q_sum)
        s.delta_sum[...] = jnp.zeros_like(s.delta_sum)
        for copy in copies.values():
            copy.wait()
        point()
        if i == 0:
            take_over(1)
            for which in (3, 0, 1, 2):
                sum_layer(1, which)
            point()
        inverse = s.inverse[...]
        inverse_high = inverse.astype(b16)
        inverse_low = (inverse - inverse_high.astype(f32)).astype(b16)

        def value_side(rows):
            members = members_of(r, seq, rows, patches)
            spread = dot_lt(members, s.mixed_grad[...])
            scale = dot_lt(members, inverse_high) + dot_lt(members, inverse_low)
            probs = s.raised[rows, :].astype(f32) * scale
            s.probs[rows, :] = probs
            s.dkv[rows, columns:] = (dot(probs.astype(b16), heads_out) * spread).astype(b16)
            prob_grad = split_dot(spread * s.v1[rows, :].astype(f32), heads_in)
            s.prob_grad[rows, :] = prob_grad
            product = probs * prob_grad
            high = product.astype(b16)
            low = (product - high.astype(f32)).astype(b16)
            s.delta_sum[...] += dot(members, high) + dot(members, low)

        for t in range(byte_count // WIDE):
            value_side(pl.ds(t * WIDE, WIDE))
            point()
        delta = s.delta_sum[...]
        delta_high = delta.astype(b16)
        delta_low = (delta - delta_high.astype(f32)).astype(b16)

        def key_side(rows):
            members = members_of(r, seq, rows, patches)
            shift = dot_lt(members, delta_high) + dot_lt(members, delta_low)
            score_grad = (s.probs[rows, :] * (s.prob_grad[rows, :] - shift)).astype(b16)
            spread = dot(score_grad, heads_out)
            s.dkv[rows, :columns] = (spread * dot_lt(members, s.q1[...]) * SCALE).astype(b16)
            s.q_sum[...] += dot(members, (spread * s.k1[rows, :].astype(f32)).astype(b16))
            source = dot_rt(s.dkv[rows, :], r.w_in[:, columns:])
            r.source_part[i, rows, :] = source.astype(b16)
            unit_block = s.source_in[rows, :].astype(f32)
            r.gain_sum[1:2, :] += (
                jnp.sum(unit_block * source, axis=0, keepdims=True) / first_gain[1:2, :]
            )

        for t in range(byte_count // WIDE):
            key_side(pl.ds(t * WIDE, WIDE))
            point()
        source_exchange(i).start()
        q_grad = (s.q_sum[...] * SCALE).astype(b16)
        query = dot_rt(q_grad, r.w_in[:, :columns])
        r.inner_part[i] = query.astype(b16)
        query_exchange(i).start()
        unit_pool = s.query_in[...].astype(f32)
        r.gain_sum[0:1, :] += (
            jnp.sum(unit_pool * query, axis=0, keepdims=True) / first_gain[0:1, :]
        )
        point()

        def add_to(target, rows, cols, value):
            if i:
                value = target[rows, cols].astype(f32) + value
            target[rows, cols] = value.astype(b16)

        for half_t in range(2):

            @pl.loop(0, half // BLOCK)
            def _(t, half_t=half_t):
                cols = pl.ds(pl.multiple_of(half_t * half + t * BLOCK, BLOCK), BLOCK)
                source = s.source_in[:, cols]
                target = r.attn_in_part.at[0]
                add_to(target, cols, slice(0, columns), dot_lt(s.query_in[:, cols], q_grad))
                add_to(target, cols, slice(columns, 3 * columns), dot_lt(source, s.dkv[...]))

            point()

        @pl.loop(0, columns // BLOCK)
        def _(t):
            cols = block_at(t)
            add_to(
                r.attn_out_part.at[0], cols, slice(None), dot_lt(s.mixed1[:, cols], branch)
            )

        point()

    def last_parts(s):
        outs = []

        own_rows = block_at(tensor, half_bytes)
        cols_keep, cols_give = block_at(section, half), block_at(1 - section, half)
        for i in range(own_count):
            seq = section * own_count + i
            finals = [
                pltpu.make_async_copy(
                    r.in_source_in.at[i, own_rows, :], s.source_in, r.first_sem.at[0]
                ),
                pltpu.make_async_copy(
                    r.in_byte_norms.at[i, own_rows, :], s.byte_norms, r.first_sem.at[1]
                ),
                pltpu.make_async_copy(r.in_query_in.at[i], s.query_in, r.first_sem.at[2]),
            ]
            for copy in finals:
                copy.start()
            query_exchange(i).wait()
            source_exchange(i).wait()
            for copy in finals:
                copy.wait()
            back, _ = back_through(
                s.query_in[...], first_gain[0:1, :], r.patch_norms[i, :, 0:1],
                r.inner_part[i].astype(f32) + r.inner_got[i].astype(f32),
            )
            counts = jnp.sum(
                jnp.where(iota((patches, byte_count), 0) == r.ids[pl.ds(seq, 1), :], 1.0, 0.0),
                axis=1, keepdims=True,
            )
            pool_grad = (r.branch[i].astype(f32) + back) / jnp.maximum(counts, 1.0)
            high = pool_grad.astype(b16)
            s.pool_high[...] = high
            s.pool_low[...] = (pool_grad - high.astype(f32)).astype(b16)

            @pl.loop(0, half_bytes // BLOCK)
            def _(t, i=i, seq=seq):
                rows = block_at(t)
                place = pl.ds(pl.multiple_of(tensor * half_bytes + t * BLOCK, BLOCK), BLOCK)
                members = members_of(r, seq, place, patches)
                spread = dot_lt(members, s.pool_high[...]) + dot_lt(members, s.pool_low[...])
                part = r.source_part[i, place, :].astype(f32)
                own, _ = back_through(
                    s.source_in[rows, :], first_gain[1:2, :], s.byte_norms[rows, 0:1],
                    part + r.source_got[i, rows, :].astype(f32),
                )
                r.source_got[i, rows, :] = (own + spread).astype(b16)

            near = pltpu.make_async_copy(
                r.source_got.at[i, :, cols_keep], r.byte_grad.at[seq], r.out_sem.at[1, i]
            )
            far = remote(
                r.source_got.at[i, :, cols_give], r.byte_grad.at[seq],
                r.out_send.at[1, i], r.out_recv.at[1, i], "section", 1 - section,
            )
            near.start()
            far.start()
            outs += [near, far]
            point()

        half_rows = patches // 2
        rows_keep, rows_give = block_at(section, half_rows), block_at(1 - section, half_rows)
        for i in range(own_count):
            seq = section * own_count + i
            s_load = pltpu.make_async_copy(r.in_latent_own.at[i], s.latent.at[i], r.first_sem.at[i])
            s_load.start()
            s_load.wait()
            latent_exchange(i).wait()
            last = jnp.max(r.ids[pl.ds(seq, 1), :], axis=1, keepdims=True)
            valid = iota((patches, 1), 0) <= last
            values = s.latent[i].astype(f32) + r.latent_got[i].astype(f32)
            s.latent[i] = jnp.where(valid, values, 0.0).astype(b16)
            near = pltpu.make_async_copy(
                s.latent.at[i, rows_keep, :], r.latents.at[seq], r.out_sem.at[0, i]
            )
            far = remote(
                s.latent.at[i, rows_give, :], r.latents.at[seq],
                r.out_send.at[0, i], r.out_recv.at[0, i], "section", 1 - section,
            )
            near.start()
            far.start()
            outs += [near, far]
        for copy in outs:
            copy.wait()

    load("w_in", r.in_w_in.at[0], r.w_in, 6)
    load("w_out", r.in_w_out.at[0], r.w_out, 7)
    loads["w_in"].wait()
    loads["w_out"].wait()
    one = dict(
        source_in=pltpu.VMEM((byte_count, width), b16),
        k1=pltpu.VMEM((byte_count, columns), b16),
        v1=pltpu.VMEM((byte_count, columns), b16),
        dkv=pltpu.VMEM((byte_count, 2 * columns), b16),
        probs=pltpu.VMEM((byte_count, LANES), f32),
        prob_grad=pltpu.VMEM((byte_count, LANES), f32),
        raised=pltpu.VMEM((byte_count, LANES), b16),
        inverse=pltpu.VMEM((patches, LANES), f32),
        q1=pltpu.VMEM((patches, columns), b16),
        mixed1=pltpu.VMEM((patches, columns), b16),
        query_in=pltpu.VMEM((patches, width), b16),
        mixed_grad=pltpu.VMEM((patches, columns), b16),
        q_sum=pltpu.VMEM((patches, columns), f32),
        delta_sum=pltpu.VMEM((patches, LANES), f32),
    )

    @functools.partial(pl.run_scoped, **one)
    def _(**scoped):
        for i in range(own_count):
            first_layer(i, scoped)

    hand_over(0)
    for i in range(own_count):
        latent_exchange(i).start()
    point()
    take_over(0)
    for which in (3, 0, 1, 2):
        sum_layer(0, which)
    point()
    gains = Gains(r, section, tensor, flows) if summing else None
    if summing:
        gains.tick()
    last = dict(
        source_in=pltpu.VMEM((half_bytes, width), b16),
        byte_norms=pltpu.VMEM((half_bytes, LANES), f32),
        query_in=pltpu.VMEM((patches, width), b16),
        pool_high=pltpu.VMEM((patches, width), b16),
        pool_low=pltpu.VMEM((patches, width), b16),
        latent=pltpu.VMEM((own_count, patches, columns), b16),
    )

    @functools.partial(pl.run_scoped, **last)
    def _(**scoped):
        last_parts(types.SimpleNamespace(**scoped))

    if summing:
        while gains.steps:
            gains.tick()
            point()
        flows.drain()
    ends = [pltpu.make_async_copy(r.gain_sum, r.gain_out, r.end_sem.at[4])]
    if not summing:
        ends += [
            pltpu.make_async_copy(r.up, r.up_sum, r.end_sem.at[0]),
            pltpu.make_async_copy(r.down, r.down_sum, r.end_sem.at[1]),
            pltpu.make_async_copy(r.attn_out_part.at[section], r.attn_out_sum, r.end_sem.at[3]),
        ]
        ends += [
            pltpu.make_async_copy(
                r.attn_in_part.at[section, :, pl.ds(j * columns, columns)], r.attn_in_sum.at[j],
                r.end_sem.at[5 + j],
            )
            for j in range(3)
        ]
    for copy in ends:
        copy.start()
    for copy in ends:
        copy.wait()


class Gains:
    def __init__(self, r, section, tensor, flows):
        self.r = r
        z = flows.z
        place = lax.axis_index("dp")
        near = place + SHORT * (1 - 2 * lax.rem(z, 2))
        far = place + 2 * SHORT * (1 - 2 * (z // 2))
        self.targets = [
            {"tensor": 1 - tensor}, {"section": 1 - section}, {"dp": flows.beside},
            {"dp": near}, {"dp": far},
        ]
        self.steps = list(range(len(self.targets) + 1))

    def copy(self, n):
        r = self.r
        return pltpu.make_async_remote_copy(
            src_ref=r.gain_held.at[n], dst_ref=r.gain_got.at[n], send_sem=r.gain_send.at[n],
            recv_sem=r.gain_recv.at[n], device_id=self.targets[n], device_id_type=MESH,
        )

    def tick(self):
        if not self.steps:
            return
        r, n = self.r, self.steps.pop(0)
        if n == 0:
            r.gain_held[0] = r.gain_sum[...]
        else:
            self.copy(n - 1).wait()
            value = r.gain_held[n - 1] + r.gain_got[n - 1]
            if n < len(self.targets):
                r.gain_held[n] = value
            else:
                r.gain_sum[...] = value
        if n < len(self.targets):
            self.copy(n).start()


def greet_grid(flows, others):
    barrier = pltpu.get_barrier_semaphore()

    def signal(place):
        pl.semaphore_signal(barrier, inc=1, device_id=place, device_id_type=MESH)

    for axis, index in others:
        signal({axis: index})
    signal({"dp": flows.beside})
    signal({"dp": lax.axis_index("dp") + 2 * SHORT * (1 - 2 * (flows.z // 2))})
    pl.when(flows.z < LONG - 1)(lambda: signal({"dp": flows.right}))
    pl.when(flows.z > 0)(lambda: signal({"dp": flows.left}))
    inner = jnp.logical_and(flows.z > 0, flows.z < LONG - 1)
    pl.semaphore_wait(barrier, jnp.where(inner, len(others) + 4, len(others) + 3))


def backward(kept, patch_ids):
    own, patches, width = kept["normed"].shape
    sequences, byte_count = patch_ids.shape
    columns = kept["q1"].shape[-1]
    hidden = kept["hidden"].shape[-1]
    half, half_bytes = width // 2, byte_count // 2
    sems = pltpu.SemaphoreType.DMA
    vmem = pltpu.VMEM
    rows16 = vmem((own, patches, width), b16)
    scratch = dict(
        inner=rows16,
        grad_in=rows16,
        inner_part=rows16,
        inner_got=rows16,
        normed=rows16,
        patch_norms=vmem((own, patches, LANES), f32),
        branch=rows16,
        normed_part=rows16,
        normed_got=rows16,
        source_part=vmem((own, byte_count, width), b16),
        source_got=vmem((own, half_bytes, width), b16),
        latent_got=vmem((own, patches, columns), b16),
        w_in=vmem((width, 3 * columns), b16),
        w_out=vmem((columns, width), b16),
        gain=vmem((2, 2, width), f32),
        gain_sum=vmem((4, width), f32),
        down_got=vmem((hidden, half), b16),
        down=vmem((hidden, half), b16),
        up=vmem((width, hidden), b16),
        attn_in_part=vmem((2, width, 3 * columns), b16),
        attn_out_part=vmem((2, columns, width), b16),
        big_got=vmem((width, 3 * columns), b16),
        attn_out_got=vmem((columns, width), b16),
        load_sem=sems((16,)),
        first_sem=sems((8,)),
        cross_send=sems((5, own)),
        cross_recv=sems((5, own)),
        give_send=sems((5,)),
        give_recv=sems((5,)),
        out_sem=sems((2, own)),
        out_send=sems((2, own)),
        out_recv=sems((2, own)),
        end_sem=sems((8,)),
        free_sem=pltpu.SemaphoreType.REGULAR,
    )
    slots = []
    if on_grid():
        arrays = [(hidden, half, 512), (half, hidden, 128), (half, hidden, 256)]
        arrays += [(columns, width, 128)] + [(width, columns, 384)] * 3
        for n, (rows, cols, cut) in enumerate(arrays):
            slots.append((f"l{n}", f"s{n}", rows, cut))
            scratch[f"l{n}"] = vmem((7 * cut // LONG, cols), b16)
            scratch[f"s{n}"] = vmem((10 * (rows - cut) // (SHORT * LONG), cols), b16)
        scratch |= dict(
            flow_send=sems((2 * len(arrays), 17)),
            flow_recv=sems((2 * len(arrays), 17)),
            flow_near=sems((2 * len(arrays),)),
            gain_held=vmem((5, 4, width), f32),
            gain_got=vmem((5, 4, width), f32),
            gain_send=sems((5,)),
            gain_recv=sems((5,)),
        )
    ins = [("ids", patch_ids, True)]
    ins += [("in_" + name, kept[name], False) for name in (*KEPT, *LAYERS)]
    outs = [
        ("latents", shape((sequences, patches // 2, columns), b16)),
        ("byte_grad", shape((sequences, half_bytes, half), b16)),
        ("attn_in_sum", shape((3, width, columns), b16)),
        ("attn_out_sum", shape((columns, width), b16)),
        ("gain_out", shape((4, width), f32)),
        ("up_sum", shape((width, hidden), b16)),
        ("down_sum", shape((hidden, half), b16)),
    ]

    def kernel(r):
        r.slots = [
            (getattr(r, long), getattr(r, short), rows, cut) for long, short, rows, cut in slots
        ]
        backward_kernel(r)

    return named_call(kernel, ins, outs, scratch, collective_id=1)


def swap(values, axis):
    return lax.ppermute(values, axis, [(0, 1), (1, 0)])


def sum_small(values):
    values = values + swap(values, "tensor")
    values = values + swap(values, "section")
    return lax.psum(values, "dp")


def per_device(byte_states, patch_ids, attn_in, attn_out, gains, ffn_in, ffn_out, latent_grad):
    width = byte_states.shape[-1]
    hidden = ffn_out.shape[0]
    half = width // 2
    is_first = lax.axis_index("section") == 0
    kept = forward(
        byte_states, patch_ids, attn_in, attn_out, gains, ffn_in.transpose(1, 0, 2), ffn_out,
        latent_grad,
    )
    got = backward(kept, patch_ids)
    sums = [got[name] for name in ("down_sum", "up_sum", "attn_in_sum", "attn_out_sum")]
    if not on_grid():
        sums = [lax.psum(value, "dp") for value in sums]
    down, up, in_sum, out_sum = [value.astype(f32) for value in sums]
    gain_sum = got["gain_out"] if on_grid() else sum_small(got["gain_out"])
    gain_out = jnp.where(is_first, gain_sum[0:2], gain_sum[2:4])
    up_out = up.reshape(2, half, hidden).transpose(1, 0, 2)
    return (
        got["latents"], got["byte_grad"], in_sum[None], out_sum[None], gain_out[None], up_out, down
    )


def solution(mesh):
    return jax.shard_map(
        per_device,
        mesh=mesh,
        in_specs=(
            P("dp", None, None),
            P("dp", None),
            P("section", None, None, "tensor"),
            P("section", "tensor", None),
            P("section", None, None),
            P(None, None, "tensor"),
            P("tensor", None),
            P("dp", None, None),
        ),
        out_specs=(
            P("dp", "section", "tensor"),
            P("dp", "tensor", "section"),
            P("section", None, None, "tensor"),
            P("section", "tensor", None),
            P("section", None, None),
            P("section", None, "tensor"),
            P("tensor", "section"),
        ),
        check_vma=False,
    )
```

```python
import functools
import types

import jax
import jax.numpy as jnp
from jax import lax
from jax.experimental import pallas as pl
from jax.experimental.pallas import tpu as pltpu
from jax.sharding import PartitionSpec as P

HD = 64
LANES = 128
BLOCK = 256
WIDE = 512
EPSILON = 1e-05
NEGATIVE = -1000000000.0
SCALE = HD ** (-0.5)
VMEM_BYTES = 63 * 1024 * 1024

f32 = jnp.float32
b16 = jnp.bfloat16


def dot(a, b):
    return jnp.dot(a, b, preferred_element_type=f32)


def dot_rt(a, b):
    return lax.dot_general(a, b, (((1,), (1,)), ((), ())), preferred_element_type=f32)


def dot_lt(a, b):
    return lax.dot_general(a, b, (((0,), (0,)), ((), ())), preferred_element_type=f32)


def inverse_rms(values):
    return lax.rsqrt(jnp.mean(values * values, axis=-1, keepdims=True) + EPSILON)


def iota(shape, dim):
    return lax.broadcasted_iota(jnp.int32, shape, dim)


def one_hot(condition):
    return jnp.where(condition, 1.0, 0.0).astype(b16)


def segment_max(values, ids):
    width = values.shape[1]
    lane = iota(ids.shape, 1)
    lowest = -3.0e38
    ahead, behind = values, values
    step = 1
    while step < width:
        left, right = step, width - step
        same_left = jnp.logical_and(pltpu.roll(ids, left, axis=1) == ids, lane >= step)
        same_right = jnp.logical_and(pltpu.roll(ids, right, axis=1) == ids, lane < right)
        ahead = jnp.maximum(ahead, jnp.where(same_left, pltpu.roll(ahead, left, axis=1), lowest))
        behind = jnp.maximum(
            behind, jnp.where(same_right, pltpu.roll(behind, right, axis=1), lowest)
        )
        step *= 2
    return jnp.maximum(ahead, behind)


def head_masks(width):
    heads_in = one_hot(iota((width, LANES), 0) // HD == iota((width, LANES), 1))
    heads_out = one_hot(iota((LANES, width), 1) // HD == iota((LANES, width), 0))
    return heads_in, heads_out


def split_dot(values, matrix):
    high = values.astype(b16)
    low = (values - high.astype(f32)).astype(b16)
    return dot(high, matrix) + dot(low, matrix)


def block_at(index, size=BLOCK):
    return pl.ds(pl.multiple_of(index * size, size), size)


def each_block(count, body, size=BLOCK):
    @pl.loop(0, count // size)
    def _(index):
        body(block_at(index, size))


MESH = pl.DeviceIdType.MESH


def remote(src, dst, send, recv, axis, index):
    return pltpu.make_async_remote_copy(
        src_ref=src, dst_ref=dst, send_sem=send, recv_sem=recv,
        device_id={axis: index}, device_id_type=MESH,
    )


def greet(places):
    barrier = pltpu.get_barrier_semaphore()
    for axis, index in places:
        pl.semaphore_signal(barrier, inc=1, device_id={axis: index}, device_id_type=MESH)
    pl.semaphore_wait(barrier, len(places))


def exchange_layer(r, section):
    columns = r.attn_in.shape[3]
    copies = []
    for n, (src, dst) in enumerate(
        [
            (r.attn_in.at[0, j], r.w_in.at[section, :, pl.ds(j * columns, columns)])
            for j in (1, 2, 0)
        ]
        + [(r.attn_out.at[0], r.w_out.at[section]), (r.gains.at[0], r.gain.at[section])]
    ):
        near = pltpu.make_async_copy(src, dst, r.near_sem.at[n])
        far = remote(src, dst, r.far_send.at[n], r.far_recv.at[n], "section", 1 - section)
        near.start()
        far.start()
        copies.append((near, far))
    return copies


def arrived(copies):
    for near, far in copies:
        near.wait()
        far.wait()


def members_of(r, seq, rows, patches):
    return one_hot(iota((patches, rows.size), 0) == r.ids[pl.ds(seq, 1), rows])


def names(**kinds):
    return tuple(kinds)


FIRST_KEPT = names(query_in=1, source_in=1, byte_norms=1)
CROSS_KEPT = names(q1=1, k1=1, v1=1, raised=1, inverse=1, mixed1=1)
SECOND_KEPT = names(normed=1, q2=1, k2=1, v2=1, totals=1, mixed2=1)
FEED_KEPT = names(
    inner=1, hidden=1, gate_grad=1, up_grad=1, grad_in=1, inner_part=1, patch_norms=1,
    latent_own=1, latent_send=1,
)
KEPT = FIRST_KEPT + CROSS_KEPT + SECOND_KEPT + FEED_KEPT
LAYERS = names(w_in=1, w_out=1, gain=1)


def forward_kernel(r):
    section, tensor = lax.axis_index("section"), lax.axis_index("tensor")
    own_count, patches, width = r.normed.shape
    byte_count = r.states.shape[1]
    columns = r.q1.shape[2]
    hidden = r.hidden.shape[2]
    heads = columns // HD
    greet([("section", 1 - section), ("tensor", 1 - tensor)])
    state_copies = [
        pltpu.make_async_copy(
            r.states.at[section * own_count + i], r.state_in.at[i], r.state_sem.at[i]
        )
        for i in range(own_count)
    ]
    for copy in state_copies:
        copy.start()
    layer = exchange_layer(r, section)
    grad_copies = [
        pltpu.make_async_copy(
            r.upstream.at[section * own_count + i], r.grad_in.at[i], r.grad_sem.at[i]
        )
        for i in range(own_count)
    ]
    feed_copies = [
        pltpu.make_async_copy(r.ffn_in, r.feed_in, r.feed_sem.at[0]),
        pltpu.make_async_copy(r.ffn_out, r.feed_out, r.feed_sem.at[1]),
    ]
    for copy in grad_copies + feed_copies:
        copy.start()
    heads_in, heads_out = head_masks(columns)

    def keep(name, i):
        n = KEPT.index(name)
        return pltpu.make_async_copy(
            getattr(r, name).at[i], getattr(r, "out_" + name).at[i], r.keep_sem.at[n, i]
        )

    def save(names, i):
        for name in names:
            keep(name, i).start()

    def exchange(step, i):
        return remote(
            r.part.at[step, i], r.got.at[step, i], r.part_send.at[step, i], r.part_recv.at[step, i],
            "tensor", 1 - tensor,
        )

    for copy in state_copies:
        copy.wait()
    layer[-1][0].wait()
    layer[-1][1].wait()
    first_gain = r.gain.at[0]

    @pl.loop(0, own_count)
    def _(i):
        seq = section * own_count + i
        r.pool_sum[...] = jnp.zeros_like(r.pool_sum)

        def pool(rows):
            block = r.state_in[i, rows, :]
            r.pool_sum[...] += dot(members_of(r, seq, rows, patches), block)
            values = block.astype(f32)
            scale = inverse_rms(values)
            r.byte_norms[i, rows, :] = jnp.broadcast_to(scale, (BLOCK, LANES))
            r.source_in[i, rows, :] = (values * scale * first_gain[1:2, :]).astype(b16)

        each_block(byte_count, pool)
        row_ids = r.ids[pl.ds(seq, 1), :]
        counts = jnp.sum(
            jnp.where(iota((patches, byte_count), 0) == row_ids, 1.0, 0.0), axis=1, keepdims=True
        )
        values = r.pool_sum[...] / jnp.maximum(counts, 1.0)
        r.pooled[i] = values
        scale = inverse_rms(values)
        r.patch_norms[i] = jnp.broadcast_to(scale, (patches, LANES))
        r.query_in[i] = (values * scale * first_gain[0:1, :]).astype(b16)
        save(FIRST_KEPT, i)

    arrived(layer[:4])
    layer_saves = [
        pltpu.make_async_copy(getattr(r, name), getattr(r, "out_" + name), r.layer_sem.at[n])
        for n, name in enumerate(LAYERS)
    ]
    for copy in layer_saves:
        copy.start()

    @pl.loop(0, own_count)
    def _(i):
        seq = section * own_count + i
        r.q1[i] = dot(r.query_in[i], r.w_in[0, :, :columns]).astype(b16)

        def project(rows):
            both = dot(r.source_in[i, rows, :], r.w_in[0, :, columns:])
            keys = both[:, :columns].astype(b16)
            r.k1[i, rows, :] = keys
            r.v1[i, rows, :] = both[:, columns:].astype(b16)
            spread = dot_lt(members_of(r, seq, rows, patches), r.q1[i])
            block_scores = split_dot(spread * keys.astype(f32), heads_in) * SCALE
            r.scores[:, rows] = block_scores.T[:heads, :]

        each_block(byte_count, project, WIDE)
        scores = r.scores[...]
        r.scores[...] = jnp.exp(scores - segment_max(scores, r.ids[pl.ds(seq, 1), :]))
        r.mix_sum[...] = jnp.zeros_like(r.mix_sum)
        r.total_sum[...] = jnp.zeros_like(r.total_sum)

        def mix(rows):
            short = r.scores[:, rows]
            filled = jnp.concatenate([short, jnp.zeros((LANES - heads, WIDE), f32)], axis=0)
            raised = filled.T.astype(b16)
            r.raised[i, rows, :] = raised
            members = members_of(r, seq, rows, patches)
            weighted = (dot(raised, heads_out) * r.v1[i, rows, :].astype(f32)).astype(b16)
            r.mix_sum[...] += dot(members, weighted)
            r.total_sum[...] += dot(members, raised)

        each_block(byte_count, mix, WIDE)
        totals = r.total_sum[...]
        inverse = jnp.where(totals > 0.0, 1.0 / totals, 0.0)
        r.inverse[i] = inverse
        mixed = (r.mix_sum[...] * split_dot(inverse, heads_out)).astype(b16)
        r.mixed1[i] = mixed
        r.part[0, i] = dot(mixed, r.w_out[0]).astype(b16)
        exchange(0, i).start()
        save(CROSS_KEPT, i)

    second_gain = r.gain.at[1]
    allowed = iota((patches, patches), 1) <= iota((patches, patches), 0)
    lane = iota((patches, LANES), 1)

    @pl.loop(0, own_count)
    def _(i):
        exchange(0, i).wait()
        latent = (
            r.pooled[i] + r.part[0, i].astype(f32) + r.got[0, i].astype(f32)
        ).astype(b16)
        r.latent[i] = latent
        values = latent.astype(f32)
        scale = inverse_rms(values)
        r.patch_norms[i] = jnp.where(lane == 1, scale, r.patch_norms[i])
        normed = (values * scale * second_gain[0:1, :]).astype(b16)
        r.normed[i] = normed
        projected = dot(normed, r.w_in[1]).astype(b16)
        query, key, value = [projected[:, j * columns : (j + 1) * columns] for j in range(3)]
        r.q2[i] = query
        r.k2[i] = key
        r.v2[i] = value
        kept = jnp.zeros((patches, LANES), f32)
        outs = []
        for head in range(heads):
            own = slice(head * HD, (head + 1) * HD)
            scores = jnp.where(allowed, dot_rt(query[:, own], key[:, own]) * SCALE, NEGATIVE)
            highest = jnp.max(scores, axis=-1, keepdims=True)
            raised = jnp.exp(scores - highest)
            total = jnp.sum(raised, axis=-1, keepdims=True)
            outs.append(dot((raised / total).astype(b16), value[:, own]))
            kept = jnp.where(lane == head, highest + jnp.log(total), kept)
        r.totals[i] = kept
        mixed = jnp.concatenate(outs, axis=1).astype(b16)
        r.mixed2[i] = mixed
        r.part[1, i] = dot(mixed, r.w_out[1]).astype(b16)
        exchange(1, i).start()
        save(SECOND_KEPT, i)

    for copy in grad_copies + feed_copies:
        copy.wait()

    @pl.loop(0, own_count)
    def _(i):
        seq = section * own_count + i
        exchange(1, i).wait()
        values = (
            r.latent[i].astype(f32) + r.part[1, i].astype(f32) + r.got[1, i].astype(f32)
        )
        r.middle[...] = values
        scale = inverse_rms(values)
        r.patch_norms[i] = jnp.where(lane == 2, scale, r.patch_norms[i])
        r.inner[i] = (values * scale * second_gain[1:2, :]).astype(b16)
        valid = iota((patches, 1), 0) <= jnp.max(r.ids[pl.ds(seq, 1), :], axis=1, keepdims=True)
        r.grad_in[i] = jnp.where(valid, r.grad_in[i].astype(f32), 0.0).astype(b16)

        gate = dot(r.inner[i], r.feed_in[0])
        up = dot(r.inner[i], r.feed_in[1])
        hidden_grad = dot_rt(r.grad_in[i], r.feed_out[...])
        gated = 1.0 / (1.0 + jnp.exp(-gate))
        act = gate * gated
        r.hidden[i] = (act * up).astype(b16)
        r.gate_grad[i] = (hidden_grad * up * (gated * (1.0 + gate * (1.0 - gated)))).astype(b16)
        r.up_grad[i] = (hidden_grad * act).astype(b16)
        inner_grad = dot_rt(r.gate_grad[i], r.feed_in[0]) + dot_rt(r.up_grad[i], r.feed_in[1])
        r.inner_part[i] = inner_grad.astype(b16)
        r.out_sum[...] = dot(r.hidden[i], r.feed_out[...])
        mine, theirs = block_at(tensor, columns), block_at(1 - tensor, columns)
        r.latent_own[i] = (r.middle[:, mine] + r.out_sum[:, mine]).astype(b16)
        r.latent_send[i] = r.out_sum[:, theirs].astype(b16)
        save(FEED_KEPT, i)

    @pl.loop(0, own_count)
    def _(i):
        for name in KEPT:
            keep(name, i).wait()

    for copy in layer_saves:
        copy.wait()


def shape(dims, dtype):
    return jax.ShapeDtypeStruct(dims, dtype)


def named_call(kernel, ins, outs, scratch, **params):
    any_space = pl.BlockSpec(memory_space=pl.ANY)
    whole = pl.BlockSpec(memory_space=pltpu.VMEM)
    names = [name for name, _, _ in ins] + [name for name, _ in outs] + list(scratch)

    def body(*refs):
        kernel(types.SimpleNamespace(**dict(zip(names, refs, strict=True))))

    got = pl.pallas_call(
        body,
        out_shape=tuple(s for _, s in outs),
        in_specs=[whole if inside else any_space for _, _, inside in ins],
        out_specs=tuple(any_space for _ in outs),
        scratch_shapes=list(scratch.values()),
        compiler_params=pltpu.CompilerParams(
            vmem_limit_bytes=VMEM_BYTES, has_side_effects=True, **params
        ),
    )(*(array for _, array, _ in ins))
    return {name: value for (name, _), value in zip(outs, got, strict=True)}


def forward(byte_states, patch_ids, attn_in, attn_out, gains, feed_in, feed_out, latent_grad):
    sequences, byte_count, width = byte_states.shape
    patches = byte_count // 4
    columns = attn_in.shape[-1]
    hidden = feed_out.shape[0]
    own = sequences // 2
    heads = columns // HD
    dims = dict(
        query_in=(own, patches, width, b16),
        source_in=(own, byte_count, width, b16),
        q1=(own, patches, columns, b16),
        k1=(own, byte_count, columns, b16),
        v1=(own, byte_count, columns, b16),
        raised=(own, byte_count, LANES, b16),
        inverse=(own, patches, LANES, f32),
        mixed1=(own, patches, columns, b16),
        byte_norms=(own, byte_count, LANES, f32),
        normed=(own, patches, width, b16),
        q2=(own, patches, columns, b16),
        k2=(own, patches, columns, b16),
        v2=(own, patches, columns, b16),
        totals=(own, patches, LANES, f32),
        mixed2=(own, patches, columns, b16),
        inner=(own, patches, width, b16),
        hidden=(own, patches, hidden, b16),
        gate_grad=(own, patches, hidden, b16),
        up_grad=(own, patches, hidden, b16),
        grad_in=(own, patches, width, b16),
        inner_part=(own, patches, width, b16),
        patch_norms=(own, patches, LANES, f32),
        latent_own=(own, patches, columns, b16),
        latent_send=(own, patches, columns, b16),
    )
    sems = pltpu.SemaphoreType.DMA
    scratch = {name: pltpu.VMEM(dims[name][:-1], dims[name][-1]) for name in KEPT}
    scratch |= dict(
        state_in=pltpu.VMEM((own, byte_count, width), b16),
        pooled=pltpu.VMEM((own, patches, width), f32),
        latent=pltpu.VMEM((own, patches, width), b16),
        middle=pltpu.VMEM((patches, width), f32),
        out_sum=pltpu.VMEM((patches, width), f32),
        w_in=pltpu.VMEM((2, width, 3 * columns), b16),
        w_out=pltpu.VMEM((2, columns, width), b16),
        gain=pltpu.VMEM((2, 2, width), f32),
        feed_in=pltpu.VMEM((2, width, hidden), b16),
        feed_out=pltpu.VMEM((hidden, width), b16),
        pool_sum=pltpu.VMEM((patches, width), f32),
        scores=pltpu.VMEM((heads, byte_count), f32),
        mix_sum=pltpu.VMEM((patches, columns), f32),
        total_sum=pltpu.VMEM((patches, LANES), f32),
        part=pltpu.VMEM((2, own, patches, width), b16),
        got=pltpu.VMEM((2, own, patches, width), b16),
        state_sem=sems((own,)),
        grad_sem=sems((own,)),
        feed_sem=sems((2,)),
        near_sem=sems((5,)),
        far_send=sems((5,)),
        far_recv=sems((5,)),
        part_send=sems((2, own)),
        part_recv=sems((2, own)),
        keep_sem=sems((len(KEPT), own)),
        layer_sem=sems((len(LAYERS),)),
    )
    ins = [
        ("states", byte_states, False), ("ids", patch_ids, True), ("attn_in", attn_in, False),
        ("attn_out", attn_out, False), ("gains", gains, False), ("ffn_in", feed_in, False),
        ("ffn_out", feed_out, False), ("upstream", latent_grad, False),
    ]
    dims |= dict(
        w_in=(2, width, 3 * columns, b16),
        w_out=(2, columns, width, b16),
        gain=(2, 2, width, f32),
    )
    names = (*KEPT, *LAYERS)
    outs = [("out_" + name, shape(dims[name][:-1], dims[name][-1])) for name in names]
    got = named_call(forward_kernel, ins, outs, scratch, collective_id=0)
    return {name: got["out_" + name] for name in names}


def flat(ref, cols):
    block = ref[:, :, cols]
    return block.reshape(block.shape[0] * block.shape[1], block.shape[2])


LONG, SHORT = 4, 2


def rows_of(ref, start, rows):
    if not isinstance(start, int):
        start = pl.multiple_of(start, 16)
    return ref.at[pl.ds(start, rows), :]


def sum_rows(target, *terms):
    rows, width = target.shape
    step = rows
    while step * width > 100 * 1408 and step % 32 == 0:
        step //= 2

    def add(at):
        value = terms[0][at, :]
        for term in terms[1:]:
            value = value + term[at, :]
        target[at, :] = value

    if step == rows:
        add(slice(None))
    else:
        each_block(rows, add, step)


def add_rows(target, *others):
    sum_rows(target, target, *others)


PLAN = ((((0,1),()),((0,1),(1,)),((),()),((1,),(0,))),(((3,0,0,0,2,2,2),(0,1,2,0,0,0,2,3,2)),((0,0,3,2),(2,3,0)),((2,1,0,3),(1,3)),((0,0,0,0,2,2,2,3),(1,0,0,0,2,2,2,3,2))),(((5,4,2,4,1,4,4),(4,4,5,1,2,4)),((),(4,5)),((4,5,0),(4,5,2)),((4,4,2,4,5,4),(4,5,1,4,4,4))),(((1,1),(4,)),((4,),(0,0)),((1,0,0),(0,0)),((1,1),())),(((),()),((1,0),()),((0,),()),((1,),())),(((),(1,1)),((2,5),(1,)),((2,),(1,0)),((),(1,1))),(((),(3,)),((0,),()),((),(2,)),((0,),())),(((3,3,0,3),()),((3,),(0,3,0,2,2)),((3,2,2),()),((3,3,3),(0,))),(((),()),((2,2),(2,)),((),(3,)),((),(3,3))),(((),()),((4,4),()),((4,),(0,2)),((),())),(((),(3,2,0)),((),(4,4)),((),(2,2)),((2,),())),(((2,5,5),()),((4,0,2),(5,2)),((2,5,4,4),(4,4,4,0)),((5,5,5),(2,))),(((),(13,8,0,11,5,3,7,9,0,6,10,5,12,12,5,10,8,8,10,6,6,6,10,2,2)),((),(6,4,4,10,1,7,0,9,11,13,2,12,8)),((),(4,6,1,11,5,0,10,2,9,8,12,7)),((),(8,3,5,5,11,7,0,12,5,9,8,10,6,6,6,8,12,10,12,13,8,10,12,6))),(((),(8,12,12)),((),()),((1,4),(13,)),((),())),(((5,),()),((4,1),()),((),()),((4,),(2,4))),(((0,0),(0,0)),((5,),(3,7)),((0,),()),((0,),(0,0))),(((0,),(4,7,7,7)),((2,),(1,1)),((),(0,)),((),(7,7,2,2))),(((2,2),(2,2)),((),()),((),(3,9,7)),((2,),())),(((0,),(9,)),((1,1),()),((2,0,1,1),(4,2,1,11)),((0,),(9,9,10,9,11))),(((),()),((),()),((),()),((2,2),(7,11,11))),(((2,),(11,)),((3,),(4,)),((),(1,)),((),())),(((4,1),(9,11)),((4,5,0,0,0,1,3),(6,)),((5,4,3,3,0),(8,)),((),())),(((),(9,)),((3,2),()),((),()),((1,0),(0,0,13))),(((),(13,13,13)),((),(11,)),((),(13,)),((),(13,13,2))),(((),()),((5,2,0,0),()),((5,1,5,2,2,4,0,0,0,3,0),(3,3,6,5,6)),((),(4,))),(((0,),(4,11,4,4)),((),(10,0,0,3,9,3,13,5,6)),((3,),()),((),())),(((),()),((0,5),(8,8)),((),(10,8)),((0,0),(2,4))),(((2,),()),((),()),((),()),((4,),())),(((),()),((),(12,10)),((),()),((2,2),())),(((),(4,)),((2,3),(0,12)),((5,),(10,0,12,12,1)),((),())),(((),()),((),(2,1)),((),(2,)),((),())),(((4,18,4,1,0,3,16,15,4,17,16,20,14,20,4,19,16,21,14,14,20,18,16,18,18,2,2,14,5),(3,)),((14,17,15,2,20,21,2,2,5,19),()),((16,17,20,15,19,14,21,4,16,18,2),()),((19,14,4,1,16,15,18,17,20,3,14,20,18,14,4,16,21,20,18,20,16,16,14,15,5,0,0,4,3,4,15,17,18,2,15,2,17,17,19,19),(1,))),(((3,0,15,15,15,17,17,2,20,19,21,4,17,21,19,19),(1,5,0,0)),((16,),(5,7,3,2,2,6,0,11,0,12,10,9,5,0,8,6)),((2,2,2),(6,5,0,0,3,7,4,8,0,0,6,8,9)),((21,19,21),(3,4))),(((),(3,1,2,6,0,4,8,10,12,4,2,2,9,4,13,6,7,6,6,6,8,11,8,5,8,8,10)),((4,4,18,18,4,15,16,20,14,14,16,20,18,4,19,4,4,15,17,21,17,19,16,21),(10,12,5,2,4,8,4,9,2,6,4,7,2,9,7,13,11,10,13,11,13,8,12,4,11,4,9,7)),((14,16,14,18,18,20,4,20,19,14,15,15,17,21,17),(11,10,10,5,12,12,2,2,2,2,7,11,5,8,7,6,4,9,13,11,10,10,12,12,13,4,9,7,4,4,9,6,8,13)),((),(3,5,6,0,4,1,0,11,12,8,4,7,10,2,13,2,6,9,4,8,10,10,5,8,10,10,6,12,12,8,8,8,12,6,6,6,4,10,12))),(((),(12,12,12,12,7,10,10,6,12)),((14,14,18,18,20,20),()),((4,19,4,4,21,20,14,18,16,16,18,14,20,15,18),(6,11)),((),())),(((21,4,14,5,16,18,20),()),((14,20),()),((16,20,15,17),(4,)),((16,18,4,14,21,20),())),(((15,),(10,8,8,9,6,6,10,10,10,11,8)),((16,15,16,18,15,17,17,19,19,15,17,21,18),(13,6,6,8,8,10,10,10,8,4,12,12,6)),((17,15,19,21,17,21,14,19),(8,6,10,12,13)),((4,15,14,14,18,5,20,16,16),(7,11,9,12))),(((4,14,14,14,14,16,16,16,16,18,18,18,18,17,20,19,15),()),((21,14),(10,6,6,10,10,8,8,8,12)),((14,19),(6,6,8,8,8,8,10,10,12,10,10,6,12,12,12)),((14,20,16,18,18,20,17,15,19),(10,13))),(((21,17,20,20,20,16,14,14,20,20,16,18,20,14,19,18,18,16,21),(12,12,13)),((14,16,16,16,18,20,19,18,20,20,14,14,21,14,14,18,16,16,16,18,20,20,20,18),(12,12,12,6)),((18,16,21,20,18,20,16,14,14,14,16,16,18,18,14,18,18,20,20,20,16,20,16),()),((21,14,14,16,16,20,17,16,18,18,19,14,16,20,20,14,20,18,21,18),(6,6,8,8,12,12,10))))


class Flows:
    def __init__(self, r, section):
        self.r = r
        self.section = section
        place = lax.axis_index("dp")
        self.z, self.y = place // SHORT, lax.rem(place, SHORT)
        self.right, self.left = place + SHORT, place - SHORT
        self.beside = place + 1 - 2 * self.y
        self.flows = []
        self.done = {(z, s): [] for z in range(LONG) for s in range(2)}
        self.points = 0

    def hop(self, src, dst, n, j, target):
        r = self.r
        return pltpu.make_async_remote_copy(
            src_ref=src, dst_ref=dst, send_sem=r.flow_send.at[n, j], recv_sem=r.flow_recv.at[n, j],
            device_id={"dp": target}, device_id_type=MESH,
        )

    def reduce_events(self, n, part, slot):
        def up(k):
            return self.hop(slot(k - 1), slot(k - 1), n, k - 1, self.right)

        def down(k):
            return self.hop(slot(3 + k), slot(3 + k), n, 3 + k, self.left)

        def pass_on(copy, held, k):
            copy(k).wait_recv()
            add_rows(held, part(k))
            copy(k).start()

        def begin(z):
            if z == 0:
                for k in (3, 2, 1):
                    self.hop(part(k), slot(k - 1), n, k - 1, self.right).start()
            if z == 3:
                for k in (0, 1, 2):
                    self.hop(part(k), slot(3 + k), n, 3 + k, self.left).start()

        def passing(at_one, at_two):
            def event(z):
                if z in (1, 2):
                    way, k = (at_one, at_two)[z - 1]
                    pass_on(*((up, slot(k - 1)) if way > 0 else (down, slot(3 + k))), k)

            return event

        def close(z):
            got = []
            if z >= 1:
                up(z).wait_recv()
                got.append(slot(z - 1))
            if z <= 2:
                down(z).wait_recv()
                got.append(slot(3 + z))
            add_rows(part(z), *got)

        def sent(z):
            for k in ((1, 2, 3), (2, 3), (3,), ())[z]:
                up(k).wait_send()
            for k in ((), (0,), (0, 1), (0, 1, 2))[z]:
                down(k).wait_send()

        passes = [
            passing((1, 3), (-1, 0)), passing((1, 2), (-1, 1)), passing((-1, 0), (1, 3)),
        ]
        return begin, passes, close, sent

    def gather_events(self, n, own, out):
        def up(src, k, d):
            return self.hop(src, out(k), n, 7 + d, self.right)

        def down(src, k, d):
            return self.hop(src, out(k), n, 10 + d, self.left)

        def near(z):
            return pltpu.make_async_copy(own(z), out(z), self.r.flow_near.at[n])

        def starts(z, d, way):
            k = z - d * way
            src = own(z) if d == 0 else out(k)
            copies = []
            if d < LONG - 1 and 0 <= z + way < LONG:
                copies.append((up if way > 0 else down)(src, k, d))
            return copies

        def begin(z):
            near(z).start()
            for copy in starts(z, 0, 1) + starts(z, 0, -1):
                copy.start()

        def step(d, way):
            def event(z):
                k = z - d * way
                if 0 <= k < LONG:
                    (up if way > 0 else down)(out(k), k, d - 1).wait_recv()
                    for copy in starts(z, d, way):
                        copy.start()

            return event

        def sent(z):
            near(z).wait()
            for way in (1, -1):
                for d in range(LONG):
                    if 0 <= z - d * way < LONG:
                        for copy in starts(z, d, way):
                            copy.wait_send()

        return begin, [step(d, way) for d in (1, 2, 3) for way in (1, -1)], sent

    def long_first(self, n, data, out, slots, start, rows):
        c = rows // LONG

        def part(k):
            return data(start + k * c, c)

        def slot(j):
            return rows_of(slots, j * c, c)

        def beside(z):
            return self.hop(part(z), slot(6), n, 6, self.beside)

        begin, passes, close, reduce_sent = self.reduce_events(n, part, slot)
        gather, steps, gather_sent = self.gather_events(
            n, lambda z: slot(6), lambda k: out(start + k * c, c)
        )

        def middle(z):
            close(z)
            beside(z).start()

        def turn(z):
            beside(z).wait_recv()
            add_rows(slot(6), part(z))
            gather(z)

        def sent(z):
            reduce_sent(z)
            beside(z).wait_send()
            gather_sent(z)

        return [begin, *passes, middle, turn, *steps], sent

    def short_first(self, n, data, out, slots, start, rows):
        half = rows // SHORT

        def mine(y):
            return data(start + y * half, half)

        def place(y):
            return out(start + y * half, half)

        def slot(j):
            return rows_of(slots, j * half, half)

        def beside():
            return self.hop(mine(1 - self.y), slot(0), n, 6, self.beside)

        inward = (self.right, self.right, self.left, self.left)
        outward = (None, self.left, self.right, None)

        def lean(z):
            middle = 1 if z in (1, 2) else 0
            return self.hop(mine(self.y), slot(1 + middle), n, middle, inward[z])

        def settle(z):
            src = slot(0) if z in (1, 2) else place(self.y)
            return self.hop(src, place(self.y), n, 7, outward[z])

        def near(z):
            return pltpu.make_async_copy(slot(0), place(self.y), self.r.flow_near.at[n])

        def spread(z):
            src = slot(0) if z in (1, 2) else place(self.y)
            return self.hop(src, place(self.y), n, 13, self.beside)

        def first(z):
            beside().start()

        def turn(z):
            beside().wait_recv()
            add_rows(mine(self.y), slot(0))
            if z in (0, 3):
                lean(z).start()

        def pair(z):
            if z in (1, 2):
                self.hop(slot(1), slot(1), n, 0, inward[z]).wait_recv()
                add_rows(mine(self.y), slot(1))
                lean(z).start()

        def close(z):
            if z in (1, 2):
                lean(z).wait_recv()
                sum_rows(slot(0), mine(self.y), slot(2))
                near(z).start()
                settle(z).start()
                spread(z).start()

        def outer(z):
            if z in (0, 3):
                self.hop(place(self.y), place(self.y), n, 7, inward[z]).wait_recv()
                spread(z).start()

        def end(z):
            there = place(1 - self.y)
            self.hop(there, there, n, 13, self.beside).wait_recv()

        def sent(z):
            beside().wait_send()
            lean(z).wait_send()
            spread(z).wait_send()
            if z in (1, 2):
                settle(z).wait_send()
                near(z).wait()

        return [first, turn, pair, close, outer, end], sent

    def open(self, only, *flows):
        for events, sent in flows:
            self.flows.append((only, events, sent))
            for counts in self.done.values():
                counts.append(0)

    def advance(self, z, s, todo):
        def body():
            for n in todo:
                self.flows[n][1][self.done[z, s][n]](z)
                self.done[z, s][n] += 1

        return body

    def choose(self, low, high, bodies):
        here = [key for key in bodies if low <= 2 * key[0] + key[1] < high]
        if not here:
            return
        if high - low == 1:
            bodies[here[0]]()
            return
        middle = (low + high) // 2
        lax.cond(
            2 * self.z + self.section < middle,
            lambda: self.choose(low, middle, bodies),
            lambda: self.choose(middle, high, bodies),
        )

    def point(self):
        plan = PLAN[self.points] if self.points < len(PLAN) else ()
        self.points += 1
        bodies = {
            (z, s): self.advance(z, s, todo)
            for z, lists in enumerate(plan)
            for s, todo in enumerate(lists)
            if todo
        }
        self.choose(0, 2 * LONG, bodies)

    def drain(self):
        def rest(z, s):
            counts = self.done[z, s]

            def body():
                mine = [n for n, flow in enumerate(self.flows) if flow[0] in (None, s)]
                for k in range(max(len(self.flows[n][1]) for n in mine)):
                    for n in mine:
                        if counts[n] <= k < len(self.flows[n][1]):
                            self.flows[n][1][k](z)
                for n in mine:
                    self.flows[n][2](z)

            return body

        self.choose(0, 2 * LONG, {place: rest(*place) for place in self.done})


def flat(ref, cols):
    block = ref[:, :, cols]
    return block.reshape(block.shape[0] * block.shape[1], block.shape[2])


LONG, SHORT = 4, 2


def rows_of(ref, start, rows):
    if not isinstance(start, int):
        start = pl.multiple_of(start, 16)
    return ref.at[pl.ds(start, rows), :]


def sum_rows(target, *terms):
    rows, width = target.shape
    step = rows
    while step * width > 100 * 1408 and step % 32 == 0:
        step //= 2

    def add(at):
        value = terms[0][at, :]
        for term in terms[1:]:
            value = value + term[at, :]
        target[at, :] = value

    if step == rows:
        add(slice(None))
    else:
        each_block(rows, add, step)


def add_rows(target, *others):
    sum_rows(target, target, *others)


PLAN = ((((0,1),()),((0,1),(1,)),((),()),((1,),(0,))),(((3,0,0,0,2,2,2),(0,1,2,0,0,0,2,3,2)),((0,0,3,2),(2,3,0)),((2,1,0,3),(1,3)),((0,0,0,0,2,2,2,3),(1,0,0,0,2,2,2,3,2))),(((5,4,2,4,1,4,4),(4,4,5,1,2,4)),((),(4,5)),((4,5,0),(4,5,2)),((4,4,2,4,5,4),(4,5,1,4,4,4))),(((1,1),(4,)),((4,),(0,0)),((1,0,0),(0,0)),((1,1),())),(((),()),((1,0),()),((0,),()),((1,),())),(((),(1,1)),((2,5),(1,)),((2,),(1,0)),((),(1,1))),(((),(3,)),((0,),()),((),(2,)),((0,),())),(((3,3,0,3),()),((3,),(0,3,0,2,2)),((3,2,2),()),((3,3,3),(0,))),(((),()),((2,2),(2,)),((),(3,)),((),(3,3))),(((),()),((4,4),()),((4,),(0,2)),((),())),(((),(3,2,0)),((),(4,4)),((),(2,2)),((2,),())),(((2,5,5),()),((4,0,2),(5,2)),((2,5,4,4),(4,4,4,0)),((5,5,5),(2,))),(((),(13,8,0,11,5,3,7,9,0,6,10,5,12,12,5,10,8,8,10,6,6,6,10,2,2)),((),(6,4,4,10,1,7,0,9,11,13,2,12,8)),((),(4,6,1,11,5,0,10,2,9,8,12,7)),((),(8,3,5,5,11,7,0,12,5,9,8,10,6,6,6,8,12,10,12,13,8,10,12,6))),(((),(8,12,12)),((),()),((1,4),(13,)),((),())),(((5,),()),((4,1),()),((),()),((4,),(2,4))),(((0,0),(0,0)),((5,),(3,7)),((0,),()),((0,),(0,0))),(((0,),(4,7,7,7)),((2,),(1,1)),((),(0,)),((),(7,7,2,2))),(((2,2),(2,2)),((),()),((),(3,9,7)),((2,),())),(((0,),(9,)),((1,1),()),((2,0,1,1),(4,2,1,11)),((0,),(9,9,10,9,11))),(((),()),((),()),((),()),((2,2),(7,11,11))),(((2,),(11,)),((3,),(4,)),((),(1,)),((),())),(((4,1),(9,11)),((4,5,0,0,0,1,3),(6,)),((5,4,3,3,0),(8,)),((),())),(((),(9,)),((3,2),()),((),()),((1,0),(0,0,13))),(((),(13,13,13)),((),(11,)),((),(13,)),((),(13,13,2))),(((),()),((5,2,0,0),()),((5,1,5,2,2,4,0,0,0,3,0),(3,3,6,5,6)),((),(4,))),(((0,),(4,11,4,4)),((),(10,0,0,3,9,3,13,5,6)),((3,),()),((),())),(((),()),((0,5),(8,8)),((),(10,8)),((0,0),(2,4))),(((2,),()),((),()),((),()),((4,),())),(((),()),((),(12,10)),((),()),((2,2),())),(((),(4,)),((2,3),(0,12)),((5,),(10,0,12,12,1)),((),())),(((),()),((),(2,1)),((),(2,)),((),())),(((4,18,4,1,0,3,16,15,4,17,16,20,14,20,4,19,16,21,14,14,20,18,16,18,18,2,2,14,5),(3,)),((14,17,15,2,20,21,2,2,5,19),()),((16,17,20,15,19,14,21,4,16,18,2),()),((19,14,4,1,16,15,18,17,20,3,14,20,18,14,4,16,21,20,18,20,16,16,14,15,5,0,0,4,3,4,15,17,18,2,15,2,17,17,19,19),(1,))),(((3,0,15,15,15,17,17,2,20,19,21,4,17,21,19,19),(1,5,0,0)),((16,),(5,7,3,2,2,6,0,11,0,12,10,9,5,0,8,6)),((2,2,2),(6,5,0,0,3,7,4,8,0,0,6,8,9)),((21,19,21),(3,4))),(((),(3,1,2,6,0,4,8,10,12,4,2,2,9,4,13,6,7,6,6,6,8,11,8,5,8,8,10)),((4,4,18,18,4,15,16,20,14,14,16,20,18,4,19,4,4,15,17,21,17,19,16,21),(10,12,5,2,4,8,4,9,2,6,4,7,2,9,7,13,11,10,13,11,13,8,12,4,11,4,9,7)),((14,16,14,18,18,20,4,20,19,14,15,15,17,21,17),(11,10,10,5,12,12,2,2,2,2,7,11,5,8,7,6,4,9,13,11,10,10,12,12,13,4,9,7,4,4,9,6,8,13)),((),(3,5,6,0,4,1,0,11,12,8,4,7,10,2,13,2,6,9,4,8,10,10,5,8,10,10,6,12,12,8,8,8,12,6,6,6,4,10,12))),(((),(12,12,12,12,7,10,10,6,12)),((14,14,18,18,20,20),()),((4,19,4,4,21,20,14,18,16,16,18,14,20,15,18),(6,11)),((),())),(((21,4,14,5,16,18,20),()),((14,20),()),((16,20,15,17),(4,)),((16,18,4,14,21,20),())),(((15,),(10,8,8,9,6,6,10,10,10,11,8)),((16,15,16,18,15,17,17,19,19,15,17,21,18),(13,6,6,8,8,10,10,10,8,4,12,12,6)),((17,15,19,21,17,21,14,19),(8,6,10,12,13)),((4,15,14,14,18,5,20,16,16),(7,11,9,12))),(((4,14,14,14,14,16,16,16,16,18,18,18,18,17,20,19,15),()),((21,14),(10,6,6,10,10,8,8,8,12)),((14,19),(6,6,8,8,8,8,10,10,12,10,10,6,12,12,12)),((14,20,16,18,18,20,17,15,19),(10,13))),(((21,17,20,20,20,16,14,14,20,20,16,18,20,14,19,18,18,16,21),(12,12,13)),((14,16,16,16,18,20,19,18,20,20,14,14,21,14,14,18,16,16,16,18,20,20,20,18),(12,12,12,6)),((18,16,21,20,18,20,16,14,14,14,16,16,18,18,14,18,18,20,20,20,16,20,16),()),((21,14,14,16,16,20,17,16,18,18,19,14,16,20,20,14,20,18,21,18),(6,6,8,8,12,12,10))))


class Flows:
    def __init__(self, r, section):
        self.r = r
        self.section = section
        place = lax.axis_index("dp")
        self.z, self.y = place // SHORT, lax.rem(place, SHORT)
        self.right, self.left = place + SHORT, place - SHORT
        self.beside = place + 1 - 2 * self.y
        self.flows = []
        self.done = {(z, s): [] for z in range(LONG) for s in range(2)}
        self.points = 0

    def hop(self, src, dst, n, j, target):
        r = self.r
        return pltpu.make_async_remote_copy(
            src_ref=src, dst_ref=dst, send_sem=r.flow_send.at[n, j], recv_sem=r.flow_recv.at[n, j],
            device_id={"dp": target}, device_id_type=MESH,
        )

    def reduce_events(self, n, part, slot):
        def up(k):
            return self.hop(slot(k - 1), slot(k - 1), n, k - 1, self.right)

        def down(k):
            return self.hop(slot(3 + k), slot(3 + k), n, 3 + k, self.left)

        def pass_on(copy, held, k):
            copy(k).wait_recv()
            add_rows(held, part(k))
            copy(k).start()

        def begin(z):
            if z == 0:
                for k in (3, 2, 1):
                    self.hop(part(k), slot(k - 1), n, k - 1, self.right).start()
            if z == 3:
                for k in (0, 1, 2):
                    self.hop(part(k), slot(3 + k), n, 3 + k, self.left).start()

        def passing(at_one, at_two):
            def event(z):
                if z in (1, 2):
                    way, k = (at_one, at_two)[z - 1]
                    pass_on(*((up, slot(k - 1)) if way > 0 else (down, slot(3 + k))), k)

            return event

        def close(z):
            got = []
            if z >= 1:
                up(z).wait_recv()
                got.append(slot(z - 1))
            if z <= 2:
                down(z).wait_recv()
                got.append(slot(3 + z))
            add_rows(part(z), *got)

        def sent(z):
            for k in ((1, 2, 3), (2, 3), (3,), ())[z]:
                up(k).wait_send()
            for k in ((), (0,), (0, 1), (0, 1, 2))[z]:
                down(k).wait_send()

        passes = [
            passing((1, 3), (-1, 0)), passing((1, 2), (-1, 1)), passing((-1, 0), (1, 3)),
        ]
        return begin, passes, close, sent

    def gather_events(self, n, own, out):
        def up(src, k, d):
            return self.hop(src, out(k), n, 7 + d, self.right)

        def down(src, k, d):
            return self.hop(src, out(k), n, 10 + d, self.left)

        def near(z):
            return pltpu.make_async_copy(own(z), out(z), self.r.flow_near.at[n])

        def starts(z, d, way):
            k = z - d * way
            src = own(z) if d == 0 else out(k)
            copies = []
            if d < LONG - 1 and 0 <= z + way < LONG:
                copies.append((up if way > 0 else down)(src, k, d))
            return copies

        def begin(z):
            near(z).start()
            for copy in starts(z, 0, 1) + starts(z, 0, -1):
                copy.start()

        def step(d, way):
            def event(z):
                k = z - d * way
                if 0 <= k < LONG:
                    (up if way > 0 else down)(out(k), k, d - 1).wait_recv()
                    for copy in starts(z, d, way):
                        copy.start()

            return event

        def sent(z):
            near(z).wait()
            for way in (1, -1):
                for d in range(LONG):
                    if 0 <= z - d * way < LONG:
                        for copy in starts(z, d, way):
                            copy.wait_send()

        return begin, [step(d, way) for d in (1, 2, 3) for way in (1, -1)], sent

    def long_first(self, n, data, out, slots, start, rows):
        c = rows // LONG

        def part(k):
            return data(start + k * c, c)

        def slot(j):
            return rows_of(slots, j * c, c)

        def beside(z):
            return self.hop(part(z), slot(6), n, 6, self.beside)

        begin, passes, close, reduce_sent = self.reduce_events(n, part, slot)
        gather, steps, gather_sent = self.gather_events(
            n, lambda z: slot(6), lambda k: out(start + k * c, c)
        )

        def middle(z):
            close(z)
            beside(z).start()

        def turn(z):
            beside(z).wait_recv()
            add_rows(slot(6), part(z))
            gather(z)

        def sent(z):
            reduce_sent(z)
            beside(z).wait_send()
            gather_sent(z)

        return [begin, *passes, middle, turn, *steps], sent

    def short_first(self, n, data, out, slots, start, rows):
        half = rows // SHORT

        def mine(y):
            return data(start + y * half, half)

        def place(y):
            return out(start + y * half, half)

        def slot(j):
            return rows_of(slots, j * half, half)

        def beside():
            return self.hop(mine(1 - self.y), slot(0), n, 6, self.beside)

        inward = (self.right, self.right, self.left, self.left)
        outward = (None, self.left, self.right, None)

        def lean(z):
            middle = 1 if z in (1, 2) else 0
            return self.hop(mine(self.y), slot(1 + middle), n, middle, inward[z])

        def settle(z):
            src = slot(0) if z in (1, 2) else place(self.y)
            return self.hop(src, place(self.y), n, 7, outward[z])

        def near(z):
            return pltpu.make_async_copy(slot(0), place(self.y), self.r.flow_near.at[n])

        def spread(z):
            src = slot(0) if z in (1, 2) else place(self.y)
            return self.hop(src, place(self.y), n, 13, self.beside)

        def first(z):
            beside().start()

        def turn(z):
            beside().wait_recv()
            add_rows(mine(self.y), slot(0))
            if z in (0, 3):
                lean(z).start()

        def pair(z):
            if z in (1, 2):
                self.hop(slot(1), slot(1), n, 0, inward[z]).wait_recv()
                add_rows(mine(self.y), slot(1))
                lean(z).start()

        def close(z):
            if z in (1, 2):
                lean(z).wait_recv()
                sum_rows(slot(0), mine(self.y), slot(2))
                near(z).start()
                settle(z).start()
                spread(z).start()

        def outer(z):
            if z in (0, 3):
                self.hop(place(self.y), place(self.y), n, 7, inward[z]).wait_recv()
                spread(z).start()

        def end(z):
            there = place(1 - self.y)
            self.hop(there, there, n, 13, self.beside).wait_recv()

        def sent(z):
            beside().wait_send()
            lean(z).wait_send()
            spread(z).wait_send()
            if z in (1, 2):
                settle(z).wait_send()
                near(z).wait()

        return [first, turn, pair, close, outer, end], sent

    def open(self, only, *flows):
        for events, sent in flows:
            self.flows.append((only, events, sent))
            for counts in self.done.values():
                counts.append(0)

    def advance(self, z, s, todo):
        def body():
            for n in todo:
                self.flows[n][1][self.done[z, s][n]](z)
                self.done[z, s][n] += 1

        return body

    def point(self):
        plan = PLAN[self.points] if self.points < len(PLAN) else ()
        self.points += 1
        for z, lists in enumerate(plan):
            first, second = self.done[z, 0], self.done[z, 1]
            if lists[0] == lists[1] and all(first[n] == second[n] for n in lists[0]):
                if lists[0]:
                    pl.when(self.z == z)(self.advance(z, 0, lists[0]))
                    for n in lists[0]:
                        second[n] = first[n]
                continue
            for s in range(2):
                here = jnp.logical_and(self.z == z, self.section == s)
                pl.when(here)(self.advance(z, s, lists[s]))

    def drain(self):
        for (z, s), counts in self.done.items():

            def body(z=z, s=s, counts=counts):
                mine = [n for n, flow in enumerate(self.flows) if flow[0] in (None, s)]
                longest = max(len(self.flows[n][1]) for n in mine)
                for k in range(longest):
                    for n in mine:
                        if counts[n] <= k < len(self.flows[n][1]):
                            self.flows[n][1][k](z)
                for n in mine:
                    self.flows[n][2](z)

            pl.when(jnp.logical_and(self.z == z, self.section == s))(body)


def on_grid():
    return lax.axis_size("dp") == LONG * SHORT


def backward_kernel(r):
    section, tensor = lax.axis_index("section"), lax.axis_index("tensor")
    own_count, patches, width = r.normed.shape
    byte_count = r.ids.shape[1]
    columns = r.w_out.shape[0]
    hidden = r.down.shape[0]
    heads = columns // HD
    half = width // 2
    half_bytes = byte_count // 2
    summing = on_grid()
    loads = {}

    def load(name, src, dst, *sem):
        copy = pltpu.make_async_copy(src, dst, r.load_sem.at[sem])
        copy.start()
        loads[name] = copy

    held_names = ("inner", "grad_in", "inner_part", "normed", "patch_norms", "gain")
    for n, name in enumerate(held_names):
        load(name, getattr(r, "in_" + name), getattr(r, name), n)
    load("w_in", r.in_w_in.at[1], r.w_in, 6)
    load("w_out", r.in_w_out.at[1], r.w_out, 7)
    others = [("section", 1 - section), ("tensor", 1 - tensor)]
    flows = Flows(r, section) if summing else None
    if summing:
        greet_grid(flows, others)
    else:
        greet(others)

    def cross(src, dst, i, sem):
        return remote(
            src, dst, r.cross_send.at[sem, i], r.cross_recv.at[sem, i], "tensor", 1 - tensor
        )

    def inner_exchange(i):
        return cross(r.in_inner_part.at[i], r.inner_got.at[i], i, 0)

    def normed_exchange(i):
        return cross(r.normed_part.at[i], r.normed_got.at[i], i, 1)

    def query_exchange(i):
        return cross(r.inner_part.at[i], r.inner_got.at[i], i, 2)

    def source_exchange(i):
        theirs = block_at(1 - tensor, half_bytes)
        return cross(r.source_part.at[i, theirs, :], r.source_got.at[i], i, 3)

    def latent_exchange(i):
        return cross(r.in_latent_send.at[i], r.latent_got.at[i], i, 4)

    for i in range(own_count):
        inner_exchange(i).start()
    def give(n, src, dst):
        return remote(src, dst, r.give_send.at[n], r.give_recv.at[n], "section", 1 - section)

    def point():
        if summing:
            flows.point()

    def summed(n, data, out, only=None):
        if summing:
            long_slots, short_slots, rows, cut = r.slots[n]
            flows.open(
                only,
                flows.long_first(2 * n, data, out, long_slots, 0, cut),
                flows.short_first(2 * n + 1, data, out, short_slots, cut, rows - cut),
            )

    def up_half(ref, n):
        return ref.at[pl.ds(n * half, half), :]

    def whole(view):
        return lambda start, rows: rows_of(view(), start, rows)

    @functools.partial(
        pl.run_scoped,
        hidden_all=pltpu.VMEM((own_count, patches, hidden), b16),
        gate_all=pltpu.VMEM((own_count, patches, hidden), b16),
        up_all=pltpu.VMEM((own_count, patches, hidden), b16),
        down_give=pltpu.VMEM((hidden, half), b16),
    )
    def _(hidden_all, gate_all, up_all, down_give):
        parts = {"hidden": hidden_all, "gate_grad": gate_all, "up_grad": up_all}
        for n, (name, ref) in enumerate(parts.items()):
            load(name, getattr(r, "in_" + name), ref, n + 8)
        for name in (*parts, "inner", "grad_in"):
            loads[name].wait()

        def down_grad(target, side):
            upstream = flat(r.grad_in, block_at(side, half))

            def tile(cols):
                target[cols, :] = dot_lt(flat(hidden_all, cols), upstream).astype(b16)

            each_block(hidden, tile)
            if hidden % BLOCK:
                tile(pl.ds(hidden - hidden % BLOCK, hidden % BLOCK))

        def up_grad(target, ref, side):
            upstream = flat(ref, slice(None))

            def tile(rows):
                cols = pl.ds(pl.multiple_of(side * half + rows.start, BLOCK), BLOCK)
                target[rows, :] = dot_lt(flat(r.inner, cols), upstream).astype(b16)

            each_block(half, tile)

        used = pl.ds(0, hidden)
        give_rows = [pl.ds(0, half), pl.ds(half, half)]
        gate_give, up_give = [r.attn_in_part.at[1, rows, used] for rows in give_rows]
        gate_got, up_got = [r.big_got.at[rows, used] for rows in give_rows]
        gate_own, up_own = [r.up.at[rows, :] for rows in give_rows]
        gifts = [
            give(0, down_give, r.down_got), give(1, gate_give, gate_got), give(2, up_give, up_got)
        ]
        other = 1 - section
        down_grad(down_give, other)
        gifts[0].start()
        down_grad(r.down, section)
        up_grad(gate_give, gate_all, other)
        gifts[1].start()
        gifts[0].wait()
        add_rows(r.down, r.down_got)
        summed(0, whole(lambda: r.down), whole(lambda: r.down_sum))
        point()
        up_grad(gate_own, gate_all, section)
        up_grad(up_give, up_all, other)
        gifts[2].start()
        gifts[1].wait()
        add_rows(gate_own, gate_got)
        summed(1, whole(lambda: up_half(r.up, 0)), whole(lambda: up_half(r.up_sum, 0)))
        point()
        up_grad(up_own, up_all, section)
        gifts[2].wait()
        add_rows(up_own, up_got)
        summed(2, whole(lambda: up_half(r.up, 1)), whole(lambda: up_half(r.up_sum, 1)))
        point()
        pl.semaphore_signal(
            r.free_sem, inc=1, device_id={"section": other}, device_id_type=MESH
        )

    def gifts_of(layer):
        return [
            give(3, r.attn_in_part.at[layer], r.big_got),
            give(4, r.attn_out_part.at[layer], r.attn_out_got),
        ]

    def hand_over(layer):
        @pl.when(section != layer)
        def _():
            pl.semaphore_wait(r.free_sem, 1)
            for gift in gifts_of(layer):
                gift.start()

    def take_over(layer):
        @pl.when(section != layer)
        def _():
            for gift in gifts_of(layer):
                gift.wait_send()

        @pl.when(section == layer)
        def _():
            for gift in gifts_of(layer):
                gift.wait_recv()
            add_rows(r.attn_out_part.at[layer], r.attn_out_got)
            add_rows(r.attn_in_part.at[layer], r.big_got)

    def sum_layer(layer, which):
        def columns_of(j):
            return whole(lambda: r.attn_in_part.at[layer, :, pl.ds(j * columns, columns)])

        if which == 3:
            summed(
                3, whole(lambda: r.attn_out_part.at[layer]), whole(lambda: r.attn_out_sum), layer
            )
        else:
            summed(4 + which, columns_of(which), whole(lambda: r.attn_in_sum.at[which]), layer)

    first_gain, second_gain = r.gain.at[0], r.gain.at[1]

    def back_through(normed, gain_row, scale, upstream):
        unit = normed.astype(f32) / gain_row
        scaled = upstream * gain_row
        mean = jnp.mean(unit * scaled, axis=-1, keepdims=True)
        return (scaled - unit * mean) * scale, unit

    @functools.partial(
        pl.run_scoped,
        q2=pltpu.VMEM((own_count, patches, columns), b16),
        k2=pltpu.VMEM((own_count, patches, columns), b16),
        v2=pltpu.VMEM((own_count, patches, columns), b16),
        totals=pltpu.VMEM((own_count, patches, LANES), f32),
        mixed2=pltpu.VMEM((own_count, patches, columns), b16),
        second_grads=pltpu.VMEM((own_count, patches, 3 * columns), b16),
        mixed_grads=pltpu.VMEM((patches, columns), b16),
    )
    def _(q2, k2, v2, totals, mixed2, second_grads, mixed_grads):
        parts = {"q2": q2, "k2": k2, "v2": v2, "totals": totals, "mixed2": mixed2}
        for n, (name, ref) in enumerate(parts.items()):
            load(name, getattr(r, "in_" + name), ref, n + 11)
        for name in (*held_names[2:], "w_in", "w_out", *parts):
            loads[name].wait()
        r.gain_sum[...] = jnp.zeros_like(r.gain_sum)
        allowed = iota((patches, patches), 1) <= iota((patches, patches), 0)
        for i in range(own_count):
            inner_exchange(i).wait()
            own_part = r.inner_part[i].astype(f32)
            back, unit = back_through(
                r.inner[i], second_gain[1:2, :], r.patch_norms[i, :, 2:3],
                own_part + r.inner_got[i].astype(f32),
            )
            r.gain_sum[3:4, :] += jnp.sum(unit * own_part, axis=0, keepdims=True)
            branch = (r.grad_in[i].astype(f32) + back).astype(b16)
            r.branch[i] = branch
            mixed_grads[...] = dot_rt(branch, r.w_out[...]).astype(b16)
            point()

            mixed_grad = mixed_grads[...]
            outs = [[], [], []]
            for head in range(heads):
                own = slice(head * HD, (head + 1) * HD)
                query, key, value = q2[i, :, own], k2[i, :, own], v2[i, :, own]
                upper = mixed_grad[:, own]
                scores = jnp.where(allowed, dot_rt(query, key) * SCALE, NEGATIVE)
                probs = jnp.exp(scores - totals[i, :, head : head + 1])
                prob_grad = dot_rt(upper, value)
                delta = jnp.sum(probs * prob_grad, axis=-1, keepdims=True)
                score_grad = (probs * (prob_grad - delta)).astype(b16)
                outs[0].append(dot(score_grad, key) * SCALE)
                outs[1].append(dot_lt(score_grad, query) * SCALE)
                outs[2].append(dot_lt(probs.astype(b16), upper))
            grads = jnp.concatenate(outs[0] + outs[1] + outs[2], axis=1).astype(b16)
            second_grads[i] = grads
            point()
            r.normed_part[i] = dot_rt(grads, r.w_in[...]).astype(b16)
            normed_exchange(i).start()
            point()

        def outer(target, rows_ref, upstream, tiles):
            @pl.loop(0, tiles)
            def _(t):
                cols = block_at(t)
                target[cols, :] = dot_lt(flat(rows_ref, cols), upstream).astype(b16)

        outer(r.attn_in_part.at[1], r.normed, flat(second_grads, slice(None)), width // BLOCK)
        point()
        outer(r.attn_out_part.at[1], mixed2, flat(r.branch, slice(None)), columns // BLOCK)
        hand_over(1)
        point()

    heads_in, heads_out = head_masks(columns)

    def first_layer(i, scoped):
        seq = section * own_count + i
        s = types.SimpleNamespace(**scoped)
        copies = {}
        kinds = names(q1=1, v1=1, raised=1, inverse=1, mixed1=1, source_in=1, query_in=1)
        for n, name in enumerate(kinds):
            copy = pltpu.make_async_copy(
                getattr(r, "in_" + name).at[i], getattr(s, name), r.first_sem.at[n]
            )
            copy.start()
            copies[name] = copy
        normed_exchange(i).wait()
        own_part = r.normed_part[i].astype(f32)
        back, unit = back_through(
            r.normed[i], second_gain[0:1, :], r.patch_norms[i, :, 1:2],
            own_part + r.normed_got[i].astype(f32),
        )
        r.gain_sum[2:3, :] += jnp.sum(unit * own_part, axis=0, keepdims=True)
        branch = (r.branch[i].astype(f32) + back).astype(b16)
        r.branch[i] = branch
        s.mixed_grad[...] = dot_rt(branch, r.w_out[...]).astype(b16)
        s.q_sum[...] = jnp.zeros_like(s.q_sum)
        s.delta_sum[...] = jnp.zeros_like(s.delta_sum)
        for copy in copies.values():
            copy.wait()
        point()
        if i == 0:
            take_over(1)
            for which in (3, 0, 1, 2):
                sum_layer(1, which)
            point()
        inverse = s.inverse[...]
        inverse_high = inverse.astype(b16)
        inverse_low = (inverse - inverse_high.astype(f32)).astype(b16)

        def value_side(rows):
            members = members_of(r, seq, rows, patches)
            spread = dot_lt(members, s.mixed_grad[...])
            scale = dot_lt(members, inverse_high) + dot_lt(members, inverse_low)
            probs = s.raised[rows, :].astype(f32) * scale
            s.probs[rows, :] = probs
            s.dkv[rows, columns:] = (dot(probs.astype(b16), heads_out) * spread).astype(b16)
            prob_grad = dot((spread * s.v1[rows, :].astype(f32)).astype(b16), heads_in)
            s.prob_grad[rows, :] = prob_grad
            product = probs * prob_grad
            high = product.astype(b16)
            low = (product - high.astype(f32)).astype(b16)
            s.delta_sum[...] += dot(members, high) + dot(members, low)

        for t in range(byte_count // WIDE):
            value_side(pl.ds(t * WIDE, WIDE))
            point()
        keys = pltpu.make_async_copy(r.in_k1.at[i], s.v1, r.first_sem.at[7])
        keys.start()
        delta = s.delta_sum[...]
        delta_high = delta.astype(b16)
        delta_low = (delta - delta_high.astype(f32)).astype(b16)

        def key_side(rows):
            members = members_of(r, seq, rows, patches)
            shift = dot_lt(members, delta_high) + dot_lt(members, delta_low)
            score_grad = (s.probs[rows, :] * (s.prob_grad[rows, :] - shift)).astype(b16)
            spread = dot(score_grad, heads_out)
            s.dkv[rows, :columns] = (spread * dot_lt(members, s.q1[...]) * SCALE).astype(b16)
            s.q_sum[...] += dot(members, (spread * s.v1[rows, :].astype(f32)).astype(b16))
            source = dot_rt(s.dkv[rows, :], r.w_in[:, columns:])
            r.source_part[i, rows, :] = source.astype(b16)
            unit_block = s.source_in[rows, :].astype(f32)
            r.gain_sum[1:2, :] += (
                jnp.sum(unit_block * source, axis=0, keepdims=True) / first_gain[1:2, :]
            )

        keys.wait()
        for t in range(byte_count // WIDE):
            for u in range(WIDE // BLOCK):
                key_side(pl.ds(t * WIDE + u * BLOCK, BLOCK))
            point()
        source_exchange(i).start()
        q_grad = (s.q_sum[...] * SCALE).astype(b16)
        query = dot_rt(q_grad, r.w_in[:, :columns])
        r.inner_part[i] = query.astype(b16)
        query_exchange(i).start()
        unit_pool = s.query_in[...].astype(f32)
        r.gain_sum[0:1, :] += (
            jnp.sum(unit_pool * query, axis=0, keepdims=True) / first_gain[0:1, :]
        )
        point()

        def add_to(target, rows, cols, value):
            if i:
                value = target[rows, cols].astype(f32) + value
            target[rows, cols] = value.astype(b16)

        for half_t in range(2):

            @pl.loop(0, half // BLOCK)
            def _(t, half_t=half_t):
                cols = pl.ds(pl.multiple_of(half_t * half + t * BLOCK, BLOCK), BLOCK)
                source = s.source_in[:, cols]
                target = r.attn_in_part.at[0]
                add_to(target, cols, slice(0, columns), dot_lt(s.query_in[:, cols], q_grad))
                add_to(target, cols, slice(columns, 3 * columns), dot_lt(source, s.dkv[...]))

            point()

        @pl.loop(0, columns // BLOCK)
        def _(t):
            cols = block_at(t)
            add_to(
                r.attn_out_part.at[0], cols, slice(None), dot_lt(s.mixed1[:, cols], branch)
            )

        point()

    def last_parts(s):
        outs = []

        own_rows = block_at(tensor, half_bytes)
        cols_keep, cols_give = block_at(section, half), block_at(1 - section, half)
        for i in range(own_count):
            seq = section * own_count + i
            finals = [
                pltpu.make_async_copy(
                    r.in_source_in.at[i, own_rows, :], s.source_in, r.first_sem.at[0]
                ),
                pltpu.make_async_copy(
                    r.in_byte_norms.at[i, own_rows, :], s.byte_norms, r.first_sem.at[1]
                ),
                pltpu.make_async_copy(r.in_query_in.at[i], s.query_in, r.first_sem.at[2]),
            ]
            for copy in finals:
                copy.start()
            query_exchange(i).wait()
            source_exchange(i).wait()
            for copy in finals:
                copy.wait()
            back, _ = back_through(
                s.query_in[...], first_gain[0:1, :], r.patch_norms[i, :, 0:1],
                r.inner_part[i].astype(f32) + r.inner_got[i].astype(f32),
            )
            counts = jnp.sum(
                jnp.where(iota((patches, byte_count), 0) == r.ids[pl.ds(seq, 1), :], 1.0, 0.0),
                axis=1, keepdims=True,
            )
            pool_grad = (r.branch[i].astype(f32) + back) / jnp.maximum(counts, 1.0)
            high = pool_grad.astype(b16)
            s.pool_high[...] = high
            s.pool_low[...] = (pool_grad - high.astype(f32)).astype(b16)

            @pl.loop(0, half_bytes // BLOCK)
            def _(t, i=i, seq=seq):
                rows = block_at(t)
                place = pl.ds(pl.multiple_of(tensor * half_bytes + t * BLOCK, BLOCK), BLOCK)
                members = members_of(r, seq, place, patches)
                spread = dot_lt(members, s.pool_high[...]) + dot_lt(members, s.pool_low[...])
                part = r.source_part[i, place, :].astype(f32)
                own, _ = back_through(
                    s.source_in[rows, :], first_gain[1:2, :], s.byte_norms[rows, 0:1],
                    part + r.source_got[i, rows, :].astype(f32),
                )
                r.source_got[i, rows, :] = (own + spread).astype(b16)

            near = pltpu.make_async_copy(
                r.source_got.at[i, :, cols_keep], r.byte_grad.at[seq], r.out_sem.at[1, i]
            )
            far = remote(
                r.source_got.at[i, :, cols_give], r.byte_grad.at[seq],
                r.out_send.at[1, i], r.out_recv.at[1, i], "section", 1 - section,
            )
            near.start()
            far.start()
            outs += [near, far]
            point()

        half_rows = patches // 2
        rows_keep, rows_give = block_at(section, half_rows), block_at(1 - section, half_rows)
        for i in range(own_count):
            seq = section * own_count + i
            s_load = pltpu.make_async_copy(r.in_latent_own.at[i], s.latent.at[i], r.first_sem.at[i])
            s_load.start()
            s_load.wait()
            latent_exchange(i).wait()
            last = jnp.max(r.ids[pl.ds(seq, 1), :], axis=1, keepdims=True)
            valid = iota((patches, 1), 0) <= last
            values = s.latent[i].astype(f32) + r.latent_got[i].astype(f32)
            s.latent[i] = jnp.where(valid, values, 0.0).astype(b16)
            near = pltpu.make_async_copy(
                s.latent.at[i, rows_keep, :], r.latents.at[seq], r.out_sem.at[0, i]
            )
            far = remote(
                s.latent.at[i, rows_give, :], r.latents.at[seq],
                r.out_send.at[0, i], r.out_recv.at[0, i], "section", 1 - section,
            )
            near.start()
            far.start()
            outs += [near, far]
        for copy in outs:
            copy.wait()

    load("w_in", r.in_w_in.at[0], r.w_in, 6)
    load("w_out", r.in_w_out.at[0], r.w_out, 7)
    loads["w_in"].wait()
    loads["w_out"].wait()
    one = dict(
        source_in=pltpu.VMEM((byte_count, width), b16),
        v1=pltpu.VMEM((byte_count, columns), b16),
        dkv=pltpu.VMEM((byte_count, 2 * columns), b16),
        probs=pltpu.VMEM((byte_count, LANES), f32),
        prob_grad=pltpu.VMEM((byte_count, LANES), f32),
        raised=pltpu.VMEM((byte_count, LANES), b16),
        inverse=pltpu.VMEM((patches, LANES), f32),
        q1=pltpu.VMEM((patches, columns), b16),
        mixed1=pltpu.VMEM((patches, columns), b16),
        query_in=pltpu.VMEM((patches, width), b16),
        mixed_grad=pltpu.VMEM((patches, columns), b16),
        q_sum=pltpu.VMEM((patches, columns), f32),
        delta_sum=pltpu.VMEM((patches, LANES), f32),
    )

    @functools.partial(pl.run_scoped, **one)
    def _(**scoped):
        for i in range(own_count):
            first_layer(i, scoped)

    hand_over(0)
    for i in range(own_count):
        latent_exchange(i).start()
    point()
    take_over(0)
    for which in (3, 0, 1, 2):
        sum_layer(0, which)
    point()
    gains = Gains(r, section, tensor, flows) if summing else None
    if summing:
        gains.tick()
    last = dict(
        source_in=pltpu.VMEM((half_bytes, width), b16),
        byte_norms=pltpu.VMEM((half_bytes, LANES), f32),
        query_in=pltpu.VMEM((patches, width), b16),
        pool_high=pltpu.VMEM((patches, width), b16),
        pool_low=pltpu.VMEM((patches, width), b16),
        latent=pltpu.VMEM((own_count, patches, columns), b16),
    )

    @functools.partial(pl.run_scoped, **last)
    def _(**scoped):
        last_parts(types.SimpleNamespace(**scoped))

    if summing:
        while gains.steps:
            gains.tick()
            point()
        flows.drain()
    ends = [pltpu.make_async_copy(r.gain_sum, r.gain_out, r.end_sem.at[4])]
    if not summing:
        ends += [
            pltpu.make_async_copy(r.up, r.up_sum, r.end_sem.at[0]),
            pltpu.make_async_copy(r.down, r.down_sum, r.end_sem.at[1]),
            pltpu.make_async_copy(r.attn_out_part.at[section], r.attn_out_sum, r.end_sem.at[3]),
        ]
        ends += [
            pltpu.make_async_copy(
                r.attn_in_part.at[section, :, pl.ds(j * columns, columns)], r.attn_in_sum.at[j],
                r.end_sem.at[5 + j],
            )
            for j in range(3)
        ]
    for copy in ends:
        copy.start()
    for copy in ends:
        copy.wait()


class Gains:
    def __init__(self, r, section, tensor, flows):
        self.r = r
        z = flows.z
        place = lax.axis_index("dp")
        near = place + SHORT * (1 - 2 * lax.rem(z, 2))
        far = place + 2 * SHORT * (1 - 2 * (z // 2))
        self.targets = [
            {"tensor": 1 - tensor}, {"section": 1 - section}, {"dp": flows.beside},
            {"dp": near}, {"dp": far},
        ]
        self.steps = list(range(len(self.targets) + 1))

    def copy(self, n):
        r = self.r
        return pltpu.make_async_remote_copy(
            src_ref=r.gain_held.at[n], dst_ref=r.gain_got.at[n], send_sem=r.gain_send.at[n],
            recv_sem=r.gain_recv.at[n], device_id=self.targets[n], device_id_type=MESH,
        )

    def tick(self):
        if not self.steps:
            return
        r, n = self.r, self.steps.pop(0)
        if n == 0:
            r.gain_held[0] = r.gain_sum[...]
        else:
            self.copy(n - 1).wait()
            value = r.gain_held[n - 1] + r.gain_got[n - 1]
            if n < len(self.targets):
                r.gain_held[n] = value
            else:
                r.gain_sum[...] = value
        if n < len(self.targets):
            self.copy(n).start()


def greet_grid(flows, others):
    barrier = pltpu.get_barrier_semaphore()

    def signal(place):
        pl.semaphore_signal(barrier, inc=1, device_id=place, device_id_type=MESH)

    for axis, index in others:
        signal({axis: index})
    signal({"dp": flows.beside})
    signal({"dp": lax.axis_index("dp") + 2 * SHORT * (1 - 2 * (flows.z // 2))})
    pl.when(flows.z < LONG - 1)(lambda: signal({"dp": flows.right}))
    pl.when(flows.z > 0)(lambda: signal({"dp": flows.left}))
    inner = jnp.logical_and(flows.z > 0, flows.z < LONG - 1)
    pl.semaphore_wait(barrier, jnp.where(inner, len(others) + 4, len(others) + 3))


def backward(kept, patch_ids):
    own, patches, width = kept["normed"].shape
    sequences, byte_count = patch_ids.shape
    columns = kept["q1"].shape[-1]
    hidden = kept["hidden"].shape[-1]
    half, half_bytes = width // 2, byte_count // 2
    sems = pltpu.SemaphoreType.DMA
    vmem = pltpu.VMEM
    rows16 = vmem((own, patches, width), b16)
    scratch = dict(
        inner=rows16,
        grad_in=rows16,
        inner_part=rows16,
        inner_got=rows16,
        normed=rows16,
        patch_norms=vmem((own, patches, LANES), f32),
        branch=rows16,
        normed_part=rows16,
        normed_got=rows16,
        source_part=vmem((own, byte_count, width), b16),
        source_got=vmem((own, half_bytes, width), b16),
        latent_got=vmem((own, patches, columns), b16),
        w_in=vmem((width, 3 * columns), b16),
        w_out=vmem((columns, width), b16),
        gain=vmem((2, 2, width), f32),
        gain_sum=vmem((4, width), f32),
        down_got=vmem((hidden, half), b16),
        down=vmem((hidden, half), b16),
        up=vmem((width, hidden), b16),
        attn_in_part=vmem((2, width, 3 * columns), b16),
        attn_out_part=vmem((2, columns, width), b16),
        big_got=vmem((width, 3 * columns), b16),
        attn_out_got=vmem((columns, width), b16),
        load_sem=sems((16,)),
        first_sem=sems((8,)),
        cross_send=sems((5, own)),
        cross_recv=sems((5, own)),
        give_send=sems((5,)),
        give_recv=sems((5,)),
        out_sem=sems((2, own)),
        out_send=sems((2, own)),
        out_recv=sems((2, own)),
        end_sem=sems((8,)),
        free_sem=pltpu.SemaphoreType.REGULAR,
    )
    slots = []
    if on_grid():
        arrays = [(hidden, half, 512), (half, hidden, 256), (half, hidden, 128)]
        arrays += [(columns, width, 128)] + [(width, columns, 256)] * 3
        for n, (rows, cols, cut) in enumerate(arrays):
            slots.append((f"l{n}", f"s{n}", rows, cut))
            scratch[f"l{n}"] = vmem((7 * cut // LONG, cols), b16)
            scratch[f"s{n}"] = vmem((3 * (rows - cut) // SHORT, cols), b16)
        scratch |= dict(
            flow_send=sems((2 * len(arrays), 17)),
            flow_recv=sems((2 * len(arrays), 17)),
            flow_near=sems((2 * len(arrays),)),
            gain_held=vmem((5, 4, width), f32),
            gain_got=vmem((5, 4, width), f32),
            gain_send=sems((5,)),
            gain_recv=sems((5,)),
        )
    ins = [("ids", patch_ids, True)]
    ins += [("in_" + name, kept[name], False) for name in (*KEPT, *LAYERS)]
    outs = [
        ("latents", shape((sequences, patches // 2, columns), b16)),
        ("byte_grad", shape((sequences, half_bytes, half), b16)),
        ("attn_in_sum", shape((3, width, columns), b16)),
        ("attn_out_sum", shape((columns, width), b16)),
        ("gain_out", shape((4, width), f32)),
        ("up_sum", shape((width, hidden), b16)),
        ("down_sum", shape((hidden, half), b16)),
    ]

    def kernel(r):
        r.slots = [
            (getattr(r, long), getattr(r, short), rows, cut) for long, short, rows, cut in slots
        ]
        backward_kernel(r)

    return named_call(kernel, ins, outs, scratch, collective_id=1)


def swap(values, axis):
    return lax.ppermute(values, axis, [(0, 1), (1, 0)])


def sum_small(values):
    values = values + swap(values, "tensor")
    values = values + swap(values, "section")
    return lax.psum(values, "dp")


def per_device(byte_states, patch_ids, attn_in, attn_out, gains, ffn_in, ffn_out, latent_grad):
    width = byte_states.shape[-1]
    hidden = ffn_out.shape[0]
    half = width // 2
    is_first = lax.axis_index("section") == 0
    kept = forward(
        byte_states, patch_ids, attn_in, attn_out, gains, ffn_in.transpose(1, 0, 2), ffn_out,
        latent_grad,
    )
    got = backward(kept, patch_ids)
    sums = [got[name] for name in ("down_sum", "up_sum", "attn_in_sum", "attn_out_sum")]
    if not on_grid():
        sums = [lax.psum(value, "dp") for value in sums]
    down, up, in_sum, out_sum = [value.astype(f32) for value in sums]
    gain_sum = got["gain_out"] if on_grid() else sum_small(got["gain_out"])
    gain_out = jnp.where(is_first, gain_sum[0:2], gain_sum[2:4])
    up_out = up.reshape(2, half, hidden).transpose(1, 0, 2)
    return (
        got["latents"], got["byte_grad"], in_sum[None], out_sum[None], gain_out[None], up_out, down
    )


def solution(mesh):
    return jax.shard_map(
        per_device,
        mesh=mesh,
        in_specs=(
            P("dp", None, None),
            P("dp", None),
            P("section", None, None, "tensor"),
            P("section", "tensor", None),
            P("section", None, None),
            P(None, None, "tensor"),
            P("tensor", None),
            P("dp", None, None),
        ),
        out_specs=(
            P("dp", "section", "tensor"),
            P("dp", "tensor", "section"),
            P("section", None, None, "tensor"),
            P("section", "tensor", None),
            P("section", None, None),
            P("section", None, "tensor"),
            P("tensor", "section"),
        ),
        check_vma=False,
    )
```

```python
import functools
import types

import jax
import jax.numpy as jnp
from jax import lax
from jax.experimental import pallas as pl
from jax.experimental.pallas import tpu as pltpu
from jax.sharding import PartitionSpec as P

HD = 64
LANES = 128
BLOCK = 256
WIDE = 512
EPSILON = 1e-05
NEGATIVE = -1000000000.0
SCALE = HD ** (-0.5)
VMEM_BYTES = 63 * 1024 * 1024

f32 = jnp.float32
b16 = jnp.bfloat16


def dot(a, b):
    return jnp.dot(a, b, preferred_element_type=f32)


def dot_rt(a, b):
    return lax.dot_general(a, b, (((1,), (1,)), ((), ())), preferred_element_type=f32)


def dot_lt(a, b):
    return lax.dot_general(a, b, (((0,), (0,)), ((), ())), preferred_element_type=f32)


def inverse_rms(values):
    return lax.rsqrt(jnp.mean(values * values, axis=-1, keepdims=True) + EPSILON)


def iota(shape, dim):
    return lax.broadcasted_iota(jnp.int32, shape, dim)


def one_hot(condition):
    return jnp.where(condition, 1.0, 0.0).astype(b16)


def segment_max(values, ids):
    width = values.shape[1]
    lane = iota(ids.shape, 1)
    lowest = -3.0e38
    ahead, behind = values, values
    step = 1
    while step < width:
        left, right = step, width - step
        same_left = jnp.logical_and(pltpu.roll(ids, left, axis=1) == ids, lane >= step)
        same_right = jnp.logical_and(pltpu.roll(ids, right, axis=1) == ids, lane < right)
        ahead = jnp.maximum(ahead, jnp.where(same_left, pltpu.roll(ahead, left, axis=1), lowest))
        behind = jnp.maximum(
            behind, jnp.where(same_right, pltpu.roll(behind, right, axis=1), lowest)
        )
        step *= 2
    return jnp.maximum(ahead, behind)


def head_masks(width):
    heads_in = one_hot(iota((width, LANES), 0) // HD == iota((width, LANES), 1))
    heads_out = one_hot(iota((LANES, width), 1) // HD == iota((LANES, width), 0))
    return heads_in, heads_out


def split_dot(values, matrix):
    high = values.astype(b16)
    low = (values - high.astype(f32)).astype(b16)
    return dot(high, matrix) + dot(low, matrix)


def block_at(index, size=BLOCK):
    return pl.ds(pl.multiple_of(index * size, size), size)


def each_block(count, body, size=BLOCK):
    @pl.loop(0, count // size)
    def _(index):
        body(block_at(index, size))


MESH = pl.DeviceIdType.MESH


def remote(src, dst, send, recv, axis, index):
    return pltpu.make_async_remote_copy(
        src_ref=src, dst_ref=dst, send_sem=send, recv_sem=recv,
        device_id={axis: index}, device_id_type=MESH,
    )


def greet(places):
    barrier = pltpu.get_barrier_semaphore()
    for axis, index in places:
        pl.semaphore_signal(barrier, inc=1, device_id={axis: index}, device_id_type=MESH)
    pl.semaphore_wait(barrier, len(places))


def exchange_layer(r, section, tensor):
    columns = r.attn_in.shape[3]
    copies = []
    for n, (src, dst) in enumerate(
        [
            (r.attn_in.at[0, j], r.w_in.at[section, :, pl.ds(j * columns, columns)])
            for j in (1, 2, 0)
        ]
        + [
            (r.attn_out.at[0], r.w_full.at[section, block_at(tensor, columns), :]),
            (r.gains.at[0], r.gain.at[section]),
        ]
    ):
        near = pltpu.make_async_copy(src, dst, r.near_sem.at[n])
        far = remote(src, dst, r.far_send.at[n], r.far_recv.at[n], "section", 1 - section)
        near.start()
        far.start()
        copies.append((near, far))
    return copies


def arrived(copies):
    for near, far in copies:
        near.wait()
        far.wait()


def members_of(r, seq, rows, patches):
    return one_hot(iota((patches, rows.size), 0) == r.ids[pl.ds(seq, 1), rows])


def names(**kinds):
    return tuple(kinds)


FIRST_KEPT = names(query_in=1, source_in=1, byte_norms=1)
CROSS_KEPT = names(q1=1, k1=1, v1=1, raised=1, inverse=1, mixed1=1)
SECOND_KEPT = names(normed=1, q2=1, k2=1, v2=1, totals=1, mixed2=1)
FEED_KEPT = names(
    inner=1, hidden=1, gate_grad=1, up_grad=1, grad_in=1, inner_part=1, patch_norms=1,
    latent_own=1, latent_send=1,
)
KEPT = FIRST_KEPT + CROSS_KEPT + SECOND_KEPT + FEED_KEPT
LAYERS = names(w_in=1, w_out=1, gain=1)


def forward_kernel(r):
    section, tensor = lax.axis_index("section"), lax.axis_index("tensor")
    own_count, patches, width = r.normed.shape
    byte_count = r.states.shape[1]
    columns = r.q1.shape[2]
    hidden = r.hidden.shape[2]
    heads = columns // HD
    greet([("section", 1 - section), ("tensor", 1 - tensor)])
    state_copies = [
        pltpu.make_async_copy(
            r.states.at[section * own_count + i], r.state_in.at[i], r.state_sem.at[i]
        )
        for i in range(own_count)
    ]
    for copy in state_copies:
        copy.start()
    layer = exchange_layer(r, section, tensor)
    grad_copies = [
        pltpu.make_async_copy(
            r.upstream.at[section * own_count + i], r.grad_in.at[i], r.grad_sem.at[i]
        )
        for i in range(own_count)
    ]
    feed_copies = [
        pltpu.make_async_copy(r.ffn_in, r.feed_in, r.feed_sem.at[0]),
        pltpu.make_async_copy(r.ffn_out, r.feed_out, r.feed_sem.at[1]),
    ]
    for copy in grad_copies + feed_copies:
        copy.start()
    heads_in, heads_out = head_masks(columns)

    def keep(name, i):
        n = KEPT.index(name)
        return pltpu.make_async_copy(
            getattr(r, name).at[i], getattr(r, "out_" + name).at[i], r.keep_sem.at[n, i]
        )

    def save(names, i):
        for name in names:
            keep(name, i).start()

    mine, theirs = block_at(tensor, columns), block_at(1 - tensor, columns)

    def exchange(step, i):
        held = r.heads_all.at[step, i, :, mine]
        return remote(
            held, held, r.part_send.at[step, i], r.part_recv.at[step, i], "tensor", 1 - tensor
        )

    def rows_across():
        return remote(
            r.attn_out.at[0], r.w_full.at[section, mine, :], r.rows_send.at[0], r.rows_recv.at[0],
            "tensor", 1 - tensor,
        )

    def rows_over():
        held = r.w_full.at[section, theirs, :]
        return remote(
            held, held, r.rows_send.at[1], r.rows_recv.at[1], "section", 1 - section
        )

    def pass_rows(layer_index):
        @pl.when(section == layer_index)
        def _():
            rows_across().wait_recv()
            rows_over().start()

    def have_rows(layer_index):
        @pl.when(section != layer_index)
        def _():
            rows_over().wait_recv()

    @pl.when(section == 0)
    def _():
        rows_across().start()

    for copy in state_copies:
        copy.wait()
    layer[-1][0].wait()
    layer[-1][1].wait()
    first_gain = r.gain.at[0]

    @pl.loop(0, own_count)
    def _(i):
        seq = section * own_count + i
        r.pool_sum[...] = jnp.zeros_like(r.pool_sum)

        def pool(rows):
            block = r.state_in[i, rows, :]
            r.pool_sum[...] += dot(members_of(r, seq, rows, patches), block)
            values = block.astype(f32)
            scale = inverse_rms(values)
            r.byte_norms[i, rows, :] = jnp.broadcast_to(scale, (BLOCK, LANES))
            r.source_in[i, rows, :] = (values * scale * first_gain[1:2, :]).astype(b16)

        each_block(byte_count, pool)
        row_ids = r.ids[pl.ds(seq, 1), :]
        counts = jnp.sum(
            jnp.where(iota((patches, byte_count), 0) == row_ids, 1.0, 0.0), axis=1, keepdims=True
        )
        values = r.pool_sum[...] / jnp.maximum(counts, 1.0)
        r.pooled[i] = values
        scale = inverse_rms(values)
        r.patch_norms[i] = jnp.broadcast_to(scale, (patches, LANES))
        r.query_in[i] = (values * scale * first_gain[0:1, :]).astype(b16)
        save(FIRST_KEPT, i)

    arrived(layer[:4])
    layer_saves = [
        pltpu.make_async_copy(src, dst, r.layer_sem.at[n])
        for n, (src, dst) in enumerate(
            ((r.w_in, r.out_w_in), (r.w_full.at[:, mine, :], r.out_w_out), (r.gain, r.out_gain))
        )
    ]
    for copy in layer_saves:
        copy.start()

    def first_layer(i):
        seq = section * own_count + i
        r.q1[i] = dot(r.query_in[i], r.w_in[0, :, :columns]).astype(b16)

        def project(rows):
            both = dot(r.source_in[i, rows, :], r.w_in[0, :, columns:])
            keys = both[:, :columns].astype(b16)
            r.k1[i, rows, :] = keys
            r.v1[i, rows, :] = both[:, columns:].astype(b16)
            spread = dot_lt(members_of(r, seq, rows, patches), r.q1[i])
            block_scores = dot((spread * keys.astype(f32)).astype(b16), heads_in) * SCALE
            r.scores[:, rows] = block_scores.T[:heads, :]

        each_block(byte_count, project, WIDE)
        scores = r.scores[...]
        r.scores[...] = jnp.exp(scores - segment_max(scores, r.ids[pl.ds(seq, 1), :]))
        r.mix_sum[...] = jnp.zeros_like(r.mix_sum)
        r.total_sum[...] = jnp.zeros_like(r.total_sum)

        def mix(rows):
            short = r.scores[:, rows]
            filled = jnp.concatenate([short, jnp.zeros((LANES - heads, WIDE), f32)], axis=0)
            raised = filled.T.astype(b16)
            r.raised[i, rows, :] = raised
            members = members_of(r, seq, rows, patches)
            weighted = (dot(raised, heads_out) * r.v1[i, rows, :].astype(f32)).astype(b16)
            r.mix_sum[...] += dot(members, weighted)
            r.total_sum[...] += dot(members, raised)

        each_block(byte_count, mix, WIDE)
        totals = r.total_sum[...]
        inverse = jnp.where(totals > 0.0, 1.0 / totals, 0.0)
        r.inverse[i] = inverse
        mixed = (r.mix_sum[...] * split_dot(inverse, heads_out)).astype(b16)
        r.mixed1[i] = mixed
        r.heads_all[0, i, :, mine] = mixed
        exchange(0, i).start()
        save(CROSS_KEPT, i)

    for i in range(own_count):
        first_layer(i)
        if i == 0:
            pl.when(section == 1)(rows_across().start)
            pass_rows(0)

    second_gain = r.gain.at[1]
    allowed = iota((patches, patches), 1) <= iota((patches, patches), 0)
    lane = iota((patches, LANES), 1)

    have_rows(0)

    def second_layer(i):
        exchange(0, i).wait()
        latent = (r.pooled[i] + dot(r.heads_all[0, i], r.w_full[0])).astype(b16)
        r.latent[i] = latent
        values = latent.astype(f32)
        scale = inverse_rms(values)
        r.patch_norms[i] = jnp.where(lane == 1, scale, r.patch_norms[i])
        normed = (values * scale * second_gain[0:1, :]).astype(b16)
        r.normed[i] = normed
        projected = dot(normed, r.w_in[1]).astype(b16)
        query, key, value = [projected[:, j * columns : (j + 1) * columns] for j in range(3)]
        r.q2[i] = query
        r.k2[i] = key
        r.v2[i] = value
        kept = jnp.zeros((patches, LANES), f32)
        outs = []
        for head in range(heads):
            own = slice(head * HD, (head + 1) * HD)
            scores = jnp.where(allowed, dot_rt(query[:, own], key[:, own]) * SCALE, NEGATIVE)
            highest = jnp.max(scores, axis=-1, keepdims=True)
            raised = jnp.exp(scores - highest)
            total = jnp.sum(raised, axis=-1, keepdims=True)
            outs.append(dot((raised / total).astype(b16), value[:, own]))
            kept = jnp.where(lane == head, highest + jnp.log(total), kept)
        r.totals[i] = kept
        mixed = jnp.concatenate(outs, axis=1).astype(b16)
        r.mixed2[i] = mixed
        r.heads_all[1, i, :, mine] = mixed
        exchange(1, i).start()
        save(SECOND_KEPT, i)

    for i in range(own_count):
        second_layer(i)
        if i == 0:
            pass_rows(1)
    have_rows(1)

    for copy in grad_copies + feed_copies:
        copy.wait()

    @pl.loop(0, own_count)
    def _(i):
        seq = section * own_count + i
        exchange(1, i).wait()
        values = r.latent[i].astype(f32) + dot(r.heads_all[1, i], r.w_full[1])
        r.middle[...] = values
        scale = inverse_rms(values)
        r.patch_norms[i] = jnp.where(lane == 2, scale, r.patch_norms[i])
        r.inner[i] = (values * scale * second_gain[1:2, :]).astype(b16)
        valid = iota((patches, 1), 0) <= jnp.max(r.ids[pl.ds(seq, 1), :], axis=1, keepdims=True)
        r.grad_in[i] = jnp.where(valid, r.grad_in[i].astype(f32), 0.0).astype(b16)

        gate = dot(r.inner[i], r.feed_in[0])
        up = dot(r.inner[i], r.feed_in[1])
        hidden_grad = dot_rt(r.grad_in[i], r.feed_out[...])
        gated = 1.0 / (1.0 + jnp.exp(-gate))
        act = gate * gated
        r.hidden[i] = (act * up).astype(b16)
        r.gate_grad[i] = (hidden_grad * up * (gated * (1.0 + gate * (1.0 - gated)))).astype(b16)
        r.up_grad[i] = (hidden_grad * act).astype(b16)
        inner_grad = dot_rt(r.gate_grad[i], r.feed_in[0]) + dot_rt(r.up_grad[i], r.feed_in[1])
        r.inner_part[i] = inner_grad.astype(b16)
        r.out_sum[...] = dot(r.hidden[i], r.feed_out[...])
        r.latent_own[i] = (r.middle[:, mine] + r.out_sum[:, mine]).astype(b16)
        r.latent_send[i] = r.out_sum[:, theirs].astype(b16)
        save(FEED_KEPT, i)

    @pl.loop(0, own_count)
    def _(i):
        for name in KEPT:
            keep(name, i).wait()

    for copy in layer_saves:
        copy.wait()
    rows_across().wait_send()
    rows_over().wait_send()


def shape(dims, dtype):
    return jax.ShapeDtypeStruct(dims, dtype)


def named_call(kernel, ins, outs, scratch, **params):
    any_space = pl.BlockSpec(memory_space=pl.ANY)
    whole = pl.BlockSpec(memory_space=pltpu.VMEM)
    names = [name for name, _, _ in ins] + [name for name, _ in outs] + list(scratch)

    def body(*refs):
        kernel(types.SimpleNamespace(**dict(zip(names, refs, strict=True))))

    got = pl.pallas_call(
        body,
        out_shape=tuple(s for _, s in outs),
        in_specs=[whole if inside else any_space for _, _, inside in ins],
        out_specs=tuple(any_space for _ in outs),
        scratch_shapes=list(scratch.values()),
        compiler_params=pltpu.CompilerParams(
            vmem_limit_bytes=VMEM_BYTES, has_side_effects=True, **params
        ),
    )(*(array for _, array, _ in ins))
    return {name: value for (name, _), value in zip(outs, got, strict=True)}


def forward(byte_states, patch_ids, attn_in, attn_out, gains, feed_in, feed_out, latent_grad):
    sequences, byte_count, width = byte_states.shape
    patches = byte_count // 4
    columns = attn_in.shape[-1]
    hidden = feed_out.shape[0]
    own = sequences // 2
    heads = columns // HD
    dims = dict(
        query_in=(own, patches, width, b16),
        source_in=(own, byte_count, width, b16),
        q1=(own, patches, columns, b16),
        k1=(own, byte_count, columns, b16),
        v1=(own, byte_count, columns, b16),
        raised=(own, byte_count, LANES, b16),
        inverse=(own, patches, LANES, f32),
        mixed1=(own, patches, columns, b16),
        byte_norms=(own, byte_count, LANES, f32),
        normed=(own, patches, width, b16),
        q2=(own, patches, columns, b16),
        k2=(own, patches, columns, b16),
        v2=(own, patches, columns, b16),
        totals=(own, patches, LANES, f32),
        mixed2=(own, patches, columns, b16),
        inner=(own, patches, width, b16),
        hidden=(own, patches, hidden, b16),
        gate_grad=(own, patches, hidden, b16),
        up_grad=(own, patches, hidden, b16),
        grad_in=(own, patches, width, b16),
        inner_part=(own, patches, width, b16),
        patch_norms=(own, patches, LANES, f32),
        latent_own=(own, patches, columns, b16),
        latent_send=(own, patches, columns, b16),
    )
    sems = pltpu.SemaphoreType.DMA
    scratch = {name: pltpu.VMEM(dims[name][:-1], dims[name][-1]) for name in KEPT}
    scratch |= dict(
        state_in=pltpu.VMEM((own, byte_count, width), b16),
        pooled=pltpu.VMEM((own, patches, width), f32),
        latent=pltpu.VMEM((own, patches, width), b16),
        middle=pltpu.VMEM((patches, width), f32),
        out_sum=pltpu.VMEM((patches, width), f32),
        w_in=pltpu.VMEM((2, width, 3 * columns), b16),
        w_full=pltpu.VMEM((2, 2 * columns, width), b16),
        gain=pltpu.VMEM((2, 2, width), f32),
        feed_in=pltpu.VMEM((2, width, hidden), b16),
        feed_out=pltpu.VMEM((hidden, width), b16),
        pool_sum=pltpu.VMEM((patches, width), f32),
        scores=pltpu.VMEM((heads, byte_count), f32),
        mix_sum=pltpu.VMEM((patches, columns), f32),
        total_sum=pltpu.VMEM((patches, LANES), f32),
        heads_all=pltpu.VMEM((2, own, patches, 2 * columns), b16),
        rows_send=sems((2,)),
        rows_recv=sems((2,)),
        state_sem=sems((own,)),
        grad_sem=sems((own,)),
        feed_sem=sems((2,)),
        near_sem=sems((5,)),
        far_send=sems((5,)),
        far_recv=sems((5,)),
        part_send=sems((2, own)),
        part_recv=sems((2, own)),
        keep_sem=sems((len(KEPT), own)),
        layer_sem=sems((len(LAYERS),)),
    )
    ins = [
        ("states", byte_states, False), ("ids", patch_ids, True), ("attn_in", attn_in, False),
        ("attn_out", attn_out, False), ("gains", gains, False), ("ffn_in", feed_in, False),
        ("ffn_out", feed_out, False), ("upstream", latent_grad, False),
    ]
    dims |= dict(
        w_in=(2, width, 3 * columns, b16),
        w_out=(2, columns, width, b16),
        gain=(2, 2, width, f32),
    )
    names = (*KEPT, *LAYERS)
    outs = [("out_" + name, shape(dims[name][:-1], dims[name][-1])) for name in names]
    got = named_call(forward_kernel, ins, outs, scratch, collective_id=0)
    return {name: got["out_" + name] for name in names}


def flat(ref, cols):
    block = ref[:, :, cols]
    return block.reshape(block.shape[0] * block.shape[1], block.shape[2])


LONG, SHORT = 4, 2


def rows_of(ref, start, rows):
    if not isinstance(start, int):
        start = pl.multiple_of(start, 16)
    return ref.at[pl.ds(start, rows), :]


def sum_rows(target, *terms):
    rows, width = target.shape
    step = rows
    while step * width > 100 * 1408 and step % 32 == 0:
        step //= 2

    def add(at):
        value = terms[0][at, :]
        for term in terms[1:]:
            value = value + term[at, :]
        target[at, :] = value

    if step == rows:
        add(slice(None))
    else:
        each_block(rows, add, step)


def add_rows(target, *others):
    sum_rows(target, target, *others)


PLAN = ((((0,1),()),((0,1),(1,)),((),()),((1,),(0,))),(((3,0,0,0,2,2,2),(0,1,2,0,0,0,2,3,2)),((0,0,3,2),(2,3,0)),((2,1,0,3),(1,3)),((0,0,0,0,2,2,2,3),(1,0,0,0,2,2,2,3,2))),(((5,4,2,4,1,4,4),(4,4,5,1,2,4)),((),(4,5)),((4,5,0),(4,5,2)),((4,4,2,4,5,4),(4,5,1,4,4,4))),(((1,1),(4,)),((4,),(0,0)),((1,0,0),(0,0)),((1,1),())),(((),()),((1,0),()),((0,),()),((1,),())),(((),(1,1)),((2,5),(1,)),((2,),(1,0)),((),(1,1))),(((),(3,)),((0,),()),((),(2,)),((0,),())),(((3,3,0,3),()),((3,),(0,3,0,2,2)),((3,2,2),()),((3,3,3),(0,))),(((),()),((2,2),(2,)),((),(3,)),((),(3,3))),(((),()),((4,4),()),((4,),(0,2)),((),())),(((),(3,2,0)),((),(4,4)),((),(2,2)),((2,),())),(((2,5,5),()),((4,0,2),(5,2)),((2,5,4,4),(4,4,4,0)),((5,5,5),(2,))),(((),(13,8,0,11,5,3,7,9,0,6,10,5,12,12,5,10,8,8,10,6,6,6,10,2,2)),((),(6,4,4,10,1,7,0,9,11,13,2,12,8)),((),(4,6,1,11,5,0,10,2,9,8,12,7)),((),(8,3,5,5,11,7,0,12,5,9,8,10,6,6,6,8,12,10,12,13,8,10,12,6))),(((),(8,12,12)),((),()),((1,4),(13,)),((),())),(((5,),()),((4,1),()),((),()),((4,),(2,4))),(((0,0),(0,0)),((5,),(3,7)),((0,),()),((0,),(0,0))),(((0,),(4,7,7,7)),((2,),(1,1)),((),(0,)),((),(7,7,2,2))),(((2,2),(2,2)),((),()),((),(3,9,7)),((2,),())),(((0,),(9,)),((1,1),()),((2,0,1,1),(4,2,1,11)),((0,),(9,9,10,9,11))),(((),()),((),()),((),()),((2,2),(7,11,11))),(((2,),(11,)),((3,),(4,)),((),(1,)),((),())),(((4,1),(9,11)),((4,5,0,0,0,1,3),(6,)),((5,4,3,3,0),(8,)),((),())),(((),(9,)),((3,2),()),((),()),((1,0),(0,0,13))),(((),(13,13,13)),((),(11,)),((),(13,)),((),(13,13,2))),(((),()),((5,2,0,0),()),((5,1,5,2,2,4,0,0,0,3,0),(3,3,6,5,6)),((),(4,))),(((0,),(4,11,4,4)),((),(10,0,0,3,9,3,13,5,6)),((3,),()),((),())),(((),()),((0,5),(8,8)),((),(10,8)),((0,0),(2,4))),(((2,),()),((),()),((),()),((4,),())),(((),()),((),(12,10)),((),()),((2,2),())),(((),(4,)),((2,3),(0,12)),((5,),(10,0,12,12,1)),((),())),(((),()),((),(2,1)),((),(2,)),((),())),(((4,18,4,1,0,3,16,15,4,17,16,20,14,20,4,19,16,21,14,14,20,18,16,18,18,2,2,14,5),(3,)),((14,17,15,2,20,21,2,2,5,19),()),((16,17,20,15,19,14,21,4,16,18,2),()),((19,14,4,1,16,15,18,17,20,3,14,20,18,14,4,16,21,20,18,20,16,16,14,15,5,0,0,4,3,4,15,17,18,2,15,2,17,17,19,19),(1,))),(((3,0,15,15,15,17,17,2,20,19,21,4,17,21,19,19),(1,5,0,0)),((16,),(5,7,3,2,2,6,0,11,0,12,10,9,5,0,8,6)),((2,2,2),(6,5,0,0,3,7,4,8,0,0,6,8,9)),((21,19,21),(3,4))),(((),(3,1,2,6,0,4,8,10,12,4,2,2,9,4,13,6,7,6,6,6,8,11,8,5,8,8,10)),((4,4,18,18,4,15,16,20,14,14,16,20,18,4,19,4,4,15,17,21,17,19,16,21),(10,12,5,2,4,8,4,9,2,6,4,7,2,9,7,13,11,10,13,11,13,8,12,4,11,4,9,7)),((14,16,14,18,18,20,4,20,19,14,15,15,17,21,17),(11,10,10,5,12,12,2,2,2,2,7,11,5,8,7,6,4,9,13,11,10,10,12,12,13,4,9,7,4,4,9,6,8,13)),((),(3,5,6,0,4,1,0,11,12,8,4,7,10,2,13,2,6,9,4,8,10,10,5,8,10,10,6,12,12,8,8,8,12,6,6,6,4,10,12))),(((),(12,12,12,12,7,10,10,6,12)),((14,14,18,18,20,20),()),((4,19,4,4,21,20,14,18,16,16,18,14,20,15,18),(6,11)),((),())),(((21,4,14,5,16,18,20),()),((14,20),()),((16,20,15,17),(4,)),((16,18,4,14,21,20),())),(((15,),(10,8,8,9,6,6,10,10,10,11,8)),((16,15,16,18,15,17,17,19,19,15,17,21,18),(13,6,6,8,8,10,10,10,8,4,12,12,6)),((17,15,19,21,17,21,14,19),(8,6,10,12,13)),((4,15,14,14,18,5,20,16,16),(7,11,9,12))),(((4,14,14,14,14,16,16,16,16,18,18,18,18,17,20,19,15),()),((21,14),(10,6,6,10,10,8,8,8,12)),((14,19),(6,6,8,8,8,8,10,10,12,10,10,6,12,12,12)),((14,20,16,18,18,20,17,15,19),(10,13))),(((21,17,20,20,20,16,14,14,20,20,16,18,20,14,19,18,18,16,21),(12,12,13)),((14,16,16,16,18,20,19,18,20,20,14,14,21,14,14,18,16,16,16,18,20,20,20,18),(12,12,12,6)),((18,16,21,20,18,20,16,14,14,14,16,16,18,18,14,18,18,20,20,20,16,20,16),()),((21,14,14,16,16,20,17,16,18,18,19,14,16,20,20,14,20,18,21,18),(6,6,8,8,12,12,10))))


class Flows:
    def __init__(self, r, section):
        self.r = r
        self.section = section
        place = lax.axis_index("dp")
        self.z, self.y = place // SHORT, lax.rem(place, SHORT)
        self.right, self.left = place + SHORT, place - SHORT
        self.beside = place + 1 - 2 * self.y
        self.flows = []
        self.done = {(z, s): [] for z in range(LONG) for s in range(2)}
        self.points = 0

    def hop(self, src, dst, n, j, target):
        r = self.r
        return pltpu.make_async_remote_copy(
            src_ref=src, dst_ref=dst, send_sem=r.flow_send.at[n, j], recv_sem=r.flow_recv.at[n, j],
            device_id={"dp": target}, device_id_type=MESH,
        )

    def reduce_events(self, n, part, slot):
        def up(k):
            return self.hop(slot(k - 1), slot(k - 1), n, k - 1, self.right)

        def down(k):
            return self.hop(slot(3 + k), slot(3 + k), n, 3 + k, self.left)

        def pass_on(copy, held, k):
            copy(k).wait_recv()
            add_rows(held, part(k))
            copy(k).start()

        def begin(z):
            if z == 0:
                for k in (3, 2, 1):
                    self.hop(part(k), slot(k - 1), n, k - 1, self.right).start()
            if z == 3:
                for k in (0, 1, 2):
                    self.hop(part(k), slot(3 + k), n, 3 + k, self.left).start()

        def passing(at_one, at_two):
            def event(z):
                if z in (1, 2):
                    way, k = (at_one, at_two)[z - 1]
                    pass_on(*((up, slot(k - 1)) if way > 0 else (down, slot(3 + k))), k)

            return event

        def close(z):
            got = []
            if z >= 1:
                up(z).wait_recv()
                got.append(slot(z - 1))
            if z <= 2:
                down(z).wait_recv()
                got.append(slot(3 + z))
            add_rows(part(z), *got)

        def sent(z):
            for k in ((1, 2, 3), (2, 3), (3,), ())[z]:
                up(k).wait_send()
            for k in ((), (0,), (0, 1), (0, 1, 2))[z]:
                down(k).wait_send()

        passes = [
            passing((1, 3), (-1, 0)), passing((1, 2), (-1, 1)), passing((-1, 0), (1, 3)),
        ]
        return begin, passes, close, sent

    def gather_events(self, n, own, out):
        def up(src, k, d):
            return self.hop(src, out(k), n, 7 + d, self.right)

        def down(src, k, d):
            return self.hop(src, out(k), n, 10 + d, self.left)

        def near(z):
            return pltpu.make_async_copy(own(z), out(z), self.r.flow_near.at[n])

        def starts(z, d, way):
            k = z - d * way
            src = own(z) if d == 0 else out(k)
            copies = []
            if d < LONG - 1 and 0 <= z + way < LONG:
                copies.append((up if way > 0 else down)(src, k, d))
            return copies

        def begin(z):
            near(z).start()
            for copy in starts(z, 0, 1) + starts(z, 0, -1):
                copy.start()

        def step(d, way):
            def event(z):
                k = z - d * way
                if 0 <= k < LONG:
                    (up if way > 0 else down)(out(k), k, d - 1).wait_recv()
                    for copy in starts(z, d, way):
                        copy.start()

            return event

        def sent(z):
            near(z).wait()
            for way in (1, -1):
                for d in range(LONG):
                    if 0 <= z - d * way < LONG:
                        for copy in starts(z, d, way):
                            copy.wait_send()

        return begin, [step(d, way) for d in (1, 2, 3) for way in (1, -1)], sent

    def long_first(self, n, data, out, slots, start, rows):
        c = rows // LONG

        def part(k):
            return data(start + k * c, c)

        def slot(j):
            return rows_of(slots, j * c, c)

        def beside(z):
            return self.hop(part(z), slot(6), n, 6, self.beside)

        begin, passes, close, reduce_sent = self.reduce_events(n, part, slot)
        gather, steps, gather_sent = self.gather_events(
            n, lambda z: slot(6), lambda k: out(start + k * c, c)
        )

        def middle(z):
            close(z)
            beside(z).start()

        def turn(z):
            beside(z).wait_recv()
            add_rows(slot(6), part(z))
            gather(z)

        def sent(z):
            reduce_sent(z)
            beside(z).wait_send()
            gather_sent(z)

        return [begin, *passes, middle, turn, *steps], sent

    def short_first(self, n, data, out, slots, start, rows):
        half = rows // SHORT

        def mine(y):
            return data(start + y * half, half)

        def place(y):
            return out(start + y * half, half)

        def slot(j):
            return rows_of(slots, j * half, half)

        def beside():
            return self.hop(mine(1 - self.y), slot(0), n, 6, self.beside)

        inward = (self.right, self.right, self.left, self.left)
        outward = (None, self.left, self.right, None)

        def lean(z):
            middle = 1 if z in (1, 2) else 0
            return self.hop(mine(self.y), slot(1 + middle), n, middle, inward[z])

        def settle(z):
            src = slot(0) if z in (1, 2) else place(self.y)
            return self.hop(src, place(self.y), n, 7, outward[z])

        def near(z):
            return pltpu.make_async_copy(slot(0), place(self.y), self.r.flow_near.at[n])

        def spread(z):
            src = slot(0) if z in (1, 2) else place(self.y)
            return self.hop(src, place(self.y), n, 13, self.beside)

        def first(z):
            beside().start()

        def turn(z):
            beside().wait_recv()
            add_rows(mine(self.y), slot(0))
            if z in (0, 3):
                lean(z).start()

        def pair(z):
            if z in (1, 2):
                self.hop(slot(1), slot(1), n, 0, inward[z]).wait_recv()
                add_rows(mine(self.y), slot(1))
                lean(z).start()

        def close(z):
            if z in (1, 2):
                lean(z).wait_recv()
                sum_rows(slot(0), mine(self.y), slot(2))
                near(z).start()
                settle(z).start()
                spread(z).start()

        def outer(z):
            if z in (0, 3):
                self.hop(place(self.y), place(self.y), n, 7, inward[z]).wait_recv()
                spread(z).start()

        def end(z):
            there = place(1 - self.y)
            self.hop(there, there, n, 13, self.beside).wait_recv()

        def sent(z):
            beside().wait_send()
            lean(z).wait_send()
            spread(z).wait_send()
            if z in (1, 2):
                settle(z).wait_send()
                near(z).wait()

        return [first, turn, pair, close, outer, end], sent

    def open(self, only, *flows):
        for events, sent in flows:
            self.flows.append((only, events, sent))
            for counts in self.done.values():
                counts.append(0)

    def advance(self, z, s, todo):
        def body():
            for n in todo:
                self.flows[n][1][self.done[z, s][n]](z)
                self.done[z, s][n] += 1

        return body

    def point(self):
        plan = PLAN[self.points] if self.points < len(PLAN) else ()
        self.points += 1
        for z, lists in enumerate(plan):
            first, second = self.done[z, 0], self.done[z, 1]
            if lists[0] == lists[1] and all(first[n] == second[n] for n in lists[0]):
                if lists[0]:
                    pl.when(self.z == z)(self.advance(z, 0, lists[0]))
                    for n in lists[0]:
                        second[n] = first[n]
                continue
            for s in range(2):
                here = jnp.logical_and(self.z == z, self.section == s)
                pl.when(here)(self.advance(z, s, lists[s]))

    def drain(self):
        for (z, s), counts in self.done.items():

            def body(z=z, s=s, counts=counts):
                mine = [n for n, flow in enumerate(self.flows) if flow[0] in (None, s)]
                longest = max(len(self.flows[n][1]) for n in mine)
                for k in range(longest):
                    for n in mine:
                        if counts[n] <= k < len(self.flows[n][1]):
                            self.flows[n][1][k](z)
                for n in mine:
                    self.flows[n][2](z)

            pl.when(jnp.logical_and(self.z == z, self.section == s))(body)


def on_grid():
    return lax.axis_size("dp") == LONG * SHORT


def backward_kernel(r):
    section, tensor = lax.axis_index("section"), lax.axis_index("tensor")
    own_count, patches, width = r.normed.shape
    byte_count = r.ids.shape[1]
    columns = r.w_out.shape[0]
    hidden = r.down.shape[0]
    heads = columns // HD
    half = width // 2
    half_bytes = byte_count // 2
    summing = on_grid()
    loads = {}

    def load(name, src, dst, *sem):
        copy = pltpu.make_async_copy(src, dst, r.load_sem.at[sem])
        copy.start()
        loads[name] = copy

    held_names = ("inner", "grad_in", "inner_part", "normed", "patch_norms", "gain")
    for n, name in enumerate(held_names):
        load(name, getattr(r, "in_" + name), getattr(r, name), n)
    load("w_in", r.in_w_in.at[1], r.w_in, 6)
    load("w_out", r.in_w_out.at[1], r.w_out, 7)
    others = [("section", 1 - section), ("tensor", 1 - tensor)]
    flows = Flows(r, section) if summing else None
    if summing:
        greet_grid(flows, others)
    else:
        greet(others)

    def cross(src, dst, i, sem):
        return remote(
            src, dst, r.cross_send.at[sem, i], r.cross_recv.at[sem, i], "tensor", 1 - tensor
        )

    def inner_exchange(i):
        return cross(r.in_inner_part.at[i], r.inner_got.at[i], i, 0)

    def normed_exchange(i):
        return cross(r.normed_part.at[i], r.normed_got.at[i], i, 1)

    def query_exchange(i):
        return cross(r.inner_part.at[i], r.inner_got.at[i], i, 2)

    def source_exchange(i):
        theirs = block_at(1 - tensor, half_bytes)
        return cross(r.source_part.at[i, theirs, :], r.source_got.at[i], i, 3)

    def latent_exchange(i):
        return cross(r.in_latent_send.at[i], r.latent_got.at[i], i, 4)

    for i in range(own_count):
        inner_exchange(i).start()
    def give(n, src, dst):
        return remote(src, dst, r.give_send.at[n], r.give_recv.at[n], "section", 1 - section)

    def point():
        if summing:
            flows.point()

    def summed(n, data, out, only=None):
        if summing:
            long_slots, short_slots, rows, cut = r.slots[n]
            flows.open(
                only,
                flows.long_first(2 * n, data, out, long_slots, 0, cut),
                flows.short_first(2 * n + 1, data, out, short_slots, cut, rows - cut),
            )

    def up_half(ref, n):
        return ref.at[pl.ds(n * half, half), :]

    def whole(view):
        return lambda start, rows: rows_of(view(), start, rows)

    @functools.partial(
        pl.run_scoped,
        hidden_all=pltpu.VMEM((own_count, patches, hidden), b16),
        gate_all=pltpu.VMEM((own_count, patches, hidden), b16),
        up_all=pltpu.VMEM((own_count, patches, hidden), b16),
        down_give=pltpu.VMEM((hidden, half), b16),
    )
    def _(hidden_all, gate_all, up_all, down_give):
        parts = {"hidden": hidden_all, "gate_grad": gate_all, "up_grad": up_all}
        for n, (name, ref) in enumerate(parts.items()):
            load(name, getattr(r, "in_" + name), ref, n + 8)
        for name in (*parts, "inner", "grad_in"):
            loads[name].wait()

        def down_grad(target, side):
            upstream = flat(r.grad_in, block_at(side, half))

            def tile(cols):
                target[cols, :] = dot_lt(flat(hidden_all, cols), upstream).astype(b16)

            each_block(hidden, tile)
            if hidden % BLOCK:
                tile(pl.ds(hidden - hidden % BLOCK, hidden % BLOCK))

        def up_grad(target, ref, side):
            upstream = flat(ref, slice(None))

            def tile(rows):
                cols = pl.ds(pl.multiple_of(side * half + rows.start, BLOCK), BLOCK)
                target[rows, :] = dot_lt(flat(r.inner, cols), upstream).astype(b16)

            each_block(half, tile)

        used = pl.ds(0, hidden)
        give_rows = [pl.ds(0, half), pl.ds(half, half)]
        gate_give, up_give = [r.attn_in_part.at[1, rows, used] for rows in give_rows]
        gate_got, up_got = [r.big_got.at[rows, used] for rows in give_rows]
        gate_own, up_own = [r.up.at[rows, :] for rows in give_rows]
        gifts = [
            give(0, down_give, r.down_got), give(1, gate_give, gate_got), give(2, up_give, up_got)
        ]
        other = 1 - section
        down_grad(down_give, other)
        gifts[0].start()
        down_grad(r.down, section)
        up_grad(gate_give, gate_all, other)
        gifts[1].start()
        gifts[0].wait()
        add_rows(r.down, r.down_got)
        summed(0, whole(lambda: r.down), whole(lambda: r.down_sum))
        point()
        up_grad(gate_own, gate_all, section)
        up_grad(up_give, up_all, other)
        gifts[2].start()
        gifts[1].wait()
        add_rows(gate_own, gate_got)
        summed(1, whole(lambda: up_half(r.up, 0)), whole(lambda: up_half(r.up_sum, 0)))
        point()
        up_grad(up_own, up_all, section)
        gifts[2].wait()
        add_rows(up_own, up_got)
        summed(2, whole(lambda: up_half(r.up, 1)), whole(lambda: up_half(r.up_sum, 1)))
        point()
        pl.semaphore_signal(
            r.free_sem, inc=1, device_id={"section": other}, device_id_type=MESH
        )

    def gifts_of(layer):
        return [
            give(3, r.attn_in_part.at[layer], r.big_got),
            give(4, r.attn_out_part.at[layer], r.attn_out_got),
        ]

    def hand_over(layer):
        @pl.when(section != layer)
        def _():
            pl.semaphore_wait(r.free_sem, 1)
            for gift in gifts_of(layer):
                gift.start()

    def take_over(layer):
        @pl.when(section != layer)
        def _():
            for gift in gifts_of(layer):
                gift.wait_send()

        @pl.when(section == layer)
        def _():
            for gift in gifts_of(layer):
                gift.wait_recv()
            add_rows(r.attn_out_part.at[layer], r.attn_out_got)
            add_rows(r.attn_in_part.at[layer], r.big_got)

    def sum_layer(layer, which):
        def columns_of(j):
            return whole(lambda: r.attn_in_part.at[layer, :, pl.ds(j * columns, columns)])

        if which == 3:
            summed(
                3, whole(lambda: r.attn_out_part.at[layer]), whole(lambda: r.attn_out_sum), layer
            )
        else:
            summed(4 + which, columns_of(which), whole(lambda: r.attn_in_sum.at[which]), layer)

    first_gain, second_gain = r.gain.at[0], r.gain.at[1]

    def back_through(normed, gain_row, scale, upstream):
        unit = normed.astype(f32) / gain_row
        scaled = upstream * gain_row
        mean = jnp.mean(unit * scaled, axis=-1, keepdims=True)
        return (scaled - unit * mean) * scale, unit

    @functools.partial(
        pl.run_scoped,
        q2=pltpu.VMEM((own_count, patches, columns), b16),
        k2=pltpu.VMEM((own_count, patches, columns), b16),
        v2=pltpu.VMEM((own_count, patches, columns), b16),
        totals=pltpu.VMEM((own_count, patches, LANES), f32),
        mixed2=pltpu.VMEM((own_count, patches, columns), b16),
        second_grads=pltpu.VMEM((own_count, patches, 3 * columns), b16),
        mixed_grads=pltpu.VMEM((patches, columns), b16),
    )
    def _(q2, k2, v2, totals, mixed2, second_grads, mixed_grads):
        parts = {"q2": q2, "k2": k2, "v2": v2, "totals": totals, "mixed2": mixed2}
        for n, (name, ref) in enumerate(parts.items()):
            load(name, getattr(r, "in_" + name), ref, n + 11)
        for name in (*held_names[2:], "w_in", "w_out", *parts):
            loads[name].wait()
        r.gain_sum[...] = jnp.zeros_like(r.gain_sum)
        allowed = iota((patches, patches), 1) <= iota((patches, patches), 0)
        for i in range(own_count):
            inner_exchange(i).wait()
            own_part = r.inner_part[i].astype(f32)
            back, unit = back_through(
                r.inner[i], second_gain[1:2, :], r.patch_norms[i, :, 2:3],
                own_part + r.inner_got[i].astype(f32),
            )
            r.gain_sum[3:4, :] += jnp.sum(unit * own_part, axis=0, keepdims=True)
            branch = (r.grad_in[i].astype(f32) + back).astype(b16)
            r.branch[i] = branch
            mixed_grads[...] = dot_rt(branch, r.w_out[...]).astype(b16)
            point()

            mixed_grad = mixed_grads[...]
            outs = [[], [], []]
            for head in range(heads):
                own = slice(head * HD, (head + 1) * HD)
                query, key, value = q2[i, :, own], k2[i, :, own], v2[i, :, own]
                upper = mixed_grad[:, own]
                scores = jnp.where(allowed, dot_rt(query, key) * SCALE, NEGATIVE)
                probs = jnp.exp(scores - totals[i, :, head : head + 1])
                prob_grad = dot_rt(upper, value)
                delta = jnp.sum(probs * prob_grad, axis=-1, keepdims=True)
                score_grad = (probs * (prob_grad - delta)).astype(b16)
                outs[0].append(dot(score_grad, key) * SCALE)
                outs[1].append(dot_lt(score_grad, query) * SCALE)
                outs[2].append(dot_lt(probs.astype(b16), upper))
            grads = jnp.concatenate(outs[0] + outs[1] + outs[2], axis=1).astype(b16)
            second_grads[i] = grads
            point()
            r.normed_part[i] = dot_rt(grads, r.w_in[...]).astype(b16)
            normed_exchange(i).start()
            point()

        def outer(target, rows_ref, upstream, tiles):
            @pl.loop(0, tiles)
            def _(t):
                cols = block_at(t)
                target[cols, :] = dot_lt(flat(rows_ref, cols), upstream).astype(b16)

        outer(r.attn_in_part.at[1], r.normed, flat(second_grads, slice(None)), width // BLOCK)
        point()
        outer(r.attn_out_part.at[1], mixed2, flat(r.branch, slice(None)), columns // BLOCK)
        hand_over(1)
        point()

    heads_in, heads_out = head_masks(columns)

    def first_layer(i, scoped):
        seq = section * own_count + i
        s = types.SimpleNamespace(**scoped)
        copies = {}
        kinds = names(q1=1, v1=1, raised=1, inverse=1, mixed1=1, source_in=1, query_in=1)
        for n, name in enumerate(kinds):
            copy = pltpu.make_async_copy(
                getattr(r, "in_" + name).at[i], getattr(s, name), r.first_sem.at[n]
            )
            copy.start()
            copies[name] = copy
        normed_exchange(i).wait()
        own_part = r.normed_part[i].astype(f32)
        back, unit = back_through(
            r.normed[i], second_gain[0:1, :], r.patch_norms[i, :, 1:2],
            own_part + r.normed_got[i].astype(f32),
        )
        r.gain_sum[2:3, :] += jnp.sum(unit * own_part, axis=0, keepdims=True)
        branch = (r.branch[i].astype(f32) + back).astype(b16)
        r.branch[i] = branch
        s.mixed_grad[...] = dot_rt(branch, r.w_out[...]).astype(b16)
        s.q_sum[...] = jnp.zeros_like(s.q_sum)
        s.delta_sum[...] = jnp.zeros_like(s.delta_sum)
        for copy in copies.values():
            copy.wait()
        point()
        if i == 0:
            take_over(1)
            for which in (3, 0, 1, 2):
                sum_layer(1, which)
            point()
        inverse = s.inverse[...]
        inverse_high = inverse.astype(b16)
        inverse_low = (inverse - inverse_high.astype(f32)).astype(b16)

        def value_side(rows):
            members = members_of(r, seq, rows, patches)
            spread = dot_lt(members, s.mixed_grad[...])
            scale = dot_lt(members, inverse_high) + dot_lt(members, inverse_low)
            probs = s.raised[rows, :].astype(f32) * scale
            s.probs[rows, :] = probs
            s.dkv[rows, columns:] = (dot(probs.astype(b16), heads_out) * spread).astype(b16)
            prob_grad = dot((spread * s.v1[rows, :].astype(f32)).astype(b16), heads_in)
            s.prob_grad[rows, :] = prob_grad
            product = probs * prob_grad
            high = product.astype(b16)
            low = (product - high.astype(f32)).astype(b16)
            s.delta_sum[...] += dot(members, high) + dot(members, low)

        for t in range(byte_count // WIDE):
            value_side(pl.ds(t * WIDE, WIDE))
            point()
        keys = pltpu.make_async_copy(r.in_k1.at[i], s.v1, r.first_sem.at[7])
        keys.start()
        delta = s.delta_sum[...]
        delta_high = delta.astype(b16)
        delta_low = (delta - delta_high.astype(f32)).astype(b16)

        def key_side(rows):
            members = members_of(r, seq, rows, patches)
            shift = dot_lt(members, delta_high) + dot_lt(members, delta_low)
            score_grad = (s.probs[rows, :] * (s.prob_grad[rows, :] - shift)).astype(b16)
            spread = dot(score_grad, heads_out)
            s.dkv[rows, :columns] = (spread * dot_lt(members, s.q1[...]) * SCALE).astype(b16)
            s.q_sum[...] += dot(members, (spread * s.v1[rows, :].astype(f32)).astype(b16))
            source = dot_rt(s.dkv[rows, :], r.w_in[:, columns:])
            r.source_part[i, rows, :] = source.astype(b16)
            unit_block = s.source_in[rows, :].astype(f32)
            r.gain_sum[1:2, :] += (
                jnp.sum(unit_block * source, axis=0, keepdims=True) / first_gain[1:2, :]
            )

        keys.wait()
        for t in range(byte_count // WIDE):
            for u in range(WIDE // BLOCK):
                key_side(pl.ds(t * WIDE + u * BLOCK, BLOCK))
            point()
        source_exchange(i).start()
        q_grad = (s.q_sum[...] * SCALE).astype(b16)
        query = dot_rt(q_grad, r.w_in[:, :columns])
        r.inner_part[i] = query.astype(b16)
        query_exchange(i).start()
        unit_pool = s.query_in[...].astype(f32)
        r.gain_sum[0:1, :] += (
            jnp.sum(unit_pool * query, axis=0, keepdims=True) / first_gain[0:1, :]
        )
        point()

        def add_to(target, rows, cols, value):
            if i:
                value = target[rows, cols].astype(f32) + value
            target[rows, cols] = value.astype(b16)

        for half_t in range(2):

            @pl.loop(0, half // BLOCK)
            def _(t, half_t=half_t):
                cols = pl.ds(pl.multiple_of(half_t * half + t * BLOCK, BLOCK), BLOCK)
                source = s.source_in[:, cols]
                target = r.attn_in_part.at[0]
                add_to(target, cols, slice(0, columns), dot_lt(s.query_in[:, cols], q_grad))
                add_to(target, cols, slice(columns, 3 * columns), dot_lt(source, s.dkv[...]))

            point()

        @pl.loop(0, columns // BLOCK)
        def _(t):
            cols = block_at(t)
            add_to(
                r.attn_out_part.at[0], cols, slice(None), dot_lt(s.mixed1[:, cols], branch)
            )

        point()

    def last_parts(s):
        outs = []

        own_rows = block_at(tensor, half_bytes)
        cols_keep, cols_give = block_at(section, half), block_at(1 - section, half)
        for i in range(own_count):
            seq = section * own_count + i
            finals = [
                pltpu.make_async_copy(
                    r.in_source_in.at[i, own_rows, :], s.source_in, r.first_sem.at[0]
                ),
                pltpu.make_async_copy(
                    r.in_byte_norms.at[i, own_rows, :], s.byte_norms, r.first_sem.at[1]
                ),
                pltpu.make_async_copy(r.in_query_in.at[i], s.query_in, r.first_sem.at[2]),
            ]
            for copy in finals:
                copy.start()
            query_exchange(i).wait()
            source_exchange(i).wait()
            for copy in finals:
                copy.wait()
            back, _ = back_through(
                s.query_in[...], first_gain[0:1, :], r.patch_norms[i, :, 0:1],
                r.inner_part[i].astype(f32) + r.inner_got[i].astype(f32),
            )
            counts = jnp.sum(
                jnp.where(iota((patches, byte_count), 0) == r.ids[pl.ds(seq, 1), :], 1.0, 0.0),
                axis=1, keepdims=True,
            )
            pool_grad = (r.branch[i].astype(f32) + back) / jnp.maximum(counts, 1.0)
            high = pool_grad.astype(b16)
            s.pool_high[...] = high
            s.pool_low[...] = (pool_grad - high.astype(f32)).astype(b16)

            @pl.loop(0, half_bytes // BLOCK)
            def _(t, i=i, seq=seq):
                rows = block_at(t)
                place = pl.ds(pl.multiple_of(tensor * half_bytes + t * BLOCK, BLOCK), BLOCK)
                members = members_of(r, seq, place, patches)
                spread = dot_lt(members, s.pool_high[...]) + dot_lt(members, s.pool_low[...])
                part = r.source_part[i, place, :].astype(f32)
                own, _ = back_through(
                    s.source_in[rows, :], first_gain[1:2, :], s.byte_norms[rows, 0:1],
                    part + r.source_got[i, rows, :].astype(f32),
                )
                r.source_got[i, rows, :] = (own + spread).astype(b16)

            near = pltpu.make_async_copy(
                r.source_got.at[i, :, cols_keep], r.byte_grad.at[seq], r.out_sem.at[1, i]
            )
            far = remote(
                r.source_got.at[i, :, cols_give], r.byte_grad.at[seq],
                r.out_send.at[1, i], r.out_recv.at[1, i], "section", 1 - section,
            )
            near.start()
            far.start()
            outs += [near, far]
            point()

        half_rows = patches // 2
        rows_keep, rows_give = block_at(section, half_rows), block_at(1 - section, half_rows)
        for i in range(own_count):
            seq = section * own_count + i
            s_load = pltpu.make_async_copy(r.in_latent_own.at[i], s.latent.at[i], r.first_sem.at[i])
            s_load.start()
            s_load.wait()
            latent_exchange(i).wait()
            last = jnp.max(r.ids[pl.ds(seq, 1), :], axis=1, keepdims=True)
            valid = iota((patches, 1), 0) <= last
            values = s.latent[i].astype(f32) + r.latent_got[i].astype(f32)
            s.latent[i] = jnp.where(valid, values, 0.0).astype(b16)
            near = pltpu.make_async_copy(
                s.latent.at[i, rows_keep, :], r.latents.at[seq], r.out_sem.at[0, i]
            )
            far = remote(
                s.latent.at[i, rows_give, :], r.latents.at[seq],
                r.out_send.at[0, i], r.out_recv.at[0, i], "section", 1 - section,
            )
            near.start()
            far.start()
            outs += [near, far]
        for copy in outs:
            copy.wait()

    load("w_in", r.in_w_in.at[0], r.w_in, 6)
    load("w_out", r.in_w_out.at[0], r.w_out, 7)
    loads["w_in"].wait()
    loads["w_out"].wait()
    one = dict(
        source_in=pltpu.VMEM((byte_count, width), b16),
        v1=pltpu.VMEM((byte_count, columns), b16),
        dkv=pltpu.VMEM((byte_count, 2 * columns), b16),
        probs=pltpu.VMEM((byte_count, LANES), f32),
        prob_grad=pltpu.VMEM((byte_count, LANES), f32),
        raised=pltpu.VMEM((byte_count, LANES), b16),
        inverse=pltpu.VMEM((patches, LANES), f32),
        q1=pltpu.VMEM((patches, columns), b16),
        mixed1=pltpu.VMEM((patches, columns), b16),
        query_in=pltpu.VMEM((patches, width), b16),
        mixed_grad=pltpu.VMEM((patches, columns), b16),
        q_sum=pltpu.VMEM((patches, columns), f32),
        delta_sum=pltpu.VMEM((patches, LANES), f32),
    )

    @functools.partial(pl.run_scoped, **one)
    def _(**scoped):
        for i in range(own_count):
            first_layer(i, scoped)

    hand_over(0)
    for i in range(own_count):
        latent_exchange(i).start()
    point()
    take_over(0)
    for which in (3, 0, 1, 2):
        sum_layer(0, which)
    point()
    gains = Gains(r, section, tensor, flows) if summing else None
    if summing:
        gains.tick()
    last = dict(
        source_in=pltpu.VMEM((half_bytes, width), b16),
        byte_norms=pltpu.VMEM((half_bytes, LANES), f32),
        query_in=pltpu.VMEM((patches, width), b16),
        pool_high=pltpu.VMEM((patches, width), b16),
        pool_low=pltpu.VMEM((patches, width), b16),
        latent=pltpu.VMEM((own_count, patches, columns), b16),
    )

    @functools.partial(pl.run_scoped, **last)
    def _(**scoped):
        last_parts(types.SimpleNamespace(**scoped))

    if summing:
        while gains.steps:
            gains.tick()
            point()
        flows.drain()
    ends = [pltpu.make_async_copy(r.gain_sum, r.gain_out, r.end_sem.at[4])]
    if not summing:
        ends += [
            pltpu.make_async_copy(r.up, r.up_sum, r.end_sem.at[0]),
            pltpu.make_async_copy(r.down, r.down_sum, r.end_sem.at[1]),
            pltpu.make_async_copy(r.attn_out_part.at[section], r.attn_out_sum, r.end_sem.at[3]),
        ]
        ends += [
            pltpu.make_async_copy(
                r.attn_in_part.at[section, :, pl.ds(j * columns, columns)], r.attn_in_sum.at[j],
                r.end_sem.at[5 + j],
            )
            for j in range(3)
        ]
    for copy in ends:
        copy.start()
    for copy in ends:
        copy.wait()


class Gains:
    def __init__(self, r, section, tensor, flows):
        self.r = r
        z = flows.z
        place = lax.axis_index("dp")
        near = place + SHORT * (1 - 2 * lax.rem(z, 2))
        far = place + 2 * SHORT * (1 - 2 * (z // 2))
        self.targets = [
            {"tensor": 1 - tensor}, {"section": 1 - section}, {"dp": flows.beside},
            {"dp": near}, {"dp": far},
        ]
        self.steps = list(range(len(self.targets) + 1))

    def copy(self, n):
        r = self.r
        return pltpu.make_async_remote_copy(
            src_ref=r.gain_held.at[n], dst_ref=r.gain_got.at[n], send_sem=r.gain_send.at[n],
            recv_sem=r.gain_recv.at[n], device_id=self.targets[n], device_id_type=MESH,
        )

    def tick(self):
        if not self.steps:
            return
        r, n = self.r, self.steps.pop(0)
        if n == 0:
            r.gain_held[0] = r.gain_sum[...]
        else:
            self.copy(n - 1).wait()
            value = r.gain_held[n - 1] + r.gain_got[n - 1]
            if n < len(self.targets):
                r.gain_held[n] = value
            else:
                r.gain_sum[...] = value
        if n < len(self.targets):
            self.copy(n).start()


def greet_grid(flows, others):
    barrier = pltpu.get_barrier_semaphore()

    def signal(place):
        pl.semaphore_signal(barrier, inc=1, device_id=place, device_id_type=MESH)

    for axis, index in others:
        signal({axis: index})
    signal({"dp": flows.beside})
    signal({"dp": lax.axis_index("dp") + 2 * SHORT * (1 - 2 * (flows.z // 2))})
    pl.when(flows.z < LONG - 1)(lambda: signal({"dp": flows.right}))
    pl.when(flows.z > 0)(lambda: signal({"dp": flows.left}))
    inner = jnp.logical_and(flows.z > 0, flows.z < LONG - 1)
    pl.semaphore_wait(barrier, jnp.where(inner, len(others) + 4, len(others) + 3))


def backward(kept, patch_ids):
    own, patches, width = kept["normed"].shape
    sequences, byte_count = patch_ids.shape
    columns = kept["q1"].shape[-1]
    hidden = kept["hidden"].shape[-1]
    half, half_bytes = width // 2, byte_count // 2
    sems = pltpu.SemaphoreType.DMA
    vmem = pltpu.VMEM
    rows16 = vmem((own, patches, width), b16)
    scratch = dict(
        inner=rows16,
        grad_in=rows16,
        inner_part=rows16,
        inner_got=rows16,
        normed=rows16,
        patch_norms=vmem((own, patches, LANES), f32),
        branch=rows16,
        normed_part=rows16,
        normed_got=rows16,
        source_part=vmem((own, byte_count, width), b16),
        source_got=vmem((own, half_bytes, width), b16),
        latent_got=vmem((own, patches, columns), b16),
        w_in=vmem((width, 3 * columns), b16),
        w_out=vmem((columns, width), b16),
        gain=vmem((2, 2, width), f32),
        gain_sum=vmem((4, width), f32),
        down_got=vmem((hidden, half), b16),
        down=vmem((hidden, half), b16),
        up=vmem((width, hidden), b16),
        attn_in_part=vmem((2, width, 3 * columns), b16),
        attn_out_part=vmem((2, columns, width), b16),
        big_got=vmem((width, 3 * columns), b16),
        attn_out_got=vmem((columns, width), b16),
        load_sem=sems((16,)),
        first_sem=sems((8,)),
        cross_send=sems((5, own)),
        cross_recv=sems((5, own)),
        give_send=sems((5,)),
        give_recv=sems((5,)),
        out_sem=sems((2, own)),
        out_send=sems((2, own)),
        out_recv=sems((2, own)),
        end_sem=sems((8,)),
        free_sem=pltpu.SemaphoreType.REGULAR,
    )
    slots = []
    if on_grid():
        arrays = [(hidden, half, 512), (half, hidden, 256), (half, hidden, 128)]
        arrays += [(columns, width, 128)] + [(width, columns, 256)] * 3
        for n, (rows, cols, cut) in enumerate(arrays):
            slots.append((f"l{n}", f"s{n}", rows, cut))
            scratch[f"l{n}"] = vmem((7 * cut // LONG, cols), b16)
            scratch[f"s{n}"] = vmem((3 * (rows - cut) // SHORT, cols), b16)
        scratch |= dict(
            flow_send=sems((2 * len(arrays), 17)),
            flow_recv=sems((2 * len(arrays), 17)),
            flow_near=sems((2 * len(arrays),)),
            gain_held=vmem((5, 4, width), f32),
            gain_got=vmem((5, 4, width), f32),
            gain_send=sems((5,)),
            gain_recv=sems((5,)),
        )
    ins = [("ids", patch_ids, True)]
    ins += [("in_" + name, kept[name], False) for name in (*KEPT, *LAYERS)]
    outs = [
        ("latents", shape((sequences, patches // 2, columns), b16)),
        ("byte_grad", shape((sequences, half_bytes, half), b16)),
        ("attn_in_sum", shape((3, width, columns), b16)),
        ("attn_out_sum", shape((columns, width), b16)),
        ("gain_out", shape((4, width), f32)),
        ("up_sum", shape((width, hidden), b16)),
        ("down_sum", shape((hidden, half), b16)),
    ]

    def kernel(r):
        r.slots = [
            (getattr(r, long), getattr(r, short), rows, cut) for long, short, rows, cut in slots
        ]
        backward_kernel(r)

    return named_call(kernel, ins, outs, scratch, collective_id=1)


def widen(up, attn_in, attn_out, down):
    half, hidden = up.shape[0] // 2, up.shape[1]
    steps = 8
    flat_in = attn_in.reshape(-1, attn_in.shape[2])

    def rows(array, offset=0):
        count = array.shape[0] // steps
        return pl.BlockSpec((count, array.shape[1]), lambda t: (t + offset, 0))

    def body(gate_in, up_in, in_in, out_in, down_in, up_o, in_o, out_o, down_o):
        up_o[:, 0, :] = gate_in[...].astype(f32)
        up_o[:, 1, :] = up_in[...].astype(f32)
        for src, dst in ((in_in, in_o), (out_in, out_o), (down_in, down_o)):
            dst[...] = src[...].astype(f32)

    part = half // steps
    feed = [pl.BlockSpec((part, hidden), lambda t: (t, 0))]
    feed += [pl.BlockSpec((part, hidden), lambda t: (t + steps, 0))]
    up_out, in_out, out_out, down_out = pl.pallas_call(
        body,
        grid=(steps,),
        out_shape=(
            shape((half, 2, hidden), f32), shape(flat_in.shape, f32), shape(attn_out.shape, f32),
            shape(down.shape, f32),
        ),
        in_specs=[*feed, rows(flat_in), rows(attn_out), rows(down)],
        out_specs=(
            pl.BlockSpec((part, 2, hidden), lambda t: (t, 0, 0)),
            rows(flat_in), rows(attn_out), rows(down),
        ),
        compiler_params=pltpu.CompilerParams(vmem_limit_bytes=VMEM_BYTES),
    )(up, up, flat_in, attn_out, down)
    return up_out, in_out.reshape(attn_in.shape), out_out, down_out


def swap(values, axis):
    return lax.ppermute(values, axis, [(0, 1), (1, 0)])


def sum_small(values):
    values = values + swap(values, "tensor")
    values = values + swap(values, "section")
    return lax.psum(values, "dp")


def per_device(byte_states, patch_ids, attn_in, attn_out, gains, ffn_in, ffn_out, latent_grad):
    is_first = lax.axis_index("section") == 0
    kept = forward(
        byte_states, patch_ids, attn_in, attn_out, gains, ffn_in.transpose(1, 0, 2), ffn_out,
        latent_grad,
    )
    got = backward(kept, patch_ids)
    sums = [got[name] for name in ("down_sum", "up_sum", "attn_in_sum", "attn_out_sum")]
    if not on_grid():
        sums = [lax.psum(value, "dp") for value in sums]
    down, up, in_sum, out_sum = sums
    up_out, in_sum, out_sum, down = widen(up, in_sum, out_sum, down)
    gain_sum = got["gain_out"] if on_grid() else sum_small(got["gain_out"])
    gain_out = jnp.where(is_first, gain_sum[0:2], gain_sum[2:4])
    return (
        got["latents"], got["byte_grad"], in_sum[None], out_sum[None], gain_out[None], up_out, down
    )


def solution(mesh):
    return jax.shard_map(
        per_device,
        mesh=mesh,
        in_specs=(
            P("dp", None, None),
            P("dp", None),
            P("section", None, None, "tensor"),
            P("section", "tensor", None),
            P("section", None, None),
            P(None, None, "tensor"),
            P("tensor", None),
            P("dp", None, None),
        ),
        out_specs=(
            P("dp", "section", "tensor"),
            P("dp", "tensor", "section"),
            P("section", None, None, "tensor"),
            P("section", "tensor", None),
            P("section", None, None),
            P("section", None, "tensor"),
            P("tensor", "section"),
        ),
        check_vma=False,
    )
```

```python
import functools
import types

import jax
import jax.numpy as jnp
from jax import lax
from jax.experimental import pallas as pl
from jax.experimental.pallas import tpu as pltpu
from jax.sharding import PartitionSpec as P

HD = 64
LANES = 128
BLOCK = 256
WIDE = 512
EPSILON = 1e-05
NEGATIVE = -1000000000.0
SCALE = HD ** (-0.5)
VMEM_BYTES = 63 * 1024 * 1024

f32 = jnp.float32
b16 = jnp.bfloat16


def dot(a, b):
    return jnp.dot(a, b, preferred_element_type=f32)


def dot_rt(a, b):
    return lax.dot_general(a, b, (((1,), (1,)), ((), ())), preferred_element_type=f32)


def dot_lt(a, b):
    return lax.dot_general(a, b, (((0,), (0,)), ((), ())), preferred_element_type=f32)


def inverse_rms(values):
    return lax.rsqrt(jnp.mean(values * values, axis=-1, keepdims=True) + EPSILON)


def iota(shape, dim):
    return lax.broadcasted_iota(jnp.int32, shape, dim)


def one_hot(condition):
    return jnp.where(condition, 1.0, 0.0).astype(b16)


def segment_max(values, ids):
    width = values.shape[1]
    lane = iota(ids.shape, 1)
    lowest = -3.0e38
    ahead, behind = values, values
    step = 1
    while step < width:
        left, right = step, width - step
        same_left = jnp.logical_and(pltpu.roll(ids, left, axis=1) == ids, lane >= step)
        same_right = jnp.logical_and(pltpu.roll(ids, right, axis=1) == ids, lane < right)
        ahead = jnp.maximum(ahead, jnp.where(same_left, pltpu.roll(ahead, left, axis=1), lowest))
        behind = jnp.maximum(
            behind, jnp.where(same_right, pltpu.roll(behind, right, axis=1), lowest)
        )
        step *= 2
    return jnp.maximum(ahead, behind)


def head_masks(width):
    heads_in = one_hot(iota((width, LANES), 0) // HD == iota((width, LANES), 1))
    heads_out = one_hot(iota((LANES, width), 1) // HD == iota((LANES, width), 0))
    return heads_in, heads_out


def split_dot(values, matrix):
    high = values.astype(b16)
    low = (values - high.astype(f32)).astype(b16)
    return dot(high, matrix) + dot(low, matrix)


def block_at(index, size=BLOCK):
    return pl.ds(pl.multiple_of(index * size, size), size)


def each_block(count, body, size=BLOCK):
    @pl.loop(0, count // size)
    def _(index):
        body(block_at(index, size))


MESH = pl.DeviceIdType.MESH


def remote(src, dst, send, recv, axis, index):
    return pltpu.make_async_remote_copy(
        src_ref=src, dst_ref=dst, send_sem=send, recv_sem=recv,
        device_id={axis: index}, device_id_type=MESH,
    )


def greet(places):
    barrier = pltpu.get_barrier_semaphore()
    for axis, index in places:
        pl.semaphore_signal(barrier, inc=1, device_id={axis: index}, device_id_type=MESH)
    pl.semaphore_wait(barrier, len(places))


def exchange_layer(r, section, tensor):
    columns = r.attn_in.shape[3]
    copies = []
    for n, (src, dst) in enumerate(
        [
            (r.attn_in.at[0, j], r.w_in.at[section, :, pl.ds(j * columns, columns)])
            for j in (1, 2, 0)
        ]
        + [
            (r.attn_out.at[0], r.w_full.at[section, block_at(tensor, columns), :]),
            (r.gains.at[0], r.gain.at[section]),
        ]
    ):
        near = pltpu.make_async_copy(src, dst, r.near_sem.at[n])
        far = remote(src, dst, r.far_send.at[n], r.far_recv.at[n], "section", 1 - section)
        near.start()
        far.start()
        copies.append((near, far))
    return copies


def arrived(copies):
    for near, far in copies:
        near.wait()
        far.wait()


def members_of(r, seq, rows, patches):
    return one_hot(iota((patches, rows.size), 0) == r.ids[pl.ds(seq, 1), rows])


def names(**kinds):
    return tuple(kinds)


FIRST_KEPT = names(query_in=1, source_in=1, byte_norms=1)
CROSS_KEPT = names(q1=1, k1=1, v1=1, raised=1, inverse=1, mixed1=1)
SECOND_KEPT = names(normed=1, q2=1, k2=1, v2=1, totals=1, mixed2=1)
FEED_KEPT = names(
    inner=1, hidden=1, gate_grad=1, up_grad=1, grad_in=1, inner_part=1, patch_norms=1,
    latent_own=1, latent_send=1,
)
KEPT = FIRST_KEPT + CROSS_KEPT + SECOND_KEPT + FEED_KEPT
LAYERS = names(w_in=1, w_out=1, gain=1)


def forward_kernel(r):
    section, tensor = lax.axis_index("section"), lax.axis_index("tensor")
    own_count, patches, width = r.normed.shape
    byte_count = r.states.shape[1]
    columns = r.q1.shape[2]
    hidden = r.hidden.shape[2]
    heads = columns // HD
    greet([("section", 1 - section), ("tensor", 1 - tensor)])
    state_copies = [
        pltpu.make_async_copy(
            r.states.at[section * own_count + i], r.state_in.at[i], r.state_sem.at[i]
        )
        for i in range(own_count)
    ]
    for copy in state_copies:
        copy.start()
    layer = exchange_layer(r, section, tensor)
    grad_copies = [
        pltpu.make_async_copy(
            r.upstream.at[section * own_count + i], r.grad_in.at[i], r.grad_sem.at[i]
        )
        for i in range(own_count)
    ]
    feed_copies = [
        pltpu.make_async_copy(r.ffn_in, r.feed_in, r.feed_sem.at[0]),
        pltpu.make_async_copy(r.ffn_out, r.feed_out, r.feed_sem.at[1]),
    ]
    for copy in grad_copies + feed_copies:
        copy.start()
    heads_in, heads_out = head_masks(columns)

    def keep(name, i):
        n = KEPT.index(name)
        return pltpu.make_async_copy(
            getattr(r, name).at[i], getattr(r, "out_" + name).at[i], r.keep_sem.at[n, i]
        )

    def save(names, i):
        for name in names:
            keep(name, i).start()

    mine, theirs = block_at(tensor, columns), block_at(1 - tensor, columns)

    def exchange(step, i):
        held = r.heads_all.at[step, i, :, mine]
        return remote(
            held, held, r.part_send.at[step, i], r.part_recv.at[step, i], "tensor", 1 - tensor
        )

    def rows_across():
        return remote(
            r.attn_out.at[0], r.w_full.at[section, mine, :], r.rows_send.at[0], r.rows_recv.at[0],
            "tensor", 1 - tensor,
        )

    def rows_over():
        held = r.w_full.at[section, theirs, :]
        return remote(
            held, held, r.rows_send.at[1], r.rows_recv.at[1], "section", 1 - section
        )

    def pass_rows(layer_index):
        @pl.when(section == layer_index)
        def _():
            rows_across().wait_recv()
            rows_over().start()

    def have_rows(layer_index):
        @pl.when(section != layer_index)
        def _():
            rows_over().wait_recv()

    @pl.when(section == 0)
    def _():
        rows_across().start()

    for copy in state_copies:
        copy.wait()
    layer[-1][0].wait()
    layer[-1][1].wait()
    first_gain = r.gain.at[0]

    @pl.loop(0, own_count)
    def _(i):
        seq = section * own_count + i
        r.pool_sum[...] = jnp.zeros_like(r.pool_sum)

        def pool(rows):
            block = r.state_in[i, rows, :]
            r.pool_sum[...] += dot(members_of(r, seq, rows, patches), block)
            values = block.astype(f32)
            scale = inverse_rms(values)
            r.byte_norms[i, rows, :] = jnp.broadcast_to(scale, (BLOCK, LANES))
            r.source_in[i, rows, :] = (values * scale * first_gain[1:2, :]).astype(b16)

        each_block(byte_count, pool)
        row_ids = r.ids[pl.ds(seq, 1), :]
        counts = jnp.sum(
            jnp.where(iota((patches, byte_count), 0) == row_ids, 1.0, 0.0), axis=1, keepdims=True
        )
        values = r.pool_sum[...] / jnp.maximum(counts, 1.0)
        r.pooled[i] = values
        scale = inverse_rms(values)
        r.patch_norms[i] = jnp.broadcast_to(scale, (patches, LANES))
        r.query_in[i] = (values * scale * first_gain[0:1, :]).astype(b16)
        save(FIRST_KEPT, i)

    arrived(layer[:4])
    layer_saves = [
        pltpu.make_async_copy(src, dst, r.layer_sem.at[n])
        for n, (src, dst) in enumerate(
            ((r.w_in, r.out_w_in), (r.w_full.at[:, mine, :], r.out_w_out), (r.gain, r.out_gain))
        )
    ]
    for copy in layer_saves:
        copy.start()

    def first_layer(i):
        seq = section * own_count + i
        r.q1[i] = dot(r.query_in[i], r.w_in[0, :, :columns]).astype(b16)

        def project(rows):
            both = dot(r.source_in[i, rows, :], r.w_in[0, :, columns:])
            keys = both[:, :columns].astype(b16)
            r.k1[i, rows, :] = keys
            r.v1[i, rows, :] = both[:, columns:].astype(b16)
            spread = dot_lt(members_of(r, seq, rows, patches), r.q1[i])
            block_scores = dot((spread * keys.astype(f32)).astype(b16), heads_in) * SCALE
            r.scores[:, rows] = block_scores.T[:heads, :]

        each_block(byte_count, project, WIDE)
        scores = r.scores[...]
        r.scores[...] = jnp.exp(scores - segment_max(scores, r.ids[pl.ds(seq, 1), :]))
        r.mix_sum[...] = jnp.zeros_like(r.mix_sum)
        r.total_sum[...] = jnp.zeros_like(r.total_sum)

        def mix(rows):
            short = r.scores[:, rows]
            filled = jnp.concatenate([short, jnp.zeros((LANES - heads, WIDE), f32)], axis=0)
            raised = filled.T.astype(b16)
            r.raised[i, rows, :] = raised
            members = members_of(r, seq, rows, patches)
            weighted = (dot(raised, heads_out) * r.v1[i, rows, :].astype(f32)).astype(b16)
            r.mix_sum[...] += dot(members, weighted)
            r.total_sum[...] += dot(members, raised)

        each_block(byte_count, mix, WIDE)
        totals = r.total_sum[...]
        inverse = jnp.where(totals > 0.0, 1.0 / totals, 0.0)
        r.inverse[i] = inverse
        mixed = (r.mix_sum[...] * split_dot(inverse, heads_out)).astype(b16)
        r.mixed1[i] = mixed
        r.heads_all[0, i, :, mine] = mixed
        exchange(0, i).start()
        save(CROSS_KEPT, i)

    for i in range(own_count):
        first_layer(i)
        if i == 0:
            pl.when(section == 1)(rows_across().start)
            pass_rows(0)

    second_gain = r.gain.at[1]
    allowed = iota((patches, patches), 1) <= iota((patches, patches), 0)
    lane = iota((patches, LANES), 1)

    have_rows(0)

    def second_layer(i):
        exchange(0, i).wait()
        latent = (r.pooled[i] + dot(r.heads_all[0, i], r.w_full[0])).astype(b16)
        r.latent[i] = latent
        values = latent.astype(f32)
        scale = inverse_rms(values)
        r.patch_norms[i] = jnp.where(lane == 1, scale, r.patch_norms[i])
        normed = (values * scale * second_gain[0:1, :]).astype(b16)
        r.normed[i] = normed
        projected = dot(normed, r.w_in[1]).astype(b16)
        query, key, value = [projected[:, j * columns : (j + 1) * columns] for j in range(3)]
        r.q2[i] = query
        r.k2[i] = key
        r.v2[i] = value
        kept = jnp.zeros((patches, LANES), f32)
        outs = []
        for head in range(heads):
            own = slice(head * HD, (head + 1) * HD)
            scores = jnp.where(allowed, dot_rt(query[:, own], key[:, own]) * SCALE, NEGATIVE)
            highest = jnp.max(scores, axis=-1, keepdims=True)
            raised = jnp.exp(scores - highest)
            total = jnp.sum(raised, axis=-1, keepdims=True)
            outs.append(dot((raised / total).astype(b16), value[:, own]))
            kept = jnp.where(lane == head, highest + jnp.log(total), kept)
        r.totals[i] = kept
        mixed = jnp.concatenate(outs, axis=1).astype(b16)
        r.mixed2[i] = mixed
        r.heads_all[1, i, :, mine] = mixed
        exchange(1, i).start()
        save(SECOND_KEPT, i)

    for i in range(own_count):
        second_layer(i)
        if i == 0:
            pass_rows(1)
    have_rows(1)

    for copy in grad_copies + feed_copies:
        copy.wait()

    @pl.loop(0, own_count)
    def _(i):
        seq = section * own_count + i
        exchange(1, i).wait()
        values = r.latent[i].astype(f32) + dot(r.heads_all[1, i], r.w_full[1])
        r.middle[...] = values
        scale = inverse_rms(values)
        r.patch_norms[i] = jnp.where(lane == 2, scale, r.patch_norms[i])
        r.inner[i] = (values * scale * second_gain[1:2, :]).astype(b16)
        valid = iota((patches, 1), 0) <= jnp.max(r.ids[pl.ds(seq, 1), :], axis=1, keepdims=True)
        r.grad_in[i] = jnp.where(valid, r.grad_in[i].astype(f32), 0.0).astype(b16)

        gate = dot(r.inner[i], r.feed_in[0])
        up = dot(r.inner[i], r.feed_in[1])
        hidden_grad = dot_rt(r.grad_in[i], r.feed_out[...])
        gated = 1.0 / (1.0 + jnp.exp(-gate))
        act = gate * gated
        r.hidden[i] = (act * up).astype(b16)
        r.gate_grad[i] = (hidden_grad * up * (gated * (1.0 + gate * (1.0 - gated)))).astype(b16)
        r.up_grad[i] = (hidden_grad * act).astype(b16)
        inner_grad = dot_rt(r.gate_grad[i], r.feed_in[0]) + dot_rt(r.up_grad[i], r.feed_in[1])
        r.inner_part[i] = inner_grad.astype(b16)
        r.out_sum[...] = dot(r.hidden[i], r.feed_out[...])
        r.latent_own[i] = (r.middle[:, mine] + r.out_sum[:, mine]).astype(b16)
        r.latent_send[i] = r.out_sum[:, theirs].astype(b16)
        save(FEED_KEPT, i)

    @pl.loop(0, own_count)
    def _(i):
        for name in KEPT:
            keep(name, i).wait()

    for copy in layer_saves:
        copy.wait()
    rows_across().wait_send()
    rows_over().wait_send()


def shape(dims, dtype):
    return jax.ShapeDtypeStruct(dims, dtype)


def named_call(kernel, ins, outs, scratch, **params):
    any_space = pl.BlockSpec(memory_space=pl.ANY)
    whole = pl.BlockSpec(memory_space=pltpu.VMEM)
    names = [name for name, _, _ in ins] + [name for name, _ in outs] + list(scratch)

    def body(*refs):
        kernel(types.SimpleNamespace(**dict(zip(names, refs, strict=True))))

    got = pl.pallas_call(
        body,
        out_shape=tuple(s for _, s in outs),
        in_specs=[whole if inside else any_space for _, _, inside in ins],
        out_specs=tuple(any_space for _ in outs),
        scratch_shapes=list(scratch.values()),
        compiler_params=pltpu.CompilerParams(
            vmem_limit_bytes=VMEM_BYTES, has_side_effects=True, **params
        ),
    )(*(array for _, array, _ in ins))
    return {name: value for (name, _), value in zip(outs, got, strict=True)}


def forward(byte_states, patch_ids, attn_in, attn_out, gains, feed_in, feed_out, latent_grad):
    sequences, byte_count, width = byte_states.shape
    patches = byte_count // 4
    columns = attn_in.shape[-1]
    hidden = feed_out.shape[0]
    own = sequences // 2
    heads = columns // HD
    dims = dict(
        query_in=(own, patches, width, b16),
        source_in=(own, byte_count, width, b16),
        q1=(own, patches, columns, b16),
        k1=(own, byte_count, columns, b16),
        v1=(own, byte_count, columns, b16),
        raised=(own, byte_count, LANES, b16),
        inverse=(own, patches, LANES, f32),
        mixed1=(own, patches, columns, b16),
        byte_norms=(own, byte_count, LANES, f32),
        normed=(own, patches, width, b16),
        q2=(own, patches, columns, b16),
        k2=(own, patches, columns, b16),
        v2=(own, patches, columns, b16),
        totals=(own, patches, LANES, f32),
        mixed2=(own, patches, columns, b16),
        inner=(own, patches, width, b16),
        hidden=(own, patches, hidden, b16),
        gate_grad=(own, patches, hidden, b16),
        up_grad=(own, patches, hidden, b16),
        grad_in=(own, patches, width, b16),
        inner_part=(own, patches, width, b16),
        patch_norms=(own, patches, LANES, f32),
        latent_own=(own, patches, columns, b16),
        latent_send=(own, patches, columns, b16),
    )
    sems = pltpu.SemaphoreType.DMA
    scratch = {name: pltpu.VMEM(dims[name][:-1], dims[name][-1]) for name in KEPT}
    scratch |= dict(
        state_in=pltpu.VMEM((own, byte_count, width), b16),
        pooled=pltpu.VMEM((own, patches, width), f32),
        latent=pltpu.VMEM((own, patches, width), b16),
        middle=pltpu.VMEM((patches, width), f32),
        out_sum=pltpu.VMEM((patches, width), f32),
        w_in=pltpu.VMEM((2, width, 3 * columns), b16),
        w_full=pltpu.VMEM((2, 2 * columns, width), b16),
        gain=pltpu.VMEM((2, 2, width), f32),
        feed_in=pltpu.VMEM((2, width, hidden), b16),
        feed_out=pltpu.VMEM((hidden, width), b16),
        pool_sum=pltpu.VMEM((patches, width), f32),
        scores=pltpu.VMEM((heads, byte_count), f32),
        mix_sum=pltpu.VMEM((patches, columns), f32),
        total_sum=pltpu.VMEM((patches, LANES), f32),
        heads_all=pltpu.VMEM((2, own, patches, 2 * columns), b16),
        rows_send=sems((2,)),
        rows_recv=sems((2,)),
        state_sem=sems((own,)),
        grad_sem=sems((own,)),
        feed_sem=sems((2,)),
        near_sem=sems((5,)),
        far_send=sems((5,)),
        far_recv=sems((5,)),
        part_send=sems((2, own)),
        part_recv=sems((2, own)),
        keep_sem=sems((len(KEPT), own)),
        layer_sem=sems((len(LAYERS),)),
    )
    ins = [
        ("states", byte_states, False), ("ids", patch_ids, True), ("attn_in", attn_in, False),
        ("attn_out", attn_out, False), ("gains", gains, False), ("ffn_in", feed_in, False),
        ("ffn_out", feed_out, False), ("upstream", latent_grad, False),
    ]
    dims |= dict(
        w_in=(2, width, 3 * columns, b16),
        w_out=(2, columns, width, b16),
        gain=(2, 2, width, f32),
    )
    names = (*KEPT, *LAYERS)
    outs = [("out_" + name, shape(dims[name][:-1], dims[name][-1])) for name in names]
    got = named_call(forward_kernel, ins, outs, scratch, collective_id=0)
    return {name: got["out_" + name] for name in names}


def flat(ref, cols):
    block = ref[:, :, cols]
    return block.reshape(block.shape[0] * block.shape[1], block.shape[2])


LONG, SHORT = 4, 2


def rows_of(ref, start, rows):
    if not isinstance(start, int):
        start = pl.multiple_of(start, 16)
    return ref.at[pl.ds(start, rows), :]


def sum_rows(target, *terms):
    rows, width = target.shape
    step = rows
    while step * width > 100 * 1408 and step % 32 == 0:
        step //= 2

    def add(at):
        value = terms[0][at, :]
        for term in terms[1:]:
            value = value + term[at, :]
        target[at, :] = value

    if step == rows:
        add(slice(None))
    else:
        each_block(rows, add, step)


def add_rows(target, *others):
    sum_rows(target, target, *others)


SHARES = ((512, (384,), (1024,)), (1408, (128,), (256, 128)), (1408, (), (512,)), (1024, (256,), (256,)), (512, (), (512, 512)), (512, (), (512, 512)), (512, (), (512, 512)))
PLAN = ((((1,),(1,)),((),(1,)),((1,),(0,)),((),())),(((0,0,0),(0,0)),((1,),(2,)),((3,4),(1,)),((0,0,0,1),(0,0,0,0,1))),(((2,2,4,0,3),(3,2,2,2)),((0,3),(4,3,0,0,0)),((0,0),(4,0,0,1)),((2,3,2,2,4,5),(4,2,2,3,5,2,2))),(((2,),(4,)),((4,0,0),(5,)),((5,),(0,)),((),())),(((1,1,1,5),(0,3)),((),(2,2)),((2,2),()),((1,1,0,1),())),(((),(0,)),((0,2,2,2),()),((0,0,1,2),(2,2,2)),((2,),())),(((2,),(1,0,2,1,1,5)),((),(0,0,1)),((),(3,)),((),(1,0))),(((3,3),()),((3,2,5,1),(2,4,2,1)),((0,2,2),(4,5,2,2)),((3,0,3,3),())),(((),()),((1,),()),((1,3),(1,)),((),(1,))),(((4,4),()),((4,),()),((4,),()),((4,4),(3,3,1,3))),(((),(0,3,4)),((),()),((),(0,)),((2,),(2,4,4))),(((),()),((0,2),()),((1,1),(3,)),((),())),(((3,4,0),(10,2,11,3,7,8,12,4,4,6,6,6,9,13)),((1,),(7,13,5,9,8,3,12,1,6,1,0,4,6,10,3)),((3,),(12,13,6,7,11,9,10,3,8,5,1,0,4)),((4,),(7,6,11,8,4,9,10,13,12,6,5,6,6))),(((),(5,5)),((),()),((),()),((),(2,5))),(((5,5),(5,)),((3,1),(2,11)),((),(4,)),((5,),())),(((2,),(2,)),((4,),(6,4)),((),(6,2)),((),())),(((),(7,8)),((3,),()),((),()),((5,),(0,1,7,7,7))),(((),()),((4,),(3,2)),((0,),(1,3,7,6,4,3)),((),())),(((),(10,0,6,0,2,8,7,7,8,10)),((4,2),(4,)),((4,4,4,3,3,5,5),()),((1,5),(5,8,8))),(((0,0),(1,)),((5,0,3),(8,0,7,5,0,9,3,8,7,2,10,6,11,2,6)),((),(5,0,2,10,7,8,10,5,0)),((),())),(((),(0,)),((5,),(12,)),((),(2,)),((),(0,))),(((),(9,2,11,9)),((),(10,13,11,5,5,0)),((),(11,13)),((),(10,))),(((5,),()),((),()),((2,),(9,5,6,6,11)),((),(9,9,8,2,2))),(((),()),((0,1),()),((0,),(8,)),((),(11,11,0,10))),(((0,2,2,2,0,1),(2,9)),((),(12,0,7,0,0,9,1,2,2,2)),((),(2,2,0,9,12,12)),((2,),(10,9,11,3,12,0))),(((3,4),(10,11,12,13,11,12,12)),((),(7,)),((),()),((2,0,0,2),(12,2,12))),(((),()),((),(8,13)),((2,),()),((0,4,0,0),())),(((0,),(13,13)),((2,2,0,5),(10,)),((0,5,1,5),(7,8,2,0,0,0,9,8,11)),((3,),(4,13,13))),(((),()),((2,),(9,9)),((0,),(1,)),((2,),())),(((),(0,)),((),(3,)),((),(3,)),((),(0,))),(((),(1,0,4,2)),((),()),((),(13,)),((),(13,0))),(((17,15,2,2,14,21,16,3,18,2,14,20,4,14,14,5),(3,)),((14,18,0,0,15,0,0,20,17,16,2,21,4,5,19,5,14,14,2,2),(11,4)),((4,0,15,0,2,18,0,16,21,17,2,2,20,2,14,14),()),((14,14,14,4,1,2,19,16,3,21,15,18,17,16),())),(((),(2,6,6,8)),((14,14),(5,8,11,6,9,12)),((19,3,14),(2,7,10,5,11,12,4)),((20,5,0,16),(2,2,2,4,6,7,0,8,1,6))),(((16,15,16,17,1,0,15,15,18,18,19,5,17,17,20,21,19,16,20,20,18,19,0,21,2,19),(3,2,5,6,7,10,8,0,9,5,6,4,10,7,11,12,6,6)),((),(13,10,8,13,12,6,7,6,6,6,6,6,10)),((15,14,14),(10,9,10,12,6,7,13,8,6,6,6,9,13)),((19,14,17,15,15,15,21,17,18,16,21,17,18,20,20,20,19,19,18,2,5,0,2),(11,9,5,3,6,6,12,8,13,9,10,7,6))),(((14,14,14,14,21),(6,13,11,9,13)),((15,15,17,16,16,15,15,18,18,17,16,20,20,3,19,19,21,14,16,17,21),()),((5,15,16,2,16,17,17,15,19,15,18,18,14,20,19,20,16,21,21,16,17,15),(6,11,6,6)),((14,14,15,14),(10,6,6,12))),(((16,14,15),()),((18,19,15,14,18,17,20,20),()),((18,19,20,21,17,17,20,19,21,19,14,16),()),((16,),())),(((17,18,16,19,17,14,14,20),(6,)),((14,14,19,17,21,19,21,21,20),()),((14,14,14,18,18,14,21),()),((17,18,19,17,20,14,16,21,15,21),(5,))),(((21,15,18,14),()),((14,16),()),((),()),((20,18,14,14,14,14),(13,))),(((20,21,19),(12,)),((14,14,18),(11,12,13)),((20,14),(12,13)),((21,19),(11,6))))


class Flows:
    def __init__(self, r, section):
        self.r = r
        self.section = section
        place = lax.axis_index("dp")
        self.z, self.y = place // SHORT, lax.rem(place, SHORT)
        self.right, self.left = place + SHORT, place - SHORT
        self.beside = place + 1 - 2 * self.y
        self.flows = []
        self.done = {(z, s): [] for z in range(LONG) for s in range(2)}
        self.points = 0

    def hop(self, src, dst, n, j, target):
        r = self.r
        return pltpu.make_async_remote_copy(
            src_ref=src, dst_ref=dst, send_sem=r.flow_send.at[n, j], recv_sem=r.flow_recv.at[n, j],
            device_id={"dp": target}, device_id_type=MESH,
        )

    def reduce_events(self, n, part, slot):
        def up(k):
            return self.hop(slot(k - 1), slot(k - 1), n, k - 1, self.right)

        def down(k):
            return self.hop(slot(3 + k), slot(3 + k), n, 3 + k, self.left)

        def pass_on(copy, held, k):
            copy(k).wait_recv()
            add_rows(held, part(k))
            copy(k).start()

        def begin(z):
            if z == 0:
                for k in (3, 2, 1):
                    self.hop(part(k), slot(k - 1), n, k - 1, self.right).start()
            if z == 3:
                for k in (0, 1, 2):
                    self.hop(part(k), slot(3 + k), n, 3 + k, self.left).start()

        def passing(at_one, at_two):
            def event(z):
                if z in (1, 2):
                    way, k = (at_one, at_two)[z - 1]
                    pass_on(*((up, slot(k - 1)) if way > 0 else (down, slot(3 + k))), k)

            return event

        def close(z):
            got = []
            if z >= 1:
                up(z).wait_recv()
                got.append(slot(z - 1))
            if z <= 2:
                down(z).wait_recv()
                got.append(slot(3 + z))
            add_rows(part(z), *got)

        def sent(z):
            for k in ((1, 2, 3), (2, 3), (3,), ())[z]:
                up(k).wait_send()
            for k in ((), (0,), (0, 1), (0, 1, 2))[z]:
                down(k).wait_send()

        passes = [
            passing((1, 3), (-1, 0)), passing((1, 2), (-1, 1)), passing((-1, 0), (1, 3)),
        ]
        return begin, passes, close, sent

    def gather_events(self, n, own, out):
        def up(src, k, d):
            return self.hop(src, out(k), n, 7 + d, self.right)

        def down(src, k, d):
            return self.hop(src, out(k), n, 10 + d, self.left)

        def near(z):
            return pltpu.make_async_copy(own(z), out(z), self.r.flow_near.at[n])

        def starts(z, d, way):
            k = z - d * way
            src = own(z) if d == 0 else out(k)
            copies = []
            if d < LONG - 1 and 0 <= z + way < LONG:
                copies.append((up if way > 0 else down)(src, k, d))
            return copies

        def begin(z):
            near(z).start()
            for copy in starts(z, 0, 1) + starts(z, 0, -1):
                copy.start()

        def step(d, way):
            def event(z):
                k = z - d * way
                if 0 <= k < LONG:
                    (up if way > 0 else down)(out(k), k, d - 1).wait_recv()
                    for copy in starts(z, d, way):
                        copy.start()

            return event

        def sent(z):
            near(z).wait()
            for way in (1, -1):
                for d in range(LONG):
                    if 0 <= z - d * way < LONG:
                        for copy in starts(z, d, way):
                            copy.wait_send()

        return begin, [step(d, way) for d in (1, 2, 3) for way in (1, -1)], sent

    def long_first(self, n, data, out, slots, start, rows):
        c = rows // LONG

        def part(k):
            return data(start + k * c, c)

        def slot(j):
            return rows_of(slots, j * c, c)

        def beside(z):
            return self.hop(part(z), slot(6), n, 6, self.beside)

        begin, passes, close, reduce_sent = self.reduce_events(n, part, slot)
        gather, steps, gather_sent = self.gather_events(
            n, lambda z: slot(6), lambda k: out(start + k * c, c)
        )

        def middle(z):
            close(z)
            beside(z).start()

        def turn(z):
            beside(z).wait_recv()
            add_rows(slot(6), part(z))
            gather(z)

        def sent(z):
            reduce_sent(z)
            beside(z).wait_send()
            gather_sent(z)

        return [begin, *passes, middle, turn, *steps], sent

    def short_first(self, n, data, out, slots, start, rows):
        half = rows // SHORT

        def mine(y):
            return data(start + y * half, half)

        def place(y):
            return out(start + y * half, half)

        def slot(j):
            return rows_of(slots, j * half, half)

        def beside():
            return self.hop(mine(1 - self.y), slot(0), n, 6, self.beside)

        inward = (self.right, self.right, self.left, self.left)
        outward = (None, self.left, self.right, None)

        def lean(z):
            middle = 1 if z in (1, 2) else 0
            return self.hop(mine(self.y), slot(1 + middle), n, middle, inward[z])

        def settle(z):
            src = slot(0) if z in (1, 2) else place(self.y)
            return self.hop(src, place(self.y), n, 7, outward[z])

        def near(z):
            return pltpu.make_async_copy(slot(0), place(self.y), self.r.flow_near.at[n])

        def spread(z):
            src = slot(0) if z in (1, 2) else place(self.y)
            return self.hop(src, place(self.y), n, 13, self.beside)

        def first(z):
            beside().start()

        def turn(z):
            beside().wait_recv()
            add_rows(mine(self.y), slot(0))
            if z in (0, 3):
                lean(z).start()

        def pair(z):
            if z in (1, 2):
                self.hop(slot(1), slot(1), n, 0, inward[z]).wait_recv()
                add_rows(mine(self.y), slot(1))
                lean(z).start()

        def close(z):
            if z in (1, 2):
                lean(z).wait_recv()
                sum_rows(slot(0), mine(self.y), slot(2))
                near(z).start()
                settle(z).start()
                spread(z).start()

        def outer(z):
            if z in (0, 3):
                self.hop(place(self.y), place(self.y), n, 7, inward[z]).wait_recv()
                spread(z).start()

        def end(z):
            there = place(1 - self.y)
            self.hop(there, there, n, 13, self.beside).wait_recv()

        def sent(z):
            beside().wait_send()
            lean(z).wait_send()
            spread(z).wait_send()
            if z in (1, 2):
                settle(z).wait_send()
                near(z).wait()

        return [first, turn, pair, close, outer, end], sent

    def open(self, only, *flows):
        for events, sent in flows:
            self.flows.append((only, events, sent))
            for counts in self.done.values():
                counts.append(0)

    def advance(self, z, s, todo):
        def body():
            for n in todo:
                self.flows[n][1][self.done[z, s][n]](z)
                self.done[z, s][n] += 1

        return body

    def point(self):
        plan = PLAN[self.points] if self.points < len(PLAN) else ()
        self.points += 1
        for z, lists in enumerate(plan):
            first, second = self.done[z, 0], self.done[z, 1]
            if lists[0] == lists[1] and all(first[n] == second[n] for n in lists[0]):
                if lists[0]:
                    pl.when(self.z == z)(self.advance(z, 0, lists[0]))
                    for n in lists[0]:
                        second[n] = first[n]
                continue
            for s in range(2):
                here = jnp.logical_and(self.z == z, self.section == s)
                pl.when(here)(self.advance(z, s, lists[s]))

    def drain(self):
        for (z, s), counts in self.done.items():

            def body(z=z, s=s, counts=counts):
                mine = [n for n, flow in enumerate(self.flows) if flow[0] in (None, s)]
                longest = max(len(self.flows[n][1]) for n in mine)
                for k in range(longest):
                    for n in mine:
                        if counts[n] <= k < len(self.flows[n][1]):
                            self.flows[n][1][k](z)
                for n in mine:
                    self.flows[n][2](z)

            pl.when(jnp.logical_and(self.z == z, self.section == s))(body)


def on_grid():
    return lax.axis_size("dp") == LONG * SHORT


def backward_kernel(r):
    section, tensor = lax.axis_index("section"), lax.axis_index("tensor")
    own_count, patches, width = r.normed.shape
    byte_count = r.ids.shape[1]
    columns = r.w_out.shape[0]
    hidden = r.down.shape[0]
    heads = columns // HD
    half = width // 2
    half_bytes = byte_count // 2
    summing = on_grid()
    loads = {}

    def load(name, src, dst, *sem):
        copy = pltpu.make_async_copy(src, dst, r.load_sem.at[sem])
        copy.start()
        loads[name] = copy

    held_names = ("inner", "grad_in", "inner_part", "normed", "patch_norms", "gain")
    for n, name in enumerate(held_names):
        load(name, getattr(r, "in_" + name), getattr(r, name), n)
    load("w_in", r.in_w_in.at[1], r.w_in, 6)
    load("w_out", r.in_w_out.at[1], r.w_out, 7)
    others = [("section", 1 - section), ("tensor", 1 - tensor)]
    flows = Flows(r, section) if summing else None
    if summing:
        greet_grid(flows, others)
    else:
        greet(others)

    def cross(src, dst, i, sem):
        return remote(
            src, dst, r.cross_send.at[sem, i], r.cross_recv.at[sem, i], "tensor", 1 - tensor
        )

    def inner_exchange(i):
        return cross(r.in_inner_part.at[i], r.inner_got.at[i], i, 0)

    def normed_exchange(i):
        return cross(r.normed_part.at[i], r.normed_got.at[i], i, 1)

    def query_exchange(i):
        return cross(r.inner_part.at[i], r.inner_got.at[i], i, 2)

    def source_exchange(i):
        theirs = block_at(1 - tensor, half_bytes)
        return cross(r.source_part.at[i, theirs, :], r.source_got.at[i], i, 3)

    def latent_exchange(i):
        return cross(r.in_latent_send.at[i], r.latent_got.at[i], i, 4)

    for i in range(own_count):
        inner_exchange(i).start()
    def give(n, src, dst):
        return remote(src, dst, r.give_send.at[n], r.give_recv.at[n], "section", 1 - section)

    def point():
        if summing:
            flows.point()

    def summed(n, data, out, only=None):
        if summing:
            for flow, goes_long, slots, start, rows in r.slots[n]:
                make = flows.long_first if goes_long else flows.short_first
                flows.open(only, make(flow, data, out, slots, start, rows))

    def up_half(ref, n):
        return ref.at[pl.ds(n * half, half), :]

    def whole(view):
        return lambda start, rows: rows_of(view(), start, rows)

    @functools.partial(
        pl.run_scoped,
        hidden_all=pltpu.VMEM((own_count, patches, hidden), b16),
        gate_all=pltpu.VMEM((own_count, patches, hidden), b16),
        up_all=pltpu.VMEM((own_count, patches, hidden), b16),
        down_give=pltpu.VMEM((hidden, half), b16),
    )
    def _(hidden_all, gate_all, up_all, down_give):
        parts = {"hidden": hidden_all, "gate_grad": gate_all, "up_grad": up_all}
        for n, (name, ref) in enumerate(parts.items()):
            load(name, getattr(r, "in_" + name), ref, n + 8)
        for name in (*parts, "inner", "grad_in"):
            loads[name].wait()

        def down_grad(target, side):
            upstream = flat(r.grad_in, block_at(side, half))

            def tile(cols):
                target[cols, :] = dot_lt(flat(hidden_all, cols), upstream).astype(b16)

            each_block(hidden, tile)
            if hidden % BLOCK:
                tile(pl.ds(hidden - hidden % BLOCK, hidden % BLOCK))

        def up_grad(target, ref, side):
            upstream = flat(ref, slice(None))

            def tile(rows):
                cols = pl.ds(pl.multiple_of(side * half + rows.start, BLOCK), BLOCK)
                target[rows, :] = dot_lt(flat(r.inner, cols), upstream).astype(b16)

            each_block(half, tile)

        used = pl.ds(0, hidden)
        give_rows = [pl.ds(0, half), pl.ds(half, half)]
        gate_give, up_give = [r.attn_in_part.at[1, rows, used] for rows in give_rows]
        gate_got, up_got = [r.big_got.at[rows, used] for rows in give_rows]
        gate_own, up_own = [r.up.at[rows, :] for rows in give_rows]
        gifts = [
            give(0, down_give, r.down_got), give(1, gate_give, gate_got), give(2, up_give, up_got)
        ]
        other = 1 - section
        down_grad(down_give, other)
        gifts[0].start()
        down_grad(r.down, section)
        up_grad(gate_give, gate_all, other)
        gifts[1].start()
        gifts[0].wait()
        add_rows(r.down, r.down_got)
        summed(0, whole(lambda: r.down), whole(lambda: r.down_sum))
        point()
        up_grad(gate_own, gate_all, section)
        up_grad(up_give, up_all, other)
        gifts[2].start()
        gifts[1].wait()
        add_rows(gate_own, gate_got)
        summed(1, whole(lambda: up_half(r.up, 0)), whole(lambda: up_half(r.up_sum, 0)))
        point()
        up_grad(up_own, up_all, section)
        gifts[2].wait()
        add_rows(up_own, up_got)
        summed(2, whole(lambda: up_half(r.up, 1)), whole(lambda: up_half(r.up_sum, 1)))
        point()
        pl.semaphore_signal(
            r.free_sem, inc=1, device_id={"section": other}, device_id_type=MESH
        )

    def gifts_of(layer):
        return [
            give(3, r.attn_in_part.at[layer], r.big_got),
            give(4, r.attn_out_part.at[layer], r.attn_out_got),
        ]

    def hand_over(layer):
        @pl.when(section != layer)
        def _():
            pl.semaphore_wait(r.free_sem, 1)
            for gift in gifts_of(layer):
                gift.start()

    def take_over(layer):
        @pl.when(section != layer)
        def _():
            for gift in gifts_of(layer):
                gift.wait_send()

        @pl.when(section == layer)
        def _():
            for gift in gifts_of(layer):
                gift.wait_recv()
            add_rows(r.attn_out_part.at[layer], r.attn_out_got)
            add_rows(r.attn_in_part.at[layer], r.big_got)

    def sum_layer(layer, which):
        def columns_of(j):
            return whole(lambda: r.attn_in_part.at[layer, :, pl.ds(j * columns, columns)])

        if which == 3:
            summed(
                3, whole(lambda: r.attn_out_part.at[layer]), whole(lambda: r.attn_out_sum), layer
            )
        else:
            summed(4 + which, columns_of(which), whole(lambda: r.attn_in_sum.at[which]), layer)

    first_gain, second_gain = r.gain.at[0], r.gain.at[1]

    def back_through(normed, gain_row, scale, upstream):
        unit = normed.astype(f32) / gain_row
        scaled = upstream * gain_row
        mean = jnp.mean(unit * scaled, axis=-1, keepdims=True)
        return (scaled - unit * mean) * scale, unit

    @functools.partial(
        pl.run_scoped,
        q2=pltpu.VMEM((own_count, patches, columns), b16),
        k2=pltpu.VMEM((own_count, patches, columns), b16),
        v2=pltpu.VMEM((own_count, patches, columns), b16),
        totals=pltpu.VMEM((own_count, patches, LANES), f32),
        mixed2=pltpu.VMEM((own_count, patches, columns), b16),
        second_grads=pltpu.VMEM((own_count, patches, 3 * columns), b16),
        mixed_grads=pltpu.VMEM((patches, columns), b16),
    )
    def _(q2, k2, v2, totals, mixed2, second_grads, mixed_grads):
        parts = {"q2": q2, "k2": k2, "v2": v2, "totals": totals, "mixed2": mixed2}
        for n, (name, ref) in enumerate(parts.items()):
            load(name, getattr(r, "in_" + name), ref, n + 11)
        for name in (*held_names[2:], "w_in", "w_out", *parts):
            loads[name].wait()
        r.gain_sum[...] = jnp.zeros_like(r.gain_sum)
        allowed = iota((patches, patches), 1) <= iota((patches, patches), 0)
        for i in range(own_count):
            inner_exchange(i).wait()
            own_part = r.inner_part[i].astype(f32)
            back, unit = back_through(
                r.inner[i], second_gain[1:2, :], r.patch_norms[i, :, 2:3],
                own_part + r.inner_got[i].astype(f32),
            )
            r.gain_sum[3:4, :] += jnp.sum(unit * own_part, axis=0, keepdims=True)
            branch = (r.grad_in[i].astype(f32) + back).astype(b16)
            r.branch[i] = branch
            mixed_grads[...] = dot_rt(branch, r.w_out[...]).astype(b16)
            point()

            mixed_grad = mixed_grads[...]
            outs = [[], [], []]
            for head in range(heads):
                own = slice(head * HD, (head + 1) * HD)
                query, key, value = q2[i, :, own], k2[i, :, own], v2[i, :, own]
                upper = mixed_grad[:, own]
                scores = jnp.where(allowed, dot_rt(query, key) * SCALE, NEGATIVE)
                probs = jnp.exp(scores - totals[i, :, head : head + 1])
                prob_grad = dot_rt(upper, value)
                delta = jnp.sum(probs * prob_grad, axis=-1, keepdims=True)
                score_grad = (probs * (prob_grad - delta)).astype(b16)
                outs[0].append(dot(score_grad, key) * SCALE)
                outs[1].append(dot_lt(score_grad, query) * SCALE)
                outs[2].append(dot_lt(probs.astype(b16), upper))
            grads = jnp.concatenate(outs[0] + outs[1] + outs[2], axis=1).astype(b16)
            second_grads[i] = grads
            point()
            r.normed_part[i] = dot_rt(grads, r.w_in[...]).astype(b16)
            normed_exchange(i).start()
            point()

        def outer(target, rows_ref, upstream, tiles):
            @pl.loop(0, tiles)
            def _(t):
                cols = block_at(t)
                target[cols, :] = dot_lt(flat(rows_ref, cols), upstream).astype(b16)

        outer(r.attn_in_part.at[1], r.normed, flat(second_grads, slice(None)), width // BLOCK)
        point()
        outer(r.attn_out_part.at[1], mixed2, flat(r.branch, slice(None)), columns // BLOCK)
        hand_over(1)
        point()

    heads_in, heads_out = head_masks(columns)

    def first_layer(i, scoped):
        seq = section * own_count + i
        s = types.SimpleNamespace(**scoped)
        copies = {}
        kinds = names(q1=1, v1=1, raised=1, inverse=1, mixed1=1, source_in=1, query_in=1)
        for n, name in enumerate(kinds):
            copy = pltpu.make_async_copy(
                getattr(r, "in_" + name).at[i], getattr(s, name), r.first_sem.at[n]
            )
            copy.start()
            copies[name] = copy
        normed_exchange(i).wait()
        own_part = r.normed_part[i].astype(f32)
        back, unit = back_through(
            r.normed[i], second_gain[0:1, :], r.patch_norms[i, :, 1:2],
            own_part + r.normed_got[i].astype(f32),
        )
        r.gain_sum[2:3, :] += jnp.sum(unit * own_part, axis=0, keepdims=True)
        branch = (r.branch[i].astype(f32) + back).astype(b16)
        r.branch[i] = branch
        s.mixed_grad[...] = dot_rt(branch, r.w_out[...]).astype(b16)
        s.q_sum[...] = jnp.zeros_like(s.q_sum)
        s.delta_sum[...] = jnp.zeros_like(s.delta_sum)
        for copy in copies.values():
            copy.wait()
        point()
        if i == 0:
            take_over(1)
            for which in (3, 0, 1, 2):
                sum_layer(1, which)
            point()
        inverse = s.inverse[...]
        inverse_high = inverse.astype(b16)
        inverse_low = (inverse - inverse_high.astype(f32)).astype(b16)

        def value_side(rows):
            members = members_of(r, seq, rows, patches)
            spread = dot_lt(members, s.mixed_grad[...])
            scale = dot_lt(members, inverse_high) + dot_lt(members, inverse_low)
            probs = s.raised[rows, :].astype(f32) * scale
            s.probs[rows, :] = probs
            s.dkv[rows, columns:] = (dot(probs.astype(b16), heads_out) * spread).astype(b16)
            prob_grad = dot((spread * s.v1[rows, :].astype(f32)).astype(b16), heads_in)
            s.prob_grad[rows, :] = prob_grad
            product = probs * prob_grad
            high = product.astype(b16)
            low = (product - high.astype(f32)).astype(b16)
            s.delta_sum[...] += dot(members, high) + dot(members, low)

        for t in range(byte_count // WIDE):
            value_side(pl.ds(t * WIDE, WIDE))
            point()
        keys = pltpu.make_async_copy(r.in_k1.at[i], s.v1, r.first_sem.at[7])
        keys.start()
        delta = s.delta_sum[...]
        delta_high = delta.astype(b16)
        delta_low = (delta - delta_high.astype(f32)).astype(b16)

        def key_side(rows):
            members = members_of(r, seq, rows, patches)
            shift = dot_lt(members, delta_high) + dot_lt(members, delta_low)
            score_grad = (s.probs[rows, :] * (s.prob_grad[rows, :] - shift)).astype(b16)
            spread = dot(score_grad, heads_out)
            s.dkv[rows, :columns] = (spread * dot_lt(members, s.q1[...]) * SCALE).astype(b16)
            s.q_sum[...] += dot(members, (spread * s.v1[rows, :].astype(f32)).astype(b16))
            source = dot_rt(s.dkv[rows, :], r.w_in[:, columns:])
            r.source_part[i, rows, :] = source.astype(b16)
            unit_block = s.source_in[rows, :].astype(f32)
            r.gain_sum[1:2, :] += (
                jnp.sum(unit_block * source, axis=0, keepdims=True) / first_gain[1:2, :]
            )

        keys.wait()
        for t in range(byte_count // WIDE):
            for u in range(WIDE // BLOCK):
                key_side(pl.ds(t * WIDE + u * BLOCK, BLOCK))
            point()
        source_exchange(i).start()
        q_grad = (s.q_sum[...] * SCALE).astype(b16)
        query = dot_rt(q_grad, r.w_in[:, :columns])
        r.inner_part[i] = query.astype(b16)
        query_exchange(i).start()
        unit_pool = s.query_in[...].astype(f32)
        r.gain_sum[0:1, :] += (
            jnp.sum(unit_pool * query, axis=0, keepdims=True) / first_gain[0:1, :]
        )
        point()

        def add_to(target, rows, cols, value):
            if i:
                value = target[rows, cols].astype(f32) + value
            target[rows, cols] = value.astype(b16)

        for half_t in range(2):

            @pl.loop(0, half // BLOCK)
            def _(t, half_t=half_t):
                cols = pl.ds(pl.multiple_of(half_t * half + t * BLOCK, BLOCK), BLOCK)
                source = s.source_in[:, cols]
                target = r.attn_in_part.at[0]
                add_to(target, cols, slice(0, columns), dot_lt(s.query_in[:, cols], q_grad))
                add_to(target, cols, slice(columns, 3 * columns), dot_lt(source, s.dkv[...]))

            point()

        @pl.loop(0, columns // BLOCK)
        def _(t):
            cols = block_at(t)
            add_to(
                r.attn_out_part.at[0], cols, slice(None), dot_lt(s.mixed1[:, cols], branch)
            )

        point()

    def last_parts(s):
        outs = []

        own_rows = block_at(tensor, half_bytes)
        cols_keep, cols_give = block_at(section, half), block_at(1 - section, half)
        for i in range(own_count):
            seq = section * own_count + i
            finals = [
                pltpu.make_async_copy(
                    r.in_source_in.at[i, own_rows, :], s.source_in, r.first_sem.at[0]
                ),
                pltpu.make_async_copy(
                    r.in_byte_norms.at[i, own_rows, :], s.byte_norms, r.first_sem.at[1]
                ),
                pltpu.make_async_copy(r.in_query_in.at[i], s.query_in, r.first_sem.at[2]),
            ]
            for copy in finals:
                copy.start()
            query_exchange(i).wait()
            source_exchange(i).wait()
            for copy in finals:
                copy.wait()
            back, _ = back_through(
                s.query_in[...], first_gain[0:1, :], r.patch_norms[i, :, 0:1],
                r.inner_part[i].astype(f32) + r.inner_got[i].astype(f32),
            )
            counts = jnp.sum(
                jnp.where(iota((patches, byte_count), 0) == r.ids[pl.ds(seq, 1), :], 1.0, 0.0),
                axis=1, keepdims=True,
            )
            pool_grad = (r.branch[i].astype(f32) + back) / jnp.maximum(counts, 1.0)
            high = pool_grad.astype(b16)
            s.pool_high[...] = high
            s.pool_low[...] = (pool_grad - high.astype(f32)).astype(b16)

            @pl.loop(0, half_bytes // BLOCK)
            def _(t, i=i, seq=seq):
                rows = block_at(t)
                place = pl.ds(pl.multiple_of(tensor * half_bytes + t * BLOCK, BLOCK), BLOCK)
                members = members_of(r, seq, place, patches)
                spread = dot_lt(members, s.pool_high[...]) + dot_lt(members, s.pool_low[...])
                part = r.source_part[i, place, :].astype(f32)
                own, _ = back_through(
                    s.source_in[rows, :], first_gain[1:2, :], s.byte_norms[rows, 0:1],
                    part + r.source_got[i, rows, :].astype(f32),
                )
                r.source_got[i, rows, :] = (own + spread).astype(b16)

            near = pltpu.make_async_copy(
                r.source_got.at[i, :, cols_keep], r.byte_grad.at[seq], r.out_sem.at[1, i]
            )
            far = remote(
                r.source_got.at[i, :, cols_give], r.byte_grad.at[seq],
                r.out_send.at[1, i], r.out_recv.at[1, i], "section", 1 - section,
            )
            near.start()
            far.start()
            outs += [near, far]
            point()

        half_rows = patches // 2
        rows_keep, rows_give = block_at(section, half_rows), block_at(1 - section, half_rows)
        for i in range(own_count):
            seq = section * own_count + i
            s_load = pltpu.make_async_copy(r.in_latent_own.at[i], s.latent.at[i], r.first_sem.at[i])
            s_load.start()
            s_load.wait()
            latent_exchange(i).wait()
            last = jnp.max(r.ids[pl.ds(seq, 1), :], axis=1, keepdims=True)
            valid = iota((patches, 1), 0) <= last
            values = s.latent[i].astype(f32) + r.latent_got[i].astype(f32)
            s.latent[i] = jnp.where(valid, values, 0.0).astype(b16)
            near = pltpu.make_async_copy(
                s.latent.at[i, rows_keep, :], r.latents.at[seq], r.out_sem.at[0, i]
            )
            far = remote(
                s.latent.at[i, rows_give, :], r.latents.at[seq],
                r.out_send.at[0, i], r.out_recv.at[0, i], "section", 1 - section,
            )
            near.start()
            far.start()
            outs += [near, far]
        for copy in outs:
            copy.wait()

    load("w_in", r.in_w_in.at[0], r.w_in, 6)
    load("w_out", r.in_w_out.at[0], r.w_out, 7)
    loads["w_in"].wait()
    loads["w_out"].wait()
    one = dict(
        source_in=pltpu.VMEM((byte_count, width), b16),
        v1=pltpu.VMEM((byte_count, columns), b16),
        dkv=pltpu.VMEM((byte_count, 2 * columns), b16),
        probs=pltpu.VMEM((byte_count, LANES), f32),
        prob_grad=pltpu.VMEM((byte_count, LANES), f32),
        raised=pltpu.VMEM((byte_count, LANES), b16),
        inverse=pltpu.VMEM((patches, LANES), f32),
        q1=pltpu.VMEM((patches, columns), b16),
        mixed1=pltpu.VMEM((patches, columns), b16),
        query_in=pltpu.VMEM((patches, width), b16),
        mixed_grad=pltpu.VMEM((patches, columns), b16),
        q_sum=pltpu.VMEM((patches, columns), f32),
        delta_sum=pltpu.VMEM((patches, LANES), f32),
    )

    @functools.partial(pl.run_scoped, **one)
    def _(**scoped):
        for i in range(own_count):
            first_layer(i, scoped)

    hand_over(0)
    for i in range(own_count):
        latent_exchange(i).start()
    point()
    take_over(0)
    for which in (3, 0, 1, 2):
        sum_layer(0, which)
    point()
    gains = Gains(r, section, tensor, flows) if summing else None
    if summing:
        gains.tick()
    last = dict(
        source_in=pltpu.VMEM((half_bytes, width), b16),
        byte_norms=pltpu.VMEM((half_bytes, LANES), f32),
        query_in=pltpu.VMEM((patches, width), b16),
        pool_high=pltpu.VMEM((patches, width), b16),
        pool_low=pltpu.VMEM((patches, width), b16),
        latent=pltpu.VMEM((own_count, patches, columns), b16),
    )

    @functools.partial(pl.run_scoped, **last)
    def _(**scoped):
        last_parts(types.SimpleNamespace(**scoped))

    if summing:
        while gains.steps:
            gains.tick()
            point()
        flows.drain()
    ends = [pltpu.make_async_copy(r.gain_sum, r.gain_out, r.end_sem.at[4])]
    if not summing:
        ends += [
            pltpu.make_async_copy(r.up, r.up_sum, r.end_sem.at[0]),
            pltpu.make_async_copy(r.down, r.down_sum, r.end_sem.at[1]),
            pltpu.make_async_copy(r.attn_out_part.at[section], r.attn_out_sum, r.end_sem.at[3]),
        ]
        ends += [
            pltpu.make_async_copy(
                r.attn_in_part.at[section, :, pl.ds(j * columns, columns)], r.attn_in_sum.at[j],
                r.end_sem.at[5 + j],
            )
            for j in range(3)
        ]
    for copy in ends:
        copy.start()
    for copy in ends:
        copy.wait()


class Gains:
    def __init__(self, r, section, tensor, flows):
        self.r = r
        z = flows.z
        place = lax.axis_index("dp")
        near = place + SHORT * (1 - 2 * lax.rem(z, 2))
        far = place + 2 * SHORT * (1 - 2 * (z // 2))
        self.targets = [
            {"tensor": 1 - tensor}, {"section": 1 - section}, {"dp": flows.beside},
            {"dp": near}, {"dp": far},
        ]
        self.steps = list(range(len(self.targets) + 1))

    def copy(self, n):
        r = self.r
        return pltpu.make_async_remote_copy(
            src_ref=r.gain_held.at[n], dst_ref=r.gain_got.at[n], send_sem=r.gain_send.at[n],
            recv_sem=r.gain_recv.at[n], device_id=self.targets[n], device_id_type=MESH,
        )

    def tick(self):
        if not self.steps:
            return
        r, n = self.r, self.steps.pop(0)
        if n == 0:
            r.gain_held[0] = r.gain_sum[...]
        else:
            self.copy(n - 1).wait()
            value = r.gain_held[n - 1] + r.gain_got[n - 1]
            if n < len(self.targets):
                r.gain_held[n] = value
            else:
                r.gain_sum[...] = value
        if n < len(self.targets):
            self.copy(n).start()


def greet_grid(flows, others):
    barrier = pltpu.get_barrier_semaphore()

    def signal(place):
        pl.semaphore_signal(barrier, inc=1, device_id=place, device_id_type=MESH)

    for axis, index in others:
        signal({axis: index})
    signal({"dp": flows.beside})
    signal({"dp": lax.axis_index("dp") + 2 * SHORT * (1 - 2 * (flows.z // 2))})
    pl.when(flows.z < LONG - 1)(lambda: signal({"dp": flows.right}))
    pl.when(flows.z > 0)(lambda: signal({"dp": flows.left}))
    inner = jnp.logical_and(flows.z > 0, flows.z < LONG - 1)
    pl.semaphore_wait(barrier, jnp.where(inner, len(others) + 4, len(others) + 3))


def backward(kept, patch_ids):
    own, patches, width = kept["normed"].shape
    sequences, byte_count = patch_ids.shape
    columns = kept["q1"].shape[-1]
    hidden = kept["hidden"].shape[-1]
    half, half_bytes = width // 2, byte_count // 2
    sems = pltpu.SemaphoreType.DMA
    vmem = pltpu.VMEM
    rows16 = vmem((own, patches, width), b16)
    scratch = dict(
        inner=rows16,
        grad_in=rows16,
        inner_part=rows16,
        inner_got=rows16,
        normed=rows16,
        patch_norms=vmem((own, patches, LANES), f32),
        branch=rows16,
        normed_part=rows16,
        normed_got=rows16,
        source_part=vmem((own, byte_count, width), b16),
        source_got=vmem((own, half_bytes, width), b16),
        latent_got=vmem((own, patches, columns), b16),
        w_in=vmem((width, 3 * columns), b16),
        w_out=vmem((columns, width), b16),
        gain=vmem((2, 2, width), f32),
        gain_sum=vmem((4, width), f32),
        down_got=vmem((hidden, half), b16),
        down=vmem((hidden, half), b16),
        up=vmem((width, hidden), b16),
        attn_in_part=vmem((2, width, 3 * columns), b16),
        attn_out_part=vmem((2, columns, width), b16),
        big_got=vmem((width, 3 * columns), b16),
        attn_out_got=vmem((columns, width), b16),
        load_sem=sems((16,)),
        first_sem=sems((8,)),
        cross_send=sems((5, own)),
        cross_recv=sems((5, own)),
        give_send=sems((5,)),
        give_recv=sems((5,)),
        out_sem=sems((2, own)),
        out_send=sems((2, own)),
        out_recv=sems((2, own)),
        end_sem=sems((8,)),
        free_sem=pltpu.SemaphoreType.REGULAR,
    )
    slots = []
    if on_grid():
        shares = SHARES
        count = 0
        for n, (cols, long, short) in enumerate(shares):
            start = 0
            for goes_long, rows in [(1, k) for k in long] + [(0, k) for k in short]:
                name = f"s{count}"
                held = 7 * rows // LONG if goes_long else 3 * rows // SHORT
                scratch[name] = vmem((held, cols), b16)
                slots.append((n, count, goes_long, name, start, rows))
                start += rows
                count += 1
        scratch |= dict(
            flow_send=sems((count, 17)),
            flow_recv=sems((count, 17)),
            flow_near=sems((count,)),
            gain_held=vmem((5, 4, width), f32),
            gain_got=vmem((5, 4, width), f32),
            gain_send=sems((5,)),
            gain_recv=sems((5,)),
        )
    ins = [("ids", patch_ids, True)]
    ins += [("in_" + name, kept[name], False) for name in (*KEPT, *LAYERS)]
    outs = [
        ("latents", shape((sequences, patches // 2, columns), b16)),
        ("byte_grad", shape((sequences, half_bytes, half), b16)),
        ("attn_in_sum", shape((3, width, columns), b16)),
        ("attn_out_sum", shape((columns, width), b16)),
        ("gain_out", shape((4, width), f32)),
        ("up_sum", shape((width, hidden), b16)),
        ("down_sum", shape((hidden, half), b16)),
    ]

    def kernel(r):
        r.slots = {}
        for n, count, goes_long, name, start, rows in slots:
            r.slots.setdefault(n, []).append((count, goes_long, getattr(r, name), start, rows))
        backward_kernel(r)

    return named_call(kernel, ins, outs, scratch, collective_id=1)


def widen(up, attn_in, attn_out, down):
    half, hidden = up.shape[0] // 2, up.shape[1]
    steps = 8
    flat_in = attn_in.reshape(-1, attn_in.shape[2])

    def rows(array, offset=0):
        count = array.shape[0] // steps
        return pl.BlockSpec((count, array.shape[1]), lambda t: (t + offset, 0))

    def body(gate_in, up_in, in_in, out_in, down_in, up_o, in_o, out_o, down_o):
        up_o[:, 0, :] = gate_in[...].astype(f32)
        up_o[:, 1, :] = up_in[...].astype(f32)
        for src, dst in ((in_in, in_o), (out_in, out_o), (down_in, down_o)):
            dst[...] = src[...].astype(f32)

    part = half // steps
    feed = [pl.BlockSpec((part, hidden), lambda t: (t, 0))]
    feed += [pl.BlockSpec((part, hidden), lambda t: (t + steps, 0))]
    up_out, in_out, out_out, down_out = pl.pallas_call(
        body,
        grid=(steps,),
        out_shape=(
            shape((half, 2, hidden), f32), shape(flat_in.shape, f32), shape(attn_out.shape, f32),
            shape(down.shape, f32),
        ),
        in_specs=[*feed, rows(flat_in), rows(attn_out), rows(down)],
        out_specs=(
            pl.BlockSpec((part, 2, hidden), lambda t: (t, 0, 0)),
            rows(flat_in), rows(attn_out), rows(down),
        ),
        compiler_params=pltpu.CompilerParams(vmem_limit_bytes=VMEM_BYTES),
    )(up, up, flat_in, attn_out, down)
    return up_out, in_out.reshape(attn_in.shape), out_out, down_out


def swap(values, axis):
    return lax.ppermute(values, axis, [(0, 1), (1, 0)])


def sum_small(values):
    values = values + swap(values, "tensor")
    values = values + swap(values, "section")
    return lax.psum(values, "dp")


def per_device(byte_states, patch_ids, attn_in, attn_out, gains, ffn_in, ffn_out, latent_grad):
    is_first = lax.axis_index("section") == 0
    kept = forward(
        byte_states, patch_ids, attn_in, attn_out, gains, ffn_in.transpose(1, 0, 2), ffn_out,
        latent_grad,
    )
    got = backward(kept, patch_ids)
    sums = [got[name] for name in ("down_sum", "up_sum", "attn_in_sum", "attn_out_sum")]
    if not on_grid():
        sums = [lax.psum(value, "dp") for value in sums]
    down, up, in_sum, out_sum = sums
    up_out, in_sum, out_sum, down = widen(up, in_sum, out_sum, down)
    gain_sum = got["gain_out"] if on_grid() else sum_small(got["gain_out"])
    gain_out = jnp.where(is_first, gain_sum[0:2], gain_sum[2:4])
    return (
        got["latents"], got["byte_grad"], in_sum[None], out_sum[None], gain_out[None], up_out, down
    )


def solution(mesh):
    return jax.shard_map(
        per_device,
        mesh=mesh,
        in_specs=(
            P("dp", None, None),
            P("dp", None),
            P("section", None, None, "tensor"),
            P("section", "tensor", None),
            P("section", None, None),
            P(None, None, "tensor"),
            P("tensor", None),
            P("dp", None, None),
        ),
        out_specs=(
            P("dp", "section", "tensor"),
            P("dp", "tensor", "section"),
            P("section", None, None, "tensor"),
            P("section", "tensor", None),
            P("section", None, None),
            P("section", None, "tensor"),
            P("tensor", "section"),
        ),
        check_vma=False,
    )
```

```python
import functools
import types

import jax
import jax.numpy as jnp
from jax import lax
from jax.experimental import pallas as pl
from jax.experimental.pallas import tpu as pltpu
from jax.sharding import PartitionSpec as P

HD = 64
LANES = 128
BLOCK = 256
WIDE = 512
EPSILON = 1e-05
NEGATIVE = -1000000000.0
SCALE = HD ** (-0.5)
VMEM_BYTES = 63 * 1024 * 1024

f32 = jnp.float32
b16 = jnp.bfloat16


def dot(a, b):
    return jnp.dot(a, b, preferred_element_type=f32)


def dot_rt(a, b):
    return lax.dot_general(a, b, (((1,), (1,)), ((), ())), preferred_element_type=f32)


def dot_lt(a, b):
    return lax.dot_general(a, b, (((0,), (0,)), ((), ())), preferred_element_type=f32)


def inverse_rms(values):
    return lax.rsqrt(jnp.mean(values * values, axis=-1, keepdims=True) + EPSILON)


def iota(shape, dim):
    return lax.broadcasted_iota(jnp.int32, shape, dim)


def one_hot(condition):
    return jnp.where(condition, 1.0, 0.0).astype(b16)


def segment_max(values, ids):
    width = values.shape[1]
    lane = iota(ids.shape, 1)
    lowest = -3.0e38
    ahead, behind = values, values
    step = 1
    while step < width:
        left, right = step, width - step
        same_left = jnp.logical_and(pltpu.roll(ids, left, axis=1) == ids, lane >= step)
        same_right = jnp.logical_and(pltpu.roll(ids, right, axis=1) == ids, lane < right)
        ahead = jnp.maximum(ahead, jnp.where(same_left, pltpu.roll(ahead, left, axis=1), lowest))
        behind = jnp.maximum(
            behind, jnp.where(same_right, pltpu.roll(behind, right, axis=1), lowest)
        )
        step *= 2
    return jnp.maximum(ahead, behind)


def head_masks(width):
    heads_in = one_hot(iota((width, LANES), 0) // HD == iota((width, LANES), 1))
    heads_out = one_hot(iota((LANES, width), 1) // HD == iota((LANES, width), 0))
    return heads_in, heads_out


def split_dot(values, matrix):
    high = values.astype(b16)
    low = (values - high.astype(f32)).astype(b16)
    return dot(high, matrix) + dot(low, matrix)


def block_at(index, size=BLOCK):
    return pl.ds(pl.multiple_of(index * size, size), size)


def each_block(count, body, size=BLOCK):
    @pl.loop(0, count // size)
    def _(index):
        body(block_at(index, size))


MESH = pl.DeviceIdType.MESH


def remote(src, dst, send, recv, axis, index):
    return pltpu.make_async_remote_copy(
        src_ref=src, dst_ref=dst, send_sem=send, recv_sem=recv,
        device_id={axis: index}, device_id_type=MESH,
    )


def greet(places):
    barrier = pltpu.get_barrier_semaphore()
    for axis, index in places:
        pl.semaphore_signal(barrier, inc=1, device_id={axis: index}, device_id_type=MESH)
    pl.semaphore_wait(barrier, len(places))


def exchange_layer(r, section, tensor):
    columns = r.attn_in.shape[3]
    copies = []
    for n, (src, dst) in enumerate(
        [
            (r.attn_in.at[0, j], r.w_in.at[section, :, pl.ds(j * columns, columns)])
            for j in (1, 2, 0)
        ]
        + [
            (r.attn_out.at[0], r.w_full.at[section, block_at(tensor, columns), :]),
            (r.gains.at[0], r.gain.at[section]),
        ]
    ):
        near = pltpu.make_async_copy(src, dst, r.near_sem.at[n])
        far = remote(src, dst, r.far_send.at[n], r.far_recv.at[n], "section", 1 - section)
        near.start()
        far.start()
        copies.append((near, far))
    return copies


def arrived(copies):
    for near, far in copies:
        near.wait()
        far.wait()


def members_of(r, seq, rows, patches):
    return one_hot(iota((patches, rows.size), 0) == r.ids[pl.ds(seq, 1), rows])


def names(**kinds):
    return tuple(kinds)


FIRST_KEPT = names(query_in=1, source_in=1, byte_norms=1)
CROSS_KEPT = names(q1=1, k1=1, v1=1, raised=1, inverse=1, mixed1=1)
SECOND_KEPT = names(normed=1, q2=1, k2=1, v2=1, totals=1, mixed2=1)
FEED_KEPT = names(
    inner=1, hidden=1, gate_grad=1, up_grad=1, grad_in=1, inner_part=1, patch_norms=1,
    latent_own=1, latent_send=1,
)
KEPT = FIRST_KEPT + CROSS_KEPT + SECOND_KEPT + FEED_KEPT
LAYERS = names(w_in=1, w_out=1, gain=1)


def forward_kernel(r):
    section, tensor = lax.axis_index("section"), lax.axis_index("tensor")
    own_count, patches, width = r.normed.shape
    byte_count = r.states.shape[1]
    columns = r.q1.shape[2]
    hidden = r.hidden.shape[2]
    heads = columns // HD
    greet([("section", 1 - section), ("tensor", 1 - tensor)])
    state_copies = [
        pltpu.make_async_copy(
            r.states.at[section * own_count + i], r.state_in.at[i], r.state_sem.at[i]
        )
        for i in range(own_count)
    ]
    for copy in state_copies:
        copy.start()
    layer = exchange_layer(r, section, tensor)
    grad_copies = [
        pltpu.make_async_copy(
            r.upstream.at[section * own_count + i], r.grad_in.at[i], r.grad_sem.at[i]
        )
        for i in range(own_count)
    ]
    feed_copies = [
        pltpu.make_async_copy(r.ffn_in, r.feed_in, r.feed_sem.at[0]),
        pltpu.make_async_copy(r.ffn_out, r.feed_out, r.feed_sem.at[1]),
    ]
    for copy in grad_copies + feed_copies:
        copy.start()
    heads_in, heads_out = head_masks(columns)

    def keep(name, i):
        n = KEPT.index(name)
        return pltpu.make_async_copy(
            getattr(r, name).at[i], getattr(r, "out_" + name).at[i], r.keep_sem.at[n, i]
        )

    def save(names, i):
        for name in names:
            keep(name, i).start()

    mine, theirs = block_at(tensor, columns), block_at(1 - tensor, columns)

    def exchange(step, i):
        held = r.heads_all.at[step, i, :, mine]
        return remote(
            held, held, r.part_send.at[step, i], r.part_recv.at[step, i], "tensor", 1 - tensor
        )

    def rows_across():
        return remote(
            r.attn_out.at[0], r.w_full.at[section, mine, :], r.rows_send.at[0], r.rows_recv.at[0],
            "tensor", 1 - tensor,
        )

    def rows_over():
        held = r.w_full.at[section, theirs, :]
        return remote(
            held, held, r.rows_send.at[1], r.rows_recv.at[1], "section", 1 - section
        )

    def pass_rows(layer_index):
        @pl.when(section == layer_index)
        def _():
            rows_across().wait_recv()
            rows_over().start()

    def have_rows(layer_index):
        @pl.when(section != layer_index)
        def _():
            rows_over().wait_recv()

    @pl.when(section == 0)
    def _():
        rows_across().start()

    for copy in state_copies:
        copy.wait()
    layer[-1][0].wait()
    layer[-1][1].wait()
    first_gain = r.gain.at[0]

    @pl.loop(0, own_count)
    def _(i):
        seq = section * own_count + i
        r.pool_sum[...] = jnp.zeros_like(r.pool_sum)

        def pool(rows):
            block = r.state_in[i, rows, :]
            r.pool_sum[...] += dot(members_of(r, seq, rows, patches), block)
            values = block.astype(f32)
            scale = inverse_rms(values)
            r.byte_norms[i, rows, :] = jnp.broadcast_to(scale, (BLOCK, LANES))
            r.source_in[i, rows, :] = (values * scale * first_gain[1:2, :]).astype(b16)

        each_block(byte_count, pool)
        row_ids = r.ids[pl.ds(seq, 1), :]
        counts = jnp.sum(
            jnp.where(iota((patches, byte_count), 0) == row_ids, 1.0, 0.0), axis=1, keepdims=True
        )
        values = r.pool_sum[...] / jnp.maximum(counts, 1.0)
        r.pooled[i] = values
        scale = inverse_rms(values)
        r.patch_norms[i] = jnp.broadcast_to(scale, (patches, LANES))
        r.query_in[i] = (values * scale * first_gain[0:1, :]).astype(b16)
        save(FIRST_KEPT, i)

    arrived(layer[:4])
    layer_saves = [
        pltpu.make_async_copy(src, dst, r.layer_sem.at[n])
        for n, (src, dst) in enumerate(
            ((r.w_in, r.out_w_in), (r.w_full.at[:, mine, :], r.out_w_out), (r.gain, r.out_gain))
        )
    ]
    for copy in layer_saves:
        copy.start()

    def first_layer(i):
        seq = section * own_count + i
        r.q1[i] = dot(r.query_in[i], r.w_in[0, :, :columns]).astype(b16)

        def project(rows):
            both = dot(r.source_in[i, rows, :], r.w_in[0, :, columns:])
            keys = both[:, :columns].astype(b16)
            r.k1[i, rows, :] = keys
            r.v1[i, rows, :] = both[:, columns:].astype(b16)
            spread = dot_lt(members_of(r, seq, rows, patches), r.q1[i])
            block_scores = dot((spread * keys.astype(f32)).astype(b16), heads_in) * SCALE
            r.scores[:, rows] = block_scores.T[:heads, :]

        each_block(byte_count, project, WIDE)
        scores = r.scores[...]
        r.scores[...] = jnp.exp(scores - segment_max(scores, r.ids[pl.ds(seq, 1), :]))
        r.mix_sum[...] = jnp.zeros_like(r.mix_sum)
        r.total_sum[...] = jnp.zeros_like(r.total_sum)

        def mix(rows):
            short = r.scores[:, rows]
            filled = jnp.concatenate([short, jnp.zeros((LANES - heads, WIDE), f32)], axis=0)
            raised = filled.T.astype(b16)
            r.raised[i, rows, :] = raised
            members = members_of(r, seq, rows, patches)
            weighted = (dot(raised, heads_out) * r.v1[i, rows, :].astype(f32)).astype(b16)
            r.mix_sum[...] += dot(members, weighted)
            r.total_sum[...] += dot(members, raised)

        each_block(byte_count, mix, WIDE)
        totals = r.total_sum[...]
        inverse = jnp.where(totals > 0.0, 1.0 / totals, 0.0)
        r.inverse[i] = inverse
        mixed = (r.mix_sum[...] * split_dot(inverse, heads_out)).astype(b16)
        r.mixed1[i] = mixed
        r.heads_all[0, i, :, mine] = mixed
        exchange(0, i).start()
        save(CROSS_KEPT, i)

    for i in range(own_count):
        first_layer(i)
        if i == 0:
            pl.when(section == 1)(rows_across().start)
            pass_rows(0)

    second_gain = r.gain.at[1]
    allowed = iota((patches, patches), 1) <= iota((patches, patches), 0)
    lane = iota((patches, LANES), 1)

    have_rows(0)

    def second_layer(i):
        exchange(0, i).wait()
        latent = (r.pooled[i] + dot(r.heads_all[0, i], r.w_full[0])).astype(b16)
        r.latent[i] = latent
        values = latent.astype(f32)
        scale = inverse_rms(values)
        r.patch_norms[i] = jnp.where(lane == 1, scale, r.patch_norms[i])
        normed = (values * scale * second_gain[0:1, :]).astype(b16)
        r.normed[i] = normed
        projected = dot(normed, r.w_in[1]).astype(b16)
        query, key, value = [projected[:, j * columns : (j + 1) * columns] for j in range(3)]
        r.q2[i] = query
        r.k2[i] = key
        r.v2[i] = value
        kept = jnp.zeros((patches, LANES), f32)
        outs = []
        for head in range(heads):
            own = slice(head * HD, (head + 1) * HD)
            scores = jnp.where(allowed, dot_rt(query[:, own], key[:, own]) * SCALE, NEGATIVE)
            highest = jnp.max(scores, axis=-1, keepdims=True)
            raised = jnp.exp(scores - highest)
            total = jnp.sum(raised, axis=-1, keepdims=True)
            outs.append(dot((raised / total).astype(b16), value[:, own]))
            kept = jnp.where(lane == head, highest + jnp.log(total), kept)
        r.totals[i] = kept
        mixed = jnp.concatenate(outs, axis=1).astype(b16)
        r.mixed2[i] = mixed
        r.heads_all[1, i, :, mine] = mixed
        exchange(1, i).start()
        save(SECOND_KEPT, i)

    for i in range(own_count):
        second_layer(i)
        if i == 0:
            pass_rows(1)
    have_rows(1)

    for copy in grad_copies + feed_copies:
        copy.wait()

    @pl.loop(0, own_count)
    def _(i):
        seq = section * own_count + i
        exchange(1, i).wait()
        values = r.latent[i].astype(f32) + dot(r.heads_all[1, i], r.w_full[1])
        r.middle[...] = values
        scale = inverse_rms(values)
        r.patch_norms[i] = jnp.where(lane == 2, scale, r.patch_norms[i])
        r.inner[i] = (values * scale * second_gain[1:2, :]).astype(b16)
        valid = iota((patches, 1), 0) <= jnp.max(r.ids[pl.ds(seq, 1), :], axis=1, keepdims=True)
        r.grad_in[i] = jnp.where(valid, r.grad_in[i].astype(f32), 0.0).astype(b16)

        gate = dot(r.inner[i], r.feed_in[0])
        up = dot(r.inner[i], r.feed_in[1])
        hidden_grad = dot_rt(r.grad_in[i], r.feed_out[...])
        gated = 1.0 / (1.0 + jnp.exp(-gate))
        act = gate * gated
        r.hidden[i] = (act * up).astype(b16)
        r.gate_grad[i] = (hidden_grad * up * (gated * (1.0 + gate * (1.0 - gated)))).astype(b16)
        r.up_grad[i] = (hidden_grad * act).astype(b16)
        inner_grad = dot_rt(r.gate_grad[i], r.feed_in[0]) + dot_rt(r.up_grad[i], r.feed_in[1])
        r.inner_part[i] = inner_grad.astype(b16)
        r.out_sum[...] = dot(r.hidden[i], r.feed_out[...])
        r.latent_own[i] = (r.middle[:, mine] + r.out_sum[:, mine]).astype(b16)
        r.latent_send[i] = r.out_sum[:, theirs].astype(b16)
        save(FEED_KEPT, i)

    @pl.loop(0, own_count)
    def _(i):
        for name in KEPT:
            keep(name, i).wait()

    for copy in layer_saves:
        copy.wait()
    rows_across().wait_send()
    rows_over().wait_send()


def shape(dims, dtype):
    return jax.ShapeDtypeStruct(dims, dtype)


def named_call(kernel, ins, outs, scratch, **params):
    any_space = pl.BlockSpec(memory_space=pl.ANY)
    whole = pl.BlockSpec(memory_space=pltpu.VMEM)
    names = [name for name, _, _ in ins] + [name for name, _ in outs] + list(scratch)

    def body(*refs):
        kernel(types.SimpleNamespace(**dict(zip(names, refs, strict=True))))

    got = pl.pallas_call(
        body,
        out_shape=tuple(s for _, s in outs),
        in_specs=[whole if inside else any_space for _, _, inside in ins],
        out_specs=tuple(any_space for _ in outs),
        scratch_shapes=list(scratch.values()),
        compiler_params=pltpu.CompilerParams(
            vmem_limit_bytes=VMEM_BYTES, has_side_effects=True, **params
        ),
    )(*(array for _, array, _ in ins))
    return {name: value for (name, _), value in zip(outs, got, strict=True)}


def forward(byte_states, patch_ids, attn_in, attn_out, gains, feed_in, feed_out, latent_grad):
    sequences, byte_count, width = byte_states.shape
    patches = byte_count // 4
    columns = attn_in.shape[-1]
    hidden = feed_out.shape[0]
    own = sequences // 2
    heads = columns // HD
    dims = dict(
        query_in=(own, patches, width, b16),
        source_in=(own, byte_count, width, b16),
        q1=(own, patches, columns, b16),
        k1=(own, byte_count, columns, b16),
        v1=(own, byte_count, columns, b16),
        raised=(own, byte_count, LANES, b16),
        inverse=(own, patches, LANES, f32),
        mixed1=(own, patches, columns, b16),
        byte_norms=(own, byte_count, LANES, f32),
        normed=(own, patches, width, b16),
        q2=(own, patches, columns, b16),
        k2=(own, patches, columns, b16),
        v2=(own, patches, columns, b16),
        totals=(own, patches, LANES, f32),
        mixed2=(own, patches, columns, b16),
        inner=(own, patches, width, b16),
        hidden=(own, patches, hidden, b16),
        gate_grad=(own, patches, hidden, b16),
        up_grad=(own, patches, hidden, b16),
        grad_in=(own, patches, width, b16),
        inner_part=(own, patches, width, b16),
        patch_norms=(own, patches, LANES, f32),
        latent_own=(own, patches, columns, b16),
        latent_send=(own, patches, columns, b16),
    )
    sems = pltpu.SemaphoreType.DMA
    scratch = {name: pltpu.VMEM(dims[name][:-1], dims[name][-1]) for name in KEPT}
    scratch |= dict(
        state_in=pltpu.VMEM((own, byte_count, width), b16),
        pooled=pltpu.VMEM((own, patches, width), f32),
        latent=pltpu.VMEM((own, patches, width), b16),
        middle=pltpu.VMEM((patches, width), f32),
        out_sum=pltpu.VMEM((patches, width), f32),
        w_in=pltpu.VMEM((2, width, 3 * columns), b16),
        w_full=pltpu.VMEM((2, 2 * columns, width), b16),
        gain=pltpu.VMEM((2, 2, width), f32),
        feed_in=pltpu.VMEM((2, width, hidden), b16),
        feed_out=pltpu.VMEM((hidden, width), b16),
        pool_sum=pltpu.VMEM((patches, width), f32),
        scores=pltpu.VMEM((heads, byte_count), f32),
        mix_sum=pltpu.VMEM((patches, columns), f32),
        total_sum=pltpu.VMEM((patches, LANES), f32),
        heads_all=pltpu.VMEM((2, own, patches, 2 * columns), b16),
        rows_send=sems((2,)),
        rows_recv=sems((2,)),
        state_sem=sems((own,)),
        grad_sem=sems((own,)),
        feed_sem=sems((2,)),
        near_sem=sems((5,)),
        far_send=sems((5,)),
        far_recv=sems((5,)),
        part_send=sems((2, own)),
        part_recv=sems((2, own)),
        keep_sem=sems((len(KEPT), own)),
        layer_sem=sems((len(LAYERS),)),
    )
    ins = [
        ("states", byte_states, False), ("ids", patch_ids, True), ("attn_in", attn_in, False),
        ("attn_out", attn_out, False), ("gains", gains, False), ("ffn_in", feed_in, False),
        ("ffn_out", feed_out, False), ("upstream", latent_grad, False),
    ]
    dims |= dict(
        w_in=(2, width, 3 * columns, b16),
        w_out=(2, columns, width, b16),
        gain=(2, 2, width, f32),
    )
    names = (*KEPT, *LAYERS)
    outs = [("out_" + name, shape(dims[name][:-1], dims[name][-1])) for name in names]
    got = named_call(forward_kernel, ins, outs, scratch, collective_id=0)
    return {name: got["out_" + name] for name in names}


def flat(ref, cols):
    block = ref[:, :, cols]
    return block.reshape(block.shape[0] * block.shape[1], block.shape[2])


LONG, SHORT = 4, 2


def rows_of(ref, start, rows):
    if not isinstance(start, int):
        start = pl.multiple_of(start, 16)
    return ref.at[pl.ds(start, rows), :]


def sum_rows(target, *terms):
    rows, width = target.shape
    step = rows
    while step * width > 100 * 1408 and step % 32 == 0:
        step //= 2

    def add(at):
        value = terms[0][at, :]
        for term in terms[1:]:
            value = value + term[at, :]
        target[at, :] = value

    if step == rows:
        add(slice(None))
    else:
        each_block(rows, add, step)


def add_rows(target, *others):
    sum_rows(target, target, *others)


SHARES = ((512, (384,), (1024,)), (1408, (128,), (256, 128)), (1408, (), (512,)), (1024, (256,), (256,)), (512, (), (512, 512)), (512, (), (512, 512)), (512, (), (512, 512)))
PLAN = ((((1,),(1,)),((),(1,)),((1,),(0,)),((),())),(((0,0,0),(0,0)),((1,),(2,)),((3,4),(1,)),((0,0,0,1),(0,0,0,0,1))),(((2,2,4,0,3),(3,2,2,2)),((0,3),(4,3,0,0,0)),((0,0),(4,0,0,1)),((2,3,2,2,4,5),(4,2,2,3,5,2,2))),(((2,),(4,)),((4,0,0),(5,)),((5,),(0,)),((),())),(((1,1,1,5),(0,3)),((),(2,2)),((2,2),()),((1,1,0,1),())),(((),(0,)),((0,2,2,2),()),((0,0,1,2),(2,2,2)),((2,),())),(((2,),(1,0,2,1,1,5)),((),(0,0,1)),((),(3,)),((),(1,0))),(((3,3),()),((3,2,5,1),(2,4,2,1)),((0,2,2),(4,5,2,2)),((3,0,3,3),())),(((),()),((1,),()),((1,3),(1,)),((),(1,))),(((4,4),()),((4,),()),((4,),()),((4,4),(3,3,1,3))),(((),(0,3,4)),((),()),((),(0,)),((2,),(2,4,4))),(((),()),((0,2),()),((1,1),(3,)),((),())),(((3,4,0),(10,2,11,3,7,8,12,4,4,6,6,6,9,13)),((1,),(7,13,5,9,8,3,12,1,6,1,0,4,6,10,3)),((3,),(12,13,6,7,11,9,10,3,8,5,1,0,4)),((4,),(7,6,11,8,4,9,10,13,12,6,5,6,6))),(((),(5,5)),((),()),((),()),((),(2,5))),(((5,5),(5,)),((3,1),(2,11)),((),(4,)),((5,),())),(((2,),(2,)),((4,),(6,4)),((),(6,2)),((),())),(((),(7,8)),((3,),()),((),()),((5,),(0,1,7,7,7))),(((),()),((4,),(3,2)),((0,),(1,3,7,6,4,3)),((),())),(((),(10,0,6,0,2,8,7,7,8,10)),((4,2),(4,)),((4,4,4,3,3,5,5),()),((1,5),(5,8,8))),(((0,0),(1,)),((5,0,3),(8,0,7,5,0,9,3,8,7,2,10,6,11,2,6)),((),(5,0,2,10,7,8,10,5,0)),((),())),(((),(0,)),((5,),(12,)),((),(2,)),((),(0,))),(((),(9,2,11,9)),((),(10,13,11,5,5,0)),((),(11,13)),((),(10,))),(((5,),()),((),()),((2,),(9,5,6,6,11)),((),(9,9,8,2,2))),(((),()),((0,1),()),((0,),(8,)),((),(11,11,0,10))),(((0,2,2,2,0,1),(2,9)),((),(12,0,7,0,0,9,1,2,2,2)),((),(2,2,0,9,12,12)),((2,),(10,9,11,3,12,0))),(((3,4),(10,11,12,13,11,12,12)),((),(7,)),((),()),((2,0,0,2),(12,2,12))),(((),()),((),(8,13)),((2,),()),((0,4,0,0),())),(((0,),(13,13)),((2,2,0,5),(10,)),((0,5,1,5),(7,8,2,0,0,0,9,8,11)),((3,),(4,13,13))),(((),()),((2,),(9,9)),((0,),(1,)),((2,),())),(((),(0,)),((),(3,)),((),(3,)),((),(0,))),(((),(1,0,4,2)),((),()),((),(13,)),((),(13,0))),(((17,15,2,2,14,21,16,3,18,2,14,20,4,14,14,5),(3,)),((14,18,0,0,15,0,0,20,17,16,2,21,4,5,19,5,14,14,2,2),(11,4)),((4,0,15,0,2,18,0,16,21,17,2,2,20,2,14,14),()),((14,14,14,4,1,2,19,16,3,21,15,18,17,16),())),(((),(2,6,6,8)),((14,14),(5,8,11,6,9,12)),((19,3,14),(2,7,10,5,11,12,4)),((20,5,0,16),(2,2,2,4,6,7,0,8,1,6))),(((16,15,16,17,1,0,15,15,18,18,19,5,17,17,20,21,19,16,20,20,18,19,0,21,2,19),(3,2,5,6,7,10,8,0,9,5,6,4,10,7,11,12,6,6)),((),(13,10,8,13,12,6,7,6,6,6,6,6,10)),((15,14,14),(10,9,10,12,6,7,13,8,6,6,6,9,13)),((19,14,17,15,15,15,21,17,18,16,21,17,18,20,20,20,19,19,18,2,5,0,2),(11,9,5,3,6,6,12,8,13,9,10,7,6))),(((14,14,14,14,21),(6,13,11,9,13)),((15,15,17,16,16,15,15,18,18,17,16,20,20,3,19,19,21,14,16,17,21),()),((5,15,16,2,16,17,17,15,19,15,18,18,14,20,19,20,16,21,21,16,17,15),(6,11,6,6)),((14,14,15,14),(10,6,6,12))),(((16,14,15),()),((18,19,15,14,18,17,20,20),()),((18,19,20,21,17,17,20,19,21,19,14,16),()),((16,),())),(((17,18,16,19,17,14,14,20),(6,)),((14,14,19,17,21,19,21,21,20),()),((14,14,14,18,18,14,21),()),((17,18,19,17,20,14,16,21,15,21),(5,))),(((21,15,18,14),()),((14,16),()),((),()),((20,18,14,14,14,14),(13,))),(((20,21,19),(12,)),((14,14,18),(11,12,13)),((20,14),(12,13)),((21,19),(11,6))))


class Flows:
    def __init__(self, r, section):
        self.r = r
        self.section = section
        place = lax.axis_index("dp")
        self.z, self.y = place // SHORT, lax.rem(place, SHORT)
        self.right, self.left = place + SHORT, place - SHORT
        self.beside = place + 1 - 2 * self.y
        self.flows = []
        self.done = {(z, s): [] for z in range(LONG) for s in range(2)}
        self.points = 0

    def hop(self, src, dst, n, j, target):
        r = self.r
        return pltpu.make_async_remote_copy(
            src_ref=src, dst_ref=dst, send_sem=r.flow_send.at[n, j], recv_sem=r.flow_recv.at[n, j],
            device_id={"dp": target}, device_id_type=MESH,
        )

    def reduce_events(self, n, part, slot):
        def up(k):
            return self.hop(slot(k - 1), slot(k - 1), n, k - 1, self.right)

        def down(k):
            return self.hop(slot(3 + k), slot(3 + k), n, 3 + k, self.left)

        def pass_on(copy, held, k):
            copy(k).wait_recv()
            add_rows(held, part(k))
            copy(k).start()

        def begin(z):
            if z == 0:
                for k in (3, 2, 1):
                    self.hop(part(k), slot(k - 1), n, k - 1, self.right).start()
            if z == 3:
                for k in (0, 1, 2):
                    self.hop(part(k), slot(3 + k), n, 3 + k, self.left).start()

        def passing(at_one, at_two):
            def event(z):
                if z in (1, 2):
                    way, k = (at_one, at_two)[z - 1]
                    pass_on(*((up, slot(k - 1)) if way > 0 else (down, slot(3 + k))), k)

            return event

        def close(z):
            got = []
            if z >= 1:
                up(z).wait_recv()
                got.append(slot(z - 1))
            if z <= 2:
                down(z).wait_recv()
                got.append(slot(3 + z))
            add_rows(part(z), *got)

        def sent(z):
            for k in ((1, 2, 3), (2, 3), (3,), ())[z]:
                up(k).wait_send()
            for k in ((), (0,), (0, 1), (0, 1, 2))[z]:
                down(k).wait_send()

        passes = [
            passing((1, 3), (-1, 0)), passing((1, 2), (-1, 1)), passing((-1, 0), (1, 3)),
        ]
        return begin, passes, close, sent

    def gather_events(self, n, own, out):
        def up(src, k, d):
            return self.hop(src, out(k), n, 7 + d, self.right)

        def down(src, k, d):
            return self.hop(src, out(k), n, 10 + d, self.left)

        def near(z):
            return pltpu.make_async_copy(own(z), out(z), self.r.flow_near.at[n])

        def starts(z, d, way):
            k = z - d * way
            src = own(z) if d == 0 else out(k)
            copies = []
            if d < LONG - 1 and 0 <= z + way < LONG:
                copies.append((up if way > 0 else down)(src, k, d))
            return copies

        def begin(z):
            near(z).start()
            for copy in starts(z, 0, 1) + starts(z, 0, -1):
                copy.start()

        def step(d, way):
            def event(z):
                k = z - d * way
                if 0 <= k < LONG:
                    (up if way > 0 else down)(out(k), k, d - 1).wait_recv()
                    for copy in starts(z, d, way):
                        copy.start()

            return event

        def sent(z):
            near(z).wait()
            for way in (1, -1):
                for d in range(LONG):
                    if 0 <= z - d * way < LONG:
                        for copy in starts(z, d, way):
                            copy.wait_send()

        return begin, [step(d, way) for d in (1, 2, 3) for way in (1, -1)], sent

    def long_first(self, n, data, out, slots, start, rows):
        c = rows // LONG

        def part(k):
            return data(start + k * c, c)

        def slot(j):
            return rows_of(slots, j * c, c)

        def beside(z):
            return self.hop(part(z), slot(6), n, 6, self.beside)

        begin, passes, close, reduce_sent = self.reduce_events(n, part, slot)
        gather, steps, gather_sent = self.gather_events(
            n, lambda z: slot(6), lambda k: out(start + k * c, c)
        )

        def middle(z):
            close(z)
            beside(z).start()

        def turn(z):
            beside(z).wait_recv()
            add_rows(slot(6), part(z))
            gather(z)

        def sent(z):
            reduce_sent(z)
            beside(z).wait_send()
            gather_sent(z)

        return [begin, *passes, middle, turn, *steps], sent

    def short_first(self, n, data, out, slots, start, rows):
        half = rows // SHORT

        def mine(y):
            return data(start + y * half, half)

        def place(y):
            return out(start + y * half, half)

        def slot(j):
            return rows_of(slots, j * half, half)

        def beside():
            return self.hop(mine(1 - self.y), slot(0), n, 6, self.beside)

        inward = (self.right, self.right, self.left, self.left)
        outward = (None, self.left, self.right, None)

        def lean(z):
            middle = 1 if z in (1, 2) else 0
            return self.hop(mine(self.y), slot(1 + middle), n, middle, inward[z])

        def settle(z):
            src = slot(0) if z in (1, 2) else place(self.y)
            return self.hop(src, place(self.y), n, 7, outward[z])

        def near(z):
            return pltpu.make_async_copy(slot(0), place(self.y), self.r.flow_near.at[n])

        def spread(z):
            src = slot(0) if z in (1, 2) else place(self.y)
            return self.hop(src, place(self.y), n, 13, self.beside)

        def first(z):
            beside().start()

        def turn(z):
            beside().wait_recv()
            add_rows(mine(self.y), slot(0))
            if z in (0, 3):
                lean(z).start()

        def pair(z):
            if z in (1, 2):
                self.hop(slot(1), slot(1), n, 0, inward[z]).wait_recv()
                add_rows(mine(self.y), slot(1))
                lean(z).start()

        def close(z):
            if z in (1, 2):
                lean(z).wait_recv()
                sum_rows(slot(0), mine(self.y), slot(2))
                near(z).start()
                settle(z).start()
                spread(z).start()

        def outer(z):
            if z in (0, 3):
                self.hop(place(self.y), place(self.y), n, 7, inward[z]).wait_recv()
                spread(z).start()

        def end(z):
            there = place(1 - self.y)
            self.hop(there, there, n, 13, self.beside).wait_recv()

        def sent(z):
            beside().wait_send()
            lean(z).wait_send()
            spread(z).wait_send()
            if z in (1, 2):
                settle(z).wait_send()
                near(z).wait()

        return [first, turn, pair, close, outer, end], sent

    def open(self, only, *flows):
        for events, sent in flows:
            self.flows.append((only, events, sent))
            for counts in self.done.values():
                counts.append(0)

    def advance(self, z, s, todo):
        def body():
            for n in todo:
                self.flows[n][1][self.done[z, s][n]](z)
                self.done[z, s][n] += 1

        return body

    def point(self):
        plan = PLAN[self.points] if self.points < len(PLAN) else ()
        self.points += 1
        for z, lists in enumerate(plan):
            first, second = self.done[z, 0], self.done[z, 1]
            if lists[0] == lists[1] and all(first[n] == second[n] for n in lists[0]):
                if lists[0]:
                    pl.when(self.z == z)(self.advance(z, 0, lists[0]))
                    for n in lists[0]:
                        second[n] = first[n]
                continue
            for s in range(2):
                here = jnp.logical_and(self.z == z, self.section == s)
                pl.when(here)(self.advance(z, s, lists[s]))

    def drain(self):
        for (z, s), counts in self.done.items():

            def body(z=z, s=s, counts=counts):
                mine = [n for n, flow in enumerate(self.flows) if flow[0] in (None, s)]
                longest = max(len(self.flows[n][1]) for n in mine)
                for k in range(longest):
                    for n in mine:
                        if counts[n] <= k < len(self.flows[n][1]):
                            self.flows[n][1][k](z)
                for n in mine:
                    self.flows[n][2](z)

            pl.when(jnp.logical_and(self.z == z, self.section == s))(body)


def on_grid():
    return lax.axis_size("dp") == LONG * SHORT


def backward_kernel(r):
    section, tensor = lax.axis_index("section"), lax.axis_index("tensor")
    own_count, patches, width = r.normed.shape
    byte_count = r.ids.shape[1]
    columns = r.w_out.shape[0]
    hidden = r.down.shape[0]
    heads = columns // HD
    half = width // 2
    half_bytes = byte_count // 2
    summing = on_grid()
    loads = {}

    def load(name, src, dst, *sem):
        copy = pltpu.make_async_copy(src, dst, r.load_sem.at[sem])
        copy.start()
        loads[name] = copy

    held_names = ("inner", "grad_in", "inner_part", "normed", "patch_norms", "gain")
    for n, name in enumerate(held_names):
        load(name, getattr(r, "in_" + name), getattr(r, name), n)
    load("w_in", r.in_w_in.at[1], r.w_in, 6)
    load("w_out", r.in_w_out.at[1], r.w_out, 7)
    others = [("section", 1 - section), ("tensor", 1 - tensor)]
    flows = Flows(r, section) if summing else None
    if summing:
        greet_grid(flows, others)
    else:
        greet(others)

    def cross(src, dst, i, sem):
        return remote(
            src, dst, r.cross_send.at[sem, i], r.cross_recv.at[sem, i], "tensor", 1 - tensor
        )

    def inner_exchange(i):
        return cross(r.in_inner_part.at[i], r.inner_got.at[i], i, 0)

    def normed_exchange(i):
        return cross(r.normed_part.at[i], r.normed_got.at[i], i, 1)

    def query_exchange(i):
        return cross(r.inner_part.at[i], r.inner_got.at[i], i, 2)

    def source_exchange(i):
        theirs = block_at(1 - tensor, half_bytes)
        return cross(r.source_part.at[i, theirs, :], r.source_got.at[i], i, 3)

    def latent_exchange(i):
        return cross(r.in_latent_send.at[i], r.latent_got.at[i], i, 4)

    for i in range(own_count):
        inner_exchange(i).start()
    def give(n, src, dst):
        return remote(src, dst, r.give_send.at[n], r.give_recv.at[n], "section", 1 - section)

    def point():
        if summing:
            flows.point()

    def summed(n, data, out, only=None):
        if summing:
            for flow, goes_long, slots, start, rows in r.slots[n]:
                make = flows.long_first if goes_long else flows.short_first
                flows.open(only, make(flow, data, out, slots, start, rows))

    def up_half(ref, n):
        return ref.at[pl.ds(n * half, half), :]

    def whole(view):
        return lambda start, rows: rows_of(view(), start, rows)

    @functools.partial(
        pl.run_scoped,
        hidden_all=pltpu.VMEM((own_count, patches, hidden), b16),
        gate_all=pltpu.VMEM((own_count, patches, hidden), b16),
        up_all=pltpu.VMEM((own_count, patches, hidden), b16),
        down_give=pltpu.VMEM((hidden, half), b16),
    )
    def _(hidden_all, gate_all, up_all, down_give):
        parts = {"hidden": hidden_all, "gate_grad": gate_all, "up_grad": up_all}
        for n, (name, ref) in enumerate(parts.items()):
            load(name, getattr(r, "in_" + name), ref, n + 8)
        for name in (*parts, "inner", "grad_in"):
            loads[name].wait()

        def down_grad(target, side):
            upstream = flat(r.grad_in, block_at(side, half))

            def tile(cols):
                target[cols, :] = dot_lt(flat(hidden_all, cols), upstream).astype(b16)

            each_block(hidden, tile)
            if hidden % BLOCK:
                tile(pl.ds(hidden - hidden % BLOCK, hidden % BLOCK))

        def up_grad(target, ref, side):
            upstream = flat(ref, slice(None))

            def tile(rows):
                cols = pl.ds(pl.multiple_of(side * half + rows.start, BLOCK), BLOCK)
                target[rows, :] = dot_lt(flat(r.inner, cols), upstream).astype(b16)

            each_block(half, tile)

        used = pl.ds(0, hidden)
        give_rows = [pl.ds(0, half), pl.ds(half, half)]
        gate_give, up_give = [r.attn_in_part.at[1, rows, used] for rows in give_rows]
        gate_got, up_got = [r.big_got.at[rows, used] for rows in give_rows]
        gate_own, up_own = [r.up.at[rows, :] for rows in give_rows]
        gifts = [
            give(0, down_give, r.down_got), give(1, gate_give, gate_got), give(2, up_give, up_got)
        ]
        other = 1 - section
        down_grad(down_give, other)
        gifts[0].start()
        down_grad(r.down, section)
        up_grad(gate_give, gate_all, other)
        gifts[1].start()
        gifts[0].wait()
        add_rows(r.down, r.down_got)
        summed(0, whole(lambda: r.down), whole(lambda: r.down_sum))
        point()
        up_grad(gate_own, gate_all, section)
        up_grad(up_give, up_all, other)
        gifts[2].start()
        gifts[1].wait()
        add_rows(gate_own, gate_got)
        summed(1, whole(lambda: up_half(r.up, 0)), whole(lambda: up_half(r.up_sum, 0)))
        point()
        up_grad(up_own, up_all, section)
        gifts[2].wait()
        add_rows(up_own, up_got)
        summed(2, whole(lambda: up_half(r.up, 1)), whole(lambda: up_half(r.up_sum, 1)))
        point()
        pl.semaphore_signal(
            r.free_sem, inc=1, device_id={"section": other}, device_id_type=MESH
        )

    def gifts_of(layer):
        return [
            give(3, r.attn_in_part.at[layer], r.big_got),
            give(4, r.attn_out_part.at[layer], r.attn_out_got),
        ]

    def hand_over(layer):
        @pl.when(section != layer)
        def _():
            pl.semaphore_wait(r.free_sem, 1)
            for gift in gifts_of(layer):
                gift.start()

    def take_over(layer):
        @pl.when(section != layer)
        def _():
            for gift in gifts_of(layer):
                gift.wait_send()

        @pl.when(section == layer)
        def _():
            for gift in gifts_of(layer):
                gift.wait_recv()
            add_rows(r.attn_out_part.at[layer], r.attn_out_got)
            add_rows(r.attn_in_part.at[layer], r.big_got)

    def sum_layer(layer, which):
        def columns_of(j):
            return whole(lambda: r.attn_in_part.at[layer, :, pl.ds(j * columns, columns)])

        if which == 3:
            summed(
                3, whole(lambda: r.attn_out_part.at[layer]), whole(lambda: r.attn_out_sum), layer
            )
        else:
            summed(4 + which, columns_of(which), whole(lambda: r.attn_in_sum.at[which]), layer)

    first_gain, second_gain = r.gain.at[0], r.gain.at[1]

    def back_through(normed, gain_row, scale, upstream):
        unit = normed.astype(f32) / gain_row
        scaled = upstream * gain_row
        mean = jnp.mean(unit * scaled, axis=-1, keepdims=True)
        return (scaled - unit * mean) * scale, unit

    @functools.partial(
        pl.run_scoped,
        q2=pltpu.VMEM((own_count, patches, columns), b16),
        k2=pltpu.VMEM((own_count, patches, columns), b16),
        v2=pltpu.VMEM((own_count, patches, columns), b16),
        totals=pltpu.VMEM((own_count, patches, LANES), f32),
        mixed2=pltpu.VMEM((own_count, patches, columns), b16),
        second_grads=pltpu.VMEM((own_count, patches, 3 * columns), b16),
        mixed_grads=pltpu.VMEM((patches, columns), b16),
    )
    def _(q2, k2, v2, totals, mixed2, second_grads, mixed_grads):
        parts = {"q2": q2, "k2": k2, "v2": v2, "totals": totals, "mixed2": mixed2}
        for n, (name, ref) in enumerate(parts.items()):
            load(name, getattr(r, "in_" + name), ref, n + 11)
        for name in (*held_names[2:], "w_in", "w_out", *parts):
            loads[name].wait()
        r.gain_sum[...] = jnp.zeros_like(r.gain_sum)
        allowed = iota((patches, patches), 1) <= iota((patches, patches), 0)
        for i in range(own_count):
            inner_exchange(i).wait()
            own_part = r.inner_part[i].astype(f32)
            back, unit = back_through(
                r.inner[i], second_gain[1:2, :], r.patch_norms[i, :, 2:3],
                own_part + r.inner_got[i].astype(f32),
            )
            r.gain_sum[3:4, :] += jnp.sum(unit * own_part, axis=0, keepdims=True)
            branch = (r.grad_in[i].astype(f32) + back).astype(b16)
            r.branch[i] = branch
            mixed_grads[...] = dot_rt(branch, r.w_out[...]).astype(b16)
            point()

            mixed_grad = mixed_grads[...]
            outs = [[], [], []]
            for head in range(heads):
                own = slice(head * HD, (head + 1) * HD)
                query, key, value = q2[i, :, own], k2[i, :, own], v2[i, :, own]
                upper = mixed_grad[:, own]
                scores = jnp.where(allowed, dot_rt(query, key) * SCALE, NEGATIVE)
                probs = jnp.exp(scores - totals[i, :, head : head + 1])
                prob_grad = dot_rt(upper, value)
                delta = jnp.sum(probs * prob_grad, axis=-1, keepdims=True)
                score_grad = (probs * (prob_grad - delta)).astype(b16)
                outs[0].append(dot(score_grad, key) * SCALE)
                outs[1].append(dot_lt(score_grad, query) * SCALE)
                outs[2].append(dot_lt(probs.astype(b16), upper))
            grads = jnp.concatenate(outs[0] + outs[1] + outs[2], axis=1).astype(b16)
            second_grads[i] = grads
            point()
            r.normed_part[i] = dot_rt(grads, r.w_in[...]).astype(b16)
            normed_exchange(i).start()
            point()

        def outer(target, rows_ref, upstream, tiles):
            @pl.loop(0, tiles)
            def _(t):
                cols = block_at(t)
                target[cols, :] = dot_lt(flat(rows_ref, cols), upstream).astype(b16)

        outer(r.attn_in_part.at[1], r.normed, flat(second_grads, slice(None)), width // BLOCK)
        point()
        outer(r.attn_out_part.at[1], mixed2, flat(r.branch, slice(None)), columns // BLOCK)
        hand_over(1)
        for i in range(own_count):
            latent_exchange(i).start()
        point()

    heads_in, heads_out = head_masks(columns)

    def first_layer(i, scoped):
        seq = section * own_count + i
        s = types.SimpleNamespace(**scoped)
        copies = {}
        kinds = names(q1=1, v1=1, raised=1, inverse=1, mixed1=1, source_in=1, query_in=1)
        for n, name in enumerate(kinds):
            copy = pltpu.make_async_copy(
                getattr(r, "in_" + name).at[i], getattr(s, name), r.first_sem.at[n]
            )
            copy.start()
            copies[name] = copy
        normed_exchange(i).wait()
        own_part = r.normed_part[i].astype(f32)
        back, unit = back_through(
            r.normed[i], second_gain[0:1, :], r.patch_norms[i, :, 1:2],
            own_part + r.normed_got[i].astype(f32),
        )
        r.gain_sum[2:3, :] += jnp.sum(unit * own_part, axis=0, keepdims=True)
        branch = (r.branch[i].astype(f32) + back).astype(b16)
        r.branch[i] = branch
        s.mixed_grad[...] = dot_rt(branch, r.w_out[...]).astype(b16)
        s.q_sum[...] = jnp.zeros_like(s.q_sum)
        s.delta_sum[...] = jnp.zeros_like(s.delta_sum)
        for copy in copies.values():
            copy.wait()
        point()
        if i == 0:
            take_over(1)
            for which in (3, 0, 1, 2):
                sum_layer(1, which)
            point()
        inverse = s.inverse[...]
        inverse_high = inverse.astype(b16)
        inverse_low = (inverse - inverse_high.astype(f32)).astype(b16)

        def value_side(rows):
            members = members_of(r, seq, rows, patches)
            spread = dot_lt(members, s.mixed_grad[...])
            scale = dot_lt(members, inverse_high) + dot_lt(members, inverse_low)
            probs = s.raised[rows, :].astype(f32) * scale
            s.probs[rows, :] = probs
            s.dkv[rows, columns:] = (dot(probs.astype(b16), heads_out) * spread).astype(b16)
            prob_grad = dot((spread * s.v1[rows, :].astype(f32)).astype(b16), heads_in)
            s.prob_grad[rows, :] = prob_grad
            product = probs * prob_grad
            high = product.astype(b16)
            low = (product - high.astype(f32)).astype(b16)
            s.delta_sum[...] += dot(members, high) + dot(members, low)

        for t in range(byte_count // WIDE):
            value_side(pl.ds(t * WIDE, WIDE))
            point()
        keys = pltpu.make_async_copy(r.in_k1.at[i], s.v1, r.first_sem.at[7])
        keys.start()
        delta = s.delta_sum[...]
        delta_high = delta.astype(b16)
        delta_low = (delta - delta_high.astype(f32)).astype(b16)

        def key_side(rows):
            members = members_of(r, seq, rows, patches)
            shift = dot_lt(members, delta_high) + dot_lt(members, delta_low)
            score_grad = (s.probs[rows, :] * (s.prob_grad[rows, :] - shift)).astype(b16)
            spread = dot(score_grad, heads_out)
            s.dkv[rows, :columns] = (spread * dot_lt(members, s.q1[...]) * SCALE).astype(b16)
            s.q_sum[...] += dot(members, (spread * s.v1[rows, :].astype(f32)).astype(b16))
            source = dot_rt(s.dkv[rows, :], r.w_in[:, columns:])
            r.source_part[i, rows, :] = source.astype(b16)
            unit_block = s.source_in[rows, :].astype(f32)
            r.gain_sum[1:2, :] += (
                jnp.sum(unit_block * source, axis=0, keepdims=True) / first_gain[1:2, :]
            )

        keys.wait()
        for t in range(byte_count // WIDE):
            for u in range(WIDE // BLOCK):
                key_side(pl.ds(t * WIDE + u * BLOCK, BLOCK))
            point()
        source_exchange(i).start()
        q_grad = (s.q_sum[...] * SCALE).astype(b16)
        query = dot_rt(q_grad, r.w_in[:, :columns])
        r.inner_part[i] = query.astype(b16)
        query_exchange(i).start()
        unit_pool = s.query_in[...].astype(f32)
        r.gain_sum[0:1, :] += (
            jnp.sum(unit_pool * query, axis=0, keepdims=True) / first_gain[0:1, :]
        )
        point()

        def add_to(target, rows, cols, value):
            if i:
                value = target[rows, cols].astype(f32) + value
            target[rows, cols] = value.astype(b16)

        for half_t in range(2):

            @pl.loop(0, half // BLOCK)
            def _(t, half_t=half_t):
                cols = pl.ds(pl.multiple_of(half_t * half + t * BLOCK, BLOCK), BLOCK)
                source = s.source_in[:, cols]
                target = r.attn_in_part.at[0]
                add_to(target, cols, slice(0, columns), dot_lt(s.query_in[:, cols], q_grad))
                add_to(target, cols, slice(columns, 3 * columns), dot_lt(source, s.dkv[...]))

            point()

        @pl.loop(0, columns // BLOCK)
        def _(t):
            cols = block_at(t)
            add_to(
                r.attn_out_part.at[0], cols, slice(None), dot_lt(s.mixed1[:, cols], branch)
            )

        point()

    def last_parts(s):
        outs = []

        own_rows = block_at(tensor, half_bytes)
        cols_keep, cols_give = block_at(section, half), block_at(1 - section, half)
        for i in range(own_count):
            seq = section * own_count + i
            finals = [
                pltpu.make_async_copy(
                    r.in_source_in.at[i, own_rows, :], s.source_in, r.first_sem.at[0]
                ),
                pltpu.make_async_copy(
                    r.in_byte_norms.at[i, own_rows, :], s.byte_norms, r.first_sem.at[1]
                ),
                pltpu.make_async_copy(r.in_query_in.at[i], s.query_in, r.first_sem.at[2]),
            ]
            for copy in finals:
                copy.start()
            query_exchange(i).wait()
            source_exchange(i).wait()
            for copy in finals:
                copy.wait()
            back, _ = back_through(
                s.query_in[...], first_gain[0:1, :], r.patch_norms[i, :, 0:1],
                r.inner_part[i].astype(f32) + r.inner_got[i].astype(f32),
            )
            counts = jnp.sum(
                jnp.where(iota((patches, byte_count), 0) == r.ids[pl.ds(seq, 1), :], 1.0, 0.0),
                axis=1, keepdims=True,
            )
            pool_grad = (r.branch[i].astype(f32) + back) / jnp.maximum(counts, 1.0)
            high = pool_grad.astype(b16)
            s.pool_high[...] = high
            s.pool_low[...] = (pool_grad - high.astype(f32)).astype(b16)

            @pl.loop(0, half_bytes // BLOCK)
            def _(t, i=i, seq=seq):
                rows = block_at(t)
                place = pl.ds(pl.multiple_of(tensor * half_bytes + t * BLOCK, BLOCK), BLOCK)
                members = members_of(r, seq, place, patches)
                spread = dot_lt(members, s.pool_high[...]) + dot_lt(members, s.pool_low[...])
                part = r.source_part[i, place, :].astype(f32)
                own, _ = back_through(
                    s.source_in[rows, :], first_gain[1:2, :], s.byte_norms[rows, 0:1],
                    part + r.source_got[i, rows, :].astype(f32),
                )
                r.source_got[i, rows, :] = (own + spread).astype(b16)

            near = pltpu.make_async_copy(
                r.source_got.at[i, :, cols_keep], r.byte_grad.at[seq], r.out_sem.at[1, i]
            )
            far = remote(
                r.source_got.at[i, :, cols_give], r.byte_grad.at[seq],
                r.out_send.at[1, i], r.out_recv.at[1, i], "section", 1 - section,
            )
            near.start()
            far.start()
            outs += [near, far]
            point()

        half_rows = patches // 2
        rows_keep, rows_give = block_at(section, half_rows), block_at(1 - section, half_rows)
        for i in range(own_count):
            seq = section * own_count + i
            s_load = pltpu.make_async_copy(r.in_latent_own.at[i], s.latent.at[i], r.first_sem.at[i])
            s_load.start()
            s_load.wait()
            latent_exchange(i).wait()
            last = jnp.max(r.ids[pl.ds(seq, 1), :], axis=1, keepdims=True)
            valid = iota((patches, 1), 0) <= last
            values = s.latent[i].astype(f32) + r.latent_got[i].astype(f32)
            s.latent[i] = jnp.where(valid, values, 0.0).astype(b16)
            near = pltpu.make_async_copy(
                s.latent.at[i, rows_keep, :], r.latents.at[seq], r.out_sem.at[0, i]
            )
            far = remote(
                s.latent.at[i, rows_give, :], r.latents.at[seq],
                r.out_send.at[0, i], r.out_recv.at[0, i], "section", 1 - section,
            )
            near.start()
            far.start()
            outs += [near, far]
        for copy in outs:
            copy.wait()

    load("w_in", r.in_w_in.at[0], r.w_in, 6)
    load("w_out", r.in_w_out.at[0], r.w_out, 7)
    loads["w_in"].wait()
    loads["w_out"].wait()
    one = dict(
        source_in=pltpu.VMEM((byte_count, width), b16),
        v1=pltpu.VMEM((byte_count, columns), b16),
        dkv=pltpu.VMEM((byte_count, 2 * columns), b16),
        probs=pltpu.VMEM((byte_count, LANES), f32),
        prob_grad=pltpu.VMEM((byte_count, LANES), f32),
        raised=pltpu.VMEM((byte_count, LANES), b16),
        inverse=pltpu.VMEM((patches, LANES), f32),
        q1=pltpu.VMEM((patches, columns), b16),
        mixed1=pltpu.VMEM((patches, columns), b16),
        query_in=pltpu.VMEM((patches, width), b16),
        mixed_grad=pltpu.VMEM((patches, columns), b16),
        q_sum=pltpu.VMEM((patches, columns), f32),
        delta_sum=pltpu.VMEM((patches, LANES), f32),
    )

    @functools.partial(pl.run_scoped, **one)
    def _(**scoped):
        for i in range(own_count):
            first_layer(i, scoped)

    hand_over(0)
    point()
    take_over(0)
    for which in (3, 0, 1, 2):
        sum_layer(0, which)
    point()
    gains = Gains(r, section, tensor, flows) if summing else None
    if summing:
        gains.tick()
    last = dict(
        source_in=pltpu.VMEM((half_bytes, width), b16),
        byte_norms=pltpu.VMEM((half_bytes, LANES), f32),
        query_in=pltpu.VMEM((patches, width), b16),
        pool_high=pltpu.VMEM((patches, width), b16),
        pool_low=pltpu.VMEM((patches, width), b16),
        latent=pltpu.VMEM((own_count, patches, columns), b16),
    )

    @functools.partial(pl.run_scoped, **last)
    def _(**scoped):
        last_parts(types.SimpleNamespace(**scoped))

    if summing:
        while gains.steps:
            gains.tick()
            point()
        flows.drain()
    ends = [pltpu.make_async_copy(r.gain_sum, r.gain_out, r.end_sem.at[4])]
    if not summing:
        ends += [
            pltpu.make_async_copy(r.up, r.up_sum, r.end_sem.at[0]),
            pltpu.make_async_copy(r.down, r.down_sum, r.end_sem.at[1]),
            pltpu.make_async_copy(r.attn_out_part.at[section], r.attn_out_sum, r.end_sem.at[3]),
        ]
        ends += [
            pltpu.make_async_copy(
                r.attn_in_part.at[section, :, pl.ds(j * columns, columns)], r.attn_in_sum.at[j],
                r.end_sem.at[5 + j],
            )
            for j in range(3)
        ]
    for copy in ends:
        copy.start()
    for copy in ends:
        copy.wait()


class Gains:
    def __init__(self, r, section, tensor, flows):
        self.r = r
        z = flows.z
        place = lax.axis_index("dp")
        near = place + SHORT * (1 - 2 * lax.rem(z, 2))
        far = place + 2 * SHORT * (1 - 2 * (z // 2))
        self.targets = [
            {"tensor": 1 - tensor}, {"section": 1 - section}, {"dp": flows.beside},
            {"dp": near}, {"dp": far},
        ]
        self.steps = list(range(len(self.targets) + 1))

    def copy(self, n):
        r = self.r
        return pltpu.make_async_remote_copy(
            src_ref=r.gain_held.at[n], dst_ref=r.gain_got.at[n], send_sem=r.gain_send.at[n],
            recv_sem=r.gain_recv.at[n], device_id=self.targets[n], device_id_type=MESH,
        )

    def tick(self):
        if not self.steps:
            return
        r, n = self.r, self.steps.pop(0)
        if n == 0:
            r.gain_held[0] = r.gain_sum[...]
        else:
            self.copy(n - 1).wait()
            value = r.gain_held[n - 1] + r.gain_got[n - 1]
            if n < len(self.targets):
                r.gain_held[n] = value
            else:
                r.gain_sum[...] = value
        if n < len(self.targets):
            self.copy(n).start()


def greet_grid(flows, others):
    barrier = pltpu.get_barrier_semaphore()

    def signal(place):
        pl.semaphore_signal(barrier, inc=1, device_id=place, device_id_type=MESH)

    for axis, index in others:
        signal({axis: index})
    signal({"dp": flows.beside})
    signal({"dp": lax.axis_index("dp") + 2 * SHORT * (1 - 2 * (flows.z // 2))})
    pl.when(flows.z < LONG - 1)(lambda: signal({"dp": flows.right}))
    pl.when(flows.z > 0)(lambda: signal({"dp": flows.left}))
    inner = jnp.logical_and(flows.z > 0, flows.z < LONG - 1)
    pl.semaphore_wait(barrier, jnp.where(inner, len(others) + 4, len(others) + 3))


def backward(kept, patch_ids):
    own, patches, width = kept["normed"].shape
    sequences, byte_count = patch_ids.shape
    columns = kept["q1"].shape[-1]
    hidden = kept["hidden"].shape[-1]
    half, half_bytes = width // 2, byte_count // 2
    sems = pltpu.SemaphoreType.DMA
    vmem = pltpu.VMEM
    rows16 = vmem((own, patches, width), b16)
    scratch = dict(
        inner=rows16,
        grad_in=rows16,
        inner_part=rows16,
        inner_got=rows16,
        normed=rows16,
        patch_norms=vmem((own, patches, LANES), f32),
        branch=rows16,
        normed_part=rows16,
        normed_got=rows16,
        source_part=vmem((own, byte_count, width), b16),
        source_got=vmem((own, half_bytes, width), b16),
        latent_got=vmem((own, patches, columns), b16),
        w_in=vmem((width, 3 * columns), b16),
        w_out=vmem((columns, width), b16),
        gain=vmem((2, 2, width), f32),
        gain_sum=vmem((4, width), f32),
        down_got=vmem((hidden, half), b16),
        down=vmem((hidden, half), b16),
        up=vmem((width, hidden), b16),
        attn_in_part=vmem((2, width, 3 * columns), b16),
        attn_out_part=vmem((2, columns, width), b16),
        big_got=vmem((width, 3 * columns), b16),
        attn_out_got=vmem((columns, width), b16),
        load_sem=sems((16,)),
        first_sem=sems((8,)),
        cross_send=sems((5, own)),
        cross_recv=sems((5, own)),
        give_send=sems((5,)),
        give_recv=sems((5,)),
        out_sem=sems((2, own)),
        out_send=sems((2, own)),
        out_recv=sems((2, own)),
        end_sem=sems((8,)),
        free_sem=pltpu.SemaphoreType.REGULAR,
    )
    slots = []
    if on_grid():
        shares = SHARES
        count = 0
        for n, (cols, long, short) in enumerate(shares):
            start = 0
            for goes_long, rows in [(1, k) for k in long] + [(0, k) for k in short]:
                name = f"s{count}"
                held = 7 * rows // LONG if goes_long else 3 * rows // SHORT
                scratch[name] = vmem((held, cols), b16)
                slots.append((n, count, goes_long, name, start, rows))
                start += rows
                count += 1
        scratch |= dict(
            flow_send=sems((count, 17)),
            flow_recv=sems((count, 17)),
            flow_near=sems((count,)),
            gain_held=vmem((5, 4, width), f32),
            gain_got=vmem((5, 4, width), f32),
            gain_send=sems((5,)),
            gain_recv=sems((5,)),
        )
    ins = [("ids", patch_ids, True)]
    ins += [("in_" + name, kept[name], False) for name in (*KEPT, *LAYERS)]
    outs = [
        ("latents", shape((sequences, patches // 2, columns), b16)),
        ("byte_grad", shape((sequences, half_bytes, half), b16)),
        ("attn_in_sum", shape((3, width, columns), b16)),
        ("attn_out_sum", shape((columns, width), b16)),
        ("gain_out", shape((4, width), f32)),
        ("up_sum", shape((width, hidden), b16)),
        ("down_sum", shape((hidden, half), b16)),
    ]

    def kernel(r):
        r.slots = {}
        for n, count, goes_long, name, start, rows in slots:
            r.slots.setdefault(n, []).append((count, goes_long, getattr(r, name), start, rows))
        backward_kernel(r)

    return named_call(kernel, ins, outs, scratch, collective_id=1)


def widen(up, attn_in, attn_out, down):
    half, hidden = up.shape[0] // 2, up.shape[1]
    steps = 8
    flat_in = attn_in.reshape(-1, attn_in.shape[2])

    def rows(array, offset=0):
        count = array.shape[0] // steps
        return pl.BlockSpec((count, array.shape[1]), lambda t: (t + offset, 0))

    def body(gate_in, up_in, in_in, out_in, down_in, up_o, in_o, out_o, down_o):
        up_o[:, 0, :] = gate_in[...].astype(f32)
        up_o[:, 1, :] = up_in[...].astype(f32)
        for src, dst in ((in_in, in_o), (out_in, out_o), (down_in, down_o)):
            dst[...] = src[...].astype(f32)

    part = half // steps
    feed = [pl.BlockSpec((part, hidden), lambda t: (t, 0))]
    feed += [pl.BlockSpec((part, hidden), lambda t: (t + steps, 0))]
    up_out, in_out, out_out, down_out = pl.pallas_call(
        body,
        grid=(steps,),
        out_shape=(
            shape((half, 2, hidden), f32), shape(flat_in.shape, f32), shape(attn_out.shape, f32),
            shape(down.shape, f32),
        ),
        in_specs=[*feed, rows(flat_in), rows(attn_out), rows(down)],
        out_specs=(
            pl.BlockSpec((part, 2, hidden), lambda t: (t, 0, 0)),
            rows(flat_in), rows(attn_out), rows(down),
        ),
        compiler_params=pltpu.CompilerParams(vmem_limit_bytes=VMEM_BYTES),
    )(up, up, flat_in, attn_out, down)
    return up_out, in_out.reshape(attn_in.shape), out_out, down_out


def swap(values, axis):
    return lax.ppermute(values, axis, [(0, 1), (1, 0)])


def sum_small(values):
    values = values + swap(values, "tensor")
    values = values + swap(values, "section")
    return lax.psum(values, "dp")


def per_device(byte_states, patch_ids, attn_in, attn_out, gains, ffn_in, ffn_out, latent_grad):
    is_first = lax.axis_index("section") == 0
    kept = forward(
        byte_states, patch_ids, attn_in, attn_out, gains, ffn_in.transpose(1, 0, 2), ffn_out,
        latent_grad,
    )
    got = backward(kept, patch_ids)
    sums = [got[name] for name in ("down_sum", "up_sum", "attn_in_sum", "attn_out_sum")]
    if not on_grid():
        sums = [lax.psum(value, "dp") for value in sums]
    down, up, in_sum, out_sum = sums
    up_out, in_sum, out_sum, down = widen(up, in_sum, out_sum, down)
    gain_sum = got["gain_out"] if on_grid() else sum_small(got["gain_out"])
    gain_out = jnp.where(is_first, gain_sum[0:2], gain_sum[2:4])
    return (
        got["latents"], got["byte_grad"], in_sum[None], out_sum[None], gain_out[None], up_out, down
    )


def solution(mesh):
    return jax.shard_map(
        per_device,
        mesh=mesh,
        in_specs=(
            P("dp", None, None),
            P("dp", None),
            P("section", None, None, "tensor"),
            P("section", "tensor", None),
            P("section", None, None),
            P(None, None, "tensor"),
            P("tensor", None),
            P("dp", None, None),
        ),
        out_specs=(
            P("dp", "section", "tensor"),
            P("dp", "tensor", "section"),
            P("section", None, None, "tensor"),
            P("section", "tensor", None),
            P("section", None, None),
            P("section", None, "tensor"),
            P("tensor", "section"),
        ),
        check_vma=False,
    )
```

```python
import functools
import types

import jax
import jax.numpy as jnp
from jax import lax
from jax.experimental import pallas as pl
from jax.experimental.pallas import tpu as pltpu
from jax.sharding import PartitionSpec as P

HD = 64
LANES = 128
BLOCK = 256
WIDE = 512
EPSILON = 1e-05
NEGATIVE = -1000000000.0
SCALE = HD ** (-0.5)
VMEM_BYTES = 63 * 1024 * 1024

f32 = jnp.float32
b16 = jnp.bfloat16


def dot(a, b):
    return jnp.dot(a, b, preferred_element_type=f32)


def dot_rt(a, b):
    return lax.dot_general(a, b, (((1,), (1,)), ((), ())), preferred_element_type=f32)


def dot_lt(a, b):
    return lax.dot_general(a, b, (((0,), (0,)), ((), ())), preferred_element_type=f32)


def inverse_rms(values):
    return lax.rsqrt(jnp.mean(values * values, axis=-1, keepdims=True) + EPSILON)


def iota(shape, dim):
    return lax.broadcasted_iota(jnp.int32, shape, dim)


def one_hot(condition):
    return jnp.where(condition, 1.0, 0.0).astype(b16)


def segment_max(values, ids):
    width = values.shape[1]
    lane = iota(ids.shape, 1)
    lowest = -3.0e38
    ahead, behind = values, values
    step = 1
    while step < width:
        left, right = step, width - step
        same_left = jnp.logical_and(pltpu.roll(ids, left, axis=1) == ids, lane >= step)
        same_right = jnp.logical_and(pltpu.roll(ids, right, axis=1) == ids, lane < right)
        ahead = jnp.maximum(ahead, jnp.where(same_left, pltpu.roll(ahead, left, axis=1), lowest))
        behind = jnp.maximum(
            behind, jnp.where(same_right, pltpu.roll(behind, right, axis=1), lowest)
        )
        step *= 2
    return jnp.maximum(ahead, behind)


def head_masks(width):
    heads_in = one_hot(iota((width, LANES), 0) // HD == iota((width, LANES), 1))
    heads_out = one_hot(iota((LANES, width), 1) // HD == iota((LANES, width), 0))
    return heads_in, heads_out


def split_dot(values, matrix):
    high = values.astype(b16)
    low = (values - high.astype(f32)).astype(b16)
    return dot(high, matrix) + dot(low, matrix)


def block_at(index, size=BLOCK):
    return pl.ds(pl.multiple_of(index * size, size), size)


def each_block(count, body, size=BLOCK):
    @pl.loop(0, count // size)
    def _(index):
        body(block_at(index, size))


MESH = pl.DeviceIdType.MESH


def remote(src, dst, send, recv, axis, index):
    return pltpu.make_async_remote_copy(
        src_ref=src, dst_ref=dst, send_sem=send, recv_sem=recv,
        device_id={axis: index}, device_id_type=MESH,
    )


def greet(places):
    barrier = pltpu.get_barrier_semaphore()
    for axis, index in places:
        pl.semaphore_signal(barrier, inc=1, device_id={axis: index}, device_id_type=MESH)
    pl.semaphore_wait(barrier, len(places))


def exchange_layer(r, section, tensor):
    columns = r.attn_in.shape[3]
    copies = []
    for n, (src, dst) in enumerate(
        [
            (r.attn_in.at[0, j], r.w_in.at[section, :, pl.ds(j * columns, columns)])
            for j in (1, 2, 0)
        ]
        + [
            (r.attn_out.at[0], r.w_full.at[section, block_at(tensor, columns), :]),
            (r.gains.at[0], r.gain.at[section]),
        ]
    ):
        near = pltpu.make_async_copy(src, dst, r.near_sem.at[n])
        far = remote(src, dst, r.far_send.at[n], r.far_recv.at[n], "section", 1 - section)
        near.start()
        far.start()
        copies.append((near, far))
    return copies


def arrived(copies):
    for near, far in copies:
        near.wait()
        far.wait()


def members_of(r, seq, rows, patches):
    return one_hot(iota((patches, rows.size), 0) == r.ids[pl.ds(seq, 1), rows])


def names(**kinds):
    return tuple(kinds)


FIRST_KEPT = names(query_in=1, source_in=1, byte_norms=1)
CROSS_KEPT = names(q1=1, k1=1, v1=1, raised=1, inverse=1, mixed1=1)
SECOND_KEPT = names(normed=1, q2=1, k2=1, v2=1, totals=1, mixed2=1)
FEED_KEPT = names(
    inner=1, hidden=1, gate_grad=1, up_grad=1, grad_in=1, inner_part=1, patch_norms=1,
    latent_own=1, latent_send=1,
)
KEPT = FIRST_KEPT + CROSS_KEPT + SECOND_KEPT + FEED_KEPT
LAYERS = names(w_in=1, w_out=1, gain=1)


def forward_kernel(r):
    section, tensor = lax.axis_index("section"), lax.axis_index("tensor")
    own_count, patches, width = r.normed.shape
    byte_count = r.states.shape[1]
    columns = r.q1.shape[2]
    hidden = r.hidden.shape[2]
    heads = columns // HD
    greet([("section", 1 - section), ("tensor", 1 - tensor)])
    state_copies = [
        pltpu.make_async_copy(
            r.states.at[section * own_count + i], r.state_in.at[i], r.state_sem.at[i]
        )
        for i in range(own_count)
    ]
    for copy in state_copies:
        copy.start()
    layer = exchange_layer(r, section, tensor)
    grad_copies = [
        pltpu.make_async_copy(
            r.upstream.at[section * own_count + i], r.grad_in.at[i], r.grad_sem.at[i]
        )
        for i in range(own_count)
    ]
    feed_copies = [
        pltpu.make_async_copy(r.ffn_in, r.feed_in, r.feed_sem.at[0]),
        pltpu.make_async_copy(r.ffn_out, r.feed_out, r.feed_sem.at[1]),
    ]
    for copy in grad_copies + feed_copies:
        copy.start()
    heads_in, heads_out = head_masks(columns)

    def keep(name, i):
        n = KEPT.index(name)
        return pltpu.make_async_copy(
            getattr(r, name).at[i], getattr(r, "out_" + name).at[i], r.keep_sem.at[n, i]
        )

    def save(names, i):
        for name in names:
            keep(name, i).start()

    mine, theirs = block_at(tensor, columns), block_at(1 - tensor, columns)

    def exchange(step, i):
        held = r.heads_all.at[step, i, :, mine]
        return remote(
            held, held, r.part_send.at[step, i], r.part_recv.at[step, i], "tensor", 1 - tensor
        )

    def rows_across():
        return remote(
            r.attn_out.at[0], r.w_full.at[section, mine, :], r.rows_send.at[0], r.rows_recv.at[0],
            "tensor", 1 - tensor,
        )

    def rows_over():
        held = r.w_full.at[section, theirs, :]
        return remote(
            held, held, r.rows_send.at[1], r.rows_recv.at[1], "section", 1 - section
        )

    def pass_rows(layer_index):
        @pl.when(section == layer_index)
        def _():
            rows_across().wait_recv()
            rows_over().start()

    def have_rows(layer_index):
        @pl.when(section != layer_index)
        def _():
            rows_over().wait_recv()

    @pl.when(section == 0)
    def _():
        rows_across().start()

    for copy in state_copies:
        copy.wait()
    layer[-1][0].wait()
    layer[-1][1].wait()
    first_gain = r.gain.at[0]

    @pl.loop(0, own_count)
    def _(i):
        seq = section * own_count + i
        r.pool_sum[...] = jnp.zeros_like(r.pool_sum)

        def pool(rows):
            block = r.state_in[i, rows, :]
            r.pool_sum[...] += dot(members_of(r, seq, rows, patches), block)
            values = block.astype(f32)
            scale = inverse_rms(values)
            r.byte_norms[i, rows, :] = jnp.broadcast_to(scale, (BLOCK, LANES))
            r.source_in[i, rows, :] = (values * scale * first_gain[1:2, :]).astype(b16)

        each_block(byte_count, pool)
        row_ids = r.ids[pl.ds(seq, 1), :]
        counts = jnp.sum(
            jnp.where(iota((patches, byte_count), 0) == row_ids, 1.0, 0.0), axis=1, keepdims=True
        )
        values = r.pool_sum[...] / jnp.maximum(counts, 1.0)
        r.pooled[i] = values
        scale = inverse_rms(values)
        r.patch_norms[i] = jnp.broadcast_to(scale, (patches, LANES))
        r.query_in[i] = (values * scale * first_gain[0:1, :]).astype(b16)
        save(FIRST_KEPT, i)

    arrived(layer[:4])
    layer_saves = [
        pltpu.make_async_copy(src, dst, r.layer_sem.at[n])
        for n, (src, dst) in enumerate(
            ((r.w_in, r.out_w_in), (r.w_full.at[:, mine, :], r.out_w_out), (r.gain, r.out_gain))
        )
    ]
    for copy in layer_saves:
        copy.start()

    def first_layer(i):
        seq = section * own_count + i
        r.q1[i] = dot(r.query_in[i], r.w_in[0, :, :columns]).astype(b16)

        def project(rows):
            both = dot(r.source_in[i, rows, :], r.w_in[0, :, columns:])
            keys = both[:, :columns].astype(b16)
            r.k1[i, rows, :] = keys
            r.v1[i, rows, :] = both[:, columns:].astype(b16)
            spread = dot_lt(members_of(r, seq, rows, patches), r.q1[i])
            block_scores = dot((spread * keys.astype(f32)).astype(b16), heads_in) * SCALE
            r.scores[:, rows] = block_scores.T[:heads, :]

        each_block(byte_count, project, WIDE)
        scores = r.scores[...]
        r.scores[...] = jnp.exp(scores - segment_max(scores, r.ids[pl.ds(seq, 1), :]))
        r.mix_sum[...] = jnp.zeros_like(r.mix_sum)
        r.total_sum[...] = jnp.zeros_like(r.total_sum)

        def mix(rows):
            short = r.scores[:, rows]
            filled = jnp.concatenate([short, jnp.zeros((LANES - heads, WIDE), f32)], axis=0)
            raised = filled.T.astype(b16)
            r.raised[i, rows, :] = raised
            members = members_of(r, seq, rows, patches)
            weighted = (dot(raised, heads_out) * r.v1[i, rows, :].astype(f32)).astype(b16)
            r.mix_sum[...] += dot(members, weighted)
            r.total_sum[...] += dot(members, raised)

        each_block(byte_count, mix, WIDE)
        totals = r.total_sum[...]
        inverse = jnp.where(totals > 0.0, 1.0 / totals, 0.0)
        r.inverse[i] = inverse
        mixed = (r.mix_sum[...] * split_dot(inverse, heads_out)).astype(b16)
        r.mixed1[i] = mixed
        r.heads_all[0, i, :, mine] = mixed
        exchange(0, i).start()
        save(CROSS_KEPT, i)

    for i in range(own_count):
        first_layer(i)
        if i == 0:
            pl.when(section == 1)(rows_across().start)
            pass_rows(0)

    second_gain = r.gain.at[1]
    allowed = iota((patches, patches), 1) <= iota((patches, patches), 0)
    lane = iota((patches, LANES), 1)

    have_rows(0)

    def second_layer(i):
        exchange(0, i).wait()
        latent = (r.pooled[i] + dot(r.heads_all[0, i], r.w_full[0])).astype(b16)
        r.latent[i] = latent
        values = latent.astype(f32)
        scale = inverse_rms(values)
        r.patch_norms[i] = jnp.where(lane == 1, scale, r.patch_norms[i])
        normed = (values * scale * second_gain[0:1, :]).astype(b16)
        r.normed[i] = normed
        projected = dot(normed, r.w_in[1]).astype(b16)
        query, key, value = [projected[:, j * columns : (j + 1) * columns] for j in range(3)]
        r.q2[i] = query
        r.k2[i] = key
        r.v2[i] = value
        kept = jnp.zeros((patches, LANES), f32)
        outs = []
        for head in range(heads):
            own = slice(head * HD, (head + 1) * HD)
            scores = jnp.where(allowed, dot_rt(query[:, own], key[:, own]) * SCALE, NEGATIVE)
            highest = jnp.max(scores, axis=-1, keepdims=True)
            raised = jnp.exp(scores - highest)
            total = jnp.sum(raised, axis=-1, keepdims=True)
            outs.append(dot((raised / total).astype(b16), value[:, own]))
            kept = jnp.where(lane == head, highest + jnp.log(total), kept)
        r.totals[i] = kept
        mixed = jnp.concatenate(outs, axis=1).astype(b16)
        r.mixed2[i] = mixed
        r.heads_all[1, i, :, mine] = mixed
        exchange(1, i).start()
        save(SECOND_KEPT, i)

    for i in range(own_count):
        second_layer(i)
        if i == 0:
            pass_rows(1)
    have_rows(1)

    for copy in grad_copies + feed_copies:
        copy.wait()

    @pl.loop(0, own_count)
    def _(i):
        seq = section * own_count + i
        exchange(1, i).wait()
        values = r.latent[i].astype(f32) + dot(r.heads_all[1, i], r.w_full[1])
        r.middle[...] = values
        scale = inverse_rms(values)
        r.patch_norms[i] = jnp.where(lane == 2, scale, r.patch_norms[i])
        r.inner[i] = (values * scale * second_gain[1:2, :]).astype(b16)
        valid = iota((patches, 1), 0) <= jnp.max(r.ids[pl.ds(seq, 1), :], axis=1, keepdims=True)
        r.grad_in[i] = jnp.where(valid, r.grad_in[i].astype(f32), 0.0).astype(b16)

        gate = dot(r.inner[i], r.feed_in[0])
        up = dot(r.inner[i], r.feed_in[1])
        hidden_grad = dot_rt(r.grad_in[i], r.feed_out[...])
        gated = 1.0 / (1.0 + jnp.exp(-gate))
        act = gate * gated
        r.hidden[i] = (act * up).astype(b16)
        r.gate_grad[i] = (hidden_grad * up * (gated * (1.0 + gate * (1.0 - gated)))).astype(b16)
        r.up_grad[i] = (hidden_grad * act).astype(b16)
        inner_grad = dot_rt(r.gate_grad[i], r.feed_in[0]) + dot_rt(r.up_grad[i], r.feed_in[1])
        r.inner_part[i] = inner_grad.astype(b16)
        r.out_sum[...] = dot(r.hidden[i], r.feed_out[...])
        r.latent_own[i] = (r.middle[:, mine] + r.out_sum[:, mine]).astype(b16)
        r.latent_send[i] = r.out_sum[:, theirs].astype(b16)
        save(FEED_KEPT, i)

    @pl.loop(0, own_count)
    def _(i):
        for name in KEPT:
            keep(name, i).wait()

    for copy in layer_saves:
        copy.wait()
    rows_across().wait_send()
    rows_over().wait_send()


def shape(dims, dtype):
    return jax.ShapeDtypeStruct(dims, dtype)


def named_call(kernel, ins, outs, scratch, **params):
    any_space = pl.BlockSpec(memory_space=pl.ANY)
    whole = pl.BlockSpec(memory_space=pltpu.VMEM)
    names = [name for name, _, _ in ins] + [name for name, _ in outs] + list(scratch)

    def body(*refs):
        kernel(types.SimpleNamespace(**dict(zip(names, refs, strict=True))))

    got = pl.pallas_call(
        body,
        out_shape=tuple(s for _, s in outs),
        in_specs=[whole if inside else any_space for _, _, inside in ins],
        out_specs=tuple(any_space for _ in outs),
        scratch_shapes=list(scratch.values()),
        compiler_params=pltpu.CompilerParams(
            vmem_limit_bytes=VMEM_BYTES, has_side_effects=True, **params
        ),
    )(*(array for _, array, _ in ins))
    return {name: value for (name, _), value in zip(outs, got, strict=True)}


def forward(byte_states, patch_ids, attn_in, attn_out, gains, feed_in, feed_out, latent_grad):
    sequences, byte_count, width = byte_states.shape
    patches = byte_count // 4
    columns = attn_in.shape[-1]
    hidden = feed_out.shape[0]
    own = sequences // 2
    heads = columns // HD
    dims = dict(
        query_in=(own, patches, width, b16),
        source_in=(own, byte_count, width, b16),
        q1=(own, patches, columns, b16),
        k1=(own, byte_count, columns, b16),
        v1=(own, byte_count, columns, b16),
        raised=(own, byte_count, LANES, b16),
        inverse=(own, patches, LANES, f32),
        mixed1=(own, patches, columns, b16),
        byte_norms=(own, byte_count, LANES, f32),
        normed=(own, patches, width, b16),
        q2=(own, patches, columns, b16),
        k2=(own, patches, columns, b16),
        v2=(own, patches, columns, b16),
        totals=(own, patches, LANES, f32),
        mixed2=(own, patches, columns, b16),
        inner=(own, patches, width, b16),
        hidden=(own, patches, hidden, b16),
        gate_grad=(own, patches, hidden, b16),
        up_grad=(own, patches, hidden, b16),
        grad_in=(own, patches, width, b16),
        inner_part=(own, patches, width, b16),
        patch_norms=(own, patches, LANES, f32),
        latent_own=(own, patches, columns, b16),
        latent_send=(own, patches, columns, b16),
    )
    sems = pltpu.SemaphoreType.DMA
    scratch = {name: pltpu.VMEM(dims[name][:-1], dims[name][-1]) for name in KEPT}
    scratch |= dict(
        state_in=pltpu.VMEM((own, byte_count, width), b16),
        pooled=pltpu.VMEM((own, patches, width), f32),
        latent=pltpu.VMEM((own, patches, width), b16),
        middle=pltpu.VMEM((patches, width), f32),
        out_sum=pltpu.VMEM((patches, width), f32),
        w_in=pltpu.VMEM((2, width, 3 * columns), b16),
        w_full=pltpu.VMEM((2, 2 * columns, width), b16),
        gain=pltpu.VMEM((2, 2, width), f32),
        feed_in=pltpu.VMEM((2, width, hidden), b16),
        feed_out=pltpu.VMEM((hidden, width), b16),
        pool_sum=pltpu.VMEM((patches, width), f32),
        scores=pltpu.VMEM((heads, byte_count), f32),
        mix_sum=pltpu.VMEM((patches, columns), f32),
        total_sum=pltpu.VMEM((patches, LANES), f32),
        heads_all=pltpu.VMEM((2, own, patches, 2 * columns), b16),
        rows_send=sems((2,)),
        rows_recv=sems((2,)),
        state_sem=sems((own,)),
        grad_sem=sems((own,)),
        feed_sem=sems((2,)),
        near_sem=sems((5,)),
        far_send=sems((5,)),
        far_recv=sems((5,)),
        part_send=sems((2, own)),
        part_recv=sems((2, own)),
        keep_sem=sems((len(KEPT), own)),
        layer_sem=sems((len(LAYERS),)),
    )
    ins = [
        ("states", byte_states, False), ("ids", patch_ids, True), ("attn_in", attn_in, False),
        ("attn_out", attn_out, False), ("gains", gains, False), ("ffn_in", feed_in, False),
        ("ffn_out", feed_out, False), ("upstream", latent_grad, False),
    ]
    dims |= dict(
        w_in=(2, width, 3 * columns, b16),
        w_out=(2, columns, width, b16),
        gain=(2, 2, width, f32),
    )
    names = (*KEPT, *LAYERS)
    outs = [("out_" + name, shape(dims[name][:-1], dims[name][-1])) for name in names]
    got = named_call(forward_kernel, ins, outs, scratch, collective_id=0)
    return {name: got["out_" + name] for name in names}


def flat(ref, cols):
    block = ref[:, :, cols]
    return block.reshape(block.shape[0] * block.shape[1], block.shape[2])


LONG, SHORT = 4, 2


def rows_of(ref, start, rows):
    if not isinstance(start, int):
        start = pl.multiple_of(start, 16)
    return ref.at[pl.ds(start, rows), :]


def sum_rows(target, *terms):
    rows, width = target.shape
    step = rows
    while step * width > 100 * 1408 and step % 32 == 0:
        step //= 2

    def add(at):
        value = terms[0][at, :]
        for term in terms[1:]:
            value = value + term[at, :]
        target[at, :] = value

    if step == rows:
        add(slice(None))
    else:
        each_block(rows, add, step)


def add_rows(target, *others):
    sum_rows(target, target, *others)


SHARES = ((512, (384,), (1024,)), (1408, (128,), (256, 128)), (1408, (), (512,)), (1024, (256,), (256,)), (512, (), (512, 512)), (512, (), (512, 512)), (512, (), (512, 512)))
PLAN = ((((1,),(1,)),((),(1,)),((1,),(0,)),((),())),(((0,0,0),(0,0)),((1,),(2,)),((3,4),(1,)),((0,0,0,1),(0,0,0,0,1))),(((2,2,4,0,3),(3,2,2,2)),((0,3),(4,3,0,0,0)),((0,0),(4,0,0,1)),((2,3,2,2,4,5),(4,2,2,3,5,2,2))),(((2,),(4,)),((4,0,0),(5,)),((5,),(0,)),((),())),(((1,1,1,5),(0,3)),((),(2,2)),((2,2),()),((1,1,0,1),())),(((),(0,)),((0,2,2,2),()),((0,0,1,2),(2,2,2)),((2,),())),(((2,),(1,0,2,1,1,5)),((),(0,0,1)),((),(3,)),((),(1,0))),(((3,3),()),((3,2,5,1),(2,4,2,1)),((0,2,2),(4,5,2,2)),((3,0,3,3),())),(((),()),((1,),()),((1,3),(1,)),((),(1,))),(((4,4),()),((4,),()),((4,),()),((4,4),(3,3,1,3))),(((),(0,3,4)),((),()),((),(0,)),((2,),(2,4,4))),(((),()),((0,2),()),((1,1),(3,)),((),())),(((3,4,0),(10,2,11,3,7,8,12,4,4,6,6,6,9,13)),((1,),(7,13,5,9,8,3,12,1,6,1,0,4,6,10,3)),((3,),(12,13,6,7,11,9,10,3,8,5,1,0,4)),((4,),(7,6,11,8,4,9,10,13,12,6,5,6,6))),(((),(5,5)),((),()),((),()),((),(2,5))),(((5,5),(5,)),((3,1),(2,11)),((),(4,)),((5,),())),(((2,),(2,)),((4,),(6,4)),((),(6,2)),((),())),(((),(7,8)),((3,),()),((),()),((5,),(0,1,7,7,7))),(((),()),((4,),(3,2)),((0,),(1,3,7,6,4,3)),((),())),(((),(10,0,6,0,2,8,7,7,8,10)),((4,2),(4,)),((4,4,4,3,3,5,5),()),((1,5),(5,8,8))),(((0,0),(1,)),((5,0,3),(8,0,7,5,0,9,3,8,7,2,10,6,11,2,6)),((),(5,0,2,10,7,8,10,5,0)),((),())),(((),(0,)),((5,),(12,)),((),(2,)),((),(0,))),(((),(9,2,11,9)),((),(10,13,11,5,5,0)),((),(11,13)),((),(10,))),(((5,),()),((),()),((2,),(9,5,6,6,11)),((),(9,9,8,2,2))),(((),()),((0,1),()),((0,),(8,)),((),(11,11,0,10))),(((0,2,2,2,0,1),(2,9)),((),(12,0,7,0,0,9,1,2,2,2)),((),(2,2,0,9,12,12)),((2,),(10,9,11,3,12,0))),(((3,4),(10,11,12,13,11,12,12)),((),(7,)),((),()),((2,0,0,2),(12,2,12))),(((),()),((),(8,13)),((2,),()),((0,4,0,0),())),(((0,),(13,13)),((2,2,0,5),(10,)),((0,5,1,5),(7,8,2,0,0,0,9,8,11)),((3,),(4,13,13))),(((),()),((2,),(9,9)),((0,),(1,)),((2,),())),(((),(0,)),((),(3,)),((),(3,)),((),(0,))),(((),(1,0,4,2)),((),()),((),(13,)),((),(13,0))),(((17,15,2,2,14,21,16,3,18,2,14,20,4,14,14,5),(3,)),((14,18,0,0,15,0,0,20,17,16,2,21,4,5,19,5,14,14,2,2),(11,4)),((4,0,15,0,2,18,0,16,21,17,2,2,20,2,14,14),()),((14,14,14,4,1,2,19,16,3,21,15,18,17,16),())),(((),(2,6,6,8)),((14,14),(5,8,11,6,9,12)),((19,3,14),(2,7,10,5,11,12,4)),((20,5,0,16),(2,2,2,4,6,7,0,8,1,6))),(((16,15,16,17,1,0,15,15,18,18,19,5,17,17,20,21,19,16,20,20,18,19,0,21,2,19),(3,2,5,6,7,10,8,0,9,5,6,4,10,7,11,12,6,6)),((),(13,10,8,13,12,6,7,6,6,6,6,6,10)),((15,14,14),(10,9,10,12,6,7,13,8,6,6,6,9,13)),((19,14,17,15,15,15,21,17,18,16,21,17,18,20,20,20,19,19,18,2,5,0,2),(11,9,5,3,6,6,12,8,13,9,10,7,6))),(((14,14,14,14,21),(6,13,11,9,13)),((15,15,17,16,16,15,15,18,18,17,16,20,20,3,19,19,21,14,16,17,21),()),((5,15,16,2,16,17,17,15,19,15,18,18,14,20,19,20,16,21,21,16,17,15),(6,11,6,6)),((14,14,15,14),(10,6,6,12))),(((16,14,15),()),((18,19,15,14,18,17,20,20),()),((18,19,20,21,17,17,20,19,21,19,14,16),()),((16,),())),(((17,18,16,19,17,14,14,20),(6,)),((14,14,19,17,21,19,21,21,20),()),((14,14,14,18,18,14,21),()),((17,18,19,17,20,14,16,21,15,21),(5,))),(((21,15,18,14),()),((14,16),()),((),()),((20,18,14,14,14,14),(13,))),(((20,21,19),(12,)),((14,14,18),(11,12,13)),((20,14),(12,13)),((21,19),(11,6))))


class Flows:
    def __init__(self, r, section):
        self.r = r
        self.section = section
        place = lax.axis_index("dp")
        self.z, self.y = place // SHORT, lax.rem(place, SHORT)
        self.right, self.left = place + SHORT, place - SHORT
        self.beside = place + 1 - 2 * self.y
        self.flows = []
        self.done = {(z, s): [] for z in range(LONG) for s in range(2)}
        self.points = 0

    def hop(self, src, dst, n, j, target):
        r = self.r
        return pltpu.make_async_remote_copy(
            src_ref=src, dst_ref=dst, send_sem=r.flow_send.at[n, j], recv_sem=r.flow_recv.at[n, j],
            device_id={"dp": target}, device_id_type=MESH,
        )

    def reduce_events(self, n, part, slot):
        def up(k):
            return self.hop(slot(k - 1), slot(k - 1), n, k - 1, self.right)

        def down(k):
            return self.hop(slot(3 + k), slot(3 + k), n, 3 + k, self.left)

        def pass_on(copy, held, k):
            copy(k).wait_recv()
            add_rows(held, part(k))
            copy(k).start()

        def begin(z):
            if z == 0:
                for k in (3, 2, 1):
                    self.hop(part(k), slot(k - 1), n, k - 1, self.right).start()
            if z == 3:
                for k in (0, 1, 2):
                    self.hop(part(k), slot(3 + k), n, 3 + k, self.left).start()

        def passing(at_one, at_two):
            def event(z):
                if z in (1, 2):
                    way, k = (at_one, at_two)[z - 1]
                    pass_on(*((up, slot(k - 1)) if way > 0 else (down, slot(3 + k))), k)

            return event

        def close(z):
            got = []
            if z >= 1:
                up(z).wait_recv()
                got.append(slot(z - 1))
            if z <= 2:
                down(z).wait_recv()
                got.append(slot(3 + z))
            add_rows(part(z), *got)

        def sent(z):
            for k in ((1, 2, 3), (2, 3), (3,), ())[z]:
                up(k).wait_send()
            for k in ((), (0,), (0, 1), (0, 1, 2))[z]:
                down(k).wait_send()

        passes = [
            passing((1, 3), (-1, 0)), passing((1, 2), (-1, 1)), passing((-1, 0), (1, 3)),
        ]
        return begin, passes, close, sent

    def gather_events(self, n, own, out):
        def up(src, k, d):
            return self.hop(src, out(k), n, 7 + d, self.right)

        def down(src, k, d):
            return self.hop(src, out(k), n, 10 + d, self.left)

        def near(z):
            return pltpu.make_async_copy(own(z), out(z), self.r.flow_near.at[n])

        def starts(z, d, way):
            k = z - d * way
            src = own(z) if d == 0 else out(k)
            copies = []
            if d < LONG - 1 and 0 <= z + way < LONG:
                copies.append((up if way > 0 else down)(src, k, d))
            return copies

        def begin(z):
            near(z).start()
            for copy in starts(z, 0, 1) + starts(z, 0, -1):
                copy.start()

        def step(d, way):
            def event(z):
                k = z - d * way
                if 0 <= k < LONG:
                    (up if way > 0 else down)(out(k), k, d - 1).wait_recv()
                    for copy in starts(z, d, way):
                        copy.start()

            return event

        def sent(z):
            near(z).wait()
            for way in (1, -1):
                for d in range(LONG):
                    if 0 <= z - d * way < LONG:
                        for copy in starts(z, d, way):
                            copy.wait_send()

        return begin, [step(d, way) for d in (1, 2, 3) for way in (1, -1)], sent

    def long_first(self, n, data, out, slots, start, rows):
        c = rows // LONG

        def part(k):
            return data(start + k * c, c)

        def slot(j):
            return rows_of(slots, j * c, c)

        def beside(z):
            return self.hop(part(z), slot(6), n, 6, self.beside)

        begin, passes, close, reduce_sent = self.reduce_events(n, part, slot)
        gather, steps, gather_sent = self.gather_events(
            n, lambda z: slot(6), lambda k: out(start + k * c, c)
        )

        def middle(z):
            close(z)
            beside(z).start()

        def turn(z):
            beside(z).wait_recv()
            add_rows(slot(6), part(z))
            gather(z)

        def sent(z):
            reduce_sent(z)
            beside(z).wait_send()
            gather_sent(z)

        return [begin, *passes, middle, turn, *steps], sent

    def short_first(self, n, data, out, slots, start, rows):
        half = rows // SHORT

        def mine(y):
            return data(start + y * half, half)

        def place(y):
            return out(start + y * half, half)

        def slot(j):
            return rows_of(slots, j * half, half)

        def beside():
            return self.hop(mine(1 - self.y), slot(0), n, 6, self.beside)

        inward = (self.right, self.right, self.left, self.left)
        outward = (None, self.left, self.right, None)

        def lean(z):
            middle = 1 if z in (1, 2) else 0
            return self.hop(mine(self.y), slot(1 + middle), n, middle, inward[z])

        def settle(z):
            src = slot(0) if z in (1, 2) else place(self.y)
            return self.hop(src, place(self.y), n, 7, outward[z])

        def near(z):
            return pltpu.make_async_copy(slot(0), place(self.y), self.r.flow_near.at[n])

        def spread(z):
            src = slot(0) if z in (1, 2) else place(self.y)
            return self.hop(src, place(self.y), n, 13, self.beside)

        def first(z):
            beside().start()

        def turn(z):
            beside().wait_recv()
            add_rows(mine(self.y), slot(0))
            if z in (0, 3):
                lean(z).start()

        def pair(z):
            if z in (1, 2):
                self.hop(slot(1), slot(1), n, 0, inward[z]).wait_recv()
                add_rows(mine(self.y), slot(1))
                lean(z).start()

        def close(z):
            if z in (1, 2):
                lean(z).wait_recv()
                sum_rows(slot(0), mine(self.y), slot(2))
                near(z).start()
                settle(z).start()
                spread(z).start()

        def outer(z):
            if z in (0, 3):
                self.hop(place(self.y), place(self.y), n, 7, inward[z]).wait_recv()
                spread(z).start()

        def end(z):
            there = place(1 - self.y)
            self.hop(there, there, n, 13, self.beside).wait_recv()

        def sent(z):
            beside().wait_send()
            lean(z).wait_send()
            spread(z).wait_send()
            if z in (1, 2):
                settle(z).wait_send()
                near(z).wait()

        return [first, turn, pair, close, outer, end], sent

    def open(self, only, *flows):
        for events, sent in flows:
            self.flows.append((only, events, sent))
            for counts in self.done.values():
                counts.append(0)

    def advance(self, z, s, todo):
        def body():
            for n in todo:
                self.flows[n][1][self.done[z, s][n]](z)
                self.done[z, s][n] += 1

        return body

    def point(self):
        plan = PLAN[self.points] if self.points < len(PLAN) else ()
        self.points += 1
        for z, lists in enumerate(plan):
            first, second = self.done[z, 0], self.done[z, 1]
            if lists[0] == lists[1] and all(first[n] == second[n] for n in lists[0]):
                if lists[0]:
                    pl.when(self.z == z)(self.advance(z, 0, lists[0]))
                    for n in lists[0]:
                        second[n] = first[n]
                continue
            for s in range(2):
                here = jnp.logical_and(self.z == z, self.section == s)
                pl.when(here)(self.advance(z, s, lists[s]))

    def drain(self):
        for (z, s), counts in self.done.items():

            def body(z=z, s=s, counts=counts):
                mine = [n for n, flow in enumerate(self.flows) if flow[0] in (None, s)]
                longest = max(len(self.flows[n][1]) for n in mine)
                for k in range(longest):
                    for n in mine:
                        if counts[n] <= k < len(self.flows[n][1]):
                            self.flows[n][1][k](z)
                for n in mine:
                    self.flows[n][2](z)

            pl.when(jnp.logical_and(self.z == z, self.section == s))(body)


def on_grid():
    return lax.axis_size("dp") == LONG * SHORT


def backward_kernel(r):
    section, tensor = lax.axis_index("section"), lax.axis_index("tensor")
    own_count, patches, width = r.normed.shape
    byte_count = r.ids.shape[1]
    columns = r.w_out.shape[0]
    hidden = r.down.shape[0]
    heads = columns // HD
    half = width // 2
    half_bytes = byte_count // 2
    summing = on_grid()
    loads = {}

    def load(name, src, dst, *sem):
        copy = pltpu.make_async_copy(src, dst, r.load_sem.at[sem])
        copy.start()
        loads[name] = copy

    held_names = ("inner", "grad_in", "inner_part", "normed", "patch_norms", "gain")
    for n, name in enumerate(held_names):
        load(name, getattr(r, "in_" + name), getattr(r, name), n)
    load("w_in", r.in_w_in.at[1], r.w_in, 6)
    load("w_out", r.in_w_out.at[1], r.w_out, 7)
    others = [("section", 1 - section), ("tensor", 1 - tensor)]
    flows = Flows(r, section) if summing else None
    if summing:
        greet_grid(flows, others)
    else:
        greet(others)

    def cross(src, dst, i, sem):
        return remote(
            src, dst, r.cross_send.at[sem, i], r.cross_recv.at[sem, i], "tensor", 1 - tensor
        )

    def inner_exchange(i):
        return cross(r.in_inner_part.at[i], r.inner_got.at[i], i, 0)

    def normed_exchange(i):
        return cross(r.normed_part.at[i], r.normed_got.at[i], i, 1)

    def query_exchange(i):
        return cross(r.inner_part.at[i], r.inner_got.at[i], i, 2)

    def source_exchange(i):
        theirs = block_at(1 - tensor, half_bytes)
        return cross(r.source_part.at[i, theirs, :], r.source_got.at[i], i, 3)

    def latent_exchange(i):
        return cross(r.in_latent_send.at[i], r.latent_got.at[i], i, 4)

    for i in range(own_count):
        inner_exchange(i).start()
    def give(n, src, dst):
        return remote(src, dst, r.give_send.at[n], r.give_recv.at[n], "section", 1 - section)

    def point():
        if summing:
            flows.point()

    def summed(n, data, out, only=None):
        if summing:
            for flow, goes_long, slots, start, rows in r.slots[n]:
                make = flows.long_first if goes_long else flows.short_first
                flows.open(only, make(flow, data, out, slots, start, rows))

    def up_half(ref, n):
        return ref.at[pl.ds(n * half, half), :]

    def whole(view):
        return lambda start, rows: rows_of(view(), start, rows)

    @functools.partial(
        pl.run_scoped,
        hidden_all=pltpu.VMEM((own_count, patches, hidden), b16),
        gate_all=pltpu.VMEM((own_count, patches, hidden), b16),
        up_all=pltpu.VMEM((own_count, patches, hidden), b16),
        down_give=pltpu.VMEM((hidden, half), b16),
    )
    def _(hidden_all, gate_all, up_all, down_give):
        parts = {"hidden": hidden_all, "gate_grad": gate_all, "up_grad": up_all}
        for n, (name, ref) in enumerate(parts.items()):
            load(name, getattr(r, "in_" + name), ref, n + 8)
        for name in (*parts, "inner", "grad_in"):
            loads[name].wait()

        def down_grad(target, side):
            upstream = flat(r.grad_in, block_at(side, half))

            def tile(cols):
                target[cols, :] = dot_lt(flat(hidden_all, cols), upstream).astype(b16)

            each_block(hidden, tile)
            if hidden % BLOCK:
                tile(pl.ds(hidden - hidden % BLOCK, hidden % BLOCK))

        def up_grad(target, ref, side):
            upstream = flat(ref, slice(None))

            def tile(rows):
                cols = pl.ds(pl.multiple_of(side * half + rows.start, BLOCK), BLOCK)
                target[rows, :] = dot_lt(flat(r.inner, cols), upstream).astype(b16)

            each_block(half, tile)

        used = pl.ds(0, hidden)
        give_rows = [pl.ds(0, half), pl.ds(half, half)]
        gate_give, up_give = [r.attn_in_part.at[1, rows, used] for rows in give_rows]
        gate_got, up_got = [r.big_got.at[rows, used] for rows in give_rows]
        gate_own, up_own = [r.up.at[rows, :] for rows in give_rows]
        gifts = [
            give(0, down_give, r.down_got), give(1, gate_give, gate_got), give(2, up_give, up_got)
        ]
        other = 1 - section
        down_grad(down_give, other)
        gifts[0].start()
        down_grad(r.down, section)
        up_grad(gate_give, gate_all, other)
        gifts[1].start()
        gifts[0].wait()
        add_rows(r.down, r.down_got)
        summed(0, whole(lambda: r.down), whole(lambda: r.down_sum))
        point()
        up_grad(gate_own, gate_all, section)
        up_grad(up_give, up_all, other)
        gifts[2].start()
        gifts[1].wait()
        add_rows(gate_own, gate_got)
        summed(1, whole(lambda: up_half(r.up, 0)), whole(lambda: up_half(r.up_sum, 0)))
        point()
        up_grad(up_own, up_all, section)
        gifts[2].wait()
        add_rows(up_own, up_got)
        summed(2, whole(lambda: up_half(r.up, 1)), whole(lambda: up_half(r.up_sum, 1)))
        point()
        pl.semaphore_signal(
            r.free_sem, inc=1, device_id={"section": other}, device_id_type=MESH
        )

    def gifts_of(layer):
        return [
            give(3, r.attn_in_part.at[layer], r.big_got),
            give(4, r.attn_out_part.at[layer], r.attn_out_got),
        ]

    def hand_over(layer):
        @pl.when(section != layer)
        def _():
            pl.semaphore_wait(r.free_sem, 1)
            for gift in gifts_of(layer):
                gift.start()

    def take_over(layer):
        @pl.when(section != layer)
        def _():
            for gift in gifts_of(layer):
                gift.wait_send()

        @pl.when(section == layer)
        def _():
            for gift in gifts_of(layer):
                gift.wait_recv()
            add_rows(r.attn_out_part.at[layer], r.attn_out_got)
            add_rows(r.attn_in_part.at[layer], r.big_got)

    def sum_layer(layer, which):
        def columns_of(j):
            return whole(lambda: r.attn_in_part.at[layer, :, pl.ds(j * columns, columns)])

        if which == 3:
            summed(
                3, whole(lambda: r.attn_out_part.at[layer]), whole(lambda: r.attn_out_sum), layer
            )
        else:
            summed(4 + which, columns_of(which), whole(lambda: r.attn_in_sum.at[which]), layer)

    first_gain, second_gain = r.gain.at[0], r.gain.at[1]

    def back_through(normed, gain_row, scale, upstream):
        unit = normed.astype(f32) / gain_row
        scaled = upstream * gain_row
        mean = jnp.mean(unit * scaled, axis=-1, keepdims=True)
        return (scaled - unit * mean) * scale, unit

    @functools.partial(
        pl.run_scoped,
        q2=pltpu.VMEM((own_count, patches, columns), b16),
        k2=pltpu.VMEM((own_count, patches, columns), b16),
        v2=pltpu.VMEM((own_count, patches, columns), b16),
        totals=pltpu.VMEM((own_count, patches, LANES), f32),
        mixed2=pltpu.VMEM((own_count, patches, columns), b16),
        second_grads=pltpu.VMEM((own_count, patches, 3 * columns), b16),
        mixed_grads=pltpu.VMEM((patches, columns), b16),
    )
    def _(q2, k2, v2, totals, mixed2, second_grads, mixed_grads):
        parts = {"q2": q2, "k2": k2, "v2": v2, "totals": totals, "mixed2": mixed2}
        for n, (name, ref) in enumerate(parts.items()):
            load(name, getattr(r, "in_" + name), ref, n + 11)
        for name in (*held_names[2:], "w_in", "w_out", *parts):
            loads[name].wait()
        r.gain_sum[...] = jnp.zeros_like(r.gain_sum)
        allowed = iota((patches, patches), 1) <= iota((patches, patches), 0)
        for i in range(own_count):
            inner_exchange(i).wait()
            own_part = r.inner_part[i].astype(f32)
            back, unit = back_through(
                r.inner[i], second_gain[1:2, :], r.patch_norms[i, :, 2:3],
                own_part + r.inner_got[i].astype(f32),
            )
            r.gain_sum[3:4, :] += jnp.sum(unit * own_part, axis=0, keepdims=True)
            branch = (r.grad_in[i].astype(f32) + back).astype(b16)
            r.branch[i] = branch
            mixed_grads[...] = dot_rt(branch, r.w_out[...]).astype(b16)
            point()

            mixed_grad = mixed_grads[...]
            outs = [[], [], []]
            for head in range(heads):
                own = slice(head * HD, (head + 1) * HD)
                query, key, value = q2[i, :, own], k2[i, :, own], v2[i, :, own]
                upper = mixed_grad[:, own]
                scores = jnp.where(allowed, dot_rt(query, key) * SCALE, NEGATIVE)
                probs = jnp.exp(scores - totals[i, :, head : head + 1])
                prob_grad = dot_rt(upper, value)
                delta = jnp.sum(probs * prob_grad, axis=-1, keepdims=True)
                score_grad = (probs * (prob_grad - delta)).astype(b16)
                outs[0].append(dot(score_grad, key) * SCALE)
                outs[1].append(dot_lt(score_grad, query) * SCALE)
                outs[2].append(dot_lt(probs.astype(b16), upper))
            grads = jnp.concatenate(outs[0] + outs[1] + outs[2], axis=1).astype(b16)
            second_grads[i] = grads
            point()
            r.normed_part[i] = dot_rt(grads, r.w_in[...]).astype(b16)
            normed_exchange(i).start()
            point()

        def outer(target, rows_ref, upstream, tiles):
            @pl.loop(0, tiles)
            def _(t):
                cols = block_at(t)
                target[cols, :] = dot_lt(flat(rows_ref, cols), upstream).astype(b16)

        outer(r.attn_in_part.at[1], r.normed, flat(second_grads, slice(None)), width // BLOCK)
        point()
        outer(r.attn_out_part.at[1], mixed2, flat(r.branch, slice(None)), columns // BLOCK)
        hand_over(1)
        for i in range(own_count):
            latent_exchange(i).start()
        point()

    heads_in, heads_out = head_masks(columns)

    def first_layer(i, scoped):
        seq = section * own_count + i
        s = types.SimpleNamespace(**scoped)
        copies = {}
        kinds = names(q1=1, v1=1, raised=1, inverse=1, mixed1=1, source_in=1, query_in=1)
        for n, name in enumerate(kinds):
            copy = pltpu.make_async_copy(
                getattr(r, "in_" + name).at[i], getattr(s, name), r.first_sem.at[n]
            )
            copy.start()
            copies[name] = copy
        normed_exchange(i).wait()
        own_part = r.normed_part[i].astype(f32)
        back, unit = back_through(
            r.normed[i], second_gain[0:1, :], r.patch_norms[i, :, 1:2],
            own_part + r.normed_got[i].astype(f32),
        )
        r.gain_sum[2:3, :] += jnp.sum(unit * own_part, axis=0, keepdims=True)
        branch = (r.branch[i].astype(f32) + back).astype(b16)
        r.branch[i] = branch
        s.mixed_grad[...] = dot_rt(branch, r.w_out[...]).astype(b16)
        s.q_sum[...] = jnp.zeros_like(s.q_sum)
        s.delta_sum[...] = jnp.zeros_like(s.delta_sum)
        for copy in copies.values():
            copy.wait()
        point()
        if i == 0:
            take_over(1)
            for which in (3, 0, 1, 2):
                sum_layer(1, which)
            point()
        inverse = s.inverse[...]
        inverse_high = inverse.astype(b16)
        inverse_low = (inverse - inverse_high.astype(f32)).astype(b16)

        def value_side(rows):
            members = members_of(r, seq, rows, patches)
            spread = dot_lt(members, s.mixed_grad[...])
            scale = dot_lt(members, inverse_high) + dot_lt(members, inverse_low)
            probs = s.raised[rows, :].astype(f32) * scale
            s.probs[rows, :] = probs
            s.dkv[rows, columns:] = (dot(probs.astype(b16), heads_out) * spread).astype(b16)
            prob_grad = dot((spread * s.v1[rows, :].astype(f32)).astype(b16), heads_in)
            s.prob_grad[rows, :] = prob_grad
            product = probs * prob_grad
            high = product.astype(b16)
            low = (product - high.astype(f32)).astype(b16)
            s.delta_sum[...] += dot(members, high) + dot(members, low)

        for t in range(byte_count // WIDE):
            value_side(pl.ds(t * WIDE, WIDE))
            point()
        keys = pltpu.make_async_copy(r.in_k1.at[i], s.v1, r.first_sem.at[7])
        keys.start()
        delta = s.delta_sum[...]
        delta_high = delta.astype(b16)
        delta_low = (delta - delta_high.astype(f32)).astype(b16)

        def key_side(rows):
            members = members_of(r, seq, rows, patches)
            shift = dot_lt(members, delta_high) + dot_lt(members, delta_low)
            score_grad = (s.probs[rows, :] * (s.prob_grad[rows, :] - shift)).astype(b16)
            spread = dot(score_grad, heads_out)
            s.dkv[rows, :columns] = (spread * dot_lt(members, s.q1[...]) * SCALE).astype(b16)
            s.q_sum[...] += dot(members, (spread * s.v1[rows, :].astype(f32)).astype(b16))
            source = dot_rt(s.dkv[rows, :], r.w_in[:, columns:])
            r.source_part[i, rows, :] = source.astype(b16)
            unit_block = s.source_in[rows, :].astype(f32)
            r.gain_sum[1:2, :] += (
                jnp.sum(unit_block * source, axis=0, keepdims=True) / first_gain[1:2, :]
            )

        keys.wait()
        for t in range(byte_count // WIDE):
            for u in range(WIDE // BLOCK):
                key_side(pl.ds(t * WIDE + u * BLOCK, BLOCK))
            point()
        source_exchange(i).start()
        q_grad = (s.q_sum[...] * SCALE).astype(b16)
        query = dot_rt(q_grad, r.w_in[:, :columns])
        r.inner_part[i] = query.astype(b16)
        query_exchange(i).start()
        unit_pool = s.query_in[...].astype(f32)
        r.gain_sum[0:1, :] += (
            jnp.sum(unit_pool * query, axis=0, keepdims=True) / first_gain[0:1, :]
        )
        point()

        def add_to(target, rows, cols, value):
            if i:
                value = target[rows, cols].astype(f32) + value
            target[rows, cols] = value.astype(b16)

        for half_t in range(2):

            @pl.loop(0, half // BLOCK)
            def _(t, half_t=half_t):
                cols = pl.ds(pl.multiple_of(half_t * half + t * BLOCK, BLOCK), BLOCK)
                source = s.source_in[:, cols]
                target = r.attn_in_part.at[0]
                add_to(target, cols, slice(0, columns), dot_lt(s.query_in[:, cols], q_grad))
                add_to(target, cols, slice(columns, 3 * columns), dot_lt(source, s.dkv[...]))

            point()

        @pl.loop(0, columns // BLOCK)
        def _(t):
            cols = block_at(t)
            add_to(
                r.attn_out_part.at[0], cols, slice(None), dot_lt(s.mixed1[:, cols], branch)
            )

        point()

    def last_parts(s):
        outs = []

        own_rows = block_at(tensor, half_bytes)
        cols_keep, cols_give = block_at(section, half), block_at(1 - section, half)
        for i in range(own_count):
            seq = section * own_count + i
            finals = [
                pltpu.make_async_copy(
                    r.in_source_in.at[i, own_rows, :], s.source_in, r.first_sem.at[0]
                ),
                pltpu.make_async_copy(
                    r.in_byte_norms.at[i, own_rows, :], s.byte_norms, r.first_sem.at[1]
                ),
                pltpu.make_async_copy(r.in_query_in.at[i], s.query_in, r.first_sem.at[2]),
            ]
            for copy in finals:
                copy.start()
            query_exchange(i).wait()
            source_exchange(i).wait()
            for copy in finals:
                copy.wait()
            back, _ = back_through(
                s.query_in[...], first_gain[0:1, :], r.patch_norms[i, :, 0:1],
                r.inner_part[i].astype(f32) + r.inner_got[i].astype(f32),
            )
            counts = jnp.sum(
                jnp.where(iota((patches, byte_count), 0) == r.ids[pl.ds(seq, 1), :], 1.0, 0.0),
                axis=1, keepdims=True,
            )
            pool_grad = (r.branch[i].astype(f32) + back) / jnp.maximum(counts, 1.0)
            high = pool_grad.astype(b16)
            s.pool_high[...] = high
            s.pool_low[...] = (pool_grad - high.astype(f32)).astype(b16)

            @pl.loop(0, half_bytes // BLOCK)
            def _(t, i=i, seq=seq):
                rows = block_at(t)
                place = pl.ds(pl.multiple_of(tensor * half_bytes + t * BLOCK, BLOCK), BLOCK)
                members = members_of(r, seq, place, patches)
                spread = dot_lt(members, s.pool_high[...]) + dot_lt(members, s.pool_low[...])
                part = r.source_part[i, place, :].astype(f32)
                own, _ = back_through(
                    s.source_in[rows, :], first_gain[1:2, :], s.byte_norms[rows, 0:1],
                    part + r.source_got[i, rows, :].astype(f32),
                )
                r.source_got[i, rows, :] = (own + spread).astype(b16)

            near = pltpu.make_async_copy(
                r.source_got.at[i, :, cols_keep], r.byte_grad.at[seq], r.out_sem.at[1, i]
            )
            far = remote(
                r.source_got.at[i, :, cols_give], r.byte_grad.at[seq],
                r.out_send.at[1, i], r.out_recv.at[1, i], "section", 1 - section,
            )
            near.start()
            far.start()
            outs += [near, far]
            point()

        for copy in outs:
            copy.wait()

    load("w_in", r.in_w_in.at[0], r.w_in, 6)
    load("w_out", r.in_w_out.at[0], r.w_out, 7)
    loads["w_in"].wait()
    loads["w_out"].wait()
    one = dict(
        source_in=pltpu.VMEM((byte_count, width), b16),
        v1=pltpu.VMEM((byte_count, columns), b16),
        dkv=pltpu.VMEM((byte_count, 2 * columns), b16),
        probs=pltpu.VMEM((byte_count, LANES), f32),
        prob_grad=pltpu.VMEM((byte_count, LANES), f32),
        raised=pltpu.VMEM((byte_count, LANES), b16),
        inverse=pltpu.VMEM((patches, LANES), f32),
        q1=pltpu.VMEM((patches, columns), b16),
        mixed1=pltpu.VMEM((patches, columns), b16),
        query_in=pltpu.VMEM((patches, width), b16),
        mixed_grad=pltpu.VMEM((patches, columns), b16),
        q_sum=pltpu.VMEM((patches, columns), f32),
        delta_sum=pltpu.VMEM((patches, LANES), f32),
    )

    @functools.partial(pl.run_scoped, **one)
    def _(**scoped):
        for i in range(own_count):
            first_layer(i, scoped)

    hand_over(0)
    latent_outs = []
    half_rows = patches // 2
    rows_keep, rows_give = block_at(section, half_rows), block_at(1 - section, half_rows)
    for i in range(own_count):
        seq = section * own_count + i
        held = r.normed_part.at[i, :, pl.ds(0, columns)]
        own_load = pltpu.make_async_copy(r.in_latent_own.at[i], held, r.first_sem.at[i])
        own_load.start()
        own_load.wait()
        latent_exchange(i).wait()
        last = jnp.max(r.ids[pl.ds(seq, 1), :], axis=1, keepdims=True)
        valid = iota((patches, 1), 0) <= last
        values = r.normed_part[i, :, :columns].astype(f32) + r.latent_got[i].astype(f32)
        r.normed_part[i, :, :columns] = jnp.where(valid, values, 0.0).astype(b16)
        near = pltpu.make_async_copy(
            r.normed_part.at[i, rows_keep, pl.ds(0, columns)], r.latents.at[seq], r.out_sem.at[0, i]
        )
        far = remote(
            r.normed_part.at[i, rows_give, pl.ds(0, columns)], r.latents.at[seq],
            r.out_send.at[0, i], r.out_recv.at[0, i], "section", 1 - section,
        )
        near.start()
        far.start()
        latent_outs += [near, far]
    point()
    take_over(0)
    for which in (3, 0, 1, 2):
        sum_layer(0, which)
    point()
    gains = Gains(r, section, tensor, flows) if summing else None
    if summing:
        gains.tick()
    last = dict(
        source_in=pltpu.VMEM((half_bytes, width), b16),
        byte_norms=pltpu.VMEM((half_bytes, LANES), f32),
        query_in=pltpu.VMEM((patches, width), b16),
        pool_high=pltpu.VMEM((patches, width), b16),
        pool_low=pltpu.VMEM((patches, width), b16),
    )

    @functools.partial(pl.run_scoped, **last)
    def _(**scoped):
        last_parts(types.SimpleNamespace(**scoped))

    if summing:
        while gains.steps:
            gains.tick()
            point()
        flows.drain()
    ends = [pltpu.make_async_copy(r.gain_sum, r.gain_out, r.end_sem.at[4])]
    if not summing:
        ends += [
            pltpu.make_async_copy(r.up, r.up_sum, r.end_sem.at[0]),
            pltpu.make_async_copy(r.down, r.down_sum, r.end_sem.at[1]),
            pltpu.make_async_copy(r.attn_out_part.at[section], r.attn_out_sum, r.end_sem.at[3]),
        ]
        ends += [
            pltpu.make_async_copy(
                r.attn_in_part.at[section, :, pl.ds(j * columns, columns)], r.attn_in_sum.at[j],
                r.end_sem.at[5 + j],
            )
            for j in range(3)
        ]
    for copy in ends:
        copy.start()
    for copy in ends + latent_outs:
        copy.wait()


class Gains:
    def __init__(self, r, section, tensor, flows):
        self.r = r
        z = flows.z
        place = lax.axis_index("dp")
        near = place + SHORT * (1 - 2 * lax.rem(z, 2))
        far = place + 2 * SHORT * (1 - 2 * (z // 2))
        self.targets = [
            {"tensor": 1 - tensor}, {"section": 1 - section}, {"dp": flows.beside},
            {"dp": near}, {"dp": far},
        ]
        self.steps = list(range(len(self.targets) + 1))

    def copy(self, n):
        r = self.r
        return pltpu.make_async_remote_copy(
            src_ref=r.gain_held.at[n], dst_ref=r.gain_got.at[n], send_sem=r.gain_send.at[n],
            recv_sem=r.gain_recv.at[n], device_id=self.targets[n], device_id_type=MESH,
        )

    def tick(self):
        if not self.steps:
            return
        r, n = self.r, self.steps.pop(0)
        if n == 0:
            r.gain_held[0] = r.gain_sum[...]
        else:
            self.copy(n - 1).wait()
            value = r.gain_held[n - 1] + r.gain_got[n - 1]
            if n < len(self.targets):
                r.gain_held[n] = value
            else:
                r.gain_sum[...] = value
        if n < len(self.targets):
            self.copy(n).start()


def greet_grid(flows, others):
    barrier = pltpu.get_barrier_semaphore()

    def signal(place):
        pl.semaphore_signal(barrier, inc=1, device_id=place, device_id_type=MESH)

    for axis, index in others:
        signal({axis: index})
    signal({"dp": flows.beside})
    signal({"dp": lax.axis_index("dp") + 2 * SHORT * (1 - 2 * (flows.z // 2))})
    pl.when(flows.z < LONG - 1)(lambda: signal({"dp": flows.right}))
    pl.when(flows.z > 0)(lambda: signal({"dp": flows.left}))
    inner = jnp.logical_and(flows.z > 0, flows.z < LONG - 1)
    pl.semaphore_wait(barrier, jnp.where(inner, len(others) + 4, len(others) + 3))


def backward(kept, patch_ids):
    own, patches, width = kept["normed"].shape
    sequences, byte_count = patch_ids.shape
    columns = kept["q1"].shape[-1]
    hidden = kept["hidden"].shape[-1]
    half, half_bytes = width // 2, byte_count // 2
    sems = pltpu.SemaphoreType.DMA
    vmem = pltpu.VMEM
    rows16 = vmem((own, patches, width), b16)
    scratch = dict(
        inner=rows16,
        grad_in=rows16,
        inner_part=rows16,
        inner_got=rows16,
        normed=rows16,
        patch_norms=vmem((own, patches, LANES), f32),
        branch=rows16,
        normed_part=rows16,
        normed_got=rows16,
        source_part=vmem((own, byte_count, width), b16),
        source_got=vmem((own, half_bytes, width), b16),
        latent_got=vmem((own, patches, columns), b16),
        w_in=vmem((width, 3 * columns), b16),
        w_out=vmem((columns, width), b16),
        gain=vmem((2, 2, width), f32),
        gain_sum=vmem((4, width), f32),
        down_got=vmem((hidden, half), b16),
        down=vmem((hidden, half), b16),
        up=vmem((width, hidden), b16),
        attn_in_part=vmem((2, width, 3 * columns), b16),
        attn_out_part=vmem((2, columns, width), b16),
        big_got=vmem((width, 3 * columns), b16),
        attn_out_got=vmem((columns, width), b16),
        load_sem=sems((16,)),
        first_sem=sems((8,)),
        cross_send=sems((5, own)),
        cross_recv=sems((5, own)),
        give_send=sems((5,)),
        give_recv=sems((5,)),
        out_sem=sems((2, own)),
        out_send=sems((2, own)),
        out_recv=sems((2, own)),
        end_sem=sems((8,)),
        free_sem=pltpu.SemaphoreType.REGULAR,
    )
    slots = []
    if on_grid():
        shares = SHARES
        count = 0
        for n, (cols, long, short) in enumerate(shares):
            start = 0
            for goes_long, rows in [(1, k) for k in long] + [(0, k) for k in short]:
                name = f"s{count}"
                held = 7 * rows // LONG if goes_long else 3 * rows // SHORT
                scratch[name] = vmem((held, cols), b16)
                slots.append((n, count, goes_long, name, start, rows))
                start += rows
                count += 1
        scratch |= dict(
            flow_send=sems((count, 17)),
            flow_recv=sems((count, 17)),
            flow_near=sems((count,)),
            gain_held=vmem((5, 4, width), f32),
            gain_got=vmem((5, 4, width), f32),
            gain_send=sems((5,)),
            gain_recv=sems((5,)),
        )
    ins = [("ids", patch_ids, True)]
    ins += [("in_" + name, kept[name], False) for name in (*KEPT, *LAYERS)]
    outs = [
        ("latents", shape((sequences, patches // 2, columns), b16)),
        ("byte_grad", shape((sequences, half_bytes, half), b16)),
        ("attn_in_sum", shape((3, width, columns), b16)),
        ("attn_out_sum", shape((columns, width), b16)),
        ("gain_out", shape((4, width), f32)),
        ("up_sum", shape((width, hidden), b16)),
        ("down_sum", shape((hidden, half), b16)),
    ]

    def kernel(r):
        r.slots = {}
        for n, count, goes_long, name, start, rows in slots:
            r.slots.setdefault(n, []).append((count, goes_long, getattr(r, name), start, rows))
        backward_kernel(r)

    return named_call(kernel, ins, outs, scratch, collective_id=1)


def widen(up, attn_in, attn_out, down):
    half, hidden = up.shape[0] // 2, up.shape[1]
    steps = 8
    flat_in = attn_in.reshape(-1, attn_in.shape[2])

    def rows(array, offset=0):
        count = array.shape[0] // steps
        return pl.BlockSpec((count, array.shape[1]), lambda t: (t + offset, 0))

    def body(gate_in, up_in, in_in, out_in, down_in, up_o, in_o, out_o, down_o):
        up_o[:, 0, :] = gate_in[...].astype(f32)
        up_o[:, 1, :] = up_in[...].astype(f32)
        for src, dst in ((in_in, in_o), (out_in, out_o), (down_in, down_o)):
            dst[...] = src[...].astype(f32)

    part = half // steps
    feed = [pl.BlockSpec((part, hidden), lambda t: (t, 0))]
    feed += [pl.BlockSpec((part, hidden), lambda t: (t + steps, 0))]
    up_out, in_out, out_out, down_out = pl.pallas_call(
        body,
        grid=(steps,),
        out_shape=(
            shape((half, 2, hidden), f32), shape(flat_in.shape, f32), shape(attn_out.shape, f32),
            shape(down.shape, f32),
        ),
        in_specs=[*feed, rows(flat_in), rows(attn_out), rows(down)],
        out_specs=(
            pl.BlockSpec((part, 2, hidden), lambda t: (t, 0, 0)),
            rows(flat_in), rows(attn_out), rows(down),
        ),
        compiler_params=pltpu.CompilerParams(vmem_limit_bytes=VMEM_BYTES),
    )(up, up, flat_in, attn_out, down)
    return up_out, in_out.reshape(attn_in.shape), out_out, down_out


def swap(values, axis):
    return lax.ppermute(values, axis, [(0, 1), (1, 0)])


def sum_small(values):
    values = values + swap(values, "tensor")
    values = values + swap(values, "section")
    return lax.psum(values, "dp")


def per_device(byte_states, patch_ids, attn_in, attn_out, gains, ffn_in, ffn_out, latent_grad):
    is_first = lax.axis_index("section") == 0
    kept = forward(
        byte_states, patch_ids, attn_in, attn_out, gains, ffn_in.transpose(1, 0, 2), ffn_out,
        latent_grad,
    )
    got = backward(kept, patch_ids)
    sums = [got[name] for name in ("down_sum", "up_sum", "attn_in_sum", "attn_out_sum")]
    if not on_grid():
        sums = [lax.psum(value, "dp") for value in sums]
    down, up, in_sum, out_sum = sums
    up_out, in_sum, out_sum, down = widen(up, in_sum, out_sum, down)
    gain_sum = got["gain_out"] if on_grid() else sum_small(got["gain_out"])
    gain_out = jnp.where(is_first, gain_sum[0:2], gain_sum[2:4])
    return (
        got["latents"], got["byte_grad"], in_sum[None], out_sum[None], gain_out[None], up_out, down
    )


def solution(mesh):
    return jax.shard_map(
        per_device,
        mesh=mesh,
        in_specs=(
            P("dp", None, None),
            P("dp", None),
            P("section", None, None, "tensor"),
            P("section", "tensor", None),
            P("section", None, None),
            P(None, None, "tensor"),
            P("tensor", None),
            P("dp", None, None),
        ),
        out_specs=(
            P("dp", "section", "tensor"),
            P("dp", "tensor", "section"),
            P("section", None, None, "tensor"),
            P("section", "tensor", None),
            P("section", None, None),
            P("section", None, "tensor"),
            P("tensor", "section"),
        ),
        check_vma=False,
    )
```
